32 devices in a mesh: groups: 2 (over x), replica: 8 (over z, y), tensor: 2 (over core).
Axes of the slice: x: 2, y: 2, z: 4, core: 2. Of those that a mesh axis runs over, the one named last changes fastest.
Arguments:
- normed_input_rows: bfloat16 [8192, 8192], P(('groups', 'replica'), 'tensor'), parts along dimension 0, may hold values from -6 to 6
- key_value_weight: bfloat16 [8192, 2048], P('tensor'), may hold values from -0.0625 to 0.0625
- lowrank_left_pieces: bfloat16 [48, 8192, 64], P('replica', 'tensor'), may hold values from -0.0625 to 0.0625
- adapter_up_factors: bfloat16 [48, 64, 2048], P('replica', None, 'tensor'), may hold values from -0.75 to 0.75
- segment_adapter_ids: int32 [256], P(('groups', 'replica')), parts along dimension 0, may hold values from 0 to 47, as said below
- residency: int32 [48], replicated, may hold values from 0 to 47, as said below
Outputs:
- projected: bfloat16 [8192, 2048], P(('groups', 'replica'), 'tensor'), parts along dimension 0
The draws below stay inside these ranges and needn't reach their ends.
There are 2 independent parts, one for each index of `groups`. The reference program is written for one: setup_inputs(seed, part) draws one part's arguments, and reference() takes and returns one part's arrays. A program takes and returns all parts, laid end to end along the dimension named above; an argument that names none is the same for every part. Nothing has to cross between parts.
Inputs may be any that keep to these rules, and one draw needn't show every extreme that they name: `segment_adapter_ids`: among the 16 segments of one replica (aligned blocks of 16 entries), at most 2 name adapters with the same value of id // 6; in every draw some value of id // 6 is named by exactly 2 segments of every replica. A permutation; residency[a] // 6 equals a // 6.
All inputs are finite; a program needn't handle non-finite values.
Results may differ from the reference program's by a relative error of at most 0.005.
Values may be sent and summed in bfloat16 or wider, within the bound.
No kernel may reach another device: no remote copies, remote signals or barrier semaphores. Data moves between devices by JAX's collectives and lax.ppermute only.
A program may use at most 192 MiB of HBM per device.

```python
import jax
import jax.numpy as jnp
from jax import lax

MODEL_WIDTH = 8192
ADAPTER_RANK = 64
CAP = 2
SEG = 32
SEGS = 16
ADAPT_DEV = 6
PROJECTED_DIMS = 2048
TOKENS = 4096
NSEG = 128
ADAPTER_TOTAL = 48


def draw_segment_adapter_ids(key, part):
    key = jax.random.fold_in(key, 11)
    replicas = NSEG // SEGS
    others = SEGS - CAP
    key_hot, key_order, key_spread, key_mix, key_local = jax.random.split(key, 5)
    popular_keeper = jax.random.randint(key_hot, (), 0, replicas).astype(jnp.int32)
    base_order = jnp.tile(jnp.arange(replicas - 1, dtype=jnp.int32), (replicas, 1))
    shuffled = jax.random.permutation(key_order, base_order, axis=1, independent=True)
    other_holders = shuffled + (shuffled >= popular_keeper).astype(jnp.int32)
    minimal_entry = (others + CAP - 1) // CAP
    highest = min(others, replicas - 1)
    spread = jax.random.randint(key_spread, (replicas, 1), minimal_entry, highest + 1).astype(jnp.int32)
    column = jnp.arange(others, dtype=jnp.int32)[None, :]
    doubled = others - spread
    pick_index = jnp.where(column < CAP * doubled, column // CAP, column - doubled)
    chosen = jnp.take_along_axis(other_holders, pick_index, axis=1)
    holders = jnp.concatenate([jnp.full((replicas, CAP), popular_keeper, dtype=jnp.int32), chosen], axis=1)
    holders = jax.random.permutation(key_mix, holders, axis=1, independent=True)
    local_slot = jax.random.randint(key_local, (replicas, SEGS), 0, ADAPT_DEV).astype(jnp.int32)
    return (holders * ADAPT_DEV + local_slot).reshape(NSEG).astype(jnp.int32)


def draw_residency(key, part):
    key = jax.random.fold_in(key, 23)
    holders = ADAPTER_TOTAL // ADAPT_DEV
    base_order = jnp.tile(jnp.arange(ADAPT_DEV, dtype=jnp.int32), (holders, 1))
    shuffled = jax.random.permutation(key, base_order, axis=1, independent=True)
    start_slot = jnp.arange(holders, dtype=jnp.int32)[:, None] * ADAPT_DEV
    return (start_slot + shuffled).reshape(ADAPTER_TOTAL).astype(jnp.int32)


def steps_of(stream_key, extent, pieces, least, top_value):
    def one(dim, blocks):
        draws = jax.random.uniform(jax.random.fold_in(jax.random.fold_in(stream_key, 6), dim), (blocks,), jnp.float32, least / len(pieces), top_value / len(pieces))
        return jnp.repeat(jnp.exp(draws), extent[dim] // blocks).reshape((-1,) + (1,) * (len(extent) - dim - 1))

    factor_of = one(*pieces[0])
    for cut in pieces[1:]:
        factor_of = factor_of * one(*cut)
    return factor_of


def noise(own_key, shape, scale, bound, cuts=(), kind=jnp.bfloat16):
    values = scale * jax.random.normal(own_key, shape, jnp.float32)
    if cuts:
        values = values * steps_of(own_key, shape, cuts, -0.22, 0.18)
    return jnp.clip(values, -bound, bound).astype(kind)


def setup_inputs(seed: int = 0, part: int = 0) -> dict:
    arg_keys = jax.random.split(jax.random.key(seed), 7)
    part_keys = jax.random.split(jax.random.fold_in(arg_keys[6], part), 7)
    normed_input_rows = noise(part_keys[0], (TOKENS, MODEL_WIDTH), 1.0, 6.0, ((0, 8), (1, 2)))
    key_value_weight = noise(arg_keys[1], (MODEL_WIDTH, PROJECTED_DIMS), MODEL_WIDTH ** -0.5, 0.0625, ((0, 2),))
    lowrank_left_pieces = noise(arg_keys[2], (ADAPTER_TOTAL, MODEL_WIDTH, ADAPTER_RANK), MODEL_WIDTH ** -0.5, 0.0625, ((0, 8), (1, 2)))
    adapter_up_factors = noise(arg_keys[3], (ADAPTER_TOTAL, ADAPTER_RANK, PROJECTED_DIMS), ADAPTER_RANK ** -0.5, 0.75, ((0, 8), (2, 2)))
    segment_adapter_ids = draw_segment_adapter_ids(jax.random.fold_in(jax.random.fold_in(arg_keys[6], part), 71), part)
    residency = draw_residency(jax.random.fold_in(arg_keys[6], 71), part)
    return dict(normed_input_rows=normed_input_rows, key_value_weight=key_value_weight, lowrank_left_pieces=lowrank_left_pieces, adapter_up_factors=adapter_up_factors, segment_adapter_ids=segment_adapter_ids, residency=residency)


def reference(normed_input_rows, key_value_weight, lowrank_left_pieces, adapter_up_factors, segment_adapter_ids, residency):
    base_sum = jnp.dot(normed_input_rows, key_value_weight, preferred_element_type=jnp.float32)
    blocked_rows = normed_input_rows.reshape(NSEG, SEG, MODEL_WIDTH)
    storage = residency[segment_adapter_ids].astype(jnp.int32)

    def one_segment(inputs):
        segment_block, storage_slot_index = inputs
        rank_reduced = jnp.dot(segment_block, lowrank_left_pieces[storage_slot_index], preferred_element_type=jnp.float32).astype(jnp.bfloat16)
        return jnp.dot(rank_reduced, adapter_up_factors[storage_slot_index], preferred_element_type=jnp.float32).astype(jnp.bfloat16)

    deltas = lax.map(one_segment, (blocked_rows, storage))
    deltas = lax.optimization_barrier(deltas)
    return (base_sum + deltas.reshape(TOKENS, PROJECTED_DIMS).astype(jnp.float32)).astype(jnp.bfloat16)
```

```python
import functools

import jax
import jax.numpy as jnp
from jax import lax
from jax.experimental import pallas as pl
from jax.experimental.pallas import tpu as pltpu
from jax.sharding import PartitionSpec as P

CAP = 2
SEG = 32
LANES = 128
VMEM_LIMIT = 40 * 1024 * 1024
ANY = pl.BlockSpec(memory_space=pl.ANY)
SMEM = pl.BlockSpec(memory_space=pltpu.SMEM)


def params():
    return pltpu.CompilerParams(vmem_limit_bytes=VMEM_LIMIT)


def pick_kernel(count, seg_ref, x_ref, *rest):
    outs, sems = rest[:-1], rest[-1]
    copies = []
    for k in range(count):
        out, part = outs[k // CAP], k % CAP
        source = x_ref.at[pl.ds(pl.multiple_of(seg_ref[k] * SEG, SEG), SEG)]
        copies.append(
            pltpu.make_async_copy(source, out.at[pl.ds(part * SEG, SEG)], sems.at[k])
        )
    for copy in copies:
        copy.start()
    for copy in copies:
        copy.wait()


def pick_rows(seg_of, x):
    count = seg_of.shape[0]
    width = x.shape[1]
    return pl.pallas_call(
        functools.partial(pick_kernel, count),
        out_shape=[jax.ShapeDtypeStruct((CAP * SEG, width), x.dtype)] * (count // CAP),
        in_specs=[SMEM, ANY],
        out_specs=[ANY] * (count // CAP),
        scratch_shapes=[pltpu.SemaphoreType.DMA((count,))],
        compiler_params=params(),
        cost_estimate=pl.CostEstimate(
            flops=0, bytes_accessed=count * SEG * width * 4, transcendentals=0
        ),
        name="pick_rows",
    )(seg_of, x)


def slot_mask(slot, shape, first, slots, share, pieces):
    column = first + lax.broadcasted_iota(jnp.int32, shape, 1)
    mask = None
    for e in range(pieces):
        low = e * slots * share + slot * share
        here = (column >= low) & (column < low + share)
        mask = here if mask is None else mask | here
    return mask


def reduce_kernel(n_rows, n_left, slots, share, pieces, *refs):
    slot_ref = refs[0]
    rows = refs[1 : 1 + n_rows]
    lefts = refs[1 + n_rows : 1 + n_rows + n_left]
    out_ref, acc = refs[-2:]
    step = pl.program_id(0)
    rows_block = jnp.concatenate([ref[...] for ref in rows], axis=0)
    left_block = jnp.concatenate([ref[...] for ref in lefts], axis=0)
    product = lax.dot_general(
        rows_block, left_block, (((1,), (1,)), ((), ())), preferred_element_type=jnp.float32
    )

    @pl.when(step == 0)
    def _():
        acc[...] = product

    @pl.when(step > 0)
    def _():
        acc[...] += product

    @pl.when(step == pl.num_programs(0) - 1)
    def _():
        for i in range(n_rows * CAP):
            span = slice(i * SEG, (i + 1) * SEG)
            total = jnp.zeros((SEG, LANES), jnp.float32)
            for first in range(0, acc.shape[1], LANES):
                mask = slot_mask(slot_ref[i], (SEG, LANES), first, slots, share, pieces)
                total += jnp.where(mask, acc[span, first : first + LANES], 0.0)
            out_ref[span, :] = total


def reduce_rank(slot, rows, lefts, slots, share, name):
    width = rows[0].shape[1]
    block = min(width, 1024)
    height = len(rows) * CAP * SEG
    columns = sum(left.shape[0] for left in lefts)
    pieces = columns // (slots * share)
    specs = [pl.BlockSpec((ref.shape[0], block), lambda k: (0, k)) for ref in (*rows, *lefts)]
    return pl.pallas_call(
        functools.partial(reduce_kernel, len(rows), len(lefts), slots, share, pieces),
        grid=(width // block,),
        out_shape=jax.ShapeDtypeStruct((height, LANES), jnp.float32),
        in_specs=[SMEM, *specs],
        out_specs=pl.BlockSpec((height, LANES), lambda k: (0, 0)),
        scratch_shapes=[pltpu.VMEM((height, columns), jnp.float32)],
        compiler_params=params(),
        cost_estimate=pl.CostEstimate(
            flops=2 * height * width * columns,
            bytes_accessed=2 * width * (height + columns),
            transcendentals=0,
        ),
        name=name,
    )(slot, *rows, *lefts)


def expand_kernel(n_up, slots, share, pieces, slot_ref, mine_ref, other_ref, *refs):
    ups, outs = refs[:n_up], refs[n_up:]
    up = jnp.concatenate([ref[...] for ref in ups], axis=0)
    low = (mine_ref[...] + other_ref[...]).astype(jnp.bfloat16)
    spread = []
    for i in range(low.shape[0] // SEG):
        part = low[i * SEG : (i + 1) * SEG]
        blocks = [
            jnp.where(slot_mask(slot_ref[i], part.shape, first, slots, share, pieces), part, 0)
            for first in range(0, up.shape[0], LANES)
        ]
        spread.append(jnp.concatenate(blocks, axis=1))
    delta = jnp.dot(
        jnp.concatenate(spread, axis=0), up, preferred_element_type=jnp.float32
    ).astype(jnp.bfloat16)
    for i, out in enumerate(outs):
        out[...] = delta[i * CAP * SEG : (i + 1) * CAP * SEG]


def expand_rank(slot, mine, other, ups, slots, share, name):
    features = ups[0].shape[1]
    columns = sum(up.shape[0] for up in ups)
    pieces = columns // (slots * share)
    count = mine.shape[0] // (CAP * SEG)
    whole = pl.BlockSpec(memory_space=pltpu.VMEM)
    return pl.pallas_call(
        functools.partial(expand_kernel, len(ups), slots, share, pieces),
        out_shape=[jax.ShapeDtypeStruct((CAP * SEG, features), jnp.bfloat16)] * count,
        in_specs=[SMEM, whole, whole] + [whole] * len(ups),
        out_specs=[whole] * count,
        compiler_params=params(),
        cost_estimate=pl.CostEstimate(
            flops=2 * mine.shape[0] * columns * features,
            bytes_accessed=2 * features * (columns + mine.shape[0]) + 8 * mine.size,
            transcendentals=0,
        ),
        name=name,
    )(slot, mine, other, *ups)


def join_kernel(seg_ref, valid_ref, mine_ref, other_ref, *refs):
    deltas, out_ref = refs[:-1], refs[-1]
    for k in range(len(deltas) * CAP):
        part = k % CAP

        @pl.when(valid_ref[k] > 0)
        def _():
            span = pl.ds(pl.multiple_of(seg_ref[k] * SEG, SEG), SEG)
            base = mine_ref[span, :] + other_ref[span, :]
            delta = deltas[k // CAP][part * SEG : (part + 1) * SEG, :]
            out_ref[span, :] = (base + delta.astype(jnp.float32)).astype(out_ref.dtype)


def join(seg_of, valid, mine, other, deltas):
    height, features = mine.shape
    block = min(features, 256)
    tall = pl.BlockSpec((height, block), lambda j: (0, j))
    short = pl.BlockSpec((CAP * SEG, block), lambda j: (0, j))
    return pl.pallas_call(
        join_kernel,
        grid=(features // block,),
        out_shape=jax.ShapeDtypeStruct((height, features), jnp.bfloat16),
        in_specs=[SMEM, SMEM, tall, tall] + [short] * len(deltas),
        out_specs=tall,
        compiler_params=params(),
        cost_estimate=pl.CostEstimate(
            flops=2 * height * features, bytes_accessed=12 * height * features, transcendentals=0
        ),
        name="join",
    )(seg_of, valid, mine, other, *deltas)


def swap(value, axis, distance):
    count = lax.axis_size(axis)
    return lax.ppermute(value, axis, [(i, i ^ distance) for i in range(count)])


def on_device(x, weight, lefts, ups, ids, residency):
    replicas = lax.axis_size("replica")
    groups = lax.axis_size("groups")
    half = replicas // 2
    me = lax.axis_index("replica")
    group = lax.axis_index("groups")
    core = lax.axis_index("tensor")
    slots, _, rank = lefts.shape
    share = rank // groups
    width = x.shape[1]
    features = ups.shape[2]

    segs = ids.shape[0]
    holder = ids // slots
    earlier = jnp.arange(segs)[None, :] < jnp.arange(segs)[:, None]
    position = jnp.sum((holder[:, None] == holder[None, :]) & earlier, axis=1)
    stored = jnp.sum(
        jnp.where(ids[:, None] == jnp.arange(residency.shape[0])[None, :], residency[None, :], 0),
        axis=1,
    )
    stored = stored - holder * slots
    offset = jnp.arange(half)
    wanted = jnp.stack([me ^ offset, me ^ offset ^ half])
    match = (holder == wanted[..., None, None]) & (
        position == jnp.arange(CAP)[None, None, :, None]
    )
    seg_of = jnp.sum(jnp.where(match, jnp.arange(segs), 0), axis=-1).astype(jnp.int32)
    slot_of = jnp.sum(jnp.where(match, stored, 0), axis=-1).astype(jnp.int32)
    valid = jnp.any(match, axis=-1).astype(jnp.int32).reshape(-1)
    slot_in = [slot_of[:, 0]] + [swap(slot_of[:, d], "replica", d) for d in range(1, half)]
    slot_in = jnp.stack(slot_in, axis=1).reshape(2, half * CAP)

    left_rows = jnp.swapaxes(lefts, 1, 2)
    left_share = lax.dynamic_slice(left_rows, (0, group * share, 0), (slots, share, width))
    up_share = lax.dynamic_slice(ups, (0, group * share, 0), (slots, share, features))
    chunk = 2
    left_in = [
        swap(left_share[c : c + chunk].reshape(chunk * share, width), "replica", half)
        for c in range(0, slots, chunk)
    ]
    up_in = swap(up_share.reshape(slots * share, features), "replica", half)
    left_all = list(left_in)
    up_all = [up_in]
    for e in range(1, groups):
        left_all += [swap(piece, "groups", e) for piece in left_in]
        up_all.append(swap(up_in, "groups", e))

    picked = pick_rows(seg_of.reshape(-1), x)
    rows_in = [
        [picked[kind * half]]
        + [swap(picked[kind * half + d], "replica", d) for d in range(1, half)]
        for kind in range(2)
    ]

    def part(which):
        columns = lax.dynamic_slice(weight, (0, which * features), (weight.shape[0], features))
        return jnp.dot(x, columns, preferred_element_type=jnp.float32)

    base_other = swap(part(1 - core), "tensor", 1)
    base_mine = part(core)

    own_left = [left_rows.reshape(slots * rank, width)]
    own_up = [ups.reshape(slots * rank, features)]
    deltas = []
    for kind, (left, up, held, name) in enumerate(
        [(own_left, own_up, rank, "own"), (left_all, up_all, share, "taken")]
    ):
        low = reduce_rank(slot_in[kind], rows_in[kind], left, slots, held, "reduce_" + name)
        other = swap(low, "tensor", 1)
        terms = expand_rank(slot_in[kind], low, other, up, slots, held, "expand_" + name)
        deltas.append(terms[0])
        deltas += [swap(terms[d], "replica", d) for d in range(1, half)]
    return join(seg_of.reshape(-1), valid, base_mine, base_other, deltas)


def solution(mesh):
    placed = (
        P(("groups", "replica"), "tensor"),
        P("tensor", None),
        P("replica", "tensor", None),
        P("replica", None, "tensor"),
        P(("groups", "replica")),
        P(),
    )
    return jax.shard_map(
        on_device,
        mesh=mesh,
        in_specs=placed,
        out_specs=P(("groups", "replica"), "tensor"),
        check_vma=False,
    )
```

```python
import functools

import jax
import jax.numpy as jnp
from jax import lax
from jax.experimental import pallas as pl
from jax.experimental.pallas import tpu as pltpu
from jax.sharding import PartitionSpec as P

CAP = 2
SEG = 32
LANES = 128
PAIR = CAP * SEG
VMEM_LIMIT = 60 * 1024 * 1024
HBM = pl.BlockSpec(memory_space=pltpu.HBM)
SMEM = pl.BlockSpec(memory_space=pltpu.SMEM)


def params():
    return pltpu.CompilerParams(vmem_limit_bytes=VMEM_LIMIT)


def pick_kernel(replicas, half, slots, me_ref, ids_ref, residency_ref, x_ref, *rest):
    outs, seg_out = rest[:half], rest[half]
    seg_ref, slot_ref, count_ref, tags, sems = rest[half + 1 :]
    width = x_ref.shape[1]
    for h in range(replicas):
        count_ref[h] = 0
        for p in range(CAP):
            seg_ref[h * CAP + p] = -1
            slot_ref[h * CAP + p] = 0
    for s in range(ids_ref.shape[0]):
        adapter = ids_ref[s]
        holder = adapter // slots
        place = holder * CAP + count_ref[holder]
        count_ref[holder] = count_ref[holder] + 1
        seg_ref[place] = s
        slot_ref[place] = residency_ref[adapter] - holder * slots
    me = me_ref[0]
    copies = []
    for d in range(half):
        for kind in range(2):
            for p in range(CAP):
                place = (me ^ (d + kind * half)) * CAP + p
                seg = seg_ref[place]
                seg_out[(kind * half + d) * CAP + p] = seg
                span = pl.ds((kind * CAP + p) * SEG, SEG)
                start = pl.multiple_of(jnp.maximum(seg, 0) * SEG, SEG)
                copy = pltpu.make_async_copy(
                    x_ref.at[pl.ds(start, SEG)],
                    outs[d].at[span, pl.ds(0, width)],
                    sems.at[len(copies)],
                )
                copy.start()
                copies.append(copy)
                slot = slot_ref[place].astype(jnp.float32)
                tags[d, span, :] = jnp.full((SEG, LANES), slot, jnp.float32).astype(tags.dtype)
    for d in range(half):
        copy = pltpu.make_async_copy(
            tags.at[d], outs[d].at[:, pl.ds(width, LANES)], sems.at[len(copies)]
        )
        copy.start()
        copies.append(copy)
    for copy in copies:
        copy.wait()


def pick_rows(me, ids, residency, x, replicas, half, slots):
    width = x.shape[1]
    count = 2 * half * CAP
    return pl.pallas_call(
        functools.partial(pick_kernel, replicas, half, slots),
        out_shape=[jax.ShapeDtypeStruct((2 * PAIR, width + LANES), x.dtype)] * half
        + [jax.ShapeDtypeStruct((count,), jnp.int32)],
        in_specs=[SMEM, SMEM, SMEM, HBM],
        out_specs=[HBM] * half + [SMEM],
        scratch_shapes=[
            pltpu.SMEM((replicas * CAP,), jnp.int32),
            pltpu.SMEM((replicas * CAP,), jnp.int32),
            pltpu.SMEM((replicas,), jnp.int32),
            pltpu.VMEM((half, 2 * PAIR, LANES), x.dtype),
            pltpu.SemaphoreType.DMA((count + half,)),
        ],
        compiler_params=params(),
        cost_estimate=pl.CostEstimate(
            flops=0, bytes_accessed=count * SEG * width * 4, transcendentals=0
        ),
        name="pick_rows",
    )(me, ids, residency, x)


def slot_mask(tags, first, slots, share):
    lane = lax.broadcasted_iota(jnp.int32, (1, LANES), 1)
    column_slot = jnp.zeros((1, LANES), jnp.float32)
    for j in range(0, LANES, share):
        slot = ((first + j) // share) % slots
        column_slot = jnp.where(lane >= j, float(slot), column_slot)
    return tags == column_slot


def reduce_kernel(n_rows, n_left, slots, share, *refs):
    rows = refs[:n_rows]
    tags = refs[n_rows : 2 * n_rows]
    lefts = refs[2 * n_rows : 2 * n_rows + n_left]
    out_ref, acc = refs[-2:]
    step = pl.program_id(0)
    rows_block = jnp.concatenate([ref[...] for ref in rows], axis=0)
    left_block = jnp.concatenate([ref[...] for ref in lefts], axis=0)
    product = lax.dot_general(
        rows_block, left_block, (((1,), (1,)), ((), ())), preferred_element_type=jnp.float32
    )

    @pl.when(step == 0)
    def _():
        acc[...] = product

    @pl.when(step > 0)
    def _():
        acc[...] += product

    @pl.when(step == pl.num_programs(0) - 1)
    def _():
        tag = jnp.concatenate([ref[...] for ref in tags], axis=0).astype(jnp.float32)
        total = jnp.zeros(out_ref.shape, jnp.float32)
        for first in range(0, acc.shape[1], LANES):
            mask = slot_mask(tag, first, slots, share)
            total += jnp.where(mask, acc[:, first : first + LANES], 0.0)
        out_ref[...] = total


def reduce_rank(kind, rows, lefts, slots, share, name):
    width = lefts[0].shape[1]
    block = min(width, 1024)
    height = len(rows) * PAIR
    columns = sum(left.shape[0] for left in lefts)
    last = width // LANES
    return pl.pallas_call(
        functools.partial(reduce_kernel, len(rows), len(lefts), slots, share),
        grid=(width // block,),
        out_shape=jax.ShapeDtypeStruct((height, LANES), jnp.float32),
        in_specs=[pl.BlockSpec((PAIR, block), lambda k: (kind, k))] * len(rows)
        + [pl.BlockSpec((PAIR, LANES), lambda k: (kind, last))] * len(rows)
        + [pl.BlockSpec((left.shape[0], block), lambda k: (0, k)) for left in lefts],
        out_specs=pl.BlockSpec((height, LANES), lambda k: (0, 0)),
        scratch_shapes=[pltpu.VMEM((height, columns), jnp.float32)],
        compiler_params=params(),
        cost_estimate=pl.CostEstimate(
            flops=2 * height * width * columns,
            bytes_accessed=2 * width * (height + columns),
            transcendentals=0,
        ),
        name=name,
    )(*rows, *rows, *lefts)


def expand_kernel(n_rows, n_up, slots, share, mine_ref, other_ref, *refs):
    tags, ups, outs = refs[:n_rows], refs[n_rows : n_rows + n_up], refs[n_rows + n_up :]
    tag = jnp.concatenate([ref[...] for ref in tags], axis=0).astype(jnp.float32)
    up = jnp.concatenate([ref[...] for ref in ups], axis=0)
    low = (mine_ref[...] + other_ref[...]).astype(jnp.bfloat16).astype(jnp.float32)
    spread = [
        jnp.where(slot_mask(tag, first, slots, share), low, 0.0).astype(jnp.bfloat16)
        for first in range(0, up.shape[0], LANES)
    ]
    delta = jnp.dot(
        jnp.concatenate(spread, axis=1), up, preferred_element_type=jnp.float32
    ).astype(jnp.bfloat16)
    for i, out in enumerate(outs):
        out[...] = delta[i * PAIR : (i + 1) * PAIR]


def expand_rank(kind, rows, mine, other, ups, slots, share, name):
    features = ups[0].shape[1]
    block = min(features, 512)
    columns = sum(up.shape[0] for up in ups)
    last = rows[0].shape[1] // LANES - 1
    low = pl.BlockSpec(mine.shape, lambda j: (0, 0))
    return pl.pallas_call(
        functools.partial(expand_kernel, len(rows), len(ups), slots, share),
        grid=(features // block,),
        out_shape=[jax.ShapeDtypeStruct((PAIR, features), jnp.bfloat16)] * len(rows),
        in_specs=[low, low]
        + [pl.BlockSpec((PAIR, LANES), lambda j: (kind, last))] * len(rows)
        + [pl.BlockSpec((up.shape[0], block), lambda j: (0, j)) for up in ups],
        out_specs=[pl.BlockSpec((PAIR, block), lambda j: (0, j))] * len(rows),
        compiler_params=params(),
        cost_estimate=pl.CostEstimate(
            flops=2 * mine.shape[0] * columns * features,
            bytes_accessed=2 * features * (columns + mine.shape[0]) + 8 * mine.size,
            transcendentals=0,
        ),
        name=name,
    )(mine, other, *rows, *ups)


def join_kernel(seg_ref, base_ref, *refs):
    deltas, out_ref = refs[:-1], refs[-1]
    for k in range(len(deltas) * CAP):
        part = k % CAP

        @pl.when(seg_ref[k] >= 0)
        def _():
            span = pl.ds(pl.multiple_of(seg_ref[k] * SEG, SEG), SEG)
            delta = deltas[k // CAP][part * SEG : (part + 1) * SEG, :]
            out_ref[span, :] = (base_ref[span, :] + delta.astype(jnp.float32)).astype(
                out_ref.dtype
            )


def join(seg_of, base, deltas):
    height, features = base.shape
    block = min(features, 256)
    tall = pl.BlockSpec((height, block), lambda j: (0, j))
    short = pl.BlockSpec((PAIR, block), lambda j: (0, j))
    return pl.pallas_call(
        join_kernel,
        grid=(features // block,),
        out_shape=jax.ShapeDtypeStruct((height, features), jnp.bfloat16),
        in_specs=[SMEM, tall] + [short] * len(deltas),
        out_specs=tall,
        compiler_params=params(),
        cost_estimate=pl.CostEstimate(
            flops=height * features, bytes_accessed=8 * height * features, transcendentals=0
        ),
        name="join",
    )(seg_of, base, *deltas)


def swap(value, axis, distance):
    count = lax.axis_size(axis)
    return lax.ppermute(value, axis, [(i, i ^ distance) for i in range(count)])


def on_device(x, weight, lefts, ups, ids, residency):
    replicas = lax.axis_size("replica")
    groups = lax.axis_size("groups")
    half = replicas // 2
    me = lax.axis_index("replica").astype(jnp.int32)
    group = lax.axis_index("groups")
    core = lax.axis_index("tensor")
    slots, width, rank = lefts.shape
    share = rank // groups
    features = ups.shape[2]

    *picked, seg_of = pick_rows(me.reshape(1), ids, residency, x, replicas, half, slots)
    rows = [picked[0]] + [swap(picked[d], "replica", d) for d in range(1, half)]

    left_rows = jnp.swapaxes(lefts, 1, 2)
    late_left_rows, _ = lax.optimization_barrier((left_rows, picked[0]))
    left_share = lax.dynamic_slice(late_left_rows, (0, group * share, 0), (slots, share, width))
    x, left_share = lax.optimization_barrier((x, left_share))
    late_ups, rows[1] = lax.optimization_barrier((ups, rows[1]))
    up_share = lax.dynamic_slice(late_ups, (0, group * share, 0), (slots, share, features))
    chunk = 2
    left_in = [
        swap(left_share[c : c + chunk].reshape(chunk * share, width), "replica", half)
        for c in range(0, slots, chunk)
    ]
    up_in = swap(up_share.reshape(slots * share, features), "replica", half)
    left_all = list(left_in)
    up_all = [up_in]
    for e in range(1, groups):
        left_all += [swap(piece, "groups", e) for piece in left_in]
        up_all.append(swap(up_in, "groups", e))

    def part(which):
        columns = lax.dynamic_slice(weight, (0, which * features), (weight.shape[0], features))
        return jnp.dot(x, columns, preferred_element_type=jnp.float32)

    base = part(core) + swap(part(1 - core), "tensor", 1)

    own_left = [left_rows.reshape(slots * rank, width)]
    own_up = [ups.reshape(slots * rank, features)]
    deltas = []
    for kind, (left, up, held, name) in enumerate(
        [(own_left, own_up, rank, "own"), (left_all, up_all, share, "taken")]
    ):
        low = reduce_rank(kind, rows, left, slots, held, "reduce_" + name)
        if kind:
            low, base = lax.optimization_barrier((low, base))
        other = swap(low, "tensor", 1)
        terms = expand_rank(kind, rows, low, other, up, slots, held, "expand_" + name)
        deltas.append(terms[0])
        deltas += [swap(terms[d], "replica", d) for d in range(1, half)]
    return join(seg_of, base, deltas)


def solution(mesh):
    placed = (
        P(("groups", "replica"), "tensor"),
        P("tensor", None),
        P("replica", "tensor", None),
        P("replica", None, "tensor"),
        P(("groups", "replica")),
        P(),
    )
    return jax.shard_map(
        on_device,
        mesh=mesh,
        in_specs=placed,
        out_specs=P(("groups", "replica"), "tensor"),
        check_vma=False,
    )
```

```python
import functools

import jax
import jax.numpy as jnp
from jax import lax
from jax.experimental import pallas as pl
from jax.experimental.pallas import tpu as pltpu
from jax.sharding import PartitionSpec as P

CAP = 2
SEG = 32
LANES = 128
PAIR = CAP * SEG
VMEM_LIMIT = 60 * 1024 * 1024
HBM = pl.BlockSpec(memory_space=pltpu.HBM)
SMEM = pl.BlockSpec(memory_space=pltpu.SMEM)


def params():
    return pltpu.CompilerParams(vmem_limit_bytes=VMEM_LIMIT)


def pick_kernel(replicas, half, slots, me_ref, ids_ref, residency_ref, x_ref, *rest):
    outs, seg_out = rest[:half], rest[half]
    seg_ref, slot_ref, count_ref, staged, tags, in_sems, sems = rest[half + 1 :]
    width = x_ref.shape[1]
    segs = ids_ref.shape[0]
    arrivals = []
    for s in range(segs):
        span = pl.ds(s * SEG, SEG)
        arrivals.append(pltpu.make_async_copy(x_ref.at[span], staged.at[span], in_sems.at[s]))
        arrivals[-1].start()
    for h in range(replicas):
        count_ref[h] = 0
        for p in range(CAP):
            seg_ref[h * CAP + p] = -1
            slot_ref[h * CAP + p] = 0
    for s in range(segs):
        adapter = ids_ref[s]
        holder = adapter // slots
        place = holder * CAP + count_ref[holder]
        count_ref[holder] = count_ref[holder] + 1
        seg_ref[place] = s
        slot_ref[place] = residency_ref[adapter] - holder * slots
    me = me_ref[0]
    for arrival in arrivals:
        arrival.wait()
    copies = []
    for d in range(half):
        for kind in range(2):
            for p in range(CAP):
                place = (me ^ (d + kind * half)) * CAP + p
                seg = seg_ref[place]
                seg_out[(kind * half + d) * CAP + p] = seg
                span = pl.ds((kind * CAP + p) * SEG, SEG)
                start = pl.multiple_of(jnp.maximum(seg, 0) * SEG, SEG)
                copy = pltpu.make_async_copy(
                    staged.at[pl.ds(start, SEG)],
                    outs[d].at[span, pl.ds(0, width)],
                    sems.at[len(copies)],
                )
                copy.start()
                copies.append(copy)
                slot = slot_ref[place].astype(jnp.float32)
                tags[d, span, :] = jnp.full((SEG, LANES), slot, jnp.float32).astype(tags.dtype)
    for d in range(half):
        copy = pltpu.make_async_copy(
            tags.at[d], outs[d].at[:, pl.ds(width, LANES)], sems.at[len(copies)]
        )
        copy.start()
        copies.append(copy)
    for copy in copies:
        copy.wait()


def pick_rows(me, ids, residency, x, replicas, half, slots):
    width = x.shape[1]
    count = 2 * half * CAP
    return pl.pallas_call(
        functools.partial(pick_kernel, replicas, half, slots),
        out_shape=[jax.ShapeDtypeStruct((2 * PAIR, width + LANES), x.dtype)] * half
        + [jax.ShapeDtypeStruct((count,), jnp.int32)],
        in_specs=[SMEM, SMEM, SMEM, HBM],
        out_specs=[HBM] * half + [SMEM],
        scratch_shapes=[
            pltpu.SMEM((replicas * CAP,), jnp.int32),
            pltpu.SMEM((replicas * CAP,), jnp.int32),
            pltpu.SMEM((replicas,), jnp.int32),
            pltpu.VMEM(x.shape, x.dtype),
            pltpu.VMEM((half, 2 * PAIR, LANES), x.dtype),
            pltpu.SemaphoreType.DMA((ids.shape[0],)),
            pltpu.SemaphoreType.DMA((count + half,)),
        ],
        compiler_params=params(),
        cost_estimate=pl.CostEstimate(
            flops=0, bytes_accessed=count * SEG * width * 4, transcendentals=0
        ),
        name="pick_rows",
    )(me, ids, residency, x)


def slot_mask(tags, first, slots, share):
    lane = lax.broadcasted_iota(jnp.int32, (1, LANES), 1)
    column_slot = jnp.zeros((1, LANES), jnp.float32)
    for j in range(0, LANES, share):
        slot = ((first + j) // share) % slots
        column_slot = jnp.where(lane >= j, float(slot), column_slot)
    return tags == column_slot


def gather_parts(refs, counts):
    total, at = None, 0
    for count in counts:
        whole = jnp.concatenate([ref[...] for ref in refs[at : at + count]], axis=0)
        total = whole if total is None else total + whole
        at += count
    return total


def reduce_kernel(n_rows, counts, slots, share, *refs):
    rows = refs[:n_rows]
    tags = refs[n_rows : 2 * n_rows]
    lefts = refs[2 * n_rows : -2]
    out_ref, acc = refs[-2:]
    step = pl.program_id(0)
    rows_block = jnp.concatenate([ref[...] for ref in rows], axis=0)
    left_block = gather_parts(lefts, counts)
    product = lax.dot_general(
        rows_block, left_block, (((1,), (1,)), ((), ())), preferred_element_type=jnp.float32
    )

    @pl.when(step == 0)
    def _():
        acc[...] = product

    @pl.when(step > 0)
    def _():
        acc[...] += product

    @pl.when(step == pl.num_programs(0) - 1)
    def _():
        tag = jnp.concatenate([ref[...] for ref in tags], axis=0).astype(jnp.float32)
        total = jnp.zeros(out_ref.shape, jnp.float32)
        for first in range(0, acc.shape[1], LANES):
            mask = slot_mask(tag, first, slots, share)
            total += jnp.where(mask, acc[:, first : first + LANES], 0.0)
        out_ref[...] = total


def reduce_rank(kind, rows, sources, slots, share, name):
    counts = [len(source) for source in sources]
    lefts = [left for source in sources for left in source]
    width = rows[0].shape[1] - LANES
    block = min(width, 1024)
    height = len(rows) * PAIR
    columns = sum(left.shape[0] for left in sources[0])
    last = width // LANES
    return pl.pallas_call(
        functools.partial(reduce_kernel, len(rows), counts, slots, share),
        grid=(width // block,),
        out_shape=jax.ShapeDtypeStruct((height, LANES), jnp.float32),
        in_specs=[pl.BlockSpec((PAIR, block), lambda k: (kind, k))] * len(rows)
        + [pl.BlockSpec((PAIR, LANES), lambda k: (kind, last))] * len(rows)
        + [pl.BlockSpec((left.shape[0], block), lambda k: (0, k)) for left in lefts],
        out_specs=pl.BlockSpec((height, LANES), lambda k: (0, 0)),
        scratch_shapes=[pltpu.VMEM((height, columns), jnp.float32)],
        compiler_params=params(),
        cost_estimate=pl.CostEstimate(
            flops=2 * height * width * columns,
            bytes_accessed=2 * width * (height + columns),
            transcendentals=0,
        ),
        name=name,
    )(*rows, *rows, *lefts)


def expand_kernel(n_rows, counts, slots, share, mine_ref, other_ref, *refs):
    n_up = sum(counts)
    tags, ups, outs = refs[:n_rows], refs[n_rows : n_rows + n_up], refs[n_rows + n_up :]
    tag = jnp.concatenate([ref[...] for ref in tags], axis=0).astype(jnp.float32)
    up = gather_parts(ups, counts)
    low = (mine_ref[...] + other_ref[...]).astype(jnp.bfloat16).astype(jnp.float32)
    spread = [
        jnp.where(slot_mask(tag, first, slots, share), low, 0.0).astype(jnp.bfloat16)
        for first in range(0, up.shape[0], LANES)
    ]
    delta = jnp.dot(
        jnp.concatenate(spread, axis=1), up, preferred_element_type=jnp.float32
    ).astype(jnp.bfloat16)
    for i, out in enumerate(outs):
        out[...] = delta[i * PAIR : (i + 1) * PAIR]


def expand_rank(kind, rows, mine, other, sources, features, slots, share, name):
    counts = [len(source) for source in sources]
    ups = [up for source in sources for up in source]
    block = min(features, 512)
    columns = sum(up.shape[0] for up in sources[0])

    def up_spec(up):
        first = (up.shape[1] - features) // block
        return pl.BlockSpec((up.shape[0], block), lambda j: (0, first + j))

    last = rows[0].shape[1] // LANES - 1
    low = pl.BlockSpec(mine.shape, lambda j: (0, 0))
    return pl.pallas_call(
        functools.partial(expand_kernel, len(rows), counts, slots, share),
        grid=(features // block,),
        out_shape=[jax.ShapeDtypeStruct((PAIR, features), jnp.bfloat16)] * len(rows),
        in_specs=[low, low]
        + [pl.BlockSpec((PAIR, LANES), lambda j: (kind, last))] * len(rows)
        + [up_spec(up) for up in ups],
        out_specs=[pl.BlockSpec((PAIR, block), lambda j: (0, j))] * len(rows),
        compiler_params=params(),
        cost_estimate=pl.CostEstimate(
            flops=2 * mine.shape[0] * columns * features,
            bytes_accessed=2 * features * (columns + mine.shape[0]) + 8 * mine.size,
            transcendentals=0,
        ),
        name=name,
    )(mine, other, *rows, *ups)


def join_kernel(seg_ref, base_ref, *refs):
    deltas, out_ref = refs[:-1], refs[-1]
    for k in range(len(deltas) * CAP):
        part = k % CAP

        @pl.when(seg_ref[k] >= 0)
        def _():
            span = pl.ds(pl.multiple_of(seg_ref[k] * SEG, SEG), SEG)
            delta = deltas[k // CAP][part * SEG : (part + 1) * SEG, :]
            out_ref[span, :] = (base_ref[span, :] + delta.astype(jnp.float32)).astype(
                out_ref.dtype
            )


def join(seg_of, base, deltas):
    height, features = base.shape
    block = min(features, 256)
    tall = pl.BlockSpec((height, block), lambda j: (0, j))
    short = pl.BlockSpec((PAIR, block), lambda j: (0, j))
    return pl.pallas_call(
        join_kernel,
        grid=(features // block,),
        out_shape=jax.ShapeDtypeStruct((height, features), jnp.bfloat16),
        in_specs=[SMEM, tall] + [short] * len(deltas),
        out_specs=tall,
        compiler_params=params(),
        cost_estimate=pl.CostEstimate(
            flops=height * features, bytes_accessed=8 * height * features, transcendentals=0
        ),
        name="join",
    )(seg_of, base, *deltas)


def swap(value, axis, distance):
    count = lax.axis_size(axis)
    return lax.ppermute(value, axis, [(i, i ^ distance) for i in range(count)])


def swap_some(value, senders, group_distance, replica_distance):
    groups, replicas = lax.axis_size("groups"), lax.axis_size("replica")
    pairs = [
        (g * replicas + r, (g ^ group_distance) * replicas + (r ^ replica_distance))
        for g in range(groups)
        for r in senders
    ]
    return lax.ppermute(value, ("groups", "replica"), pairs)


def on_device(x, weight, lefts, ups, ids, residency):
    replicas = lax.axis_size("replica")
    groups = lax.axis_size("groups")
    half = replicas // 2
    me = lax.axis_index("replica").astype(jnp.int32)
    group = lax.axis_index("groups")
    slots, width, rank = lefts.shape
    share = rank // groups
    features = ups.shape[2]
    inner = range(replicas // 4, 3 * replicas // 4)
    outer = [r for r in range(replicas) if r not in inner]

    *picked, seg_of = pick_rows(me.reshape(1), ids, residency, x, replicas, half, slots)
    rows = [picked[0]] + [swap(picked[d], "replica", d) for d in range(1, half)]

    left_rows = jnp.swapaxes(lefts, 1, 2)

    def shares(left, up):
        return (
            lax.dynamic_slice(left, (0, group * share, 0), (slots, share, width)),
            lax.dynamic_slice(up, (0, group * share, 0), (slots, share, features)),
        )

    left_share, up_share = shares(left_rows, ups)
    early_up = swap_some(up_share.reshape(slots * share, features), inner, 0, half)
    early_left = swap_some(left_share.reshape(slots * share, width), inner, 0, half)

    late_x, early_up, _ = lax.optimization_barrier((x, early_up, picked[0]))
    partial_sum = jnp.dot(late_x, weight, preferred_element_type=jnp.float32)

    rows, early_left, early_up, left_rows, ups, partial_sum = lax.optimization_barrier(
        (rows, early_left, early_up, left_rows, ups, partial_sum)
    )
    left_share, up_share = shares(left_rows, ups)
    chunk = 2
    left_in = [
        swap_some(left_share[c : c + chunk].reshape(chunk * share, width), outer, 0, half)
        for c in range(0, slots, chunk)
    ]
    up_in = swap_some(up_share.reshape(slots * share, features), outer, 0, half)
    early_lefts, early_ups = [early_left], [early_up]
    late_lefts, late_ups = list(left_in), [up_in]
    for e in range(1, groups):
        early_lefts.append(swap_some(early_left, outer, e, 0))
        early_ups.append(swap_some(early_up, outer, e, 0))
        late_lefts += [swap_some(piece, inner, e, 0) for piece in left_in]
        late_ups.append(swap_some(up_in, inner, e, 0))
    base = lax.psum_scatter(partial_sum, "tensor", scatter_dimension=1, tiled=True)

    own_left = [[left_rows.reshape(slots * rank, width)]]
    own_up = [[ups.reshape(slots * rank, features)]]
    deltas = []
    for kind, (left, up, held, name) in enumerate(
        [
            (own_left, own_up, rank, "own"),
            ([early_lefts, late_lefts], [early_ups, late_ups], share, "taken"),
        ]
    ):
        low = reduce_rank(kind, rows, left, slots, held, "reduce_" + name)
        if kind:
            low, base = lax.optimization_barrier((low, base))
        other = swap(low, "tensor", 1)
        terms = expand_rank(
            kind, rows, low, other, up, features, slots, held, "expand_" + name
        )
        deltas.append(terms[0])
        deltas += [swap(terms[d], "replica", d) for d in range(1, half)]
    return join(seg_of, base, deltas)


def solution(mesh):
    placed = (
        P(("groups", "replica"), "tensor"),
        P("tensor", None),
        P("replica", "tensor", None),
        P("replica", None, "tensor"),
        P(("groups", "replica")),
        P(),
    )
    return jax.shard_map(
        on_device,
        mesh=mesh,
        in_specs=placed,
        out_specs=P(("groups", "replica"), "tensor"),
        check_vma=False,
    )
```

```python
import functools

import jax
import jax.numpy as jnp
from jax import lax
from jax.experimental import pallas as pl
from jax.experimental.pallas import tpu as pltpu
from jax.sharding import PartitionSpec as P

CAP = 2
SEG = 32
LANES = 128
PAIR = CAP * SEG
VMEM_LIMIT = 60 * 1024 * 1024
HBM = pl.BlockSpec(memory_space=pltpu.HBM)
SMEM = pl.BlockSpec(memory_space=pltpu.SMEM)
VMEM = pl.BlockSpec(memory_space=pltpu.VMEM)


class Plan:
    def __init__(self, replicas, groups, slots, rank, width, features):
        self.replicas, self.groups, self.slots, self.rank = replicas, groups, slots, rank
        self.width, self.features = width, features
        self.half = replicas // 2
        self.turn = self.half // 2
        self.near = [d for d in range(self.half) if not d & self.turn]
        self.cross = [d for d in range(self.half) if d & self.turn]
        self.share = rank // groups
        self.left_rows = slots * self.share
        beside = width // features
        self.up_rows = -(-self.left_rows // (beside * 16)) * 16
        self.up_piece = self.left_rows // PAIR
        self.up_first = self.left_rows % PAIR
        assert self.up_first + self.up_rows <= PAIR
        self.pieces = self.up_piece + 1
        self.wide = max(len(self.cross), -(-self.pieces // 2))
        self.narrow = max(2 * len(self.cross), self.pieces)
        self.outer = [r for r in range(replicas) if self.is_outer(r)]
        self.inner = [r for r in range(replicas) if not self.is_outer(r)]

    def is_outer(self, r):
        return (r < self.turn) or (r >= self.replicas - self.turn)

    def up_columns(self):
        for j, row in enumerate(range(0, self.left_rows, self.up_rows)):
            yield row, min(self.up_rows, self.left_rows - row), j * self.features

    def left_spans(self):
        for piece in range(self.pieces):
            rows = min(PAIR, self.left_rows - piece * PAIR)
            if rows > 0:
                yield piece, rows


def params():
    return pltpu.CompilerParams(vmem_limit_bytes=VMEM_LIMIT)


def am_outer(plan):
    me = lax.axis_index("replica")
    return (me < plan.turn) | (me >= plan.replicas - plan.turn)


def of_wide(refs, piece):
    return refs[piece // 2].at[pl.ds((piece % 2) * PAIR, PAIR)]


def lay_kernel(plan, ids_ref, residency_ref, x_ref, left_ref, up_ref, *rest):
    n_near, n_wide, n_narrow = len(plan.near), plan.wide, plan.narrow
    near, rest = rest[:n_near], rest[n_near:]
    wide, rest = rest[:n_wide], rest[n_wide:]
    narrow, rest = rest[:n_narrow], rest[n_narrow:]
    seg_out, seg_ref, slot_ref, count_ref, staged, tags, left, up, in_sems, sems = rest
    half, slots, width, share = plan.half, plan.slots, plan.width, plan.share
    segs = ids_ref.shape[0]
    me = lax.axis_index("replica")
    first = pl.multiple_of(lax.axis_index("groups") * share, share)

    arrivals = []

    def arrive(source, target):
        arrivals.append(pltpu.make_async_copy(source, target, in_sems.at[len(arrivals)]))
        arrivals[-1].start()

    for s in range(segs):
        span = pl.ds(s * SEG, SEG)
        arrive(x_ref.at[span], staged.at[span])
    for slot in range(slots):
        span = pl.ds(slot * share, share)
        arrive(left_ref.at[slot, pl.ds(first, share)], left.at[span])
        arrive(up_ref.at[slot, pl.ds(first, share)], up.at[span])

    for h in range(plan.replicas):
        count_ref[h] = 0
        for p in range(CAP):
            seg_ref[h * CAP + p] = -1
            slot_ref[h * CAP + p] = 0
    for s in range(segs):
        adapter = ids_ref[s]
        holder = adapter // slots
        place = holder * CAP + count_ref[holder]
        count_ref[holder] = count_ref[holder] + 1
        seg_ref[place] = s
        slot_ref[place] = residency_ref[adapter] - holder * slots
    for d in range(half):
        for kind in range(2):
            for p in range(CAP):
                place = (me ^ (d + kind * half)) * CAP + p
                seg_out[(kind * half + d) * CAP + p] = seg_ref[place]
                slot = slot_ref[place].astype(jnp.float32)
                tags[d, pl.ds((kind * CAP + p) * SEG, SEG), :] = jnp.full(
                    (SEG, LANES), slot, jnp.float32
                ).astype(tags.dtype)
    for arrival in arrivals:
        arrival.wait()

    def send_rows(d, kind, target, copies):
        def send(source, part):
            copies.append(pltpu.make_async_copy(source, part, sems.at[len(copies)]))
            copies[-1].start()

        for p in range(CAP):
            seg = jnp.maximum(seg_out[(kind * half + d) * CAP + p], 0)
            source = staged.at[pl.ds(pl.multiple_of(seg * SEG, SEG), SEG)]
            send(source, target.at[pl.ds(p * SEG, SEG), pl.ds(0, width)])
        send(tags.at[d, pl.ds(kind * PAIR, PAIR)], target.at[:, pl.ds(width, LANES)])

    def send_adapters(target_of, copies):
        def send(source, part):
            copies.append(pltpu.make_async_copy(source, part, sems.at[len(copies)]))
            copies[-1].start()

        for piece, rows in plan.left_spans():
            send(
                left.at[pl.ds(piece * PAIR, rows)],
                target_of(piece).at[pl.ds(0, rows), pl.ds(0, width)],
            )
        for row, rows, column in plan.up_columns():
            send(
                up.at[pl.ds(row, rows)],
                target_of(plan.up_piece).at[
                    pl.ds(plan.up_first, rows), pl.ds(column, plan.features)
                ],
            )

    def by_role(rows_of, adapters_of):
        copies = []
        for i, d in enumerate(plan.near):
            for kind in range(2):
                send_rows(d, kind, near[i].at[pl.ds(kind * PAIR, PAIR)], copies)
        for i, d in enumerate(plan.cross):
            for kind in range(2):
                send_rows(d, kind, rows_of(2 * i + kind), copies)
        send_adapters(adapters_of, copies)
        for copy in copies:
            copy.wait()

    outer = am_outer(plan)
    pl.when(outer)(lambda: by_role(lambda k: of_wide(wide, k), lambda k: narrow[k]))
    pl.when(jnp.logical_not(outer))(
        lambda: by_role(lambda k: narrow[k], lambda k: of_wide(wide, k))
    )


def lay_out(plan, ids, residency, x, left_rows, ups):
    count = 2 * plan.half * CAP
    wide = jax.ShapeDtypeStruct((2 * PAIR, plan.width + LANES), x.dtype)
    narrow = jax.ShapeDtypeStruct((PAIR, plan.width + LANES), x.dtype)
    n_out = len(plan.near) + plan.wide + plan.narrow
    n_sems = 3 * 2 * plan.half + plan.pieces + len(list(plan.up_columns()))
    out = pl.pallas_call(
        functools.partial(lay_kernel, plan),
        out_shape=[wide] * (len(plan.near) + plan.wide)
        + [narrow] * plan.narrow
        + [jax.ShapeDtypeStruct((count,), jnp.int32)],
        in_specs=[SMEM, SMEM, HBM, HBM, HBM],
        out_specs=[HBM] * n_out + [SMEM],
        scratch_shapes=[
            pltpu.SMEM((plan.replicas * CAP,), jnp.int32),
            pltpu.SMEM((plan.replicas * CAP,), jnp.int32),
            pltpu.SMEM((plan.replicas,), jnp.int32),
            pltpu.VMEM(x.shape, x.dtype),
            pltpu.VMEM((plan.half, 2 * PAIR, LANES), x.dtype),
            pltpu.VMEM((plan.left_rows, plan.width), x.dtype),
            pltpu.VMEM((plan.left_rows, plan.features), x.dtype),
            pltpu.SemaphoreType.DMA((ids.shape[0] + 2 * plan.slots,)),
            pltpu.SemaphoreType.DMA((n_sems,)),
        ],
        compiler_params=params(),
        cost_estimate=pl.CostEstimate(
            flops=0, bytes_accessed=6 * x.size, transcendentals=0
        ),
        name="lay_out",
    )(ids, residency, x, left_rows, ups)
    n_near = len(plan.near)
    return out[:n_near], out[n_near : n_near + plan.wide], out[n_near + plan.wide : -1], out[-1]


def slot_mask(tags, first, slots, share):
    lane = lax.broadcasted_iota(jnp.int32, (1, LANES), 1)
    column_slot = jnp.zeros((1, LANES), jnp.float32)
    for j in range(0, LANES, share):
        slot = ((first + j) // share) % slots
        column_slot = jnp.where(lane >= j, float(slot), column_slot)
    return tags == column_slot


class Copies:
    def __init__(self, outer, sems):
        self.outer, self.sems, self.waits = outer, sems, []

    def start(self, target, outer_source, inner_source=None):
        sem = self.sems.at[len(self.waits)]
        copy = pltpu.make_async_copy(outer_source, target, sem)
        if inner_source is None:
            copy.start()
        else:
            pl.when(self.outer)(copy.start)
            pl.when(jnp.logical_not(self.outer))(
                pltpu.make_async_copy(inner_source, target, sem).start
            )
        self.waits.append(copy)

    def wait(self):
        for copy in self.waits:
            copy.wait()


def reduce_kernel(plan, kind, n_steps, near, wide, narrow, lefts, low_ref, tag_ref, *scratch):
    rows, left, acc, tag, sems = scratch
    block = plan.width // n_steps
    outer = am_outer(plan)
    steps = []
    used = 0
    for k in range(n_steps + 1):
        copies = Copies(outer, sems.at[pl.ds(used, sems.shape[0] - used)])
        columns = pl.ds(k * block, block)
        if k == n_steps:
            columns = pl.ds(plan.width, LANES)
        span = pl.ds(kind * PAIR, PAIR)
        target = tag if k == n_steps else rows.at[:, columns]
        for i, d in enumerate(plan.near):
            copies.start(target.at[pl.ds(d * PAIR, PAIR)], near[i].at[span, columns])
        for i, d in enumerate(plan.cross):
            copies.start(
                target.at[pl.ds(d * PAIR, PAIR)],
                narrow[2 * i + kind].at[:, columns],
                wide[i].at[span, columns],
            )
        if k < n_steps:
            if kind == 0:
                copies.start(left.at[:, columns], lefts[0].at[:, columns])
            else:
                for e, (wide_left, narrow_left) in enumerate(lefts):
                    for piece, count in plan.left_spans():
                        first = e * plan.left_rows + piece * PAIR
                        copies.start(
                            left.at[pl.ds(first, count), columns],
                            of_wide(wide_left, piece).at[pl.ds(0, count), columns],
                            narrow_left[piece].at[pl.ds(0, count), columns],
                        )
        used += len(copies.waits)
        steps.append(copies)
    for k in range(n_steps):
        steps[k].wait()
        columns = pl.ds(k * block, block)
        product = lax.dot_general(
            rows[:, columns],
            left[:, columns],
            (((1,), (1,)), ((), ())),
            preferred_element_type=jnp.float32,
        )
        if k:
            acc[...] += product
        else:
            acc[...] = product
    steps[n_steps].wait()
    tags = tag[...].astype(jnp.float32)
    tag_ref[...] = tags
    share = plan.rank if kind == 0 else plan.share
    total = jnp.zeros(low_ref.shape, jnp.float32)
    for first in range(0, acc.shape[1], LANES):
        total += jnp.where(
            slot_mask(tags, first, plan.slots, share), acc[:, first : first + LANES], 0.0
        )
    low_ref[...] = total


def blocks_call(kernel, plan, blocks, out_shape, out_specs, scratch, flops, moved, name, extra=()):
    flat, tree = jax.tree.flatten(blocks)
    n_extra = len(extra)

    def body(*refs):
        head, rest = refs[:n_extra], refs[n_extra:]
        nested = jax.tree.unflatten(tree, rest[: len(flat)])
        kernel(*head, *nested, *rest[len(flat) :])

    return pl.pallas_call(
        body,
        out_shape=out_shape,
        in_specs=[VMEM] * n_extra + [HBM] * len(flat),
        out_specs=out_specs,
        scratch_shapes=scratch,
        compiler_params=params(),
        cost_estimate=pl.CostEstimate(flops=flops, bytes_accessed=moved, transcendentals=0),
        name=name,
    )(*extra, *flat)


def reduce_rank(plan, kind, near, wide, narrow, lefts, name):
    height = plan.half * PAIR
    columns = plan.slots * plan.rank
    n_steps = 4
    n_copies = (n_steps + 1) * (plan.half + plan.groups * plan.pieces)
    dtype = near[0].dtype
    return blocks_call(
        functools.partial(reduce_kernel, plan, kind, n_steps),
        plan,
        [near, wide, narrow, lefts],
        [jax.ShapeDtypeStruct((height, LANES), jnp.float32)] * 2,
        [VMEM, VMEM],
        [
            pltpu.VMEM((height, plan.width), dtype),
            pltpu.VMEM((columns, plan.width), dtype),
            pltpu.VMEM((height, columns), jnp.float32),
            pltpu.VMEM((height, LANES), dtype),
            pltpu.SemaphoreType.DMA((n_copies,)),
        ],
        2 * height * plan.width * columns,
        2 * plan.width * (height + columns),
        name,
    )


def expand_kernel(plan, kind, mine_ref, other_ref, tag_ref, ups, *rest):
    outs, (up, sems) = rest[:-2], rest[-2:]
    copies = Copies(am_outer(plan), sems)
    if kind == 0:
        copies.start(up, ups[0])
    else:
        for e, (wide, narrow) in enumerate(ups):
            for row, rows, column in plan.up_columns():
                part = pl.ds(plan.up_first, rows), pl.ds(column, plan.features)
                copies.start(
                    up.at[pl.ds(e * plan.left_rows + row, rows)],
                    of_wide(wide, plan.up_piece).at[part],
                    narrow[plan.up_piece].at[part],
                )
    share = plan.rank if kind == 0 else plan.share
    low = (mine_ref[...] + other_ref[...]).astype(jnp.bfloat16).astype(jnp.float32)
    tags = tag_ref[...]
    spread = [
        jnp.where(slot_mask(tags, first, plan.slots, share), low, 0.0).astype(jnp.bfloat16)
        for first in range(0, up.shape[0], LANES)
    ]
    spread = jnp.concatenate(spread, axis=1)
    copies.wait()
    delta = jnp.dot(spread, up[...], preferred_element_type=jnp.float32).astype(jnp.bfloat16)
    for i, out in enumerate(outs):
        out[...] = delta[i * PAIR : (i + 1) * PAIR]


def expand_rank(plan, kind, low, other, tag, ups, name):
    columns = plan.slots * plan.rank
    height = low.shape[0]
    return blocks_call(
        functools.partial(expand_kernel, plan, kind),
        plan,
        [ups],
        [jax.ShapeDtypeStruct((PAIR, plan.features), jnp.bfloat16)] * plan.half,
        [VMEM] * plan.half,
        [
            pltpu.VMEM((columns, plan.features), jnp.bfloat16),
            pltpu.SemaphoreType.DMA((plan.groups * len(list(plan.up_columns())),)),
        ],
        2 * height * columns * plan.features,
        2 * plan.features * (columns + height) + 12 * low.size,
        name,
        extra=(low, other, tag),
    )


def join_kernel(seg_ref, base_ref, *refs):
    deltas, out_ref = refs[:-1], refs[-1]
    for k in range(len(deltas) * CAP):
        part = k % CAP

        @pl.when(seg_ref[k] >= 0)
        def _():
            span = pl.ds(pl.multiple_of(seg_ref[k] * SEG, SEG), SEG)
            delta = deltas[k // CAP][part * SEG : (part + 1) * SEG, :]
            out_ref[span, :] = (base_ref[span, :] + delta.astype(jnp.float32)).astype(
                out_ref.dtype
            )


def join(seg_of, base, deltas):
    height, features = base.shape
    block = min(features, 512)
    tall = pl.BlockSpec((height, block), lambda j: (0, j))
    short = pl.BlockSpec((PAIR, block), lambda j: (0, j))
    return pl.pallas_call(
        join_kernel,
        grid=(features // block,),
        out_shape=jax.ShapeDtypeStruct((height, features), jnp.bfloat16),
        in_specs=[SMEM, tall] + [short] * len(deltas),
        out_specs=tall,
        compiler_params=params(),
        cost_estimate=pl.CostEstimate(
            flops=height * features, bytes_accessed=8 * height * features, transcendentals=0
        ),
        name="join",
    )(seg_of, base, *deltas)


def swap(value, axis, distance):
    count = lax.axis_size(axis)
    return lax.ppermute(value, axis, [(i, i ^ distance) for i in range(count)])


def send(plan, value, moves):
    pairs = [
        (g * plan.replicas + r, (g ^ group_distance) * plan.replicas + (r ^ replica_distance))
        for senders, group_distance, replica_distance in moves
        for g in range(plan.groups)
        for r in senders
    ]
    return lax.ppermute(value, ("groups", "replica"), pairs)


def on_device(x, weight, lefts, ups, ids, residency):
    slots, width, rank = lefts.shape
    features = ups.shape[2]
    plan = Plan(
        lax.axis_size("replica"), lax.axis_size("groups"), slots, rank, width, features
    )
    half, pieces = plan.half, plan.pieces
    left_rows = jnp.swapaxes(lefts, 1, 2)
    near, wide, narrow, seg_of = lay_out(plan, ids, residency, x, left_rows, ups)

    near = [near[0]] + [swap(near[i], "replica", d) for i, d in enumerate(plan.near) if d]
    wide_in = []
    for i in range(plan.wide):
        moves = []
        if i < len(plan.cross):
            moves.append((plan.outer, 0, plan.cross[i]))
        if 2 * i < pieces:
            moves.append((plan.inner, 0, half))
        wide_in.append(send(plan, wide[i], moves))

    partial_sum = jnp.dot(x, weight, preferred_element_type=jnp.float32)
    near, wide_in, narrow, partial_sum = lax.optimization_barrier(
        (near, wide_in, narrow, partial_sum)
    )
    narrow_in = []
    for j in range(plan.narrow):
        moves = []
        if j < 2 * len(plan.cross):
            moves.append((plan.inner, 0, plan.cross[j // 2]))
        if j < pieces:
            moves.append((plan.outer, 0, half))
        narrow_in.append(send(plan, narrow[j], moves))
    base = lax.psum_scatter(partial_sum, "tensor", scatter_dimension=1, tiled=True)

    shares = [(wide_in, narrow_in)]
    for e in range(1, plan.groups):
        shares.append(
            (
                [send(plan, block, [(plan.outer, e, 0)]) for block in wide_in[: -(-pieces // 2)]],
                [send(plan, block, [(plan.inner, e, 0)]) for block in narrow_in[:pieces]],
            )
        )

    deltas = []
    for kind, (left, up, name) in enumerate(
        [
            ([left_rows.reshape(slots * rank, width)], [ups.reshape(slots * rank, features)], "own"),
            (shares, shares, "taken"),
        ]
    ):
        if kind:
            left = [(w, n[: len(list(plan.left_spans()))]) for w, n in left]
        low, tag = reduce_rank(plan, kind, near, wide_in, narrow_in, left, "reduce_" + name)
        if kind:
            low, base = lax.optimization_barrier((low, base))
        other = swap(low, "tensor", 1)
        terms = expand_rank(plan, kind, low, other, tag, up, "expand_" + name)
        deltas.append(terms[0])
        deltas += [swap(terms[d], "replica", d) for d in range(1, half)]
    return join(seg_of, base, deltas)


def solution(mesh):
    placed = (
        P(("groups", "replica"), "tensor"),
        P("tensor", None),
        P("replica", "tensor", None),
        P("replica", None, "tensor"),
        P(("groups", "replica")),
        P(),
    )
    return jax.shard_map(
        on_device,
        mesh=mesh,
        in_specs=placed,
        out_specs=P(("groups", "replica"), "tensor"),
        check_vma=False,
    )
```

```python
import functools

import jax
import jax.numpy as jnp
from jax import lax
from jax.experimental import pallas as pl
from jax.experimental.pallas import tpu as pltpu
from jax.sharding import PartitionSpec as P

CAP = 2
SEG = 32
LANES = 128
PAIR = CAP * SEG
VMEM_LIMIT = 24 * 1024 * 1024
HBM = pl.BlockSpec(memory_space=pltpu.HBM)
SMEM = pl.BlockSpec(memory_space=pltpu.SMEM)
VMEM = pl.BlockSpec(memory_space=pltpu.VMEM)


class Plan:
    def __init__(self, replicas, groups, slots, rank, width, features):
        self.replicas, self.groups, self.slots, self.rank = replicas, groups, slots, rank
        self.width, self.features = width, features
        self.half = replicas // 2
        self.turn = self.half // 2
        self.near = [d for d in range(self.half) if not d & self.turn]
        self.cross = [d for d in range(self.half) if d & self.turn]
        self.share = rank // groups
        self.left_rows = slots * self.share
        self.padded = -(-self.left_rows // LANES) * LANES
        beside = width // features
        self.up_rows = -(-self.left_rows // (beside * 16)) * 16
        self.left_pieces = -(-self.left_rows // PAIR)
        self.pieces = self.left_pieces + 1
        assert self.up_rows <= PAIR
        self.adapter_wide = -(-self.pieces // 2)
        self.wide = max(len(self.cross), self.adapter_wide)
        self.narrow = max(2 * len(self.cross), self.pieces)
        self.outer = [r for r in range(replicas) if self.is_outer(r)]
        self.inner = [r for r in range(replicas) if not self.is_outer(r)]

    def is_outer(self, r):
        return (r < self.turn) or (r >= self.replicas - self.turn)

    def up_columns(self):
        for j, row in enumerate(range(0, self.left_rows, self.up_rows)):
            yield row, min(self.up_rows, self.left_rows - row), j * self.features

    def left_spans(self):
        for piece in range(self.left_pieces):
            yield piece, min(PAIR, self.left_rows - piece * PAIR)

    def narrow_rows(self, i, kind):
        return kind * len(self.cross) + i


def params(limit=VMEM_LIMIT):
    return pltpu.CompilerParams(vmem_limit_bytes=limit)


def am_outer(plan):
    me = lax.axis_index("replica")
    return (me < plan.turn) | (me >= plan.replicas - plan.turn)


def of_wide(refs, piece):
    return refs[piece // 2].at[pl.ds((piece % 2) * PAIR, PAIR)]


def narrow_adapters(narrow, piece, plan):
    return narrow[0] if piece == plan.left_pieces else narrow[1 + piece]


def lay_kernel(plan, first_call, ids_ref, residency_ref, x_ref, left_ref, up_ref, *rest):
    n_near = len(plan.near) - 1 if first_call else 1
    n_blocks = plan.wide if first_call else plan.narrow
    near, rest = rest[:n_near], rest[n_near:]
    blocks, rest = rest[:n_blocks], rest[n_blocks:]
    seg_out, seg_ref, slot_ref, count_ref, staged, tags, left, up, in_sems, sems = rest
    half, slots, width, share = plan.half, plan.slots, plan.width, plan.share
    me = lax.axis_index("replica")
    first = pl.multiple_of(lax.axis_index("groups") * share, share)
    outer = am_outer(plan)
    rows_outer = outer if first_call else jnp.logical_not(outer)

    for h in range(plan.replicas):
        count_ref[h] = 0
        for p in range(CAP):
            seg_ref[h * CAP + p] = -1
            slot_ref[h * CAP + p] = 0
    for s in range(ids_ref.shape[0]):
        adapter = ids_ref[s]
        holder = adapter // slots
        place = holder * CAP + count_ref[holder]
        count_ref[holder] = count_ref[holder] + 1
        seg_ref[place] = s
        slot_ref[place] = residency_ref[adapter] - holder * slots
    for d in range(half):
        for kind in range(2):
            for p in range(CAP):
                seg_out[(kind * half + d) * CAP + p] = seg_ref[
                    (me ^ (d + kind * half)) * CAP + p
                ]

    def move(moves, tagged):
        arrivals = []
        for source, stage, _ in moves:
            arrivals.append(pltpu.make_async_copy(source, stage, in_sems.at[len(arrivals)]))
            arrivals[-1].start()
        departures = []

        def depart(source, target):
            departures.append(pltpu.make_async_copy(source, target, sems.at[len(departures)]))
            departures[-1].start()

        for d, kind, target in tagged:
            for p in range(CAP):
                slot = slot_ref[(me ^ (d + kind * half)) * CAP + p].astype(jnp.float32)
                tags[d, pl.ds((kind * CAP + p) * SEG, SEG), :] = jnp.full(
                    (SEG, LANES), slot, jnp.float32
                ).astype(tags.dtype)
        for d, kind, target in tagged:
            depart(tags.at[d, pl.ds(kind * PAIR, PAIR)], target.at[:, pl.ds(width, LANES)])
        for arrival, (_, stage, target) in zip(arrivals, moves):
            arrival.wait()
            if target is not None:
                for part, place in target:
                    depart(part, place)
        for departure in departures:
            departure.wait()

    def row_moves(targets):
        moves = []
        for d, kind, target in targets:
            for p in range(CAP):
                seg = jnp.maximum(seg_out[(kind * half + d) * CAP + p], 0)
                stage = staged.at[pl.ds(((kind * half + d) * CAP + p) * SEG, SEG)]
                moves.append(
                    (
                        x_ref.at[pl.ds(pl.multiple_of(seg * SEG, SEG), SEG)],
                        stage,
                        [(stage, target.at[pl.ds(p * SEG, SEG), pl.ds(0, width)])],
                    )
                )
        return moves

    def adapter_moves(target_of):
        moves = []
        for slot in range(slots):
            span = pl.ds(slot * share, share)
            source = pl.ds(first, share)
            moves.append((up_ref.at[slot, source], up.at[span], None))
            moves.append((left_ref.at[slot, source], left.at[span], None))
        outs = [
            (
                up.at[pl.ds(row, rows)],
                target_of(plan.left_pieces).at[pl.ds(0, rows), pl.ds(column, plan.features)],
            )
            for row, rows, column in plan.up_columns()
        ]
        outs += [
            (
                left.at[pl.ds(piece * PAIR, rows)],
                target_of(piece).at[pl.ds(0, rows), pl.ds(0, width)],
            )
            for piece, rows in plan.left_spans()
        ]
        source, stage, _ = moves[-1]
        moves[-1] = (source, stage, outs)
        return moves

    near_d = plan.near[1:] if first_call else plan.near[:1]
    near_targets = [
        (d, kind, near[i].at[pl.ds(kind * PAIR, PAIR)])
        for i, d in enumerate(near_d)
        for kind in range(2)
    ]
    if first_call:
        cross_targets = [
            (d, kind, of_wide(blocks, 2 * i + kind))
            for i, d in enumerate(plan.cross)
            for kind in range(2)
        ]
    else:
        cross_targets = [
            (d, kind, blocks[plan.narrow_rows(i, kind)])
            for i, d in enumerate(plan.cross)
            for kind in range(2)
        ]

    @pl.when(rows_outer)
    def _():
        targets = cross_targets + near_targets
        move(row_moves(targets), targets)

    @pl.when(jnp.logical_not(rows_outer))
    def _():
        if first_call:
            adapters = adapter_moves(lambda piece: of_wide(blocks, piece))
        else:
            adapters = adapter_moves(lambda piece: narrow_adapters(blocks, piece, plan))
        move(adapters + row_moves(near_targets), near_targets)


def lay_out(plan, first_call, ids, residency, x, left_rows, ups):
    count = 2 * plan.half * CAP
    wide = jax.ShapeDtypeStruct((2 * PAIR, plan.width + LANES), x.dtype)
    narrow = jax.ShapeDtypeStruct((PAIR, plan.width + LANES), x.dtype)
    near = [wide] * (len(plan.near) - 1 if first_call else 1)
    blocks = [wide] * plan.wide if first_call else [narrow] * plan.narrow
    out = pl.pallas_call(
        functools.partial(lay_kernel, plan, first_call),
        out_shape=near + blocks + [jax.ShapeDtypeStruct((count,), jnp.int32)],
        in_specs=[SMEM, SMEM, HBM, HBM, HBM],
        out_specs=[HBM] * (len(near) + len(blocks)) + [SMEM],
        scratch_shapes=[
            pltpu.SMEM((plan.replicas * CAP,), jnp.int32),
            pltpu.SMEM((plan.replicas * CAP,), jnp.int32),
            pltpu.SMEM((plan.replicas,), jnp.int32),
            pltpu.VMEM((count * SEG, plan.width), x.dtype),
            pltpu.VMEM((plan.half, 2 * PAIR, LANES), x.dtype),
            pltpu.VMEM((plan.left_rows, plan.width), x.dtype),
            pltpu.VMEM((plan.left_rows, plan.features), x.dtype),
            pltpu.SemaphoreType.DMA((count + 2 * plan.slots,)),
            pltpu.SemaphoreType.DMA((2 * count + 2 * plan.pieces,)),
        ],
        compiler_params=params(60 * 1024 * 1024),
        cost_estimate=pl.CostEstimate(
            flops=0, bytes_accessed=3 * x.size, transcendentals=0
        ),
        name="lay_out_first" if first_call else "lay_out_second",
    )(ids, residency, x, left_rows, ups)
    return list(out[: len(near)]), list(out[len(near) : -1]), out[-1]


def slot_mask(tags, first, columns, slots, share):
    lane = lax.broadcasted_iota(jnp.int32, (1, LANES), 1)
    column_slot = jnp.zeros((1, LANES), jnp.float32)
    for j in range(0, LANES, share):
        slot = (first + j) // share if first + j < columns else -1
        column_slot = jnp.where(lane >= j, float(slot), column_slot)
    return tags == column_slot


class Copies:
    def __init__(self, outer, sems):
        self.outer, self.sems, self.waits = outer, sems, []

    def both(self, target, outer_source, inner_source=None):
        sem = self.sems.at[len(self.waits)]
        copy = pltpu.make_async_copy(outer_source, target, sem)
        if inner_source is None:
            copy.start()
        else:
            pl.when(self.outer)(copy.start)
            pl.when(jnp.logical_not(self.outer))(
                pltpu.make_async_copy(inner_source, target, sem).start
            )
        self.waits.append((None, copy))

    def one(self, wanted, target, source):
        copy = pltpu.make_async_copy(source, target, self.sems.at[len(self.waits)])
        pl.when(wanted)(copy.start)
        self.waits.append((wanted, copy))

    def wait(self):
        for wanted, copy in self.waits:
            if wanted is None:
                copy.wait()
            else:
                pl.when(wanted)(copy.wait)


def fold(product, tags, columns, slots, share):
    total = jnp.zeros(tags.shape, jnp.float32)
    for first in range(0, product.shape[1], LANES):
        mask = slot_mask(tags, first, columns, slots, share)
        total += jnp.where(mask, product[:, first : first + LANES], 0.0)
    return total


def copy_rows(copies, plan, kind, target, columns, near, wide, narrow):
    span = pl.ds(kind * PAIR, PAIR)
    for i, d in enumerate(plan.near):
        copies.both(target.at[pl.ds(d * PAIR, PAIR)], near[i].at[span, columns])
    for i, d in enumerate(plan.cross):
        copies.both(
            target.at[pl.ds(d * PAIR, PAIR)],
            narrow[plan.narrow_rows(i, kind)].at[:, columns],
            wide[i].at[span, columns],
        )


def product_of(rows, left):
    return lax.dot_general(
        rows, left, (((1,), (1,)), ((), ())), preferred_element_type=jnp.float32
    )


def reduce_own_kernel(plan, n_steps, near, wide, narrow, own, low_ref, tag_ref, *scratch):
    rows, left, acc, tag, sems = scratch
    block = plan.width // n_steps
    outer = am_outer(plan)
    each = plan.half + 1
    steps = []
    for k in range(n_steps + 1):
        copies = Copies(outer, sems.at[pl.ds(k * each, each)])
        columns = pl.ds(k * block, block) if k < n_steps else pl.ds(plan.width, LANES)
        target = rows.at[:, columns] if k < n_steps else tag
        copy_rows(copies, plan, 0, target, columns, near, wide, narrow)
        if k < n_steps:
            copies.both(left.at[:, columns], own.at[:, columns])
        steps.append(copies)
    for k in range(n_steps):
        steps[k].wait()
        columns = pl.ds(k * block, block)
        product = product_of(rows[:, columns], left[:, columns])
        acc[...] = acc[...] + product if k else product
    steps[n_steps].wait()
    tags = tag[...].astype(jnp.float32)
    tag_ref[...] = tags
    low_ref[...] = fold(acc, tags, acc.shape[1], plan.slots, plan.rank)


def reduce_taken_kernel(plan, n_steps, near, wide, narrow, across, *rest):
    lows, tag_ref = rest[: plan.groups], rest[plan.groups]
    rows, left, acc, tag, sems = rest[plan.groups + 1 :]
    block = plan.width // n_steps
    outer = am_outer(plan)
    inner = jnp.logical_not(outer)
    more = plan.groups - 1
    each = plan.half + plan.left_pieces + more * (plan.half + plan.left_pieces)
    steps = []
    for k in range(n_steps + 1):
        copies = Copies(outer, sems.at[pl.ds(k * each, each)])
        columns = pl.ds(k * block, block) if k < n_steps else pl.ds(plan.width, LANES)
        target = rows.at[0, :, columns] if k < n_steps else tag.at[0]
        copy_rows(copies, plan, 1, target, columns, near, wide, narrow)
        for e in range(1, plan.groups):
            for i, d in enumerate(plan.near + plan.cross):
                target = rows.at[e, :, columns] if k < n_steps else tag.at[e]
                copies.one(
                    inner,
                    target.at[pl.ds(d * PAIR, PAIR)],
                    of_wide(across[e - 1], i).at[:, columns],
                )
        if k < n_steps:
            for piece, count in plan.left_spans():
                span = pl.ds(0, count), columns
                copies.both(
                    left.at[0, pl.ds(piece * PAIR, count), columns],
                    of_wide(wide, piece).at[span],
                    narrow_adapters(narrow, piece, plan).at[span],
                )
                for e in range(1, plan.groups):
                    copies.one(
                        outer,
                        left.at[e, pl.ds(piece * PAIR, count), columns],
                        of_wide(across[e - 1], piece).at[span],
                    )
        steps.append(copies)
    for k in range(n_steps):
        steps[k].wait()
        columns = pl.ds(k * block, block)
        for e in range(plan.groups):
            rows_at = jnp.where(inner, e, 0)
            left_at = jnp.where(outer, e, 0)
            product = product_of(rows[rows_at, :, columns], left[left_at, :, columns])
            acc[e] = acc[e] + product if k else product
    steps[n_steps].wait()
    tag_ref[...] = tag[0].astype(jnp.float32)
    for e in range(plan.groups):
        tags = tag[jnp.where(inner, e, 0)].astype(jnp.float32)
        lows[e][...] = fold(acc.at[e], tags, plan.left_rows, plan.slots, plan.share)


def blocks_call(kernel, blocks, out_shape, out_specs, scratch, flops, moved, name, extra=()):
    flat, tree = jax.tree.flatten(blocks)
    n_extra = len(extra)

    def body(*refs):
        head, rest = refs[:n_extra], refs[n_extra:]
        nested = jax.tree.unflatten(tree, rest[: len(flat)])
        kernel(*head, *nested, *rest[len(flat) :])

    return pl.pallas_call(
        body,
        out_shape=out_shape,
        in_specs=[VMEM] * n_extra + [HBM] * len(flat),
        out_specs=out_specs,
        scratch_shapes=scratch,
        compiler_params=params(),
        cost_estimate=pl.CostEstimate(flops=flops, bytes_accessed=moved, transcendentals=0),
        name=name,
    )(*extra, *flat)


def reduce_own(plan, near, wide, narrow, own):
    height = plan.half * PAIR
    columns = own.shape[0]
    n_steps = 4
    dtype = own.dtype
    return blocks_call(
        functools.partial(reduce_own_kernel, plan, n_steps),
        [near, wide, narrow, own],
        [jax.ShapeDtypeStruct((height, LANES), jnp.float32)] * 2,
        [VMEM] * 2,
        [
            pltpu.VMEM((height, plan.width), dtype),
            pltpu.VMEM((columns, plan.width), dtype),
            pltpu.VMEM((height, columns), jnp.float32),
            pltpu.VMEM((height, LANES), dtype),
            pltpu.SemaphoreType.DMA(((n_steps + 1) * (plan.half + 1),)),
        ],
        2 * height * plan.width * columns,
        2 * plan.width * (height + columns),
        "reduce_own",
    )


def reduce_taken(plan, near, wide, narrow, across):
    height = plan.half * PAIR
    n_steps = 4
    dtype = near[0].dtype
    groups, padded = plan.groups, plan.padded
    *lows, tag = blocks_call(
        functools.partial(reduce_taken_kernel, plan, n_steps),
        [near, wide, narrow, across],
        [jax.ShapeDtypeStruct((height, LANES), jnp.float32)] * (groups + 1),
        [VMEM] * (groups + 1),
        [
            pltpu.VMEM((groups, height, plan.width), dtype),
            pltpu.VMEM((groups, padded, plan.width), dtype),
            pltpu.VMEM((groups, height, padded), jnp.float32),
            pltpu.VMEM((groups, height, LANES), dtype),
            pltpu.SemaphoreType.DMA(((n_steps + 1) * groups * (plan.half + plan.left_pieces),)),
        ],
        2 * height * plan.width * groups * padded,
        2 * plan.width * (height + padded) * groups,
        "reduce_taken",
    )
    return lows, tag


def add_low(mine_ref, other_ref):
    return (mine_ref[...] + other_ref[...]).astype(jnp.bfloat16).astype(jnp.float32)


def spread(low, tags, columns, slots, share):
    blocks = [
        jnp.where(slot_mask(tags, first, columns, slots, share), low, 0.0).astype(jnp.bfloat16)
        for first in range(0, columns, LANES)
    ]
    return jnp.concatenate(blocks, axis=1)


def write_deltas(delta, outs):
    delta = delta.astype(jnp.bfloat16)
    for i, out in enumerate(outs):
        out[...] = delta[i * PAIR : (i + 1) * PAIR]


def expand_own_kernel(plan, mine_ref, other_ref, tag_ref, own, *rest):
    outs, (up, sem) = rest[:-2], rest[-2:]
    copy = pltpu.make_async_copy(own, up, sem)
    copy.start()
    low = add_low(mine_ref, other_ref)
    wide_low = spread(low, tag_ref[...], up.shape[0], plan.slots, plan.rank)
    copy.wait()
    write_deltas(jnp.dot(wide_low, up[...], preferred_element_type=jnp.float32), outs)


def expand_own(plan, mine, other, tag, own):
    columns, features = own.shape
    return blocks_call(
        functools.partial(expand_own_kernel, plan),
        [own],
        [jax.ShapeDtypeStruct((PAIR, features), jnp.bfloat16)] * plan.half,
        [VMEM] * plan.half,
        [pltpu.VMEM(own.shape, own.dtype), pltpu.SemaphoreType.DMA(())],
        2 * mine.shape[0] * columns * features,
        2 * features * (columns + mine.shape[0]),
        "expand_own",
        extra=(mine, other, tag),
    )


def expand_taken_kernel(plan, *refs):
    lows, tag_ref, refs = refs[: 2 * plan.groups], refs[2 * plan.groups], refs[2 * plan.groups + 1 :]
    wide, narrow, across_wide, across_narrow = refs[:4]
    outs, (up, sems) = refs[4:-2], refs[-2:]
    copies = Copies(am_outer(plan), sems)
    for row, rows, column in plan.up_columns():
        part = pl.ds(0, rows), pl.ds(column, plan.features)
        for e in range(plan.groups):
            copies.both(
                up.at[e, pl.ds(row, rows)],
                of_wide(wide if e == 0 else across_wide[e - 1], plan.left_pieces).at[part],
                (narrow if e == 0 else across_narrow[e - 1]).at[part],
            )
    if plan.padded > plan.left_rows:
        up[:, plan.left_rows :, :] = jnp.zeros(
            (plan.groups, plan.padded - plan.left_rows, plan.features), up.dtype
        )
    tags = tag_ref[...]
    wides = [
        spread(
            add_low(lows[2 * e], lows[2 * e + 1]), tags, plan.left_rows, plan.slots, plan.share
        )
        for e in range(plan.groups)
    ]
    copies.wait()
    delta = None
    for e in range(plan.groups):
        product = jnp.dot(wides[e], up[e], preferred_element_type=jnp.float32)
        delta = product if delta is None else delta + product
    write_deltas(delta, outs)


def expand_taken(plan, lows, tag, wide, narrow, across_wide, across_narrow):
    height, features = lows[0].shape[0], plan.features
    return blocks_call(
        functools.partial(expand_taken_kernel, plan),
        [wide, narrow, across_wide, across_narrow],
        [jax.ShapeDtypeStruct((PAIR, features), jnp.bfloat16)] * plan.half,
        [VMEM] * plan.half,
        [
            pltpu.VMEM((plan.groups, plan.padded, features), jnp.bfloat16),
            pltpu.SemaphoreType.DMA((plan.groups * len(list(plan.up_columns())),)),
        ],
        2 * height * plan.groups * plan.padded * features,
        2 * features * (plan.groups * plan.padded + height),
        "expand_taken",
        extra=(*lows, tag),
    )


def join_kernel(seg_ref, base_ref, *refs):
    deltas, out_ref = refs[:-1], refs[-1]
    for k in range(len(deltas) * CAP):
        part = k % CAP

        @pl.when(seg_ref[k] >= 0)
        def _():
            span = pl.ds(pl.multiple_of(seg_ref[k] * SEG, SEG), SEG)
            delta = deltas[k // CAP][part * SEG : (part + 1) * SEG, :]
            out_ref[span, :] = (base_ref[span, :] + delta.astype(jnp.float32)).astype(
                out_ref.dtype
            )


def join(seg_of, base, deltas):
    height, features = base.shape
    block = min(features, 512)
    tall = pl.BlockSpec((height, block), lambda j: (0, j))
    short = pl.BlockSpec((PAIR, block), lambda j: (0, j))
    return pl.pallas_call(
        join_kernel,
        grid=(features // block,),
        out_shape=jax.ShapeDtypeStruct((height, features), jnp.bfloat16),
        in_specs=[SMEM, tall] + [short] * len(deltas),
        out_specs=tall,
        compiler_params=params(),
        cost_estimate=pl.CostEstimate(
            flops=height * features, bytes_accessed=8 * height * features, transcendentals=0
        ),
        name="join",
    )(seg_of, base, *deltas)


def swap(value, axis, distance):
    count = lax.axis_size(axis)
    return lax.ppermute(value, axis, [(i, i ^ distance) for i in range(count)])


def send(plan, value, moves):
    shape = (plan.groups, plan.replicas, lax.axis_size("tensor"))

    def place(g, r, c):
        return (g * shape[1] + r) * shape[2] + c

    pairs = [
        (place(g, r, c), place(g ^ flips[0], r ^ flips[1], c ^ flips[2]))
        for senders, *flips in moves
        for g in range(shape[0])
        for r in senders
        for c in range(shape[2])
    ]
    return lax.ppermute(value, ("groups", "replica", "tensor"), pairs)


def on_device(x, weight, lefts, ups, ids, residency):
    slots, width, rank = lefts.shape
    features = ups.shape[2]
    plan = Plan(
        lax.axis_size("replica"), lax.axis_size("groups"), slots, rank, width, features
    )
    half, n_cross = plan.half, len(plan.cross)
    core = lax.axis_index("tensor")
    outer = am_outer(plan)
    left_rows = jnp.swapaxes(lefts, 1, 2)
    near, wide, seg_of = lay_out(plan, True, ids, residency, x, left_rows, ups)

    near = [swap(block, "replica", d) for block, d in zip(near, plan.near[1:])]
    wide_in = []
    for i in range(plan.wide):
        moves = []
        if i < n_cross:
            moves.append((plan.outer, 0, plan.cross[i], 0))
        if i < plan.adapter_wide:
            moves.append((plan.inner, 0, half, 0))
        wide_in.append(send(plan, wide[i], moves))

    def part(which):
        columns = lax.dynamic_slice(weight, (0, which * features), (weight.shape[0], features))
        return jnp.dot(x, columns, preferred_element_type=jnp.float32)

    base_other = part(1 - core)
    late_ids, _ = lax.optimization_barrier((ids, seg_of))
    own_rows, narrow, _ = lay_out(plan, False, late_ids, residency, x, left_rows, ups)
    near = own_rows + near
    near, wide_in[0], narrow[:2], base_other = lax.optimization_barrier(
        (near, wide_in[0], narrow[:2], base_other)
    )

    def narrow_send(j):
        moves = []
        if j < 2 * n_cross:
            moves.append((plan.inner, 0, plan.cross[j % n_cross], 0))
        if j < plan.pieces:
            moves.append((plan.outer, 0, half, 0))
        return send(plan, narrow[j], moves)

    def taken_rows(i):
        return near[i][PAIR:] if i < len(plan.near) else wide_in[i - len(plan.near)][PAIR:]

    def across_send(i):
        value = jnp.concatenate([taken_rows(2 * i), taken_rows(2 * i + 1)], axis=0)
        if i < plan.adapter_wide:
            value = jnp.where(outer, wide_in[i], value)
        return [
            send(plan, value, [(plan.outer, e, 0, 0), (plan.inner, e, 0, 0)])
            for e in range(1, plan.groups)
        ]

    across = [across_send(0)]
    narrow_in = [narrow_send(0), narrow_send(1)]
    wide_in, narrow[2:] = lax.optimization_barrier((wide_in, narrow[2:]))
    across += [across_send(i) for i in range(1, half // 2)]
    narrow_in += [narrow_send(j) for j in range(2, plan.narrow)]
    across = [[blocks[e] for blocks in across] for e in range(plan.groups - 1)]
    across_up = [send(plan, narrow_in[0], [(plan.inner, e, 0, 0)]) for e in range(1, plan.groups)]
    base = part(core) + swap(base_other, "tensor", 1)

    own_left = left_rows.reshape(slots * rank, width)
    low, tag = reduce_own(plan, near, wide_in[:n_cross], narrow_in[:n_cross], own_left)
    other = swap(low, "tensor", 1)
    terms = expand_own(plan, low, other, tag, ups.reshape(slots * rank, features))
    deltas = [terms[0]] + [swap(terms[d], "replica", d) for d in range(1, half)]

    narrow_in[-1], base, deltas[0] = lax.optimization_barrier((narrow_in[-1], base, deltas[0]))
    lows, tag = reduce_taken(plan, near, wide_in, narrow_in, across)
    pairs = [lows[0], swap(lows[0], "tensor", 1)]
    for e in range(1, plan.groups):
        pairs.append(send(plan, lows[e], [(plan.outer, 0, 0, 0), (plan.inner, e, 0, 0)]))
        pairs.append(send(plan, lows[e], [(plan.outer, 0, 0, 1), (plan.inner, e, 0, 1)]))
    pairs, deltas = lax.optimization_barrier((pairs, deltas))
    across_wide = [blocks[: plan.adapter_wide] for blocks in across]
    terms = expand_taken(
        plan, pairs, tag, wide_in[: plan.adapter_wide], narrow_in[0], across_wide, across_up
    )
    deltas += [terms[0]] + [swap(terms[d], "replica", d) for d in range(1, half)]
    return join(seg_of, base, deltas)


def solution(mesh):
    placed = (
        P(("groups", "replica"), "tensor"),
        P("tensor", None),
        P("replica", "tensor", None),
        P("replica", None, "tensor"),
        P(("groups", "replica")),
        P(),
    )
    return jax.shard_map(
        on_device,
        mesh=mesh,
        in_specs=placed,
        out_specs=P(("groups", "replica"), "tensor"),
        check_vma=False,
    )
```

```python
import functools

import jax
import jax.numpy as jnp
from jax import lax
from jax.experimental import pallas as pl
from jax.experimental.pallas import tpu as pltpu
from jax.sharding import PartitionSpec as P

CAP = 2
SEG = 32
LANES = 128
PAIR = CAP * SEG
VMEM_LIMIT = 24 * 1024 * 1024
HBM = pl.BlockSpec(memory_space=pltpu.HBM)
SMEM = pl.BlockSpec(memory_space=pltpu.SMEM)
VMEM = pl.BlockSpec(memory_space=pltpu.VMEM)


class Plan:
    def __init__(self, replicas, groups, slots, rank, width, features):
        self.replicas, self.groups, self.slots, self.rank = replicas, groups, slots, rank
        self.width, self.features = width, features
        self.half = replicas // 2
        self.turn = self.half // 2
        self.near = [d for d in range(self.half) if not d & self.turn]
        self.cross = [d for d in range(self.half) if d & self.turn]
        self.share = rank // groups
        self.left_rows = slots * self.share
        self.padded = -(-self.left_rows // LANES) * LANES
        beside = width // features
        self.up_rows = -(-self.left_rows // (beside * 16)) * 16
        self.left_pieces = -(-self.left_rows // PAIR)
        self.pieces = self.left_pieces + 1
        assert self.up_rows <= PAIR
        self.adapter_wide = -(-self.pieces // 2)
        self.wide = max(len(self.cross), self.adapter_wide)
        self.narrow = max(2 * len(self.cross), self.pieces)
        self.outer = [r for r in range(replicas) if self.is_outer(r)]
        self.inner = [r for r in range(replicas) if not self.is_outer(r)]

    def is_outer(self, r):
        return (r < self.turn) or (r >= self.replicas - self.turn)

    def up_columns(self):
        for j, row in enumerate(range(0, self.left_rows, self.up_rows)):
            yield row, min(self.up_rows, self.left_rows - row), j * self.features

    def left_spans(self):
        for piece in range(self.left_pieces):
            yield piece, min(PAIR, self.left_rows - piece * PAIR)

    def narrow_rows(self, i, kind):
        return kind * len(self.cross) + i


def params(limit=VMEM_LIMIT):
    return pltpu.CompilerParams(vmem_limit_bytes=limit)


def am_outer(plan):
    me = lax.axis_index("replica")
    return (me < plan.turn) | (me >= plan.replicas - plan.turn)


def of_wide(refs, piece):
    return refs[piece // 2].at[pl.ds((piece % 2) * PAIR, PAIR)]


def narrow_adapters(narrow, piece, plan):
    return narrow[0] if piece == plan.left_pieces else narrow[1 + piece]


def lay_kernel(plan, first_call, ids_ref, residency_ref, x_ref, left_ref, up_ref, *rest):
    n_near = len(plan.near) - 1 if first_call else 1
    n_blocks = plan.wide if first_call else plan.narrow
    near, rest = rest[:n_near], rest[n_near:]
    blocks, rest = rest[:n_blocks], rest[n_blocks:]
    seg_out, seg_ref, slot_ref, count_ref, staged, tags, left, up, in_sems, sems = rest
    half, slots, width, share = plan.half, plan.slots, plan.width, plan.share
    me = lax.axis_index("replica")
    first = pl.multiple_of(lax.axis_index("groups") * share, share)
    outer = am_outer(plan)
    rows_outer = outer if first_call else jnp.logical_not(outer)

    for h in range(plan.replicas):
        count_ref[h] = 0
        for p in range(CAP):
            seg_ref[h * CAP + p] = -1
            slot_ref[h * CAP + p] = 0
    for s in range(ids_ref.shape[0]):
        adapter = ids_ref[s]
        holder = adapter // slots
        place = holder * CAP + count_ref[holder]
        count_ref[holder] = count_ref[holder] + 1
        seg_ref[place] = s
        slot_ref[place] = residency_ref[adapter] - holder * slots
    for d in range(half):
        for kind in range(2):
            for p in range(CAP):
                seg_out[(kind * half + d) * CAP + p] = seg_ref[
                    (me ^ (d + kind * half)) * CAP + p
                ]

    def move(moves, tagged):
        arrivals = []
        for source, stage, _ in moves:
            arrivals.append(pltpu.make_async_copy(source, stage, in_sems.at[len(arrivals)]))
            arrivals[-1].start()
        departures = []

        def depart(source, target):
            departures.append(pltpu.make_async_copy(source, target, sems.at[len(departures)]))
            departures[-1].start()

        for d, kind, target in tagged:
            for p in range(CAP):
                slot = slot_ref[(me ^ (d + kind * half)) * CAP + p].astype(jnp.float32)
                tags[d, pl.ds((kind * CAP + p) * SEG, SEG), :] = jnp.full(
                    (SEG, LANES), slot, jnp.float32
                ).astype(tags.dtype)
        for d, kind, target in tagged:
            depart(tags.at[d, pl.ds(kind * PAIR, PAIR)], target.at[:, pl.ds(width, LANES)])
        for arrival, (_, stage, target) in zip(arrivals, moves):
            arrival.wait()
            if target is not None:
                for part, place in target:
                    depart(part, place)
        for departure in departures:
            departure.wait()

    def row_moves(targets):
        moves = []
        for d, kind, target in targets:
            for p in range(CAP):
                seg = jnp.maximum(seg_out[(kind * half + d) * CAP + p], 0)
                stage = staged.at[pl.ds(((kind * half + d) * CAP + p) * SEG, SEG)]
                moves.append(
                    (
                        x_ref.at[pl.ds(pl.multiple_of(seg * SEG, SEG), SEG)],
                        stage,
                        [(stage, target.at[pl.ds(p * SEG, SEG), pl.ds(0, width)])],
                    )
                )
        return moves

    def adapter_moves(target_of):
        moves = []
        for slot in range(slots):
            span = pl.ds(slot * share, share)
            source = pl.ds(first, share)
            moves.append((up_ref.at[slot, source], up.at[span], None))
            moves.append((left_ref.at[slot, source], left.at[span], None))
        outs = [
            (
                up.at[pl.ds(row, rows)],
                target_of(plan.left_pieces).at[pl.ds(0, rows), pl.ds(column, plan.features)],
            )
            for row, rows, column in plan.up_columns()
        ]
        outs += [
            (
                left.at[pl.ds(piece * PAIR, rows)],
                target_of(piece).at[pl.ds(0, rows), pl.ds(0, width)],
            )
            for piece, rows in plan.left_spans()
        ]
        source, stage, _ = moves[-1]
        moves[-1] = (source, stage, outs)
        return moves

    near_d = plan.near[1:] if first_call else plan.near[:1]
    near_targets = [
        (d, kind, near[i].at[pl.ds(kind * PAIR, PAIR)])
        for i, d in enumerate(near_d)
        for kind in range(2)
    ]
    if first_call:
        cross_targets = [
            (d, kind, of_wide(blocks, 2 * i + kind))
            for i, d in enumerate(plan.cross)
            for kind in range(2)
        ]
    else:
        cross_targets = [
            (d, kind, blocks[plan.narrow_rows(i, kind)])
            for i, d in enumerate(plan.cross)
            for kind in range(2)
        ]

    @pl.when(rows_outer)
    def _():
        targets = cross_targets + near_targets
        move(row_moves(targets), targets)

    @pl.when(jnp.logical_not(rows_outer))
    def _():
        if first_call:
            adapters = adapter_moves(lambda piece: of_wide(blocks, piece))
        else:
            adapters = adapter_moves(lambda piece: narrow_adapters(blocks, piece, plan))
        move(adapters + row_moves(near_targets), near_targets)


def lay_out(plan, first_call, ids, residency, x, left_rows, ups):
    count = 2 * plan.half * CAP
    wide = jax.ShapeDtypeStruct((2 * PAIR, plan.width + LANES), x.dtype)
    narrow = jax.ShapeDtypeStruct((PAIR, plan.width + LANES), x.dtype)
    near = [wide] * (len(plan.near) - 1 if first_call else 1)
    blocks = [wide] * plan.wide if first_call else [narrow] * plan.narrow
    out = pl.pallas_call(
        functools.partial(lay_kernel, plan, first_call),
        out_shape=near + blocks + [jax.ShapeDtypeStruct((count,), jnp.int32)],
        in_specs=[SMEM, SMEM, HBM, HBM, HBM],
        out_specs=[HBM] * (len(near) + len(blocks)) + [SMEM],
        scratch_shapes=[
            pltpu.SMEM((plan.replicas * CAP,), jnp.int32),
            pltpu.SMEM((plan.replicas * CAP,), jnp.int32),
            pltpu.SMEM((plan.replicas,), jnp.int32),
            pltpu.VMEM((count * SEG, plan.width), x.dtype),
            pltpu.VMEM((plan.half, 2 * PAIR, LANES), x.dtype),
            pltpu.VMEM((plan.left_rows, plan.width), x.dtype),
            pltpu.VMEM((plan.left_rows, plan.features), x.dtype),
            pltpu.SemaphoreType.DMA((count + 2 * plan.slots,)),
            pltpu.SemaphoreType.DMA((2 * count + 2 * plan.pieces,)),
        ],
        compiler_params=params(60 * 1024 * 1024),
        cost_estimate=pl.CostEstimate(
            flops=0, bytes_accessed=3 * x.size, transcendentals=0
        ),
        name="lay_out_first" if first_call else "lay_out_second",
    )(ids, residency, x, left_rows, ups)
    return list(out[: len(near)]), list(out[len(near) : -1]), out[-1]


def slot_mask(tags, first, columns, slots, share):
    lane = lax.broadcasted_iota(jnp.int32, (1, LANES), 1)
    column_slot = jnp.zeros((1, LANES), jnp.float32)
    for j in range(0, LANES, share):
        slot = (first + j) // share if first + j < columns else -1
        column_slot = jnp.where(lane >= j, float(slot), column_slot)
    return tags == column_slot


class Copies:
    def __init__(self, outer, sems):
        self.outer, self.sems, self.waits = outer, sems, []

    def both(self, target, outer_source, inner_source=None):
        sem = self.sems.at[len(self.waits)]
        copy = pltpu.make_async_copy(outer_source, target, sem)
        if inner_source is None:
            copy.start()
        else:
            pl.when(self.outer)(copy.start)
            pl.when(jnp.logical_not(self.outer))(
                pltpu.make_async_copy(inner_source, target, sem).start
            )
        self.waits.append((None, copy))

    def one(self, wanted, target, source):
        copy = pltpu.make_async_copy(source, target, self.sems.at[len(self.waits)])
        pl.when(wanted)(copy.start)
        self.waits.append((wanted, copy))

    def wait(self):
        for wanted, copy in self.waits:
            if wanted is None:
                copy.wait()
            else:
                pl.when(wanted)(copy.wait)


def lane_group(share):
    return lax.broadcasted_iota(jnp.int32, (1, LANES), 1) // share


def spread_lanes(value, share):
    total = value
    for shift in range(share, LANES, share):
        total += pltpu.roll(value, shift, 1)
    return total


def pack(low, share):
    count = LANES // share
    height = low.shape[0] // count
    everywhere = spread_lanes(low, share)
    packed = jnp.zeros((height, LANES), jnp.float32)
    for i in range(count):
        rows = everywhere[i * height : (i + 1) * height]
        packed = jnp.where(lane_group(share) == i, rows, packed)
    return packed


def unpack(packed, share):
    rows = [
        spread_lanes(jnp.where(lane_group(share) == i, packed, 0.0), share)
        for i in range(LANES // share)
    ]
    return jnp.concatenate(rows, axis=0)


def fold(product, tags, columns, slots, share):
    total = jnp.zeros(tags.shape, jnp.float32)
    for first in range(0, product.shape[1], LANES):
        mask = slot_mask(tags, first, columns, slots, share)
        total += jnp.where(mask, product[:, first : first + LANES], 0.0)
    return total


def copy_rows(copies, plan, kind, target, columns, near, wide, narrow):
    span = pl.ds(kind * PAIR, PAIR)
    for i, d in enumerate(plan.near):
        copies.both(target.at[pl.ds(d * PAIR, PAIR)], near[i].at[span, columns])
    for i, d in enumerate(plan.cross):
        copies.both(
            target.at[pl.ds(d * PAIR, PAIR)],
            narrow[plan.narrow_rows(i, kind)].at[:, columns],
            wide[i].at[span, columns],
        )


def product_of(rows, left):
    return lax.dot_general(
        rows, left, (((1,), (1,)), ((), ())), preferred_element_type=jnp.float32
    )


def reduce_own_kernel(plan, n_steps, near, wide, narrow, own, low_ref, tag_ref, *scratch):
    rows, left, acc, tag, sems = scratch
    block = plan.width // n_steps
    outer = am_outer(plan)
    each = plan.half + 1
    steps = []
    for k in range(n_steps + 1):
        copies = Copies(outer, sems.at[pl.ds(k * each, each)])
        columns = pl.ds(k * block, block) if k < n_steps else pl.ds(plan.width, LANES)
        target = rows.at[:, columns] if k < n_steps else tag
        copy_rows(copies, plan, 0, target, columns, near, wide, narrow)
        if k < n_steps:
            copies.both(left.at[:, columns], own.at[:, columns])
        steps.append(copies)
    for k in range(n_steps):
        steps[k].wait()
        columns = pl.ds(k * block, block)
        product = product_of(rows[:, columns], left[:, columns])
        acc[...] = acc[...] + product if k else product
    steps[n_steps].wait()
    tags = tag[...].astype(jnp.float32)
    tag_ref[...] = tags
    low_ref[...] = pack(fold(acc, tags, acc.shape[1], plan.slots, plan.rank), plan.rank)


def reduce_taken_kernel(plan, n_steps, near, wide, narrow, across, *rest):
    lows, tag_ref = rest[: plan.groups], rest[plan.groups]
    rows, left, acc, tag, sems = rest[plan.groups + 1 :]
    block = plan.width // n_steps
    outer = am_outer(plan)
    inner = jnp.logical_not(outer)
    more = plan.groups - 1
    each = plan.half + plan.left_pieces + more * (plan.half + plan.left_pieces)
    steps = []
    for k in range(n_steps + 1):
        copies = Copies(outer, sems.at[pl.ds(k * each, each)])
        columns = pl.ds(k * block, block) if k < n_steps else pl.ds(plan.width, LANES)
        target = rows.at[0, :, columns] if k < n_steps else tag.at[0]
        copy_rows(copies, plan, 1, target, columns, near, wide, narrow)
        for e in range(1, plan.groups):
            for i, d in enumerate(plan.near + plan.cross):
                target = rows.at[e, :, columns] if k < n_steps else tag.at[e]
                copies.one(
                    inner,
                    target.at[pl.ds(d * PAIR, PAIR)],
                    of_wide(across[e - 1], i).at[:, columns],
                )
        if k < n_steps:
            for piece, count in plan.left_spans():
                span = pl.ds(0, count), columns
                copies.both(
                    left.at[0, pl.ds(piece * PAIR, count), columns],
                    of_wide(wide, piece).at[span],
                    narrow_adapters(narrow, piece, plan).at[span],
                )
                for e in range(1, plan.groups):
                    copies.one(
                        outer,
                        left.at[e, pl.ds(piece * PAIR, count), columns],
                        of_wide(across[e - 1], piece).at[span],
                    )
        steps.append(copies)
    for k in range(n_steps):
        steps[k].wait()
        columns = pl.ds(k * block, block)
        for e in range(plan.groups):
            rows_at = jnp.where(inner, e, 0)
            left_at = jnp.where(outer, e, 0)
            product = product_of(rows[rows_at, :, columns], left[left_at, :, columns])
            acc[e] = acc[e] + product if k else product
    steps[n_steps].wait()
    tag_ref[...] = tag[0].astype(jnp.float32)
    for e in range(plan.groups):
        tags = tag[jnp.where(inner, e, 0)].astype(jnp.float32)
        low = fold(acc.at[e], tags, plan.left_rows, plan.slots, plan.share)
        lows[e][...] = pack(low, plan.share)


def blocks_call(kernel, blocks, out_shape, out_specs, scratch, flops, moved, name, extra=()):
    flat, tree = jax.tree.flatten(blocks)
    n_extra = len(extra)

    def body(*refs):
        head, rest = refs[:n_extra], refs[n_extra:]
        nested = jax.tree.unflatten(tree, rest[: len(flat)])
        kernel(*head, *nested, *rest[len(flat) :])

    return pl.pallas_call(
        body,
        out_shape=out_shape,
        in_specs=[VMEM] * n_extra + [HBM] * len(flat),
        out_specs=out_specs,
        scratch_shapes=scratch,
        compiler_params=params(),
        cost_estimate=pl.CostEstimate(flops=flops, bytes_accessed=moved, transcendentals=0),
        name=name,
    )(*extra, *flat)


def reduce_own(plan, near, wide, narrow, own):
    height = plan.half * PAIR
    columns = own.shape[0]
    n_steps = 4
    dtype = own.dtype
    return blocks_call(
        functools.partial(reduce_own_kernel, plan, n_steps),
        [near, wide, narrow, own],
        [
            jax.ShapeDtypeStruct((height * plan.rank // LANES, LANES), jnp.float32),
            jax.ShapeDtypeStruct((height, LANES), jnp.float32),
        ],
        [VMEM] * 2,
        [
            pltpu.VMEM((height, plan.width), dtype),
            pltpu.VMEM((columns, plan.width), dtype),
            pltpu.VMEM((height, columns), jnp.float32),
            pltpu.VMEM((height, LANES), dtype),
            pltpu.SemaphoreType.DMA(((n_steps + 1) * (plan.half + 1),)),
        ],
        2 * height * plan.width * columns,
        2 * plan.width * (height + columns),
        "reduce_own",
    )


def reduce_taken(plan, near, wide, narrow, across):
    height = plan.half * PAIR
    n_steps = 4
    dtype = near[0].dtype
    groups, padded = plan.groups, plan.padded
    *lows, tag = blocks_call(
        functools.partial(reduce_taken_kernel, plan, n_steps),
        [near, wide, narrow, across],
        [jax.ShapeDtypeStruct((height * plan.share // LANES, LANES), jnp.float32)] * groups
        + [jax.ShapeDtypeStruct((height, LANES), jnp.float32)],
        [VMEM] * (groups + 1),
        [
            pltpu.VMEM((groups, height, plan.width), dtype),
            pltpu.VMEM((groups, padded, plan.width), dtype),
            pltpu.VMEM((groups, height, padded), jnp.float32),
            pltpu.VMEM((groups, height, LANES), dtype),
            pltpu.SemaphoreType.DMA(((n_steps + 1) * groups * (plan.half + plan.left_pieces),)),
        ],
        2 * height * plan.width * groups * padded,
        2 * plan.width * (height + padded) * groups,
        "reduce_taken",
    )
    return lows, tag


def add_low(mine_ref, other_ref, share):
    low = (mine_ref[...] + other_ref[...]).astype(jnp.bfloat16).astype(jnp.float32)
    return unpack(low, share)


def spread(low, tags, columns, slots, share):
    blocks = [
        jnp.where(slot_mask(tags, first, columns, slots, share), low, 0.0).astype(jnp.bfloat16)
        for first in range(0, columns, LANES)
    ]
    return jnp.concatenate(blocks, axis=1)


def write_deltas(delta, outs):
    delta = delta.astype(jnp.bfloat16)
    for i, out in enumerate(outs):
        out[...] = delta[i * PAIR : (i + 1) * PAIR]


def expand_own_kernel(plan, mine_ref, other_ref, tag_ref, own, *rest):
    outs, (up, sem) = rest[:-2], rest[-2:]
    copy = pltpu.make_async_copy(own, up, sem)
    copy.start()
    low = add_low(mine_ref, other_ref, plan.rank)
    wide_low = spread(low, tag_ref[...], up.shape[0], plan.slots, plan.rank)
    copy.wait()
    write_deltas(jnp.dot(wide_low, up[...], preferred_element_type=jnp.float32), outs)


def expand_own(plan, mine, other, tag, own):
    columns, features = own.shape
    return blocks_call(
        functools.partial(expand_own_kernel, plan),
        [own],
        [jax.ShapeDtypeStruct((PAIR, features), jnp.bfloat16)] * plan.half,
        [VMEM] * plan.half,
        [pltpu.VMEM(own.shape, own.dtype), pltpu.SemaphoreType.DMA(())],
        2 * tag.shape[0] * columns * features,
        2 * features * (columns + tag.shape[0]),
        "expand_own",
        extra=(mine, other, tag),
    )


def expand_taken_kernel(plan, *refs):
    lows, tag_ref, refs = refs[: 2 * plan.groups], refs[2 * plan.groups], refs[2 * plan.groups + 1 :]
    wide, narrow, across_wide, across_narrow = refs[:4]
    outs, (up, sems) = refs[4:-2], refs[-2:]
    copies = Copies(am_outer(plan), sems)
    for row, rows, column in plan.up_columns():
        part = pl.ds(0, rows), pl.ds(column, plan.features)
        for e in range(plan.groups):
            copies.both(
                up.at[e, pl.ds(row, rows)],
                of_wide(wide if e == 0 else across_wide[e - 1], plan.left_pieces).at[part],
                (narrow if e == 0 else across_narrow[e - 1]).at[part],
            )
    if plan.padded > plan.left_rows:
        up[:, plan.left_rows :, :] = jnp.zeros(
            (plan.groups, plan.padded - plan.left_rows, plan.features), up.dtype
        )
    tags = tag_ref[...]
    wides = [
        spread(
            add_low(lows[2 * e], lows[2 * e + 1], plan.share),
            tags,
            plan.left_rows,
            plan.slots,
            plan.share,
        )
        for e in range(plan.groups)
    ]
    copies.wait()
    delta = None
    for e in range(plan.groups):
        product = jnp.dot(wides[e], up[e], preferred_element_type=jnp.float32)
        delta = product if delta is None else delta + product
    write_deltas(delta, outs)


def expand_taken(plan, lows, tag, wide, narrow, across_wide, across_narrow):
    height, features = tag.shape[0], plan.features
    return blocks_call(
        functools.partial(expand_taken_kernel, plan),
        [wide, narrow, across_wide, across_narrow],
        [jax.ShapeDtypeStruct((PAIR, features), jnp.bfloat16)] * plan.half,
        [VMEM] * plan.half,
        [
            pltpu.VMEM((plan.groups, plan.padded, features), jnp.bfloat16),
            pltpu.SemaphoreType.DMA((plan.groups * len(list(plan.up_columns())),)),
        ],
        2 * height * plan.groups * plan.padded * features,
        2 * features * (plan.groups * plan.padded + height),
        "expand_taken",
        extra=(*lows, tag),
    )


def join_kernel(seg_ref, base_ref, *refs):
    deltas, out_ref = refs[:-1], refs[-1]
    for k in range(len(deltas) * CAP):
        part = k % CAP

        @pl.when(seg_ref[k] >= 0)
        def _():
            span = pl.ds(pl.multiple_of(seg_ref[k] * SEG, SEG), SEG)
            delta = deltas[k // CAP][part * SEG : (part + 1) * SEG, :]
            out_ref[span, :] = (base_ref[span, :] + delta.astype(jnp.float32)).astype(
                out_ref.dtype
            )


def join(seg_of, base, deltas):
    height, features = base.shape
    block = min(features, 512)
    tall = pl.BlockSpec((height, block), lambda j: (0, j))
    short = pl.BlockSpec((PAIR, block), lambda j: (0, j))
    return pl.pallas_call(
        join_kernel,
        grid=(features // block,),
        out_shape=jax.ShapeDtypeStruct((height, features), jnp.bfloat16),
        in_specs=[SMEM, tall] + [short] * len(deltas),
        out_specs=tall,
        compiler_params=params(),
        cost_estimate=pl.CostEstimate(
            flops=height * features, bytes_accessed=8 * height * features, transcendentals=0
        ),
        name="join",
    )(seg_of, base, *deltas)


def swap(value, axis, distance):
    count = lax.axis_size(axis)
    return lax.ppermute(value, axis, [(i, i ^ distance) for i in range(count)])


def send(plan, value, moves):
    shape = (plan.groups, plan.replicas, lax.axis_size("tensor"))

    def place(g, r, c):
        return (g * shape[1] + r) * shape[2] + c

    pairs = [
        (place(g, r, c), place(g ^ flips[0], r ^ flips[1], c ^ flips[2]))
        for senders, *flips in moves
        for g in range(shape[0])
        for r in senders
        for c in range(shape[2])
    ]
    return lax.ppermute(value, ("groups", "replica", "tensor"), pairs)


def on_device(x, weight, lefts, ups, ids, residency):
    slots, width, rank = lefts.shape
    features = ups.shape[2]
    plan = Plan(
        lax.axis_size("replica"), lax.axis_size("groups"), slots, rank, width, features
    )
    half, n_cross = plan.half, len(plan.cross)
    core = lax.axis_index("tensor")
    outer = am_outer(plan)
    left_rows = jnp.swapaxes(lefts, 1, 2)
    near, wide, seg_of = lay_out(plan, True, ids, residency, x, left_rows, ups)

    wide_in = []
    for i in range(plan.wide):
        moves = []
        if i < n_cross:
            moves.append((plan.outer, 0, plan.cross[i], 0))
        if i < plan.adapter_wide:
            moves.append((plan.inner, 0, half, 0))
        wide_in.append(send(plan, wide[i], moves))
    near = [swap(block, "replica", d) for block, d in zip(near, plan.near[1:])]

    late_ids, _ = lax.optimization_barrier((ids, seg_of))
    own_rows, narrow, _ = lay_out(plan, False, late_ids, residency, x, left_rows, ups)
    near = own_rows + near

    def part(which):
        columns = lax.dynamic_slice(weight, (0, which * features), (weight.shape[0], features))
        return jnp.dot(x, columns, preferred_element_type=jnp.float32)

    base_other, base_mine = part(1 - core), part(core)
    near, wide_in[0], narrow[:2], base_other, base_mine = lax.optimization_barrier(
        (near, wide_in[0], narrow[:2], base_other, base_mine)
    )

    def narrow_send(j):
        moves = []
        if j < 2 * n_cross:
            moves.append((plan.inner, 0, plan.cross[j % n_cross], 0))
        if j < plan.pieces:
            moves.append((plan.outer, 0, half, 0))
        return send(plan, narrow[j], moves)

    def taken_rows(i):
        return near[i][PAIR:] if i < len(plan.near) else wide_in[i - len(plan.near)][PAIR:]

    def across_send(i):
        value = jnp.concatenate([taken_rows(2 * i), taken_rows(2 * i + 1)], axis=0)
        if i < plan.adapter_wide:
            value = jnp.where(outer, wide_in[i], value)
        return [
            send(plan, value, [(plan.outer, e, 0, 0), (plan.inner, e, 0, 0)])
            for e in range(1, plan.groups)
        ]

    across = [across_send(0)]
    narrow_in = [narrow_send(0), narrow_send(1)]
    across += [across_send(i) for i in range(1, half // 2)]
    narrow_in[0], narrow[2:], base_other = lax.optimization_barrier(
        (narrow_in[0], narrow[2:], base_other)
    )
    base = base_mine + swap(base_other, "tensor", 1)
    across_up = [send(plan, narrow_in[0], [(plan.inner, e, 0, 0)]) for e in range(1, plan.groups)]
    base, across[0], narrow[3:] = lax.optimization_barrier((base, across[0], narrow[3:]))
    narrow_in += [narrow_send(j) for j in range(2, plan.narrow)]
    across = [[blocks[e] for blocks in across] for e in range(plan.groups - 1)]

    own_left = left_rows.reshape(slots * rank, width)
    low, tag = reduce_own(plan, near, wide_in[:n_cross], narrow_in[:n_cross], own_left)
    other = swap(low, "tensor", 1)
    terms = expand_own(plan, low, other, tag, ups.reshape(slots * rank, features))
    deltas = [terms[0]] + [swap(terms[d], "replica", d) for d in range(1, half)]

    narrow_in[-1], base, deltas[0] = lax.optimization_barrier((narrow_in[-1], base, deltas[0]))
    lows, tag = reduce_taken(plan, near, wide_in, narrow_in, across)
    pairs = [lows[0], swap(lows[0], "tensor", 1)]
    for e in range(1, plan.groups):
        pairs.append(send(plan, lows[e], [(plan.outer, 0, 0, 0), (plan.inner, e, 0, 0)]))
        pairs.append(send(plan, lows[e], [(plan.outer, 0, 0, 1), (plan.inner, e, 0, 1)]))
    pairs, deltas = lax.optimization_barrier((pairs, deltas))
    across_wide = [blocks[: plan.adapter_wide] for blocks in across]
    terms = expand_taken(
        plan, pairs, tag, wide_in[: plan.adapter_wide], narrow_in[0], across_wide, across_up
    )
    deltas += [terms[0]] + [swap(terms[d], "replica", d) for d in range(1, half)]
    return join(seg_of, base, deltas)


def solution(mesh):
    placed = (
        P(("groups", "replica"), "tensor"),
        P("tensor", None),
        P("replica", "tensor", None),
        P("replica", None, "tensor"),
        P(("groups", "replica")),
        P(),
    )
    return jax.shard_map(
        on_device,
        mesh=mesh,
        in_specs=placed,
        out_specs=P(("groups", "replica"), "tensor"),
        check_vma=False,
    )
```

```python
import functools

import jax
import jax.numpy as jnp
from jax import lax
from jax.experimental import pallas as pl
from jax.experimental.pallas import tpu as pltpu
from jax.sharding import PartitionSpec as P

CAP = 2
SEG = 32
LANES = 128
PAIR = CAP * SEG
VMEM_LIMIT = 24 * 1024 * 1024
HBM = pl.BlockSpec(memory_space=pltpu.HBM)
SMEM = pl.BlockSpec(memory_space=pltpu.SMEM)
VMEM = pl.BlockSpec(memory_space=pltpu.VMEM)


class Plan:
    def __init__(self, replicas, groups, slots, rank, width, features):
        self.replicas, self.groups, self.slots, self.rank = replicas, groups, slots, rank
        self.width, self.features = width, features
        self.half = replicas // 2
        self.turn = self.half // 2
        self.near = [d for d in range(self.half) if not d & self.turn]
        self.cross = [d for d in range(self.half) if d & self.turn]
        self.share = rank // groups
        self.left_rows = slots * self.share
        self.padded = -(-self.left_rows // LANES) * LANES
        beside = width // features
        self.up_rows = -(-self.left_rows // (beside * 16)) * 16
        self.left_pieces = -(-self.left_rows // PAIR)
        self.pieces = self.left_pieces + 1
        assert self.up_rows <= PAIR
        self.adapter_wide = -(-self.pieces // 2)
        self.units = 2 * len(self.cross)
        assert self.pieces <= self.units and self.adapter_wide <= len(self.cross)
        self.wide = len(self.cross)
        self.outer = [r for r in range(replicas) if self.is_outer(r)]
        self.inner = [r for r in range(replicas) if not self.is_outer(r)]

    def is_outer(self, r):
        return (r < self.turn) or (r >= self.replicas - self.turn)

    def up_columns(self):
        for j, row in enumerate(range(0, self.left_rows, self.up_rows)):
            yield row, min(self.up_rows, self.left_rows - row), j * self.features

    def left_spans(self):
        for piece in range(self.left_pieces):
            yield piece, min(PAIR, self.left_rows - piece * PAIR)

    def late_blocks(self):
        blocks = [(self.cross[0], 1, 0)]
        blocks += [(d, 2, 2 * i - 1) for i, d in enumerate(self.cross) if i]
        return blocks + [(self.cross[0], 1, self.units - 1)]

    def late_unit(self, refs, unit):
        if unit in (0, self.units - 1):
            return refs[0 if unit == 0 else -1]
        return refs[(unit + 1) // 2].at[pl.ds((unit - 1) % 2 * PAIR, PAIR)]

    def late_rows(self, refs, i, kind):
        if i == 0:
            return self.late_unit(refs, 0 if kind == 0 else self.units - 1)
        return self.late_unit(refs, 2 * i - 1 + kind)


def params(limit=VMEM_LIMIT):
    return pltpu.CompilerParams(vmem_limit_bytes=limit)


def am_outer(plan):
    me = lax.axis_index("replica")
    return (me < plan.turn) | (me >= plan.replicas - plan.turn)


def of_wide(refs, piece):
    return refs[piece // 2].at[pl.ds((piece % 2) * PAIR, PAIR)]


def late_adapters(late, piece, plan):
    return plan.late_unit(late, 0 if piece == plan.left_pieces else 1 + piece)


def lay_kernel(plan, first_call, ids_ref, residency_ref, x_ref, left_ref, up_ref, *rest):
    n_near = 0 if first_call else len(plan.near)
    n_blocks = plan.wide if first_call else len(plan.late_blocks())
    near, rest = rest[:n_near], rest[n_near:]
    blocks, rest = rest[:n_blocks], rest[n_blocks:]
    seg_out, seg_ref, slot_ref, count_ref, staged, tags, left, up, in_sems, sems = rest
    half, slots, width, share = plan.half, plan.slots, plan.width, plan.share
    me = lax.axis_index("replica")
    first = pl.multiple_of(lax.axis_index("groups") * share, share)
    outer = am_outer(plan)
    rows_outer = outer if first_call else jnp.logical_not(outer)

    for h in range(plan.replicas):
        count_ref[h] = 0
        for p in range(CAP):
            seg_ref[h * CAP + p] = -1
            slot_ref[h * CAP + p] = 0
    for s in range(ids_ref.shape[0]):
        adapter = ids_ref[s]
        holder = adapter // slots
        place = holder * CAP + count_ref[holder]
        count_ref[holder] = count_ref[holder] + 1
        seg_ref[place] = s
        slot_ref[place] = residency_ref[adapter] - holder * slots
    for d in range(half):
        for kind in range(2):
            for p in range(CAP):
                seg_out[(kind * half + d) * CAP + p] = seg_ref[
                    (me ^ (d + kind * half)) * CAP + p
                ]

    def move(moves, tagged):
        arrivals = []
        for source, stage, _ in moves:
            arrivals.append(pltpu.make_async_copy(source, stage, in_sems.at[len(arrivals)]))
            arrivals[-1].start()
        departures = []

        def depart(source, target):
            departures.append(pltpu.make_async_copy(source, target, sems.at[len(departures)]))
            departures[-1].start()

        for d, kind, target in tagged:
            for p in range(CAP):
                slot = slot_ref[(me ^ (d + kind * half)) * CAP + p].astype(jnp.float32)
                tags[d, pl.ds((kind * CAP + p) * SEG, SEG), :] = jnp.full(
                    (SEG, LANES), slot, jnp.float32
                ).astype(tags.dtype)
        for d, kind, target in tagged:
            depart(tags.at[d, pl.ds(kind * PAIR, PAIR)], target.at[:, pl.ds(width, LANES)])
        for arrival, (_, stage, target) in zip(arrivals, moves):
            arrival.wait()
            if target is not None:
                for part, place in target:
                    depart(part, place)
        for departure in departures:
            departure.wait()

    def row_moves(targets):
        moves = []
        for d, kind, target in targets:
            for p in range(CAP):
                seg = jnp.maximum(seg_out[(kind * half + d) * CAP + p], 0)
                stage = staged.at[pl.ds(((kind * half + d) * CAP + p) * SEG, SEG)]
                moves.append(
                    (
                        x_ref.at[pl.ds(pl.multiple_of(seg * SEG, SEG), SEG)],
                        stage,
                        [(stage, target.at[pl.ds(p * SEG, SEG), pl.ds(0, width)])],
                    )
                )
        return moves

    def adapter_moves(target_of):
        moves = []
        for slot in range(slots):
            span = pl.ds(slot * share, share)
            source = pl.ds(first, share)
            moves.append((up_ref.at[slot, source], up.at[span], None))
            moves.append((left_ref.at[slot, source], left.at[span], None))
        outs = [
            (
                up.at[pl.ds(row, rows)],
                target_of(plan.left_pieces).at[pl.ds(0, rows), pl.ds(column, plan.features)],
            )
            for row, rows, column in plan.up_columns()
        ]
        outs += [
            (
                left.at[pl.ds(piece * PAIR, rows)],
                target_of(piece).at[pl.ds(0, rows), pl.ds(0, width)],
            )
            for piece, rows in plan.left_spans()
        ]
        source, stage, _ = moves[-1]
        moves[-1] = (source, stage, outs)
        return moves

    near_d = [] if first_call else plan.near
    near_targets = [
        (d, kind, near[i].at[pl.ds(kind * PAIR, PAIR)])
        for i, d in enumerate(near_d)
        for kind in range(2)
    ]
    if first_call:
        cross_targets = [
            (d, kind, of_wide(blocks, 2 * i + kind))
            for i, d in enumerate(plan.cross)
            for kind in range(2)
        ]
    else:
        cross_targets = [
            (d, kind, plan.late_rows(blocks, i, kind))
            for i, d in enumerate(plan.cross)
            for kind in range(2)
        ]

    @pl.when(rows_outer)
    def _():
        targets = cross_targets + near_targets
        move(row_moves(targets), targets)

    @pl.when(jnp.logical_not(rows_outer))
    def _():
        if first_call:
            adapters = adapter_moves(lambda piece: of_wide(blocks, piece))
        else:
            adapters = adapter_moves(lambda piece: late_adapters(blocks, piece, plan))
        move(adapters + row_moves(near_targets), near_targets)


def lay_out(plan, first_call, ids, residency, x, left_rows, ups):
    count = 2 * plan.half * CAP
    wide = jax.ShapeDtypeStruct((2 * PAIR, plan.width + LANES), x.dtype)
    late = [
        jax.ShapeDtypeStruct((n * PAIR, plan.width + LANES), x.dtype)
        for _, n, _ in plan.late_blocks()
    ]
    near = [] if first_call else [wide] * len(plan.near)
    blocks = [wide] * plan.wide if first_call else late
    out = pl.pallas_call(
        functools.partial(lay_kernel, plan, first_call),
        out_shape=near + blocks + [jax.ShapeDtypeStruct((count,), jnp.int32)],
        in_specs=[SMEM, SMEM, HBM, HBM, HBM],
        out_specs=[HBM] * (len(near) + len(blocks)) + [SMEM],
        scratch_shapes=[
            pltpu.SMEM((plan.replicas * CAP,), jnp.int32),
            pltpu.SMEM((plan.replicas * CAP,), jnp.int32),
            pltpu.SMEM((plan.replicas,), jnp.int32),
            pltpu.VMEM((count * SEG, plan.width), x.dtype),
            pltpu.VMEM((plan.half, 2 * PAIR, LANES), x.dtype),
            pltpu.VMEM((plan.left_rows, plan.width), x.dtype),
            pltpu.VMEM((plan.left_rows, plan.features), x.dtype),
            pltpu.SemaphoreType.DMA((count + 2 * plan.slots,)),
            pltpu.SemaphoreType.DMA((2 * count + 2 * plan.pieces,)),
        ],
        compiler_params=params(60 * 1024 * 1024),
        cost_estimate=pl.CostEstimate(flops=0, bytes_accessed=x.size, transcendentals=0),
        name="lay_out_first" if first_call else "lay_out_second",
    )(ids, residency, x, left_rows, ups)
    return list(out[: len(near)]), list(out[len(near) : -1]), out[-1]


def slot_mask(tags, first, columns, slots, share):
    lane = lax.broadcasted_iota(jnp.int32, (1, LANES), 1)
    column_slot = jnp.zeros((1, LANES), jnp.float32)
    for j in range(0, LANES, share):
        slot = (first + j) // share if first + j < columns else -1
        column_slot = jnp.where(lane >= j, float(slot), column_slot)
    return tags == column_slot


class Copies:
    def __init__(self, outer, sems):
        self.outer, self.sems, self.waits = outer, sems, []

    def both(self, target, outer_source, inner_source=None):
        sem = self.sems.at[len(self.waits)]
        copy = pltpu.make_async_copy(outer_source, target, sem)
        if inner_source is None:
            copy.start()
        else:
            pl.when(self.outer)(copy.start)
            pl.when(jnp.logical_not(self.outer))(
                pltpu.make_async_copy(inner_source, target, sem).start
            )
        self.waits.append((None, copy))

    def one(self, wanted, target, source):
        copy = pltpu.make_async_copy(source, target, self.sems.at[len(self.waits)])
        pl.when(wanted)(copy.start)
        self.waits.append((wanted, copy))

    def wait(self):
        for wanted, copy in self.waits:
            if wanted is None:
                copy.wait()
            else:
                pl.when(wanted)(copy.wait)


def lane_group(share):
    return lax.broadcasted_iota(jnp.int32, (1, LANES), 1) // share


def spread_lanes(value, share):
    total = value
    for shift in range(share, LANES, share):
        total += pltpu.roll(value, shift, 1)
    return total


def pack(low, share):
    count = LANES // share
    height = low.shape[0] // count
    everywhere = spread_lanes(low, share)
    packed = jnp.zeros((height, LANES), jnp.float32)
    for i in range(count):
        rows = everywhere[i * height : (i + 1) * height]
        packed = jnp.where(lane_group(share) == i, rows, packed)
    return packed


def unpack(packed, share):
    rows = [
        spread_lanes(jnp.where(lane_group(share) == i, packed, 0.0), share)
        for i in range(LANES // share)
    ]
    return jnp.concatenate(rows, axis=0)


def fold(product, tags, columns, slots, share):
    total = jnp.zeros(tags.shape, jnp.float32)
    for first in range(0, product.shape[1], LANES):
        mask = slot_mask(tags, first, columns, slots, share)
        total += jnp.where(mask, product[:, first : first + LANES], 0.0)
    return total


def copy_rows(copies, plan, kind, target, columns, near, wide, narrow):
    span = pl.ds(kind * PAIR, PAIR)
    for i, d in enumerate(plan.near):
        copies.both(target.at[pl.ds(d * PAIR, PAIR)], near[i].at[span, columns])
    for i, d in enumerate(plan.cross):
        copies.both(
            target.at[pl.ds(d * PAIR, PAIR)],
            plan.late_rows(narrow, i, kind).at[:, columns],
            wide[i].at[span, columns],
        )


def product_of(rows, left):
    return lax.dot_general(
        rows, left, (((1,), (1,)), ((), ())), preferred_element_type=jnp.float32
    )


def reduce_own_kernel(plan, n_steps, near, wide, narrow, own, low_ref, tag_ref, *scratch):
    rows, left, acc, tag, sems = scratch
    block = plan.width // n_steps
    outer = am_outer(plan)
    each = plan.half + 1
    steps = []
    for k in range(n_steps + 1):
        copies = Copies(outer, sems.at[pl.ds(k * each, each)])
        columns = pl.ds(k * block, block) if k < n_steps else pl.ds(plan.width, LANES)
        target = rows.at[:, columns] if k < n_steps else tag
        copy_rows(copies, plan, 0, target, columns, near, wide, narrow)
        if k < n_steps:
            copies.both(left.at[:, columns], own.at[:, columns])
        steps.append(copies)
    for k in range(n_steps):
        steps[k].wait()
        columns = pl.ds(k * block, block)
        product = product_of(rows[:, columns], left[:, columns])
        acc[...] = acc[...] + product if k else product
    steps[n_steps].wait()
    tags = tag[...].astype(jnp.float32)
    tag_ref[...] = tags
    low_ref[...] = pack(fold(acc, tags, acc.shape[1], plan.slots, plan.rank), plan.rank)


def reduce_taken_kernel(plan, n_steps, near, wide, narrow, across, *rest):
    lows, tag_ref = rest[: plan.groups], rest[plan.groups]
    rows, left, acc, tag, sems = rest[plan.groups + 1 :]
    block = plan.width // n_steps
    outer = am_outer(plan)
    inner = jnp.logical_not(outer)
    more = plan.groups - 1
    each = plan.half + plan.left_pieces + more * (plan.half + plan.left_pieces)
    steps = []
    for k in range(n_steps + 1):
        copies = Copies(outer, sems.at[pl.ds(k * each, each)])
        columns = pl.ds(k * block, block) if k < n_steps else pl.ds(plan.width, LANES)
        target = rows.at[0, :, columns] if k < n_steps else tag.at[0]
        copy_rows(copies, plan, 1, target, columns, near, wide, narrow)
        for e in range(1, plan.groups):
            for i, d in enumerate(plan.near + plan.cross):
                target = rows.at[e, :, columns] if k < n_steps else tag.at[e]
                copies.one(
                    inner,
                    target.at[pl.ds(d * PAIR, PAIR)],
                    across[e - 1][i].at[:, columns],
                )
        if k < n_steps:
            for piece, count in plan.left_spans():
                span = pl.ds(0, count), columns
                copies.both(
                    left.at[0, pl.ds(piece * PAIR, count), columns],
                    of_wide(wide, piece).at[span],
                    late_adapters(narrow, piece, plan).at[span],
                )
                for e in range(1, plan.groups):
                    copies.one(
                        outer,
                        left.at[e, pl.ds(piece * PAIR, count), columns],
                        across[e - 1][piece].at[span],
                    )
        steps.append(copies)
    for k in range(n_steps):
        steps[k].wait()
        columns = pl.ds(k * block, block)
        for e in range(plan.groups):
            rows_at = jnp.where(inner, e, 0)
            left_at = jnp.where(outer, e, 0)
            product = product_of(rows[rows_at, :, columns], left[left_at, :, columns])
            acc[e] = acc[e] + product if k else product
    steps[n_steps].wait()
    tag_ref[...] = tag[0].astype(jnp.float32)
    for e in range(plan.groups):
        tags = tag[jnp.where(inner, e, 0)].astype(jnp.float32)
        low = fold(acc.at[e], tags, plan.left_rows, plan.slots, plan.share)
        lows[e][...] = pack(low, plan.share)


def blocks_call(kernel, blocks, out_shape, out_specs, scratch, flops, moved, name, extra=()):
    flat, tree = jax.tree.flatten(blocks)
    n_extra = len(extra)

    def body(*refs):
        head, rest = refs[:n_extra], refs[n_extra:]
        nested = jax.tree.unflatten(tree, rest[: len(flat)])
        kernel(*head, *nested, *rest[len(flat) :])

    return pl.pallas_call(
        body,
        out_shape=out_shape,
        in_specs=[VMEM] * n_extra + [HBM] * len(flat),
        out_specs=out_specs,
        scratch_shapes=scratch,
        compiler_params=params(),
        cost_estimate=pl.CostEstimate(flops=1, bytes_accessed=1, transcendentals=0),
        name=name,
    )(*extra, *flat)


def reduce_own(plan, near, wide, narrow, own):
    height = plan.half * PAIR
    columns = own.shape[0]
    n_steps = 4
    dtype = own.dtype
    return blocks_call(
        functools.partial(reduce_own_kernel, plan, n_steps),
        [near, wide, narrow, own],
        [
            jax.ShapeDtypeStruct((height * plan.rank // LANES, LANES), jnp.float32),
            jax.ShapeDtypeStruct((height, LANES), jnp.float32),
        ],
        [VMEM] * 2,
        [
            pltpu.VMEM((height, plan.width), dtype),
            pltpu.VMEM((columns, plan.width), dtype),
            pltpu.VMEM((height, columns), jnp.float32),
            pltpu.VMEM((height, LANES), dtype),
            pltpu.SemaphoreType.DMA(((n_steps + 1) * (plan.half + 1),)),
        ],
        2 * height * plan.width * columns,
        2 * plan.width * (height + columns),
        "reduce_own",
    )


def reduce_taken(plan, near, wide, narrow, across):
    height = plan.half * PAIR
    n_steps = 4
    dtype = near[0].dtype
    groups, padded = plan.groups, plan.padded
    *lows, tag = blocks_call(
        functools.partial(reduce_taken_kernel, plan, n_steps),
        [near, wide, narrow, across],
        [jax.ShapeDtypeStruct((height * plan.share // LANES, LANES), jnp.float32)] * groups
        + [jax.ShapeDtypeStruct((height, LANES), jnp.float32)],
        [VMEM] * (groups + 1),
        [
            pltpu.VMEM((groups, height, plan.width), dtype),
            pltpu.VMEM((groups, padded, plan.width), dtype),
            pltpu.VMEM((groups, height, padded), jnp.float32),
            pltpu.VMEM((groups, height, LANES), dtype),
            pltpu.SemaphoreType.DMA(((n_steps + 1) * groups * (plan.half + plan.left_pieces),)),
        ],
        2 * height * plan.width * groups * padded,
        2 * plan.width * (height + padded) * groups,
        "reduce_taken",
    )
    return lows, tag


def add_low(mine_ref, other_ref, share):
    low = (mine_ref[...] + other_ref[...]).astype(jnp.bfloat16).astype(jnp.float32)
    return unpack(low, share)


def spread(low, tags, columns, slots, share):
    blocks = [
        jnp.where(slot_mask(tags, first, columns, slots, share), low, 0.0).astype(jnp.bfloat16)
        for first in range(0, columns, LANES)
    ]
    return jnp.concatenate(blocks, axis=1)


def write_deltas(delta, outs):
    delta = delta.astype(jnp.bfloat16)
    for i, out in enumerate(outs):
        out[...] = delta[i * PAIR : (i + 1) * PAIR]


def expand_own_kernel(plan, mine_ref, other_ref, tag_ref, own, *rest):
    outs, (up, sem) = rest[:-2], rest[-2:]
    copy = pltpu.make_async_copy(own, up, sem)
    copy.start()
    low = add_low(mine_ref, other_ref, plan.rank)
    wide_low = spread(low, tag_ref[...], up.shape[0], plan.slots, plan.rank)
    copy.wait()
    write_deltas(jnp.dot(wide_low, up[...], preferred_element_type=jnp.float32), outs)


def expand_own(plan, mine, other, tag, own):
    columns, features = own.shape
    return blocks_call(
        functools.partial(expand_own_kernel, plan),
        [own],
        [jax.ShapeDtypeStruct((PAIR, features), jnp.bfloat16)] * plan.half,
        [VMEM] * plan.half,
        [pltpu.VMEM(own.shape, own.dtype), pltpu.SemaphoreType.DMA(())],
        2 * tag.shape[0] * columns * features,
        2 * features * (columns + tag.shape[0]),
        "expand_own",
        extra=(mine, other, tag),
    )


def expand_taken_kernel(plan, *refs):
    lows, tag_ref, refs = refs[: 2 * plan.groups], refs[2 * plan.groups], refs[2 * plan.groups + 1 :]
    wide, narrow, across_wide, across_narrow = refs[:4]
    outs, (up, sems) = refs[4:-2], refs[-2:]
    copies = Copies(am_outer(plan), sems)
    for row, rows, column in plan.up_columns():
        part = pl.ds(0, rows), pl.ds(column, plan.features)
        for e in range(plan.groups):
            copies.both(
                up.at[e, pl.ds(row, rows)],
                (of_wide(wide, plan.left_pieces) if e == 0 else across_wide[e - 1]).at[part],
                (narrow if e == 0 else across_narrow[e - 1]).at[part],
            )
    if plan.padded > plan.left_rows:
        up[:, plan.left_rows :, :] = jnp.zeros(
            (plan.groups, plan.padded - plan.left_rows, plan.features), up.dtype
        )
    tags = tag_ref[...]
    wides = [
        spread(
            add_low(lows[2 * e], lows[2 * e + 1], plan.share),
            tags,
            plan.left_rows,
            plan.slots,
            plan.share,
        )
        for e in range(plan.groups)
    ]
    copies.wait()
    delta = None
    for e in range(plan.groups):
        product = jnp.dot(wides[e], up[e], preferred_element_type=jnp.float32)
        delta = product if delta is None else delta + product
    write_deltas(delta, outs)


def expand_taken(plan, lows, tag, wide, narrow, across_wide, across_narrow):
    height, features = tag.shape[0], plan.features
    return blocks_call(
        functools.partial(expand_taken_kernel, plan),
        [wide, narrow, across_wide, across_narrow],
        [jax.ShapeDtypeStruct((PAIR, features), jnp.bfloat16)] * plan.half,
        [VMEM] * plan.half,
        [
            pltpu.VMEM((plan.groups, plan.padded, features), jnp.bfloat16),
            pltpu.SemaphoreType.DMA((plan.groups * len(list(plan.up_columns())),)),
        ],
        2 * height * plan.groups * plan.padded * features,
        2 * features * (plan.groups * plan.padded + height),
        "expand_taken",
        extra=(*lows, tag),
    )


def join_kernel(seg_ref, base_ref, *refs):
    deltas, out_ref = refs[:-1], refs[-1]
    for k in range(len(deltas) * CAP):
        part = k % CAP

        @pl.when(seg_ref[k] >= 0)
        def _():
            span = pl.ds(pl.multiple_of(seg_ref[k] * SEG, SEG), SEG)
            delta = deltas[k // CAP][part * SEG : (part + 1) * SEG, :]
            out_ref[span, :] = (base_ref[span, :] + delta.astype(jnp.float32)).astype(
                out_ref.dtype
            )


def join(seg_of, base, deltas):
    height, features = base.shape
    block = min(features, 512)
    tall = pl.BlockSpec((height, block), lambda j: (0, j))
    short = pl.BlockSpec((PAIR, block), lambda j: (0, j))
    return pl.pallas_call(
        join_kernel,
        grid=(features // block,),
        out_shape=jax.ShapeDtypeStruct((height, features), jnp.bfloat16),
        in_specs=[SMEM, tall] + [short] * len(deltas),
        out_specs=tall,
        compiler_params=params(),
        cost_estimate=pl.CostEstimate(
            flops=height * features, bytes_accessed=8 * height * features, transcendentals=0
        ),
        name="join",
    )(seg_of, base, *deltas)


def swap(value, axis, distance):
    count = lax.axis_size(axis)
    return lax.ppermute(value, axis, [(i, i ^ distance) for i in range(count)])


def send(plan, value, moves):
    shape = (plan.groups, plan.replicas, lax.axis_size("tensor"))

    def place(g, r, c):
        return (g * shape[1] + r) * shape[2] + c

    pairs = [
        (place(g, r, c), place(g ^ flips[0], r ^ flips[1], c ^ flips[2]))
        for senders, *flips in moves
        for g in range(shape[0])
        for r in senders
        for c in range(shape[2])
    ]
    return lax.ppermute(value, ("groups", "replica", "tensor"), pairs)


def on_device(x, weight, lefts, ups, ids, residency):
    slots, width, rank = lefts.shape
    features = ups.shape[2]
    plan = Plan(
        lax.axis_size("replica"), lax.axis_size("groups"), slots, rank, width, features
    )
    half, n_cross = plan.half, len(plan.cross)
    core = lax.axis_index("tensor")
    outer = am_outer(plan)
    left_rows = jnp.swapaxes(lefts, 1, 2)
    _, wide, seg_of = lay_out(plan, True, ids, residency, x, left_rows, ups)

    wide_in = []
    for i in range(plan.wide):
        moves = []
        if i < n_cross:
            moves.append((plan.outer, 0, plan.cross[i], 0))
        if i < plan.adapter_wide:
            moves.append((plan.inner, 0, half, 0))
        wide_in.append(send(plan, wide[i], moves))

    def part(which):
        columns = lax.dynamic_slice(weight, (0, which * features), (weight.shape[0], features))
        return jnp.dot(x, columns, preferred_element_type=jnp.float32)

    base_other = part(1 - core)
    late_ids, base_other, _ = lax.optimization_barrier((ids, base_other, seg_of))
    near, late, _ = lay_out(plan, False, late_ids, residency, x, left_rows, ups)
    near = near[:1] + [swap(near[i], "replica", d) for i, d in enumerate(plan.near) if d]
    base_mine = part(core)
    def across_send(i):
        if i < len(plan.near):
            value = near[i][PAIR:]
        else:
            value = wide_in[i - len(plan.near)][PAIR:]
        if i < plan.pieces:
            piece = wide_in[i // 2][(i % 2) * PAIR : (i % 2 + 1) * PAIR]
            value = jnp.where(outer, piece, value)
        return [
            send(plan, value, [(plan.outer, e, 0, 0), (plan.inner, e, 0, 0)])
            for e in range(1, plan.groups)
        ]

    across = [across_send(0)]

    base = base_mine + swap(base_other, "tensor", 1)
    wide_in, near, across, late, base = lax.optimization_barrier(
        (wide_in, near, across, late, base)
    )
    across += [across_send(i) for i in range(1, half)]
    late_in = []
    for block, (d, _, unit) in zip(late, plan.late_blocks()):
        moves = [(plan.inner, 0, d, 0)]
        if unit < plan.pieces:
            moves.append((plan.outer, 0, half, 0))
        if unit == plan.units - 1:
            late_in[0], block = lax.optimization_barrier((late_in[0], block))
        late_in.append(send(plan, block, moves))
    across_up = [
        send(plan, late_in[0], [(plan.inner, e, 0, 0)]) for e in range(1, plan.groups)
    ]
    late_in[:-1], across = lax.optimization_barrier((late_in[:-1], across))
    across = [[blocks[e] for blocks in across] for e in range(plan.groups - 1)]

    own_left = left_rows.reshape(slots * rank, width)
    low, tag = reduce_own(plan, near, wide_in, late_in[:-1], own_left)
    other = swap(low, "tensor", 1)
    terms = expand_own(plan, low, other, tag, ups.reshape(slots * rank, features))
    deltas = [terms[0]] + [swap(terms[d], "replica", d) for d in range(1, half)]

    late_in[-1], deltas[:2], across_up = lax.optimization_barrier(
        (late_in[-1], deltas[:2], across_up)
    )
    lows, tag = reduce_taken(plan, near, wide_in, late_in, across)
    pairs = [lows[0], swap(lows[0], "tensor", 1)]
    for e in range(1, plan.groups):
        pairs.append(send(plan, lows[e], [(plan.outer, 0, 0, 0), (plan.inner, e, 0, 0)]))
        pairs.append(send(plan, lows[e], [(plan.outer, 0, 0, 1), (plan.inner, e, 0, 1)]))
    pairs, deltas = lax.optimization_barrier((pairs, deltas))
    across_wide = [blocks[plan.left_pieces] for blocks in across]
    terms = expand_taken(plan, pairs, tag, wide_in, late_in[0], across_wide, across_up)
    deltas += [terms[0]] + [swap(terms[d], "replica", d) for d in range(1, half)]
    return join(seg_of, base, deltas)


def solution(mesh):
    placed = (
        P(("groups", "replica"), "tensor"),
        P("tensor", None),
        P("replica", "tensor", None),
        P("replica", None, "tensor"),
        P(("groups", "replica")),
        P(),
    )
    return jax.shard_map(
        on_device,
        mesh=mesh,
        in_specs=placed,
        out_specs=P(("groups", "replica"), "tensor"),
        check_vma=False,
    )
```

```python
import functools

import jax
import jax.numpy as jnp
from jax import lax
from jax.experimental import pallas as pl
from jax.experimental.pallas import tpu as pltpu
from jax.sharding import PartitionSpec as P

CAP = 2
SEG = 32
LANES = 128
PAIR = CAP * SEG
VMEM_LIMIT = 24 * 1024 * 1024
HBM = pl.BlockSpec(memory_space=pltpu.HBM)
SMEM = pl.BlockSpec(memory_space=pltpu.SMEM)
VMEM = pl.BlockSpec(memory_space=pltpu.VMEM)


class Plan:
    def __init__(self, replicas, groups, slots, rank, width, features):
        self.replicas, self.groups, self.slots, self.rank = replicas, groups, slots, rank
        self.width, self.features = width, features
        self.half = replicas // 2
        self.turn = self.half // 2
        self.near = [d for d in range(self.half) if not d & self.turn]
        self.cross = [d for d in range(self.half) if d & self.turn]
        self.across = self.near[1:] + self.near[:1] + self.cross
        self.share = rank // groups
        self.left_rows = slots * self.share
        self.padded = -(-self.left_rows // LANES) * LANES
        beside = width // features
        self.up_rows = -(-self.left_rows // (beside * 16)) * 16
        self.left_pieces = -(-self.left_rows // PAIR)
        self.pieces = self.left_pieces + 1
        assert self.up_rows <= PAIR
        self.adapter_wide = -(-self.pieces // 2)
        self.units = 2 * len(self.cross)
        assert self.pieces <= self.units and self.adapter_wide <= len(self.cross)
        self.wide = len(self.cross)
        self.outer = [r for r in range(replicas) if self.is_outer(r)]
        self.inner = [r for r in range(replicas) if not self.is_outer(r)]

    def is_outer(self, r):
        return (r < self.turn) or (r >= self.replicas - self.turn)

    def up_columns(self):
        for j, row in enumerate(range(0, self.left_rows, self.up_rows)):
            yield row, min(self.up_rows, self.left_rows - row), j * self.features

    def left_spans(self):
        for piece in range(self.left_pieces):
            yield piece, min(PAIR, self.left_rows - piece * PAIR)

    def late_blocks(self):
        blocks = [(self.cross[0], 1, 0)]
        blocks += [(d, 2, 2 * i - 1) for i, d in enumerate(self.cross) if i]
        return blocks + [(self.cross[0], 1, self.units - 1)]

    def late_unit(self, refs, unit):
        if unit in (0, self.units - 1):
            return refs[0 if unit == 0 else -1]
        return refs[(unit + 1) // 2].at[pl.ds((unit - 1) % 2 * PAIR, PAIR)]

    def late_rows(self, refs, i, kind):
        if i == 0:
            return self.late_unit(refs, 0 if kind == 0 else self.units - 1)
        return self.late_unit(refs, 2 * i - 1 + kind)


def params(limit=VMEM_LIMIT):
    return pltpu.CompilerParams(vmem_limit_bytes=limit)


def am_outer(plan):
    me = lax.axis_index("replica")
    return (me < plan.turn) | (me >= plan.replicas - plan.turn)


def of_wide(refs, piece):
    return refs[piece // 2].at[pl.ds((piece % 2) * PAIR, PAIR)]


def late_adapters(late, piece, plan):
    return plan.late_unit(late, 0 if piece == plan.left_pieces else 1 + piece)


def lay_kernel(plan, first_call, ids_ref, residency_ref, x_ref, left_ref, up_ref, *rest):
    n_near = len(plan.near) - 1 if first_call else 1
    n_blocks = plan.wide if first_call else len(plan.late_blocks())
    near, rest = rest[:n_near], rest[n_near:]
    blocks, rest = rest[:n_blocks], rest[n_blocks:]
    seg_out, seg_ref, slot_ref, count_ref, staged, tags, left, up, in_sems, sems = rest
    half, slots, width, share = plan.half, plan.slots, plan.width, plan.share
    me = lax.axis_index("replica")
    first = pl.multiple_of(lax.axis_index("groups") * share, share)
    outer = am_outer(plan)
    rows_outer = outer if first_call else jnp.logical_not(outer)

    for h in range(plan.replicas):
        count_ref[h] = 0
        for p in range(CAP):
            seg_ref[h * CAP + p] = -1
            slot_ref[h * CAP + p] = 0
    for s in range(ids_ref.shape[0]):
        adapter = ids_ref[s]
        holder = adapter // slots
        place = holder * CAP + count_ref[holder]
        count_ref[holder] = count_ref[holder] + 1
        seg_ref[place] = s
        slot_ref[place] = residency_ref[adapter] - holder * slots
    for d in range(half):
        for kind in range(2):
            for p in range(CAP):
                seg_out[(kind * half + d) * CAP + p] = seg_ref[
                    (me ^ (d + kind * half)) * CAP + p
                ]

    def move(moves, tagged):
        arrivals = []
        for source, stage, _ in moves:
            arrivals.append(pltpu.make_async_copy(source, stage, in_sems.at[len(arrivals)]))
            arrivals[-1].start()
        departures = []

        def depart(source, target):
            departures.append(pltpu.make_async_copy(source, target, sems.at[len(departures)]))
            departures[-1].start()

        for d, kind, target in tagged:
            for p in range(CAP):
                slot = slot_ref[(me ^ (d + kind * half)) * CAP + p].astype(jnp.float32)
                tags[d, pl.ds((kind * CAP + p) * SEG, SEG), :] = jnp.full(
                    (SEG, LANES), slot, jnp.float32
                ).astype(tags.dtype)
        for d, kind, target in tagged:
            depart(tags.at[d, pl.ds(kind * PAIR, PAIR)], target.at[:, pl.ds(width, LANES)])
        for arrival, (_, stage, target) in zip(arrivals, moves):
            arrival.wait()
            if target is not None:
                for part, place in target:
                    depart(part, place)
        for departure in departures:
            departure.wait()

    def row_moves(targets):
        moves = []
        for d, kind, target in targets:
            for p in range(CAP):
                seg = jnp.maximum(seg_out[(kind * half + d) * CAP + p], 0)
                stage = staged.at[pl.ds(((kind * half + d) * CAP + p) * SEG, SEG)]
                moves.append(
                    (
                        x_ref.at[pl.ds(pl.multiple_of(seg * SEG, SEG), SEG)],
                        stage,
                        [(stage, target.at[pl.ds(p * SEG, SEG), pl.ds(0, width)])],
                    )
                )
        return moves

    def adapter_moves(target_of):
        moves = []
        for slot in range(slots):
            span = pl.ds(slot * share, share)
            source = pl.ds(first, share)
            moves.append((up_ref.at[slot, source], up.at[span], None))
            moves.append((left_ref.at[slot, source], left.at[span], None))
        outs = [
            (
                up.at[pl.ds(row, rows)],
                target_of(plan.left_pieces).at[pl.ds(0, rows), pl.ds(column, plan.features)],
            )
            for row, rows, column in plan.up_columns()
        ]
        outs += [
            (
                left.at[pl.ds(piece * PAIR, rows)],
                target_of(piece).at[pl.ds(0, rows), pl.ds(0, width)],
            )
            for piece, rows in plan.left_spans()
        ]
        source, stage, _ = moves[-1]
        moves[-1] = (source, stage, outs)
        return moves

    near_d = plan.near[1:] if first_call else plan.near[:1]
    near_targets = [
        (d, kind, near[i].at[pl.ds(kind * PAIR, PAIR)])
        for i, d in enumerate(near_d)
        for kind in range(2)
    ]
    if first_call:
        cross_targets = [
            (d, kind, of_wide(blocks, 2 * i + kind))
            for i, d in enumerate(plan.cross)
            for kind in range(2)
        ]
    else:
        cross_targets = [
            (d, kind, plan.late_rows(blocks, i, kind))
            for i, d in enumerate(plan.cross)
            for kind in range(2)
        ]

    @pl.when(rows_outer)
    def _():
        targets = cross_targets + near_targets
        move(row_moves(targets), targets)

    @pl.when(jnp.logical_not(rows_outer))
    def _():
        if first_call:
            adapters = adapter_moves(lambda piece: of_wide(blocks, piece))
        else:
            adapters = adapter_moves(lambda piece: late_adapters(blocks, piece, plan))
        move(adapters + row_moves(near_targets), near_targets)


def lay_out(plan, first_call, ids, residency, x, left_rows, ups):
    count = 2 * plan.half * CAP
    wide = jax.ShapeDtypeStruct((2 * PAIR, plan.width + LANES), x.dtype)
    late = [
        jax.ShapeDtypeStruct((n * PAIR, plan.width + LANES), x.dtype)
        for _, n, _ in plan.late_blocks()
    ]
    near = [wide] * (len(plan.near) - 1 if first_call else 1)
    blocks = [wide] * plan.wide if first_call else late
    out = pl.pallas_call(
        functools.partial(lay_kernel, plan, first_call),
        out_shape=near + blocks + [jax.ShapeDtypeStruct((count,), jnp.int32)],
        in_specs=[SMEM, SMEM, HBM, HBM, HBM],
        out_specs=[HBM] * (len(near) + len(blocks)) + [SMEM],
        scratch_shapes=[
            pltpu.SMEM((plan.replicas * CAP,), jnp.int32),
            pltpu.SMEM((plan.replicas * CAP,), jnp.int32),
            pltpu.SMEM((plan.replicas,), jnp.int32),
            pltpu.VMEM((count * SEG, plan.width), x.dtype),
            pltpu.VMEM((plan.half, 2 * PAIR, LANES), x.dtype),
            pltpu.VMEM((plan.left_rows, plan.width), x.dtype),
            pltpu.VMEM((plan.left_rows, plan.features), x.dtype),
            pltpu.SemaphoreType.DMA((count + 2 * plan.slots,)),
            pltpu.SemaphoreType.DMA((2 * count + 2 * plan.pieces,)),
        ],
        compiler_params=params(60 * 1024 * 1024),
        cost_estimate=pl.CostEstimate(flops=0, bytes_accessed=x.size, transcendentals=0),
        name="lay_out_first" if first_call else "lay_out_second",
    )(ids, residency, x, left_rows, ups)
    return list(out[: len(near)]), list(out[len(near) : -1]), out[-1]


def slot_mask(tags, first, columns, slots, share):
    lane = lax.broadcasted_iota(jnp.int32, (1, LANES), 1)
    column_slot = jnp.zeros((1, LANES), jnp.float32)
    for j in range(0, LANES, share):
        slot = (first + j) // share if first + j < columns else -1
        column_slot = jnp.where(lane >= j, float(slot), column_slot)
    return tags == column_slot


class Copies:
    def __init__(self, outer, sems):
        self.outer, self.sems, self.waits = outer, sems, []

    def both(self, target, outer_source, inner_source=None):
        sem = self.sems.at[len(self.waits)]
        copy = pltpu.make_async_copy(outer_source, target, sem)
        if inner_source is None:
            copy.start()
        else:
            pl.when(self.outer)(copy.start)
            pl.when(jnp.logical_not(self.outer))(
                pltpu.make_async_copy(inner_source, target, sem).start
            )
        self.waits.append((None, copy))

    def one(self, wanted, target, source):
        copy = pltpu.make_async_copy(source, target, self.sems.at[len(self.waits)])
        pl.when(wanted)(copy.start)
        self.waits.append((wanted, copy))

    def wait(self):
        for wanted, copy in self.waits:
            if wanted is None:
                copy.wait()
            else:
                pl.when(wanted)(copy.wait)


def lane_group(share):
    return lax.broadcasted_iota(jnp.int32, (1, LANES), 1) // share


def spread_lanes(value, share):
    total = value
    for shift in range(share, LANES, share):
        total += pltpu.roll(value, shift, 1)
    return total


def pack(low, share):
    count = LANES // share
    height = low.shape[0] // count
    everywhere = spread_lanes(low, share)
    packed = jnp.zeros((height, LANES), jnp.float32)
    for i in range(count):
        rows = everywhere[i * height : (i + 1) * height]
        packed = jnp.where(lane_group(share) == i, rows, packed)
    return packed


def unpack(packed, share):
    rows = [
        spread_lanes(jnp.where(lane_group(share) == i, packed, 0.0), share)
        for i in range(LANES // share)
    ]
    return jnp.concatenate(rows, axis=0)


def fold(product, tags, columns, slots, share):
    total = jnp.zeros(tags.shape, jnp.float32)
    for first in range(0, product.shape[1], LANES):
        mask = slot_mask(tags, first, columns, slots, share)
        total += jnp.where(mask, product[:, first : first + LANES], 0.0)
    return total


def copy_rows(copies, plan, kind, target, columns, near, wide, narrow):
    span = pl.ds(kind * PAIR, PAIR)
    for i, d in enumerate(plan.near):
        copies.both(target.at[pl.ds(d * PAIR, PAIR)], near[i].at[span, columns])
    for i, d in enumerate(plan.cross):
        copies.both(
            target.at[pl.ds(d * PAIR, PAIR)],
            plan.late_rows(narrow, i, kind).at[:, columns],
            wide[i].at[span, columns],
        )


def product_of(rows, left):
    return lax.dot_general(
        rows, left, (((1,), (1,)), ((), ())), preferred_element_type=jnp.float32
    )


def reduce_own_kernel(plan, n_steps, near, wide, narrow, own, low_ref, tag_ref, *scratch):
    rows, left, acc, tag, sems = scratch
    block = plan.width // n_steps
    outer = am_outer(plan)
    each = plan.half + 1
    steps = []
    for k in range(n_steps + 1):
        copies = Copies(outer, sems.at[pl.ds(k * each, each)])
        columns = pl.ds(k * block, block) if k < n_steps else pl.ds(plan.width, LANES)
        target = rows.at[:, columns] if k < n_steps else tag
        copy_rows(copies, plan, 0, target, columns, near, wide, narrow)
        if k < n_steps:
            copies.both(left.at[:, columns], own.at[:, columns])
        steps.append(copies)
    for k in range(n_steps):
        steps[k].wait()
        columns = pl.ds(k * block, block)
        product = product_of(rows[:, columns], left[:, columns])
        acc[...] = acc[...] + product if k else product
    steps[n_steps].wait()
    tags = tag[...].astype(jnp.float32)
    tag_ref[...] = tags
    low_ref[...] = pack(fold(acc, tags, acc.shape[1], plan.slots, plan.rank), plan.rank)


def reduce_taken_kernel(plan, n_steps, near, wide, narrow, across, *rest):
    lows, tag_ref = rest[: plan.groups], rest[plan.groups]
    rows, left, acc, tag, sems = rest[plan.groups + 1 :]
    block = plan.width // n_steps
    outer = am_outer(plan)
    inner = jnp.logical_not(outer)
    more = plan.groups - 1
    each = plan.half + plan.left_pieces + more * (plan.half + plan.left_pieces)
    steps = []
    for k in range(n_steps + 1):
        copies = Copies(outer, sems.at[pl.ds(k * each, each)])
        columns = pl.ds(k * block, block) if k < n_steps else pl.ds(plan.width, LANES)
        target = rows.at[0, :, columns] if k < n_steps else tag.at[0]
        copy_rows(copies, plan, 1, target, columns, near, wide, narrow)
        for e in range(1, plan.groups):
            for i, d in enumerate(plan.across):
                target = rows.at[e, :, columns] if k < n_steps else tag.at[e]
                copies.one(
                    inner,
                    target.at[pl.ds(d * PAIR, PAIR)],
                    across[e - 1][i].at[:, columns],
                )
        if k < n_steps:
            for piece, count in plan.left_spans():
                span = pl.ds(0, count), columns
                copies.both(
                    left.at[0, pl.ds(piece * PAIR, count), columns],
                    of_wide(wide, piece).at[span],
                    late_adapters(narrow, piece, plan).at[span],
                )
                for e in range(1, plan.groups):
                    copies.one(
                        outer,
                        left.at[e, pl.ds(piece * PAIR, count), columns],
                        across[e - 1][piece].at[span],
                    )
        steps.append(copies)
    for k in range(n_steps):
        steps[k].wait()
        columns = pl.ds(k * block, block)
        for e in range(plan.groups):
            rows_at = jnp.where(inner, e, 0)
            left_at = jnp.where(outer, e, 0)
            product = product_of(rows[rows_at, :, columns], left[left_at, :, columns])
            acc[e] = acc[e] + product if k else product
    steps[n_steps].wait()
    tag_ref[...] = tag[0].astype(jnp.float32)
    for e in range(plan.groups):
        tags = tag[jnp.where(inner, e, 0)].astype(jnp.float32)
        low = fold(acc.at[e], tags, plan.left_rows, plan.slots, plan.share)
        lows[e][...] = pack(low, plan.share)


def blocks_call(kernel, blocks, out_shape, out_specs, scratch, flops, moved, name, extra=()):
    flat, tree = jax.tree.flatten(blocks)
    n_extra = len(extra)

    def body(*refs):
        head, rest = refs[:n_extra], refs[n_extra:]
        nested = jax.tree.unflatten(tree, rest[: len(flat)])
        kernel(*head, *nested, *rest[len(flat) :])

    return pl.pallas_call(
        body,
        out_shape=out_shape,
        in_specs=[VMEM] * n_extra + [HBM] * len(flat),
        out_specs=out_specs,
        scratch_shapes=scratch,
        compiler_params=params(),
        cost_estimate=pl.CostEstimate(flops=1, bytes_accessed=1, transcendentals=0),
        name=name,
    )(*extra, *flat)


def reduce_own(plan, near, wide, narrow, own):
    height = plan.half * PAIR
    columns = own.shape[0]
    n_steps = 4
    dtype = own.dtype
    return blocks_call(
        functools.partial(reduce_own_kernel, plan, n_steps),
        [near, wide, narrow, own],
        [
            jax.ShapeDtypeStruct((height * plan.rank // LANES, LANES), jnp.float32),
            jax.ShapeDtypeStruct((height, LANES), jnp.float32),
        ],
        [VMEM] * 2,
        [
            pltpu.VMEM((height, plan.width), dtype),
            pltpu.VMEM((columns, plan.width), dtype),
            pltpu.VMEM((height, columns), jnp.float32),
            pltpu.VMEM((height, LANES), dtype),
            pltpu.SemaphoreType.DMA(((n_steps + 1) * (plan.half + 1),)),
        ],
        2 * height * plan.width * columns,
        2 * plan.width * (height + columns),
        "reduce_own",
    )


def reduce_taken(plan, near, wide, narrow, across):
    height = plan.half * PAIR
    n_steps = 4
    dtype = near[0].dtype
    groups, padded = plan.groups, plan.padded
    *lows, tag = blocks_call(
        functools.partial(reduce_taken_kernel, plan, n_steps),
        [near, wide, narrow, across],
        [jax.ShapeDtypeStruct((height * plan.share // LANES, LANES), jnp.float32)] * groups
        + [jax.ShapeDtypeStruct((height, LANES), jnp.float32)],
        [VMEM] * (groups + 1),
        [
            pltpu.VMEM((groups, height, plan.width), dtype),
            pltpu.VMEM((groups, padded, plan.width), dtype),
            pltpu.VMEM((groups, height, padded), jnp.float32),
            pltpu.VMEM((groups, height, LANES), dtype),
            pltpu.SemaphoreType.DMA(((n_steps + 1) * groups * (plan.half + plan.left_pieces),)),
        ],
        2 * height * plan.width * groups * padded,
        2 * plan.width * (height + padded) * groups,
        "reduce_taken",
    )
    return lows, tag


def add_low(mine_ref, other_ref, share):
    low = (mine_ref[...] + other_ref[...]).astype(jnp.bfloat16).astype(jnp.float32)
    return unpack(low, share)


def spread(low, tags, columns, slots, share):
    blocks = [
        jnp.where(slot_mask(tags, first, columns, slots, share), low, 0.0).astype(jnp.bfloat16)
        for first in range(0, columns, LANES)
    ]
    return jnp.concatenate(blocks, axis=1)


def write_deltas(delta, outs):
    delta = delta.astype(jnp.bfloat16)
    for i, out in enumerate(outs):
        out[...] = delta[i * PAIR : (i + 1) * PAIR]


def expand_own_kernel(plan, mine_ref, other_ref, tag_ref, own, *rest):
    outs, (up, sem) = rest[:-2], rest[-2:]
    copy = pltpu.make_async_copy(own, up, sem)
    copy.start()
    low = add_low(mine_ref, other_ref, plan.rank)
    wide_low = spread(low, tag_ref[...], up.shape[0], plan.slots, plan.rank)
    copy.wait()
    write_deltas(jnp.dot(wide_low, up[...], preferred_element_type=jnp.float32), outs)


def expand_own(plan, mine, other, tag, own):
    columns, features = own.shape
    return blocks_call(
        functools.partial(expand_own_kernel, plan),
        [own],
        [jax.ShapeDtypeStruct((PAIR, features), jnp.bfloat16)] * plan.half,
        [VMEM] * plan.half,
        [pltpu.VMEM(own.shape, own.dtype), pltpu.SemaphoreType.DMA(())],
        2 * tag.shape[0] * columns * features,
        2 * features * (columns + tag.shape[0]),
        "expand_own",
        extra=(mine, other, tag),
    )


def expand_taken_kernel(plan, *refs):
    lows, tag_ref, refs = refs[: 2 * plan.groups], refs[2 * plan.groups], refs[2 * plan.groups + 1 :]
    wide, narrow, across_wide, across_narrow = refs[:4]
    outs, (up, sems) = refs[4:-2], refs[-2:]
    copies = Copies(am_outer(plan), sems)
    for row, rows, column in plan.up_columns():
        part = pl.ds(0, rows), pl.ds(column, plan.features)
        for e in range(plan.groups):
            copies.both(
                up.at[e, pl.ds(row, rows)],
                (of_wide(wide, plan.left_pieces) if e == 0 else across_wide[e - 1]).at[part],
                (narrow if e == 0 else across_narrow[e - 1]).at[part],
            )
    if plan.padded > plan.left_rows:
        up[:, plan.left_rows :, :] = jnp.zeros(
            (plan.groups, plan.padded - plan.left_rows, plan.features), up.dtype
        )
    tags = tag_ref[...]
    wides = [
        spread(
            add_low(lows[2 * e], lows[2 * e + 1], plan.share),
            tags,
            plan.left_rows,
            plan.slots,
            plan.share,
        )
        for e in range(plan.groups)
    ]
    copies.wait()
    delta = None
    for e in range(plan.groups):
        product = jnp.dot(wides[e], up[e], preferred_element_type=jnp.float32)
        delta = product if delta is None else delta + product
    write_deltas(delta, outs)


def expand_taken(plan, lows, tag, wide, narrow, across_wide, across_narrow):
    height, features = tag.shape[0], plan.features
    return blocks_call(
        functools.partial(expand_taken_kernel, plan),
        [wide, narrow, across_wide, across_narrow],
        [jax.ShapeDtypeStruct((PAIR, features), jnp.bfloat16)] * plan.half,
        [VMEM] * plan.half,
        [
            pltpu.VMEM((plan.groups, plan.padded, features), jnp.bfloat16),
            pltpu.SemaphoreType.DMA((plan.groups * len(list(plan.up_columns())),)),
        ],
        2 * height * plan.groups * plan.padded * features,
        2 * features * (plan.groups * plan.padded + height),
        "expand_taken",
        extra=(*lows, tag),
    )


def join_kernel(seg_ref, base_ref, *refs):
    deltas, out_ref = refs[:-1], refs[-1]
    for k in range(len(deltas) * CAP):
        part = k % CAP

        @pl.when(seg_ref[k] >= 0)
        def _():
            span = pl.ds(pl.multiple_of(seg_ref[k] * SEG, SEG), SEG)
            delta = deltas[k // CAP][part * SEG : (part + 1) * SEG, :]
            out_ref[span, :] = (base_ref[span, :] + delta.astype(jnp.float32)).astype(
                out_ref.dtype
            )


def join(seg_of, base, deltas):
    height, features = base.shape
    block = min(features, 512)
    tall = pl.BlockSpec((height, block), lambda j: (0, j))
    short = pl.BlockSpec((PAIR, block), lambda j: (0, j))
    return pl.pallas_call(
        join_kernel,
        grid=(features // block,),
        out_shape=jax.ShapeDtypeStruct((height, features), jnp.bfloat16),
        in_specs=[SMEM, tall] + [short] * len(deltas),
        out_specs=tall,
        compiler_params=params(),
        cost_estimate=pl.CostEstimate(
            flops=height * features, bytes_accessed=8 * height * features, transcendentals=0
        ),
        name="join",
    )(seg_of, base, *deltas)


def swap(value, axis, distance):
    count = lax.axis_size(axis)
    return lax.ppermute(value, axis, [(i, i ^ distance) for i in range(count)])


def send(plan, value, moves):
    shape = (plan.groups, plan.replicas, lax.axis_size("tensor"))

    def place(g, r, c):
        return (g * shape[1] + r) * shape[2] + c

    pairs = [
        (place(g, r, c), place(g ^ flips[0], r ^ flips[1], c ^ flips[2]))
        for senders, *flips in moves
        for g in range(shape[0])
        for r in senders
        for c in range(shape[2])
    ]
    return lax.ppermute(value, ("groups", "replica", "tensor"), pairs)


def on_device(x, weight, lefts, ups, ids, residency):
    slots, width, rank = lefts.shape
    features = ups.shape[2]
    plan = Plan(
        lax.axis_size("replica"), lax.axis_size("groups"), slots, rank, width, features
    )
    half, n_cross = plan.half, len(plan.cross)
    core = lax.axis_index("tensor")
    outer = am_outer(plan)
    left_rows = jnp.swapaxes(lefts, 1, 2)
    near, wide, seg_of = lay_out(plan, True, ids, residency, x, left_rows, ups)

    near = [swap(block, "replica", d) for block, d in zip(near, plan.near[1:])]
    wide_in = []
    for i in range(plan.wide):
        moves = []
        if i < n_cross:
            moves.append((plan.outer, 0, plan.cross[i], 0))
        if i < plan.adapter_wide:
            moves.append((plan.inner, 0, half, 0))
        wide_in.append(send(plan, wide[i], moves))

    def part(which):
        columns = lax.dynamic_slice(weight, (0, which * features), (weight.shape[0], features))
        return jnp.dot(x, columns, preferred_element_type=jnp.float32)

    base_other = part(1 - core)
    late_ids, base_other, _ = lax.optimization_barrier((ids, base_other, seg_of))
    own_rows, late, _ = lay_out(plan, False, late_ids, residency, x, left_rows, ups)
    near = own_rows + near
    base_mine = part(core)
    def across_send(i):
        d = plan.across[i]
        block = near[plan.near.index(d)] if d in plan.near else wide_in[plan.cross.index(d)]
        value = block[PAIR:]
        if i < plan.pieces:
            piece = wide_in[i // 2][(i % 2) * PAIR : (i % 2 + 1) * PAIR]
            value = jnp.where(outer, piece, value)
        return [
            send(plan, value, [(plan.outer, e, 0, 0), (plan.inner, e, 0, 0)])
            for e in range(1, plan.groups)
        ]

    across = [across_send(0)]

    base = base_mine + swap(base_other, "tensor", 1)
    wide_in, near, across, late, base = lax.optimization_barrier(
        (wide_in, near, across, late, base)
    )
    across += [across_send(i) for i in range(1, half)]
    late_in = []
    for block, (d, _, unit) in zip(late, plan.late_blocks()):
        moves = [(plan.inner, 0, d, 0)]
        if unit < plan.pieces:
            moves.append((plan.outer, 0, half, 0))
        if unit == plan.units - 1:
            late_in[0], block = lax.optimization_barrier((late_in[0], block))
        late_in.append(send(plan, block, moves))
    across_up = [
        send(plan, late_in[0], [(plan.inner, e, 0, 0)]) for e in range(1, plan.groups)
    ]
    late_in[:-1], across = lax.optimization_barrier((late_in[:-1], across))
    across = [[blocks[e] for blocks in across] for e in range(plan.groups - 1)]

    own_left = left_rows.reshape(slots * rank, width)
    low, tag = reduce_own(plan, near, wide_in, late_in[:-1], own_left)
    other = swap(low, "tensor", 1)
    terms = expand_own(plan, low, other, tag, ups.reshape(slots * rank, features))
    deltas = [terms[0]] + [swap(terms[d], "replica", d) for d in range(1, half)]

    late_in[-1], deltas[:2], across_up = lax.optimization_barrier(
        (late_in[-1], deltas[:2], across_up)
    )
    lows, tag = reduce_taken(plan, near, wide_in, late_in, across)
    pairs = [lows[0], swap(lows[0], "tensor", 1)]
    for e in range(1, plan.groups):
        pairs.append(send(plan, lows[e], [(plan.outer, 0, 0, 0), (plan.inner, e, 0, 0)]))
        pairs.append(send(plan, lows[e], [(plan.outer, 0, 0, 1), (plan.inner, e, 0, 1)]))
    pairs, deltas = lax.optimization_barrier((pairs, deltas))
    across_wide = [blocks[plan.left_pieces] for blocks in across]
    terms = expand_taken(plan, pairs, tag, wide_in, late_in[0], across_wide, across_up)
    deltas += [terms[0]] + [swap(terms[d], "replica", d) for d in range(1, half)]
    return join(seg_of, base, deltas)


def solution(mesh):
    placed = (
        P(("groups", "replica"), "tensor"),
        P("tensor", None),
        P("replica", "tensor", None),
        P("replica", None, "tensor"),
        P(("groups", "replica")),
        P(),
    )
    return jax.shard_map(
        on_device,
        mesh=mesh,
        in_specs=placed,
        out_specs=P(("groups", "replica"), "tensor"),
        check_vma=False,
    )
```

```python
import functools

import jax
import jax.numpy as jnp
from jax import lax
from jax.experimental import pallas as pl
from jax.experimental.pallas import tpu as pltpu
from jax.sharding import PartitionSpec as P

CAP = 2
SEG = 32
LANES = 128
PAIR = CAP * SEG
VMEM_LIMIT = 24 * 1024 * 1024
HBM = pl.BlockSpec(memory_space=pltpu.HBM)
SMEM = pl.BlockSpec(memory_space=pltpu.SMEM)
VMEM = pl.BlockSpec(memory_space=pltpu.VMEM)


class Plan:
    def __init__(self, replicas, groups, slots, rank, width, features):
        self.replicas, self.groups, self.slots, self.rank = replicas, groups, slots, rank
        self.width, self.features = width, features
        self.half = replicas // 2
        self.turn = self.half // 2
        self.near = [d for d in range(self.half) if not d & self.turn]
        self.cross = [d for d in range(self.half) if d & self.turn]
        self.across = self.near[1:] + self.near[:1] + self.cross
        self.share = rank // groups
        self.left_rows = slots * self.share
        self.padded = -(-self.left_rows // LANES) * LANES
        beside = width // features
        self.up_rows = -(-self.left_rows // (beside * 16)) * 16
        self.left_pieces = -(-self.left_rows // PAIR)
        self.pieces = self.left_pieces + 1
        assert self.up_rows <= PAIR
        self.adapter_wide = -(-self.pieces // 2)
        self.units = 2 * len(self.cross)
        assert self.pieces <= self.units and self.adapter_wide <= len(self.cross)
        self.wide = len(self.cross)
        self.outer = [r for r in range(replicas) if self.is_outer(r)]
        self.inner = [r for r in range(replicas) if not self.is_outer(r)]

    def is_outer(self, r):
        return (r < self.turn) or (r >= self.replicas - self.turn)

    def up_columns(self):
        for j, row in enumerate(range(0, self.left_rows, self.up_rows)):
            yield row, min(self.up_rows, self.left_rows - row), j * self.features

    def left_spans(self):
        for piece in range(self.left_pieces):
            yield piece, min(PAIR, self.left_rows - piece * PAIR)

    def late_blocks(self):
        blocks = [(self.cross[0], 1, 0)]
        blocks += [(d, 2, 2 * i - 1) for i, d in enumerate(self.cross) if i]
        return blocks + [(self.cross[0], 1, self.units - 1)]

    def late_unit(self, refs, unit):
        if unit in (0, self.units - 1):
            return refs[0 if unit == 0 else -1]
        return refs[(unit + 1) // 2].at[pl.ds((unit - 1) % 2 * PAIR, PAIR)]

    def late_rows(self, refs, i, kind):
        if i == 0:
            return self.late_unit(refs, 0 if kind == 0 else self.units - 1)
        return self.late_unit(refs, 2 * i - 1 + kind)


def params(limit=VMEM_LIMIT):
    return pltpu.CompilerParams(vmem_limit_bytes=limit)


def am_outer(plan):
    me = lax.axis_index("replica")
    return (me < plan.turn) | (me >= plan.replicas - plan.turn)


def of_wide(refs, piece):
    return refs[piece // 2].at[pl.ds((piece % 2) * PAIR, PAIR)]


def late_adapters(late, piece, plan):
    return plan.late_unit(late, 0 if piece == plan.left_pieces else 1 + piece)


def lay_kernel(plan, first_call, ids_ref, residency_ref, x_ref, left_ref, up_ref, *rest):
    n_near = len(plan.near) - 1 if first_call else 1
    n_blocks = plan.wide if first_call else len(plan.late_blocks())
    near, rest = rest[:n_near], rest[n_near:]
    blocks, rest = rest[:n_blocks], rest[n_blocks:]
    seg_out, seg_ref, slot_ref, count_ref, staged, tags, left, up, in_sems, sems = rest
    half, slots, width, share = plan.half, plan.slots, plan.width, plan.share
    me = lax.axis_index("replica")
    first = pl.multiple_of(lax.axis_index("groups") * share, share)
    outer = am_outer(plan)
    rows_outer = outer if first_call else jnp.logical_not(outer)

    for h in range(plan.replicas):
        count_ref[h] = 0
        for p in range(CAP):
            seg_ref[h * CAP + p] = -1
            slot_ref[h * CAP + p] = 0
    for s in range(ids_ref.shape[0]):
        adapter = ids_ref[s]
        holder = adapter // slots
        place = holder * CAP + count_ref[holder]
        count_ref[holder] = count_ref[holder] + 1
        seg_ref[place] = s
        slot_ref[place] = residency_ref[adapter] - holder * slots
    for d in range(half):
        for kind in range(2):
            for p in range(CAP):
                seg_out[(kind * half + d) * CAP + p] = seg_ref[
                    (me ^ (d + kind * half)) * CAP + p
                ]

    def move(moves, tagged):
        arrivals = []
        for source, stage, _ in moves:
            arrivals.append(pltpu.make_async_copy(source, stage, in_sems.at[len(arrivals)]))
            arrivals[-1].start()
        departures = []

        def depart(source, target):
            departures.append(pltpu.make_async_copy(source, target, sems.at[len(departures)]))
            departures[-1].start()

        for d, kind, target in tagged:
            for p in range(CAP):
                slot = slot_ref[(me ^ (d + kind * half)) * CAP + p].astype(jnp.float32)
                tags[d, pl.ds((kind * CAP + p) * SEG, SEG), :] = jnp.full(
                    (SEG, LANES), slot, jnp.float32
                ).astype(tags.dtype)
        for d, kind, target in tagged:
            depart(tags.at[d, pl.ds(kind * PAIR, PAIR)], target.at[:, pl.ds(width, LANES)])
        for arrival, (_, stage, target) in zip(arrivals, moves):
            arrival.wait()
            if target is not None:
                for part, place in target:
                    depart(part, place)
        for departure in departures:
            departure.wait()

    def row_moves(targets):
        moves = []
        for d, kind, target in targets:
            for p in range(CAP):
                seg = jnp.maximum(seg_out[(kind * half + d) * CAP + p], 0)
                stage = staged.at[pl.ds(((kind * half + d) * CAP + p) * SEG, SEG)]
                moves.append(
                    (
                        x_ref.at[pl.ds(pl.multiple_of(seg * SEG, SEG), SEG)],
                        stage,
                        [(stage, target.at[pl.ds(p * SEG, SEG), pl.ds(0, width)])],
                    )
                )
        return moves

    def adapter_moves(target_of):
        moves = []
        for slot in range(slots):
            span = pl.ds(slot * share, share)
            source = pl.ds(first, share)
            moves.append((up_ref.at[slot, source], up.at[span], None))
            moves.append((left_ref.at[slot, source], left.at[span], None))
        outs = [
            (
                up.at[pl.ds(row, rows)],
                target_of(plan.left_pieces).at[pl.ds(0, rows), pl.ds(column, plan.features)],
            )
            for row, rows, column in plan.up_columns()
        ]
        outs += [
            (
                left.at[pl.ds(piece * PAIR, rows)],
                target_of(piece).at[pl.ds(0, rows), pl.ds(0, width)],
            )
            for piece, rows in plan.left_spans()
        ]
        source, stage, _ = moves[-1]
        moves[-1] = (source, stage, outs)
        return moves

    near_d = plan.near[1:] if first_call else plan.near[:1]
    near_targets = [
        (d, kind, near[i].at[pl.ds(kind * PAIR, PAIR)])
        for i, d in enumerate(near_d)
        for kind in range(2)
    ]
    if first_call:
        cross_targets = [
            (d, kind, of_wide(blocks, 2 * i + kind))
            for i, d in enumerate(plan.cross)
            for kind in range(2)
        ]
    else:
        cross_targets = [
            (d, kind, plan.late_rows(blocks, i, kind))
            for i, d in enumerate(plan.cross)
            for kind in range(2)
        ]

    @pl.when(rows_outer)
    def _():
        targets = cross_targets + near_targets
        move(row_moves(targets), targets)

    @pl.when(jnp.logical_not(rows_outer))
    def _():
        if first_call:
            adapters = adapter_moves(lambda piece: of_wide(blocks, piece))
        else:
            adapters = adapter_moves(lambda piece: late_adapters(blocks, piece, plan))
        move(adapters + row_moves(near_targets), near_targets)


def lay_out(plan, first_call, ids, residency, x, left_rows, ups):
    count = 2 * plan.half * CAP
    wide = jax.ShapeDtypeStruct((2 * PAIR, plan.width + LANES), x.dtype)
    late = [
        jax.ShapeDtypeStruct((n * PAIR, plan.width + LANES), x.dtype)
        for _, n, _ in plan.late_blocks()
    ]
    near = [wide] * (len(plan.near) - 1 if first_call else 1)
    blocks = [wide] * plan.wide if first_call else late
    out = pl.pallas_call(
        functools.partial(lay_kernel, plan, first_call),
        out_shape=near + blocks + [jax.ShapeDtypeStruct((count,), jnp.int32)],
        in_specs=[SMEM, SMEM, HBM, HBM, HBM],
        out_specs=[HBM] * (len(near) + len(blocks)) + [SMEM],
        scratch_shapes=[
            pltpu.SMEM((plan.replicas * CAP,), jnp.int32),
            pltpu.SMEM((plan.replicas * CAP,), jnp.int32),
            pltpu.SMEM((plan.replicas,), jnp.int32),
            pltpu.VMEM((count * SEG, plan.width), x.dtype),
            pltpu.VMEM((plan.half, 2 * PAIR, LANES), x.dtype),
            pltpu.VMEM((plan.left_rows, plan.width), x.dtype),
            pltpu.VMEM((plan.left_rows, plan.features), x.dtype),
            pltpu.SemaphoreType.DMA((count + 2 * plan.slots,)),
            pltpu.SemaphoreType.DMA((2 * count + 2 * plan.pieces,)),
        ],
        compiler_params=params(60 * 1024 * 1024),
        cost_estimate=pl.CostEstimate(flops=0, bytes_accessed=x.size, transcendentals=0),
        name="lay_out_first" if first_call else "lay_out_second",
    )(ids, residency, x, left_rows, ups)
    return list(out[: len(near)]), list(out[len(near) : -1]), out[-1]


def slot_mask(tags, first, columns, slots, share):
    lane = lax.broadcasted_iota(jnp.int32, (1, LANES), 1)
    column_slot = jnp.zeros((1, LANES), jnp.float32)
    for j in range(0, LANES, share):
        slot = (first + j) // share if first + j < columns else -1
        column_slot = jnp.where(lane >= j, float(slot), column_slot)
    return tags == column_slot


class Copies:
    def __init__(self, outer, sems):
        self.outer, self.sems, self.waits = outer, sems, []

    def both(self, target, outer_source, inner_source=None):
        sem = self.sems.at[len(self.waits)]
        copy = pltpu.make_async_copy(outer_source, target, sem)
        if inner_source is None:
            copy.start()
        else:
            pl.when(self.outer)(copy.start)
            pl.when(jnp.logical_not(self.outer))(
                pltpu.make_async_copy(inner_source, target, sem).start
            )
        self.waits.append((None, copy))

    def one(self, wanted, target, source):
        copy = pltpu.make_async_copy(source, target, self.sems.at[len(self.waits)])
        pl.when(wanted)(copy.start)
        self.waits.append((wanted, copy))

    def wait(self):
        for wanted, copy in self.waits:
            if wanted is None:
                copy.wait()
            else:
                pl.when(wanted)(copy.wait)


def lane_group(share):
    return lax.broadcasted_iota(jnp.int32, (1, LANES), 1) // share


def spread_lanes(value, share):
    total = value
    for shift in range(share, LANES, share):
        total += pltpu.roll(value, shift, 1)
    return total


def pack(low, share):
    count = LANES // share
    height = low.shape[0] // count
    everywhere = spread_lanes(low, share)
    packed = jnp.zeros((height, LANES), jnp.float32)
    for i in range(count):
        rows = everywhere[i * height : (i + 1) * height]
        packed = jnp.where(lane_group(share) == i, rows, packed)
    return packed


def unpack(packed, share):
    rows = [
        spread_lanes(jnp.where(lane_group(share) == i, packed, 0.0), share)
        for i in range(LANES // share)
    ]
    return jnp.concatenate(rows, axis=0)


def fold(product, tags, columns, slots, share):
    total = jnp.zeros(tags.shape, jnp.float32)
    for first in range(0, product.shape[1], LANES):
        mask = slot_mask(tags, first, columns, slots, share)
        total += jnp.where(mask, product[:, first : first + LANES], 0.0)
    return total


def copy_rows(copies, plan, kind, target, columns, near, wide, narrow):
    span = pl.ds(kind * PAIR, PAIR)
    for i, d in enumerate(plan.near):
        copies.both(target.at[pl.ds(d * PAIR, PAIR)], near[i].at[span, columns])
    for i, d in enumerate(plan.cross):
        copies.both(
            target.at[pl.ds(d * PAIR, PAIR)],
            plan.late_rows(narrow, i, kind).at[:, columns],
            wide[i].at[span, columns],
        )


def product_of(rows, left):
    return lax.dot_general(
        rows, left, (((1,), (1,)), ((), ())), preferred_element_type=jnp.float32
    )


def reduce_own_kernel(plan, n_steps, near, wide, narrow, own, low_ref, tag_ref, *scratch):
    rows, left, acc, tag, sems = scratch
    block = plan.width // n_steps
    outer = am_outer(plan)
    each = plan.half + 1
    steps = []
    for k in range(n_steps + 1):
        copies = Copies(outer, sems.at[pl.ds(k * each, each)])
        columns = pl.ds(k * block, block) if k < n_steps else pl.ds(plan.width, LANES)
        target = rows.at[:, columns] if k < n_steps else tag
        copy_rows(copies, plan, 0, target, columns, near, wide, narrow)
        if k < n_steps:
            copies.both(left.at[:, columns], own.at[:, columns])
        steps.append(copies)
    for k in range(n_steps):
        steps[k].wait()
        columns = pl.ds(k * block, block)
        product = product_of(rows[:, columns], left[:, columns])
        acc[...] = acc[...] + product if k else product
    steps[n_steps].wait()
    tags = tag[...].astype(jnp.float32)
    tag_ref[...] = tags
    low_ref[...] = pack(fold(acc, tags, acc.shape[1], plan.slots, plan.rank), plan.rank)


def reduce_taken_kernel(plan, n_steps, near, wide, narrow, across, *rest):
    lows, tag_ref = rest[: plan.groups], rest[plan.groups]
    rows, left, acc, tag, sems = rest[plan.groups + 1 :]
    block = plan.width // n_steps
    outer = am_outer(plan)
    inner = jnp.logical_not(outer)
    more = plan.groups - 1
    each = plan.half + plan.left_pieces + more * (plan.half + plan.left_pieces)
    steps = []
    for k in range(n_steps + 1):
        copies = Copies(outer, sems.at[pl.ds(k * each, each)])
        columns = pl.ds(k * block, block) if k < n_steps else pl.ds(plan.width, LANES)
        target = rows.at[0, :, columns] if k < n_steps else tag.at[0]
        copy_rows(copies, plan, 1, target, columns, near, wide, narrow)
        for e in range(1, plan.groups):
            for i, d in enumerate(plan.across):
                target = rows.at[e, :, columns] if k < n_steps else tag.at[e]
                copies.one(
                    inner,
                    target.at[pl.ds(d * PAIR, PAIR)],
                    across[e - 1][i].at[:, columns],
                )
        if k < n_steps:
            for piece, count in plan.left_spans():
                span = pl.ds(0, count), columns
                copies.both(
                    left.at[0, pl.ds(piece * PAIR, count), columns],
                    of_wide(wide, piece).at[span],
                    late_adapters(narrow, piece, plan).at[span],
                )
                for e in range(1, plan.groups):
                    copies.one(
                        outer,
                        left.at[e, pl.ds(piece * PAIR, count), columns],
                        across[e - 1][piece].at[span],
                    )
        steps.append(copies)
    for k in range(n_steps):
        steps[k].wait()
        columns = pl.ds(k * block, block)
        for e in range(plan.groups):
            rows_at = jnp.where(inner, e, 0)
            left_at = jnp.where(outer, e, 0)
            product = product_of(rows[rows_at, :, columns], left[left_at, :, columns])
            acc[e] = acc[e] + product if k else product
    steps[n_steps].wait()
    tag_ref[...] = tag[0].astype(jnp.float32)
    for e in range(plan.groups):
        tags = tag[jnp.where(inner, e, 0)].astype(jnp.float32)
        low = fold(acc.at[e], tags, plan.left_rows, plan.slots, plan.share)
        lows[e][...] = pack(low, plan.share)


def blocks_call(kernel, blocks, out_shape, out_specs, scratch, flops, moved, name, extra=()):
    flat, tree = jax.tree.flatten(blocks)
    n_extra = len(extra)

    def body(*refs):
        head, rest = refs[:n_extra], refs[n_extra:]
        nested = jax.tree.unflatten(tree, rest[: len(flat)])
        kernel(*head, *nested, *rest[len(flat) :])

    return pl.pallas_call(
        body,
        out_shape=out_shape,
        in_specs=[VMEM] * n_extra + [HBM] * len(flat),
        out_specs=out_specs,
        scratch_shapes=scratch,
        compiler_params=params(),
        cost_estimate=pl.CostEstimate(flops=1, bytes_accessed=1, transcendentals=0),
        name=name,
    )(*extra, *flat)


def reduce_own(plan, near, wide, narrow, own):
    height = plan.half * PAIR
    columns = own.shape[0]
    n_steps = 4
    dtype = own.dtype
    return blocks_call(
        functools.partial(reduce_own_kernel, plan, n_steps),
        [near, wide, narrow, own],
        [
            jax.ShapeDtypeStruct((height * plan.rank // LANES, LANES), jnp.float32),
            jax.ShapeDtypeStruct((height, LANES), jnp.float32),
        ],
        [VMEM] * 2,
        [
            pltpu.VMEM((height, plan.width), dtype),
            pltpu.VMEM((columns, plan.width), dtype),
            pltpu.VMEM((height, columns), jnp.float32),
            pltpu.VMEM((height, LANES), dtype),
            pltpu.SemaphoreType.DMA(((n_steps + 1) * (plan.half + 1),)),
        ],
        2 * height * plan.width * columns,
        2 * plan.width * (height + columns),
        "reduce_own",
    )


def reduce_taken(plan, near, wide, narrow, across):
    height = plan.half * PAIR
    n_steps = 4
    dtype = near[0].dtype
    groups, padded = plan.groups, plan.padded
    *lows, tag = blocks_call(
        functools.partial(reduce_taken_kernel, plan, n_steps),
        [near, wide, narrow, across],
        [jax.ShapeDtypeStruct((height * plan.share // LANES, LANES), jnp.float32)] * groups
        + [jax.ShapeDtypeStruct((height, LANES), jnp.float32)],
        [VMEM] * (groups + 1),
        [
            pltpu.VMEM((groups, height, plan.width), dtype),
            pltpu.VMEM((groups, padded, plan.width), dtype),
            pltpu.VMEM((groups, height, padded), jnp.float32),
            pltpu.VMEM((groups, height, LANES), dtype),
            pltpu.SemaphoreType.DMA(((n_steps + 1) * groups * (plan.half + plan.left_pieces),)),
        ],
        2 * height * plan.width * groups * padded,
        2 * plan.width * (height + padded) * groups,
        "reduce_taken",
    )
    return lows, tag


def add_low(mine_ref, other_ref, share):
    low = (mine_ref[...] + other_ref[...]).astype(jnp.bfloat16).astype(jnp.float32)
    return unpack(low, share)


def spread(low, tags, columns, slots, share):
    blocks = [
        jnp.where(slot_mask(tags, first, columns, slots, share), low, 0.0).astype(jnp.bfloat16)
        for first in range(0, columns, LANES)
    ]
    return jnp.concatenate(blocks, axis=1)


def write_deltas(delta, outs):
    delta = delta.astype(jnp.bfloat16)
    for i, out in enumerate(outs):
        out[...] = delta[i * PAIR : (i + 1) * PAIR]


def expand_own_kernel(plan, mine_ref, other_ref, tag_ref, own, *rest):
    outs, (up, sem) = rest[:-2], rest[-2:]
    copy = pltpu.make_async_copy(own, up, sem)
    copy.start()
    low = add_low(mine_ref, other_ref, plan.rank)
    wide_low = spread(low, tag_ref[...], up.shape[0], plan.slots, plan.rank)
    copy.wait()
    write_deltas(jnp.dot(wide_low, up[...], preferred_element_type=jnp.float32), outs)


def expand_own(plan, mine, other, tag, own):
    columns, features = own.shape
    return blocks_call(
        functools.partial(expand_own_kernel, plan),
        [own],
        [jax.ShapeDtypeStruct((PAIR, features), jnp.bfloat16)] * plan.half,
        [VMEM] * plan.half,
        [pltpu.VMEM(own.shape, own.dtype), pltpu.SemaphoreType.DMA(())],
        2 * tag.shape[0] * columns * features,
        2 * features * (columns + tag.shape[0]),
        "expand_own",
        extra=(mine, other, tag),
    )


def expand_taken_kernel(plan, *refs):
    lows, tag_ref, refs = refs[: 2 * plan.groups], refs[2 * plan.groups], refs[2 * plan.groups + 1 :]
    wide, narrow, across_wide, across_narrow = refs[:4]
    outs, (up, sems) = refs[4:-2], refs[-2:]
    copies = Copies(am_outer(plan), sems)
    for row, rows, column in plan.up_columns():
        part = pl.ds(0, rows), pl.ds(column, plan.features)
        for e in range(plan.groups):
            copies.both(
                up.at[e, pl.ds(row, rows)],
                (of_wide(wide, plan.left_pieces) if e == 0 else across_wide[e - 1]).at[part],
                (narrow if e == 0 else across_narrow[e - 1]).at[part],
            )
    if plan.padded > plan.left_rows:
        up[:, plan.left_rows :, :] = jnp.zeros(
            (plan.groups, plan.padded - plan.left_rows, plan.features), up.dtype
        )
    tags = tag_ref[...]
    wides = [
        spread(
            add_low(lows[2 * e], lows[2 * e + 1], plan.share),
            tags,
            plan.left_rows,
            plan.slots,
            plan.share,
        )
        for e in range(plan.groups)
    ]
    copies.wait()
    delta = None
    for e in range(plan.groups):
        product = jnp.dot(wides[e], up[e], preferred_element_type=jnp.float32)
        delta = product if delta is None else delta + product
    write_deltas(delta, outs)


def expand_taken(plan, lows, tag, wide, narrow, across_wide, across_narrow):
    height, features = tag.shape[0], plan.features
    return blocks_call(
        functools.partial(expand_taken_kernel, plan),
        [wide, narrow, across_wide, across_narrow],
        [jax.ShapeDtypeStruct((PAIR, features), jnp.bfloat16)] * plan.half,
        [VMEM] * plan.half,
        [
            pltpu.VMEM((plan.groups, plan.padded, features), jnp.bfloat16),
            pltpu.SemaphoreType.DMA((plan.groups * len(list(plan.up_columns())),)),
        ],
        2 * height * plan.groups * plan.padded * features,
        2 * features * (plan.groups * plan.padded + height),
        "expand_taken",
        extra=(*lows, tag),
    )


def join_kernel(seg_ref, base_ref, *refs):
    deltas, out_ref = refs[:-1], refs[-1]
    for k in range(len(deltas) * CAP):
        part = k % CAP

        @pl.when(seg_ref[k] >= 0)
        def _():
            span = pl.ds(pl.multiple_of(seg_ref[k] * SEG, SEG), SEG)
            delta = deltas[k // CAP][part * SEG : (part + 1) * SEG, :]
            out_ref[span, :] = (base_ref[span, :] + delta.astype(jnp.float32)).astype(
                out_ref.dtype
            )


def join(seg_of, base, deltas):
    height, features = base.shape
    block = min(features, 512)
    tall = pl.BlockSpec((height, block), lambda j: (0, j))
    short = pl.BlockSpec((PAIR, block), lambda j: (0, j))
    return pl.pallas_call(
        join_kernel,
        grid=(features // block,),
        out_shape=jax.ShapeDtypeStruct((height, features), jnp.bfloat16),
        in_specs=[SMEM, tall] + [short] * len(deltas),
        out_specs=tall,
        compiler_params=params(),
        cost_estimate=pl.CostEstimate(
            flops=height * features, bytes_accessed=8 * height * features, transcendentals=0
        ),
        name="join",
    )(seg_of, base, *deltas)


def swap(value, axis, distance):
    count = lax.axis_size(axis)
    return lax.ppermute(value, axis, [(i, i ^ distance) for i in range(count)])


def send(plan, value, moves):
    shape = (plan.groups, plan.replicas, lax.axis_size("tensor"))

    def place(g, r, c):
        return (g * shape[1] + r) * shape[2] + c

    pairs = [
        (place(g, r, c), place(g ^ flips[0], r ^ flips[1], c ^ flips[2]))
        for senders, *flips in moves
        for g in range(shape[0])
        for r in senders
        for c in range(shape[2])
    ]
    return lax.ppermute(value, ("groups", "replica", "tensor"), pairs)


def on_device(x, weight, lefts, ups, ids, residency):
    slots, width, rank = lefts.shape
    features = ups.shape[2]
    plan = Plan(
        lax.axis_size("replica"), lax.axis_size("groups"), slots, rank, width, features
    )
    half, n_cross = plan.half, len(plan.cross)
    core = lax.axis_index("tensor")
    outer = am_outer(plan)
    left_rows = jnp.swapaxes(lefts, 1, 2)
    near, wide, seg_of = lay_out(plan, True, ids, residency, x, left_rows, ups)

    near = [swap(block, "replica", d) for block, d in zip(near, plan.near[1:])]
    wide_in = []
    for i in range(plan.wide):
        moves = []
        if i < n_cross:
            moves.append((plan.outer, 0, plan.cross[i], 0))
        if i < plan.adapter_wide:
            moves.append((plan.inner, 0, half, 0))
        wide_in.append(send(plan, wide[i], moves))

    def part(which):
        columns = lax.dynamic_slice(weight, (0, which * features), (weight.shape[0], features))
        return jnp.dot(x, columns, preferred_element_type=jnp.float32)

    late_ids, near = lax.optimization_barrier((ids, near))
    own_rows, late, _ = lay_out(plan, False, late_ids, residency, x, left_rows, ups)
    near = own_rows + near
    base_other, base_mine = part(1 - core), part(core)

    def across_send(i):
        d = plan.across[i]
        block = near[plan.near.index(d)] if d in plan.near else wide_in[plan.cross.index(d)]
        value = block[PAIR:]
        if i < plan.pieces:
            piece = wide_in[i // 2][(i % 2) * PAIR : (i % 2 + 1) * PAIR]
            value = jnp.where(outer, piece, value)
        return [
            send(plan, value, [(plan.outer, e, 0, 0), (plan.inner, e, 0, 0)])
            for e in range(1, plan.groups)
        ]

    across = [across_send(0)]

    wide_in, near, across, late, base_other, base_mine = lax.optimization_barrier(
        (wide_in, near, across, late, base_other, base_mine)
    )
    across += [across_send(i) for i in range(1, half)]
    late_in = []
    for block, (d, _, unit) in zip(late, plan.late_blocks()):
        moves = [(plan.inner, 0, d, 0)]
        if unit < plan.pieces:
            moves.append((plan.outer, 0, half, 0))
        if unit == plan.units - 1:
            late_in[0], block = lax.optimization_barrier((late_in[0], block))
        late_in.append(send(plan, block, moves))
    across_up = [
        send(plan, late_in[0], [(plan.inner, e, 0, 0)]) for e in range(1, plan.groups)
    ]
    base = base_mine + swap(base_other, "tensor", 1)
    late_in[:-1], across = lax.optimization_barrier((late_in[:-1], across))
    across = [[blocks[e] for blocks in across] for e in range(plan.groups - 1)]

    own_left = left_rows.reshape(slots * rank, width)
    low, tag = reduce_own(plan, near, wide_in, late_in[:-1], own_left)
    other = swap(low, "tensor", 1)
    terms = expand_own(plan, low, other, tag, ups.reshape(slots * rank, features))
    deltas = [terms[0]] + [swap(terms[d], "replica", d) for d in range(1, half)]

    late_in[-1], deltas[:2], across_up, base = lax.optimization_barrier(
        (late_in[-1], deltas[:2], across_up, base)
    )
    lows, tag = reduce_taken(plan, near, wide_in, late_in, across)
    pairs = [lows[0], swap(lows[0], "tensor", 1)]
    for e in range(1, plan.groups):
        pairs.append(send(plan, lows[e], [(plan.outer, 0, 0, 0), (plan.inner, e, 0, 0)]))
        pairs.append(send(plan, lows[e], [(plan.outer, 0, 0, 1), (plan.inner, e, 0, 1)]))
    pairs, deltas = lax.optimization_barrier((pairs, deltas))
    across_wide = [blocks[plan.left_pieces] for blocks in across]
    terms = expand_taken(plan, pairs, tag, wide_in, late_in[0], across_wide, across_up)
    deltas += [terms[0]] + [swap(terms[d], "replica", d) for d in range(1, half)]
    return join(seg_of, base, deltas)


def solution(mesh):
    placed = (
        P(("groups", "replica"), "tensor"),
        P("tensor", None),
        P("replica", "tensor", None),
        P("replica", None, "tensor"),
        P(("groups", "replica")),
        P(),
    )
    return jax.shard_map(
        on_device,
        mesh=mesh,
        in_specs=placed,
        out_specs=P(("groups", "replica"), "tensor"),
        check_vma=False,
    )
```

```python
import functools

import jax
import jax.numpy as jnp
from jax import lax
from jax.experimental import pallas as pl
from jax.experimental.pallas import tpu as pltpu
from jax.sharding import PartitionSpec as P

CAP = 2
SEG = 32
LANES = 128
PAIR = CAP * SEG
VMEM_LIMIT = 24 * 1024 * 1024
HBM = pl.BlockSpec(memory_space=pltpu.HBM)
SMEM = pl.BlockSpec(memory_space=pltpu.SMEM)
VMEM = pl.BlockSpec(memory_space=pltpu.VMEM)


class Plan:
    def __init__(self, replicas, groups, slots, rank, width, features):
        self.replicas, self.groups, self.slots, self.rank = replicas, groups, slots, rank
        self.width, self.features = width, features
        self.half = replicas // 2
        self.turn = self.half // 2
        self.near = [d for d in range(self.half) if not d & self.turn]
        self.cross = [d for d in range(self.half) if d & self.turn]
        self.across = self.near[1:] + self.near[:1] + self.cross
        self.share = rank // groups
        self.left_rows = slots * self.share
        self.padded = -(-self.left_rows // LANES) * LANES
        beside = width // features
        self.up_rows = -(-self.left_rows // (beside * 16)) * 16
        self.left_pieces = -(-self.left_rows // PAIR)
        self.pieces = self.left_pieces + 1
        assert self.up_rows <= PAIR
        self.adapter_wide = -(-self.pieces // 2)
        self.units = 2 * len(self.cross)
        self.last_piece = self.units - 2 if self.units - 2 < self.left_pieces else None
        assert self.pieces <= self.units and self.adapter_wide <= len(self.cross)
        self.wide = len(self.cross)
        self.outer = [r for r in range(replicas) if self.is_outer(r)]
        self.inner = [r for r in range(replicas) if not self.is_outer(r)]

    def is_outer(self, r):
        return (r < self.turn) or (r >= self.replicas - self.turn)

    def up_columns(self):
        for j, row in enumerate(range(0, self.left_rows, self.up_rows)):
            yield row, min(self.up_rows, self.left_rows - row), j * self.features

    def left_spans(self):
        for piece in range(self.left_pieces):
            yield piece, min(PAIR, self.left_rows - piece * PAIR)

    def late_blocks(self):
        blocks = [(self.cross[0], 1, 0)]
        blocks += [(d, 2, 2 * i - 1) for i, d in enumerate(self.cross) if i]
        return blocks + [(self.cross[0], 1, self.units - 1)]

    def late_unit(self, refs, unit):
        if unit in (0, self.units - 1):
            return refs[0 if unit == 0 else -1]
        return refs[(unit + 1) // 2].at[pl.ds((unit - 1) % 2 * PAIR, PAIR)]

    def late_rows(self, refs, i, kind):
        if i == 0:
            return self.late_unit(refs, 0 if kind == 0 else self.units - 1)
        return self.late_unit(refs, 2 * i - 1 + kind)


def params(limit=VMEM_LIMIT):
    return pltpu.CompilerParams(vmem_limit_bytes=limit)


def am_outer(plan):
    me = lax.axis_index("replica")
    return (me < plan.turn) | (me >= plan.replicas - plan.turn)


def of_wide(refs, piece):
    return refs[piece // 2].at[pl.ds((piece % 2) * PAIR, PAIR)]


def late_adapters(late, piece, plan):
    return plan.late_unit(late, 0 if piece == plan.left_pieces else 1 + piece)


def lay_kernel(plan, first_call, ids_ref, residency_ref, x_ref, left_ref, up_ref, *rest):
    n_near = len(plan.near) - 1 if first_call else 1
    n_blocks = plan.wide if first_call else len(plan.late_blocks())
    near, rest = rest[:n_near], rest[n_near:]
    blocks, rest = rest[:n_blocks], rest[n_blocks:]
    seg_out, seg_ref, slot_ref, count_ref, staged, tags, left, up, in_sems, sems = rest
    half, slots, width, share = plan.half, plan.slots, plan.width, plan.share
    me = lax.axis_index("replica")
    first = pl.multiple_of(lax.axis_index("groups") * share, share)
    outer = am_outer(plan)
    rows_outer = outer if first_call else jnp.logical_not(outer)

    for h in range(plan.replicas):
        count_ref[h] = 0
        for p in range(CAP):
            seg_ref[h * CAP + p] = -1
            slot_ref[h * CAP + p] = 0
    for s in range(ids_ref.shape[0]):
        adapter = ids_ref[s]
        holder = adapter // slots
        place = holder * CAP + count_ref[holder]
        count_ref[holder] = count_ref[holder] + 1
        seg_ref[place] = s
        slot_ref[place] = residency_ref[adapter] - holder * slots
    for d in range(half):
        for kind in range(2):
            for p in range(CAP):
                seg_out[(kind * half + d) * CAP + p] = seg_ref[
                    (me ^ (d + kind * half)) * CAP + p
                ]

    def move(moves, tagged):
        arrivals = []
        for source, stage, _ in moves:
            arrivals.append(pltpu.make_async_copy(source, stage, in_sems.at[len(arrivals)]))
            arrivals[-1].start()
        departures = []

        def depart(source, target):
            departures.append(pltpu.make_async_copy(source, target, sems.at[len(departures)]))
            departures[-1].start()

        for d, kind, target in tagged:
            for p in range(CAP):
                slot = slot_ref[(me ^ (d + kind * half)) * CAP + p].astype(jnp.float32)
                tags[d, pl.ds((kind * CAP + p) * SEG, SEG), :] = jnp.full(
                    (SEG, LANES), slot, jnp.float32
                ).astype(tags.dtype)
        for d, kind, target in tagged:
            depart(tags.at[d, pl.ds(kind * PAIR, PAIR)], target.at[:, pl.ds(width, LANES)])
        for arrival, (_, stage, target) in zip(arrivals, moves):
            arrival.wait()
            if target is not None:
                for part, place in target:
                    depart(part, place)
        for departure in departures:
            departure.wait()

    def row_moves(targets):
        moves = []
        for d, kind, target in targets:
            for p in range(CAP):
                seg = jnp.maximum(seg_out[(kind * half + d) * CAP + p], 0)
                stage = staged.at[pl.ds(((kind * half + d) * CAP + p) * SEG, SEG)]
                moves.append(
                    (
                        x_ref.at[pl.ds(pl.multiple_of(seg * SEG, SEG), SEG)],
                        stage,
                        [(stage, target.at[pl.ds(p * SEG, SEG), pl.ds(0, width)])],
                    )
                )
        return moves

    def adapter_moves(target_of):
        moves = []
        for slot in range(slots):
            span = pl.ds(slot * share, share)
            source = pl.ds(first, share)
            moves.append((up_ref.at[slot, source], up.at[span], None))
            moves.append((left_ref.at[slot, source], left.at[span], None))
        outs = [
            (
                up.at[pl.ds(row, rows)],
                target_of(plan.left_pieces).at[pl.ds(0, rows), pl.ds(column, plan.features)],
            )
            for row, rows, column in plan.up_columns()
        ]
        outs += [
            (
                left.at[pl.ds(piece * PAIR, rows)],
                target_of(piece).at[pl.ds(0, rows), pl.ds(0, width)],
            )
            for piece, rows in plan.left_spans()
        ]
        source, stage, _ = moves[-1]
        moves[-1] = (source, stage, outs)
        return moves

    near_d = plan.near[1:] if first_call else plan.near[:1]
    near_targets = [
        (d, kind, near[i].at[pl.ds(kind * PAIR, PAIR)])
        for i, d in enumerate(near_d)
        for kind in range(2)
    ]
    if first_call:
        cross_targets = [
            (d, kind, of_wide(blocks, 2 * i + kind))
            for i, d in enumerate(plan.cross)
            for kind in range(2)
        ]
    else:
        cross_targets = [
            (d, kind, plan.late_rows(blocks, i, kind))
            for i, d in enumerate(plan.cross)
            for kind in range(2)
        ]

    @pl.when(rows_outer)
    def _():
        targets = cross_targets + near_targets
        move(row_moves(targets), targets)

    @pl.when(jnp.logical_not(rows_outer))
    def _():
        if first_call:
            adapters = adapter_moves(lambda piece: of_wide(blocks, piece))
        else:
            adapters = adapter_moves(lambda piece: late_adapters(blocks, piece, plan))
        move(adapters + row_moves(near_targets), near_targets)


def lay_out(plan, first_call, ids, residency, x, left_rows, ups):
    count = 2 * plan.half * CAP
    wide = jax.ShapeDtypeStruct((2 * PAIR, plan.width + LANES), x.dtype)
    late = [
        jax.ShapeDtypeStruct((n * PAIR, plan.width + LANES), x.dtype)
        for _, n, _ in plan.late_blocks()
    ]
    near = [wide] * (len(plan.near) - 1 if first_call else 1)
    blocks = [wide] * plan.wide if first_call else late
    out = pl.pallas_call(
        functools.partial(lay_kernel, plan, first_call),
        out_shape=near + blocks + [jax.ShapeDtypeStruct((count,), jnp.int32)],
        in_specs=[SMEM, SMEM, HBM, HBM, HBM],
        out_specs=[HBM] * (len(near) + len(blocks)) + [SMEM],
        scratch_shapes=[
            pltpu.SMEM((plan.replicas * CAP,), jnp.int32),
            pltpu.SMEM((plan.replicas * CAP,), jnp.int32),
            pltpu.SMEM((plan.replicas,), jnp.int32),
            pltpu.VMEM((count * SEG, plan.width), x.dtype),
            pltpu.VMEM((plan.half, 2 * PAIR, LANES), x.dtype),
            pltpu.VMEM((plan.left_rows, plan.width), x.dtype),
            pltpu.VMEM((plan.left_rows, plan.features), x.dtype),
            pltpu.SemaphoreType.DMA((count + 2 * plan.slots,)),
            pltpu.SemaphoreType.DMA((2 * count + 2 * plan.pieces,)),
        ],
        compiler_params=params(60 * 1024 * 1024),
        cost_estimate=pl.CostEstimate(flops=0, bytes_accessed=x.size, transcendentals=0),
        name="lay_out_first" if first_call else "lay_out_second",
    )(ids, residency, x, left_rows, ups)
    return list(out[: len(near)]), list(out[len(near) : -1]), out[-1]


def slot_mask(tags, first, columns, slots, share):
    lane = lax.broadcasted_iota(jnp.int32, (1, LANES), 1)
    column_slot = jnp.zeros((1, LANES), jnp.float32)
    for j in range(0, LANES, share):
        slot = (first + j) // share if first + j < columns else -1
        column_slot = jnp.where(lane >= j, float(slot), column_slot)
    return tags == column_slot


class Copies:
    def __init__(self, outer, sems):
        self.outer, self.sems, self.waits = outer, sems, []

    def both(self, target, outer_source, inner_source=None):
        sem = self.sems.at[len(self.waits)]
        copy = pltpu.make_async_copy(outer_source, target, sem)
        if inner_source is None:
            copy.start()
        else:
            pl.when(self.outer)(copy.start)
            pl.when(jnp.logical_not(self.outer))(
                pltpu.make_async_copy(inner_source, target, sem).start
            )
        self.waits.append((None, copy))

    def one(self, wanted, target, source):
        copy = pltpu.make_async_copy(source, target, self.sems.at[len(self.waits)])
        pl.when(wanted)(copy.start)
        self.waits.append((wanted, copy))

    def wait(self):
        for wanted, copy in self.waits:
            if wanted is None:
                copy.wait()
            else:
                pl.when(wanted)(copy.wait)


def lane_group(share):
    return lax.broadcasted_iota(jnp.int32, (1, LANES), 1) // share


def spread_lanes(value, share):
    total = value
    for shift in range(share, LANES, share):
        total += pltpu.roll(value, shift, 1)
    return total


def pack(low, share):
    count = LANES // share
    height = low.shape[0] // count
    everywhere = spread_lanes(low, share)
    packed = jnp.zeros((height, LANES), jnp.float32)
    for i in range(count):
        rows = everywhere[i * height : (i + 1) * height]
        packed = jnp.where(lane_group(share) == i, rows, packed)
    return packed


def unpack(packed, share):
    rows = [
        spread_lanes(jnp.where(lane_group(share) == i, packed, 0.0), share)
        for i in range(LANES // share)
    ]
    return jnp.concatenate(rows, axis=0)


def fold(product, tags, columns, slots, share):
    total = jnp.zeros(tags.shape, jnp.float32)
    for first in range(0, product.shape[1], LANES):
        mask = slot_mask(tags, first, columns, slots, share)
        total += jnp.where(mask, product[:, first : first + LANES], 0.0)
    return total


def copy_rows(copies, plan, kind, target, columns, near, wide, narrow):
    span = pl.ds(kind * PAIR, PAIR)
    for i, d in enumerate(plan.near):
        copies.both(target.at[pl.ds(d * PAIR, PAIR)], near[i].at[span, columns])
    for i, d in enumerate(plan.cross):
        place = target.at[pl.ds(d * PAIR, PAIR)]
        if i == 0 and kind == 1:
            copies.one(jnp.logical_not(copies.outer), place, wide[i].at[span, columns])
        else:
            copies.both(
                place, plan.late_rows(narrow, i, kind).at[:, columns], wide[i].at[span, columns]
            )


def product_of(rows, left):
    return lax.dot_general(
        rows, left, (((1,), (1,)), ((), ())), preferred_element_type=jnp.float32
    )


def reduce_own_kernel(plan, n_steps, near, wide, narrow, own, low_ref, tag_ref, *scratch):
    rows, left, acc, tag, sems = scratch
    block = plan.width // n_steps
    outer = am_outer(plan)
    each = plan.half + 1
    steps = []
    for k in range(n_steps + 1):
        copies = Copies(outer, sems.at[pl.ds(k * each, each)])
        columns = pl.ds(k * block, block) if k < n_steps else pl.ds(plan.width, LANES)
        target = rows.at[:, columns] if k < n_steps else tag
        copy_rows(copies, plan, 0, target, columns, near, wide, narrow)
        if k < n_steps:
            copies.both(left.at[:, columns], own.at[:, columns])
        steps.append(copies)
    for k in range(n_steps):
        steps[k].wait()
        columns = pl.ds(k * block, block)
        product = product_of(rows[:, columns], left[:, columns])
        acc[...] = acc[...] + product if k else product
    steps[n_steps].wait()
    tags = tag[...].astype(jnp.float32)
    tag_ref[...] = tags
    low_ref[...] = pack(fold(acc, tags, acc.shape[1], plan.slots, plan.rank), plan.rank)


def reduce_taken_kernel(plan, n_steps, near, wide, narrow, across, *rest):
    lows, tag_ref = rest[: plan.groups], rest[plan.groups]
    rows, left, acc, tag, sems = rest[plan.groups + 1 :]
    block = plan.width // n_steps
    outer = am_outer(plan)
    inner = jnp.logical_not(outer)
    more = plan.groups - 1
    each = plan.half + plan.left_pieces + more * (plan.half + plan.left_pieces)
    missing = pl.ds(plan.cross[0] * PAIR, PAIR)

    @pl.when(outer)
    def _():
        rows[0, missing, :] = jnp.zeros((PAIR, plan.width), rows.dtype)
        tag[0, missing, :] = jnp.zeros((PAIR, LANES), tag.dtype)

    if plan.last_piece is not None:

        @pl.when(inner)
        def _():
            left[0, pl.ds(plan.last_piece * PAIR, PAIR), :] = jnp.zeros(
                (PAIR, plan.width), left.dtype
            )

    steps = []
    for k in range(n_steps + 1):
        copies = Copies(outer, sems.at[pl.ds(k * each, each)])
        columns = pl.ds(k * block, block) if k < n_steps else pl.ds(plan.width, LANES)
        target = rows.at[0, :, columns] if k < n_steps else tag.at[0]
        copy_rows(copies, plan, 1, target, columns, near, wide, narrow)
        for e in range(1, plan.groups):
            for i, d in enumerate(plan.across):
                target = rows.at[e, :, columns] if k < n_steps else tag.at[e]
                copies.one(
                    inner,
                    target.at[pl.ds(d * PAIR, PAIR)],
                    across[e - 1][i].at[:, columns],
                )
        if k < n_steps:
            for piece, count in plan.left_spans():
                span = pl.ds(0, count), columns
                place = left.at[0, pl.ds(piece * PAIR, count), columns]
                if piece == plan.last_piece:
                    copies.one(outer, place, of_wide(wide, piece).at[span])
                else:
                    copies.both(
                        place,
                        of_wide(wide, piece).at[span],
                        late_adapters(narrow, piece, plan).at[span],
                    )
                for e in range(1, plan.groups):
                    copies.one(
                        outer,
                        left.at[e, pl.ds(piece * PAIR, count), columns],
                        across[e - 1][piece].at[span],
                    )
        steps.append(copies)
    for k in range(n_steps):
        steps[k].wait()
        columns = pl.ds(k * block, block)
        for e in range(plan.groups):
            rows_at = jnp.where(inner, e, 0)
            left_at = jnp.where(outer, e, 0)
            product = product_of(rows[rows_at, :, columns], left[left_at, :, columns])
            acc[e] = acc[e] + product if k else product
    steps[n_steps].wait()
    tag_ref[...] = tag[0].astype(jnp.float32)
    for e in range(plan.groups):
        tags = tag[jnp.where(inner, e, 0)].astype(jnp.float32)
        low = fold(acc.at[e], tags, plan.left_rows, plan.slots, plan.share)
        lows[e][...] = pack(low, plan.share)


def reduce_last_kernel(plan, *refs):
    groups, width = plan.groups, plan.width
    before, tag_ref, refs = refs[:groups], refs[groups], refs[groups + 1 :]
    near, wide, last, across = refs[:4]
    lows, tag_out = refs[4 : 4 + groups], refs[4 + groups]
    outer = am_outer(plan)
    inner = jnp.logical_not(outer)
    first_row = plan.cross[0] * PAIR

    def padded(parts, height):
        rows = sum(part.shape[0] for part in parts)
        if rows < height:
            parts = parts + [jnp.zeros((height - rows, width), last.dtype)]
        return jnp.concatenate(parts, axis=0)

    @pl.when(outer)
    def _():
        tags = last[:, width:].astype(jnp.float32)
        tag_out[...] = tag_ref[...]
        tag_out[first_row : first_row + PAIR, :] = tags
        rows = last[:, :width]
        for e in range(groups):
            total = jnp.zeros((PAIR, LANES), jnp.float32)
            for first in range(0, plan.padded, LANES):
                parts = []
                for piece, count in plan.left_spans():
                    if first <= piece * PAIR < first + LANES:
                        source = of_wide(wide, piece) if e == 0 else across[e - 1][piece]
                        parts.append(source[:count, :width])
                product = product_of(rows, padded(parts, LANES))
                mask = slot_mask(tags, first, plan.left_rows, plan.slots, plan.share)
                total += jnp.where(mask, product, 0.0)
            whole = [jnp.zeros((PAIR, LANES), jnp.float32)] * plan.half
            whole[plan.cross[0]] = total
            lows[e][...] = before[e][...] + pack(jnp.concatenate(whole, axis=0), plan.share)

    @pl.when(inner)
    def _():
        tag_out[...] = tag_ref[...]
        if plan.last_piece is None:
            for e in range(groups):
                lows[e][...] = before[e][...]
            return
        at = plan.last_piece * PAIR
        first = at // LANES * LANES
        count = min(PAIR, plan.left_rows - at)
        parts = [jnp.zeros((at - first, width), last.dtype)] if at > first else []
        left = padded(parts + [last[:count, :width]], LANES)
        for e in range(groups):
            if e == 0:
                blocks = {d: near[i][PAIR:] for i, d in enumerate(plan.near)}
                blocks.update({d: wide[i][PAIR:] for i, d in enumerate(plan.cross)})
            else:
                blocks = {d: across[e - 1][i][...] for i, d in enumerate(plan.across)}
            whole = jnp.concatenate([blocks[d] for d in range(plan.half)], axis=0)
            product = product_of(whole[:, :width], left)
            tags = whole[:, width:].astype(jnp.float32)
            mask = slot_mask(tags, first, plan.left_rows, plan.slots, plan.share)
            low = pack(jnp.where(mask, product, 0.0), plan.share)
            lows[e][...] = before[e][...] + low


def reduce_last(plan, lows, tag, near, wide, last, across):
    flat, tree = jax.tree.flatten([near, wide, last, across])
    n_head = plan.groups + 1

    def body(*refs):
        nested = jax.tree.unflatten(tree, refs[n_head : n_head + len(flat)])
        reduce_last_kernel(plan, *refs[:n_head], *nested, *refs[n_head + len(flat) :])

    shapes = [jax.ShapeDtypeStruct(a.shape, a.dtype) for a in (*lows, tag)]
    *lows, tag = pl.pallas_call(
        body,
        out_shape=shapes,
        in_specs=[VMEM] * (n_head + len(flat)),
        out_specs=[VMEM] * n_head,
        compiler_params=params(),
        cost_estimate=pl.CostEstimate(flops=1, bytes_accessed=1, transcendentals=0),
        name="reduce_last",
    )(*lows, tag, *flat)
    return lows, tag


def blocks_call(kernel, blocks, out_shape, out_specs, scratch, flops, moved, name, extra=()):
    flat, tree = jax.tree.flatten(blocks)
    n_extra = len(extra)

    def body(*refs):
        head, rest = refs[:n_extra], refs[n_extra:]
        nested = jax.tree.unflatten(tree, rest[: len(flat)])
        kernel(*head, *nested, *rest[len(flat) :])

    return pl.pallas_call(
        body,
        out_shape=out_shape,
        in_specs=[VMEM] * n_extra + [HBM] * len(flat),
        out_specs=out_specs,
        scratch_shapes=scratch,
        compiler_params=params(),
        cost_estimate=pl.CostEstimate(flops=1, bytes_accessed=1, transcendentals=0),
        name=name,
    )(*extra, *flat)


def reduce_own(plan, near, wide, narrow, own):
    height = plan.half * PAIR
    columns = own.shape[0]
    n_steps = 2
    dtype = own.dtype
    return blocks_call(
        functools.partial(reduce_own_kernel, plan, n_steps),
        [near, wide, narrow, own],
        [
            jax.ShapeDtypeStruct((height * plan.rank // LANES, LANES), jnp.float32),
            jax.ShapeDtypeStruct((height, LANES), jnp.float32),
        ],
        [VMEM] * 2,
        [
            pltpu.VMEM((height, plan.width), dtype),
            pltpu.VMEM((columns, plan.width), dtype),
            pltpu.VMEM((height, columns), jnp.float32),
            pltpu.VMEM((height, LANES), dtype),
            pltpu.SemaphoreType.DMA(((n_steps + 1) * (plan.half + 1),)),
        ],
        2 * height * plan.width * columns,
        2 * plan.width * (height + columns),
        "reduce_own",
    )


def reduce_taken(plan, near, wide, narrow, across):
    height = plan.half * PAIR
    n_steps = 2
    dtype = near[0].dtype
    groups, padded = plan.groups, plan.padded
    *lows, tag = blocks_call(
        functools.partial(reduce_taken_kernel, plan, n_steps),
        [near, wide, narrow, across],
        [jax.ShapeDtypeStruct((height * plan.share // LANES, LANES), jnp.float32)] * groups
        + [jax.ShapeDtypeStruct((height, LANES), jnp.float32)],
        [VMEM] * (groups + 1),
        [
            pltpu.VMEM((groups, height, plan.width), dtype),
            pltpu.VMEM((groups, padded, plan.width), dtype),
            pltpu.VMEM((groups, height, padded), jnp.float32),
            pltpu.VMEM((groups, height, LANES), dtype),
            pltpu.SemaphoreType.DMA(((n_steps + 1) * groups * (plan.half + plan.left_pieces),)),
        ],
        2 * height * plan.width * groups * padded,
        2 * plan.width * (height + padded) * groups,
        "reduce_taken",
    )
    return lows, tag


def add_low(mine_ref, other_ref, share):
    low = (mine_ref[...] + other_ref[...]).astype(jnp.bfloat16).astype(jnp.float32)
    return unpack(low, share)


def spread(low, tags, columns, slots, share):
    blocks = [
        jnp.where(slot_mask(tags, first, columns, slots, share), low, 0.0).astype(jnp.bfloat16)
        for first in range(0, columns, LANES)
    ]
    return jnp.concatenate(blocks, axis=1)


def write_deltas(delta, outs):
    delta = delta.astype(jnp.bfloat16)
    for i, out in enumerate(outs):
        out[...] = delta[i * PAIR : (i + 1) * PAIR]


def expand_own_kernel(plan, mine_ref, other_ref, tag_ref, own, *rest):
    outs, (up, sem) = rest[:-2], rest[-2:]
    copy = pltpu.make_async_copy(own, up, sem)
    copy.start()
    low = add_low(mine_ref, other_ref, plan.rank)
    wide_low = spread(low, tag_ref[...], up.shape[0], plan.slots, plan.rank)
    copy.wait()
    write_deltas(jnp.dot(wide_low, up[...], preferred_element_type=jnp.float32), outs)


def expand_own(plan, mine, other, tag, own):
    columns, features = own.shape
    return blocks_call(
        functools.partial(expand_own_kernel, plan),
        [own],
        [jax.ShapeDtypeStruct((PAIR, features), jnp.bfloat16)] * plan.half,
        [VMEM] * plan.half,
        [pltpu.VMEM(own.shape, own.dtype), pltpu.SemaphoreType.DMA(())],
        2 * tag.shape[0] * columns * features,
        2 * features * (columns + tag.shape[0]),
        "expand_own",
        extra=(mine, other, tag),
    )


def expand_taken_kernel(plan, *refs):
    lows, tag_ref, refs = refs[: 2 * plan.groups], refs[2 * plan.groups], refs[2 * plan.groups + 1 :]
    wide, narrow, across_wide, across_narrow = refs[:4]
    outs, (up, sems) = refs[4:-2], refs[-2:]
    copies = Copies(am_outer(plan), sems)
    for row, rows, column in plan.up_columns():
        part = pl.ds(0, rows), pl.ds(column, plan.features)
        for e in range(plan.groups):
            copies.both(
                up.at[e, pl.ds(row, rows)],
                (of_wide(wide, plan.left_pieces) if e == 0 else across_wide[e - 1]).at[part],
                (narrow if e == 0 else across_narrow[e - 1]).at[part],
            )
    if plan.padded > plan.left_rows:
        up[:, plan.left_rows :, :] = jnp.zeros(
            (plan.groups, plan.padded - plan.left_rows, plan.features), up.dtype
        )
    tags = tag_ref[...]
    wides = [
        spread(
            add_low(lows[2 * e], lows[2 * e + 1], plan.share),
            tags,
            plan.left_rows,
            plan.slots,
            plan.share,
        )
        for e in range(plan.groups)
    ]
    copies.wait()
    delta = None
    for e in range(plan.groups):
        product = jnp.dot(wides[e], up[e], preferred_element_type=jnp.float32)
        delta = product if delta is None else delta + product
    write_deltas(delta, outs)


def expand_taken(plan, lows, tag, wide, narrow, across_wide, across_narrow):
    height, features = tag.shape[0], plan.features
    return blocks_call(
        functools.partial(expand_taken_kernel, plan),
        [wide, narrow, across_wide, across_narrow],
        [jax.ShapeDtypeStruct((PAIR, features), jnp.bfloat16)] * plan.half,
        [VMEM] * plan.half,
        [
            pltpu.VMEM((plan.groups, plan.padded, features), jnp.bfloat16),
            pltpu.SemaphoreType.DMA((plan.groups * len(list(plan.up_columns())),)),
        ],
        2 * height * plan.groups * plan.padded * features,
        2 * features * (plan.groups * plan.padded + height),
        "expand_taken",
        extra=(*lows, tag),
    )


def join_kernel(seg_ref, base_ref, *refs):
    deltas, out_ref = refs[:-1], refs[-1]
    for k in range(len(deltas) * CAP):
        part = k % CAP

        @pl.when(seg_ref[k] >= 0)
        def _():
            span = pl.ds(pl.multiple_of(seg_ref[k] * SEG, SEG), SEG)
            delta = deltas[k // CAP][part * SEG : (part + 1) * SEG, :]
            out_ref[span, :] = (base_ref[span, :] + delta.astype(jnp.float32)).astype(
                out_ref.dtype
            )


def join(seg_of, base, deltas):
    height, features = base.shape
    return pl.pallas_call(
        join_kernel,
        out_shape=jax.ShapeDtypeStruct((height, features), jnp.bfloat16),
        in_specs=[SMEM, VMEM] + [VMEM] * len(deltas),
        out_specs=VMEM,
        compiler_params=params(),
        cost_estimate=pl.CostEstimate(
            flops=height * features, bytes_accessed=8 * height * features, transcendentals=0
        ),
        name="join",
    )(seg_of, base, *deltas)


def swap(value, axis, distance):
    count = lax.axis_size(axis)
    return lax.ppermute(value, axis, [(i, i ^ distance) for i in range(count)])


def send(plan, value, moves):
    shape = (plan.groups, plan.replicas, lax.axis_size("tensor"))

    def place(g, r, c):
        return (g * shape[1] + r) * shape[2] + c

    pairs = [
        (place(g, r, c), place(g ^ flips[0], r ^ flips[1], c ^ flips[2]))
        for senders, *flips in moves
        for g in range(shape[0])
        for r in senders
        for c in range(shape[2])
    ]
    return lax.ppermute(value, ("groups", "replica", "tensor"), pairs)


def on_device(x, weight, lefts, ups, ids, residency):
    slots, width, rank = lefts.shape
    features = ups.shape[2]
    plan = Plan(
        lax.axis_size("replica"), lax.axis_size("groups"), slots, rank, width, features
    )
    half, n_cross = plan.half, len(plan.cross)
    core = lax.axis_index("tensor")
    outer = am_outer(plan)
    left_rows = jnp.swapaxes(lefts, 1, 2)
    near, wide, seg_of = lay_out(plan, True, ids, residency, x, left_rows, ups)

    near = [swap(block, "replica", d) for block, d in zip(near, plan.near[1:])]
    wide_in = []
    for i in range(plan.wide):
        moves = []
        if i < n_cross:
            moves.append((plan.outer, 0, plan.cross[i], 0))
        if i < plan.adapter_wide:
            moves.append((plan.inner, 0, half, 0))
        wide_in.append(send(plan, wide[i], moves))

    late_ids, near, late_x = lax.optimization_barrier((ids, near, x))
    own_rows, late, _ = lay_out(plan, False, late_ids, residency, x, left_rows, ups)
    near = own_rows + near
    def part(which):
        columns = lax.dynamic_slice(weight, (0, which * features), (weight.shape[0], features))
        return jnp.dot(late_x, columns, preferred_element_type=jnp.float32)

    base_other, base_mine = part(1 - core), part(core)

    def across_send(i):
        d = plan.across[i]
        block = near[plan.near.index(d)] if d in plan.near else wide_in[plan.cross.index(d)]
        value = block[PAIR:]
        if i < plan.pieces:
            piece = wide_in[i // 2][(i % 2) * PAIR : (i % 2 + 1) * PAIR]
            value = jnp.where(outer, piece, value)
        return [
            send(plan, value, [(plan.outer, e, 0, 0), (plan.inner, e, 0, 0)])
            for e in range(1, plan.groups)
        ]

    across = [across_send(0)]

    wide_in, near, across, late, base_other, base_mine = lax.optimization_barrier(
        (wide_in, near, across, late, base_other, base_mine)
    )
    across += [across_send(i) for i in range(1, half)]
    late_in = []
    for block, (d, _, unit) in zip(late, plan.late_blocks()):
        moves = [(plan.inner, 0, d, 0)]
        if unit < plan.pieces:
            moves.append((plan.outer, 0, half, 0))
        if unit == plan.units - 1:
            late_in[0], block = lax.optimization_barrier((late_in[0], block))
        late_in.append(send(plan, block, moves))
    across_up = [
        send(plan, late_in[0], [(plan.inner, e, 0, 0)]) for e in range(1, plan.groups)
    ]
    base = base_mine + swap(base_other, "tensor", 1)
    late_in[:-1], across = lax.optimization_barrier((late_in[:-1], across))
    across = [[blocks[e] for blocks in across] for e in range(plan.groups - 1)]

    own_left = left_rows.reshape(slots * rank, width)
    low, tag = reduce_own(plan, near, wide_in, late_in[:-1], own_left)
    other = swap(low, "tensor", 1)
    terms = expand_own(plan, low, other, tag, ups.reshape(slots * rank, features))
    deltas = [terms[0]] + [swap(terms[d], "replica", d) for d in range(1, half)]

    lows, tag = reduce_taken(plan, near, wide_in, late_in[:-1], across)
    late_in[-1], deltas[:2], across_up, base, lows = lax.optimization_barrier(
        (late_in[-1], deltas[:2], across_up, base, lows)
    )
    lows, tag = reduce_last(plan, lows, tag, near, wide_in, late_in[-1], across)
    pairs = [lows[0], swap(lows[0], "tensor", 1)]
    for e in range(1, plan.groups):
        pairs.append(send(plan, lows[e], [(plan.outer, 0, 0, 0), (plan.inner, e, 0, 0)]))
        pairs.append(send(plan, lows[e], [(plan.outer, 0, 0, 1), (plan.inner, e, 0, 1)]))
    pairs, deltas = lax.optimization_barrier((pairs, deltas))
    across_wide = [blocks[plan.left_pieces] for blocks in across]
    terms = expand_taken(plan, pairs, tag, wide_in, late_in[0], across_wide, across_up)
    deltas += [terms[0]] + [swap(terms[d], "replica", d) for d in range(1, half)]
    return join(seg_of, base, deltas)


def solution(mesh):
    placed = (
        P(("groups", "replica"), "tensor"),
        P("tensor", None),
        P("replica", "tensor", None),
        P("replica", None, "tensor"),
        P(("groups", "replica")),
        P(),
    )
    return jax.shard_map(
        on_device,
        mesh=mesh,
        in_specs=placed,
        out_specs=P(("groups", "replica"), "tensor"),
        check_vma=False,
    )
```

```python
import functools

import jax
import jax.numpy as jnp
from jax import lax
from jax.experimental import pallas as pl
from jax.experimental.pallas import tpu as pltpu
from jax.sharding import PartitionSpec as P

CAP = 2
SEG = 32
LANES = 128
PAIR = CAP * SEG
VMEM_LIMIT = 24 * 1024 * 1024
HBM = pl.BlockSpec(memory_space=pltpu.HBM)
SMEM = pl.BlockSpec(memory_space=pltpu.SMEM)
VMEM = pl.BlockSpec(memory_space=pltpu.VMEM)


class Plan:
    def __init__(self, replicas, groups, slots, rank, width, features):
        self.replicas, self.groups, self.slots, self.rank = replicas, groups, slots, rank
        self.width, self.features = width, features
        self.half = replicas // 2
        self.turn = self.half // 2
        self.near = [d for d in range(self.half) if not d & self.turn]
        self.cross = [d for d in range(self.half) if d & self.turn]
        self.across = self.near[1:] + self.near[:1] + self.cross
        self.share = rank // groups
        self.left_rows = slots * self.share
        self.padded = -(-self.left_rows // LANES) * LANES
        beside = width // features
        self.up_rows = -(-self.left_rows // (beside * 16)) * 16
        self.left_pieces = -(-self.left_rows // PAIR)
        self.pieces = self.left_pieces + 1
        assert self.up_rows <= PAIR
        self.adapter_wide = -(-self.pieces // 2)
        self.units = 2 * len(self.cross)
        self.last_piece = self.units - 2 if self.units - 2 < self.left_pieces else None
        assert self.pieces <= self.units and self.adapter_wide <= len(self.cross)
        self.wide = len(self.cross)
        self.outer = [r for r in range(replicas) if self.is_outer(r)]
        self.inner = [r for r in range(replicas) if not self.is_outer(r)]

    def is_outer(self, r):
        return (r < self.turn) or (r >= self.replicas - self.turn)

    def up_columns(self):
        for j, row in enumerate(range(0, self.left_rows, self.up_rows)):
            yield row, min(self.up_rows, self.left_rows - row), j * self.features

    def left_spans(self):
        for piece in range(self.left_pieces):
            yield piece, min(PAIR, self.left_rows - piece * PAIR)

    def late_blocks(self):
        blocks = [(self.cross[0], 1, 0)]
        blocks += [(d, 2, 2 * i - 1) for i, d in enumerate(self.cross) if i]
        return blocks + [(self.cross[0], 1, self.units - 1)]

    def late_unit(self, refs, unit):
        if unit in (0, self.units - 1):
            return refs[0 if unit == 0 else -1]
        return refs[(unit + 1) // 2].at[pl.ds((unit - 1) % 2 * PAIR, PAIR)]

    def late_rows(self, refs, i, kind):
        if i == 0:
            return self.late_unit(refs, 0 if kind == 0 else self.units - 1)
        return self.late_unit(refs, 2 * i - 1 + kind)


def params(limit=VMEM_LIMIT):
    return pltpu.CompilerParams(vmem_limit_bytes=limit)


def am_outer(plan):
    me = lax.axis_index("replica")
    return (me < plan.turn) | (me >= plan.replicas - plan.turn)


def of_wide(refs, piece):
    return refs[piece // 2].at[pl.ds((piece % 2) * PAIR, PAIR)]


def late_adapters(late, piece, plan):
    return plan.late_unit(late, 0 if piece == plan.left_pieces else 1 + piece)


def lay_kernel(plan, first_call, ids_ref, residency_ref, x_ref, left_ref, up_ref, *rest):
    n_near = len(plan.near) - 1 if first_call else 1
    n_blocks = plan.wide if first_call else len(plan.late_blocks())
    near, rest = rest[:n_near], rest[n_near:]
    blocks, rest = rest[:n_blocks], rest[n_blocks:]
    seg_out, seg_ref, slot_ref, count_ref, staged, tags, left, up, in_sems, sems = rest
    half, slots, width, share = plan.half, plan.slots, plan.width, plan.share
    me = lax.axis_index("replica")
    first = pl.multiple_of(lax.axis_index("groups") * share, share)
    outer = am_outer(plan)
    rows_outer = outer if first_call else jnp.logical_not(outer)

    for h in range(plan.replicas):
        count_ref[h] = 0
        for p in range(CAP):
            seg_ref[h * CAP + p] = -1
            slot_ref[h * CAP + p] = 0
    for s in range(ids_ref.shape[0]):
        adapter = ids_ref[s]
        holder = adapter // slots
        place = holder * CAP + count_ref[holder]
        count_ref[holder] = count_ref[holder] + 1
        seg_ref[place] = s
        slot_ref[place] = residency_ref[adapter] - holder * slots
    for d in range(half):
        for kind in range(2):
            for p in range(CAP):
                seg_out[(kind * half + d) * CAP + p] = seg_ref[
                    (me ^ (d + kind * half)) * CAP + p
                ]

    def move(moves, tagged):
        arrivals = []
        for source, stage, _ in moves:
            arrivals.append(pltpu.make_async_copy(source, stage, in_sems.at[len(arrivals)]))
            arrivals[-1].start()
        departures = []

        def depart(source, target):
            departures.append(pltpu.make_async_copy(source, target, sems.at[len(departures)]))
            departures[-1].start()

        for d, kind, target in tagged:
            for p in range(CAP):
                slot = slot_ref[(me ^ (d + kind * half)) * CAP + p].astype(jnp.float32)
                tags[d, pl.ds((kind * CAP + p) * SEG, SEG), :] = jnp.full(
                    (SEG, LANES), slot, jnp.float32
                ).astype(tags.dtype)
        for d, kind, target in tagged:
            depart(tags.at[d, pl.ds(kind * PAIR, PAIR)], target.at[:, pl.ds(width, LANES)])
        for arrival, (_, stage, target) in zip(arrivals, moves):
            arrival.wait()
            if target is not None:
                for part, place in target:
                    depart(part, place)
        for departure in departures:
            departure.wait()

    def row_moves(targets):
        moves = []
        for d, kind, target in targets:
            for p in range(CAP):
                seg = jnp.maximum(seg_out[(kind * half + d) * CAP + p], 0)
                stage = staged.at[pl.ds(((kind * half + d) * CAP + p) * SEG, SEG)]
                moves.append(
                    (
                        x_ref.at[pl.ds(pl.multiple_of(seg * SEG, SEG), SEG)],
                        stage,
                        [(stage, target.at[pl.ds(p * SEG, SEG), pl.ds(0, width)])],
                    )
                )
        return moves

    def adapter_moves(target_of):
        moves = []
        for slot in range(slots):
            span = pl.ds(slot * share, share)
            source = pl.ds(first, share)
            moves.append((up_ref.at[slot, source], up.at[span], None))
            moves.append((left_ref.at[slot, source], left.at[span], None))
        outs = [
            (
                up.at[pl.ds(row, rows)],
                target_of(plan.left_pieces).at[pl.ds(0, rows), pl.ds(column, plan.features)],
            )
            for row, rows, column in plan.up_columns()
        ]
        outs += [
            (
                left.at[pl.ds(piece * PAIR, rows)],
                target_of(piece).at[pl.ds(0, rows), pl.ds(0, width)],
            )
            for piece, rows in plan.left_spans()
        ]
        source, stage, _ = moves[-1]
        moves[-1] = (source, stage, outs)
        return moves

    near_d = plan.near[1:] if first_call else plan.near[:1]
    near_targets = [
        (d, kind, near[i].at[pl.ds(kind * PAIR, PAIR)])
        for i, d in enumerate(near_d)
        for kind in range(2)
    ]
    if first_call:
        cross_targets = [
            (d, kind, of_wide(blocks, 2 * i + kind))
            for i, d in enumerate(plan.cross)
            for kind in range(2)
        ]
    else:
        cross_targets = [
            (d, kind, plan.late_rows(blocks, i, kind))
            for i, d in enumerate(plan.cross)
            for kind in range(2)
        ]

    @pl.when(rows_outer)
    def _():
        targets = cross_targets + near_targets
        move(row_moves(targets), targets)

    @pl.when(jnp.logical_not(rows_outer))
    def _():
        if first_call:
            adapters = adapter_moves(lambda piece: of_wide(blocks, piece))
        else:
            adapters = adapter_moves(lambda piece: late_adapters(blocks, piece, plan))
        move(adapters + row_moves(near_targets), near_targets)


def lay_out(plan, first_call, ids, residency, x, left_rows, ups):
    count = 2 * plan.half * CAP
    wide = jax.ShapeDtypeStruct((2 * PAIR, plan.width + LANES), x.dtype)
    late = [
        jax.ShapeDtypeStruct((n * PAIR, plan.width + LANES), x.dtype)
        for _, n, _ in plan.late_blocks()
    ]
    near = [wide] * (len(plan.near) - 1 if first_call else 1)
    blocks = [wide] * plan.wide if first_call else late
    out = pl.pallas_call(
        functools.partial(lay_kernel, plan, first_call),
        out_shape=near + blocks + [jax.ShapeDtypeStruct((count,), jnp.int32)],
        in_specs=[SMEM, SMEM, HBM, HBM, HBM],
        out_specs=[HBM] * (len(near) + len(blocks)) + [SMEM],
        scratch_shapes=[
            pltpu.SMEM((plan.replicas * CAP,), jnp.int32),
            pltpu.SMEM((plan.replicas * CAP,), jnp.int32),
            pltpu.SMEM((plan.replicas,), jnp.int32),
            pltpu.VMEM((count * SEG, plan.width), x.dtype),
            pltpu.VMEM((plan.half, 2 * PAIR, LANES), x.dtype),
            pltpu.VMEM((plan.left_rows, plan.width), x.dtype),
            pltpu.VMEM((plan.left_rows, plan.features), x.dtype),
            pltpu.SemaphoreType.DMA((count + 2 * plan.slots,)),
            pltpu.SemaphoreType.DMA((2 * count + 2 * plan.pieces,)),
        ],
        compiler_params=params(60 * 1024 * 1024),
        cost_estimate=pl.CostEstimate(flops=0, bytes_accessed=x.size, transcendentals=0),
        name="lay_out_first" if first_call else "lay_out_second",
    )(ids, residency, x, left_rows, ups)
    return list(out[: len(near)]), list(out[len(near) : -1]), out[-1]


def slot_mask(tags, first, columns, slots, share):
    lane = lax.broadcasted_iota(jnp.int32, (1, LANES), 1)
    column_slot = jnp.zeros((1, LANES), jnp.float32)
    for j in range(0, LANES, share):
        slot = (first + j) // share if first + j < columns else -1
        column_slot = jnp.where(lane >= j, float(slot), column_slot)
    return tags == column_slot


class Copies:
    def __init__(self, outer, sems):
        self.outer, self.sems, self.waits = outer, sems, []

    def both(self, target, outer_source, inner_source=None):
        sem = self.sems.at[len(self.waits)]
        copy = pltpu.make_async_copy(outer_source, target, sem)
        if inner_source is None:
            copy.start()
        else:
            pl.when(self.outer)(copy.start)
            pl.when(jnp.logical_not(self.outer))(
                pltpu.make_async_copy(inner_source, target, sem).start
            )
        self.waits.append((None, copy))

    def one(self, wanted, target, source):
        copy = pltpu.make_async_copy(source, target, self.sems.at[len(self.waits)])
        pl.when(wanted)(copy.start)
        self.waits.append((wanted, copy))

    def wait(self):
        for wanted, copy in self.waits:
            if wanted is None:
                copy.wait()
            else:
                pl.when(wanted)(copy.wait)


def lane_group(share):
    return lax.broadcasted_iota(jnp.int32, (1, LANES), 1) // share


def spread_lanes(value, share):
    total = value
    for shift in range(share, LANES, share):
        total += pltpu.roll(value, shift, 1)
    return total


def pack(low, share):
    count = LANES // share
    height = low.shape[0] // count
    everywhere = spread_lanes(low, share)
    packed = jnp.zeros((height, LANES), jnp.float32)
    for i in range(count):
        rows = everywhere[i * height : (i + 1) * height]
        packed = jnp.where(lane_group(share) == i, rows, packed)
    return packed


def unpack(packed, share):
    rows = [
        spread_lanes(jnp.where(lane_group(share) == i, packed, 0.0), share)
        for i in range(LANES // share)
    ]
    return jnp.concatenate(rows, axis=0)


def fold(product, tags, columns, slots, share):
    total = jnp.zeros(tags.shape, jnp.float32)
    for first in range(0, product.shape[1], LANES):
        mask = slot_mask(tags, first, columns, slots, share)
        total += jnp.where(mask, product[:, first : first + LANES], 0.0)
    return total


def copy_rows(copies, plan, kind, target, columns, near, wide, narrow):
    span = pl.ds(kind * PAIR, PAIR)
    for i, d in enumerate(plan.near):
        copies.both(target.at[pl.ds(d * PAIR, PAIR)], near[i].at[span, columns])
    for i, d in enumerate(plan.cross):
        place = target.at[pl.ds(d * PAIR, PAIR)]
        if i == 0 and kind == 1:
            copies.one(jnp.logical_not(copies.outer), place, wide[i].at[span, columns])
        else:
            copies.both(
                place, plan.late_rows(narrow, i, kind).at[:, columns], wide[i].at[span, columns]
            )


def product_of(rows, left):
    return lax.dot_general(
        rows, left, (((1,), (1,)), ((), ())), preferred_element_type=jnp.float32
    )


def reduce_own_kernel(plan, n_steps, near, wide, narrow, own, low_ref, tag_ref, *scratch):
    rows, left, acc, tag, sems = scratch
    block = plan.width // n_steps
    outer = am_outer(plan)
    each = plan.half + 1
    steps = []
    for k in range(n_steps + 1):
        copies = Copies(outer, sems.at[pl.ds(k * each, each)])
        columns = pl.ds(k * block, block) if k < n_steps else pl.ds(plan.width, LANES)
        target = rows.at[:, columns] if k < n_steps else tag
        copy_rows(copies, plan, 0, target, columns, near, wide, narrow)
        if k < n_steps:
            copies.both(left.at[:, columns], own.at[:, columns])
        steps.append(copies)
    for k in range(n_steps):
        steps[k].wait()
        columns = pl.ds(k * block, block)
        product = product_of(rows[:, columns], left[:, columns])
        acc[...] = acc[...] + product if k else product
    steps[n_steps].wait()
    tags = tag[...].astype(jnp.float32)
    tag_ref[...] = tags
    low_ref[...] = pack(fold(acc, tags, acc.shape[1], plan.slots, plan.rank), plan.rank)


def reduce_taken_kernel(plan, n_steps, near, wide, narrow, across, *rest):
    lows, tag_ref = rest[: plan.groups], rest[plan.groups]
    rows, left, acc, tag, sems = rest[plan.groups + 1 :]
    block = plan.width // n_steps
    outer = am_outer(plan)
    inner = jnp.logical_not(outer)
    more = plan.groups - 1
    each = plan.half + plan.left_pieces + more * (plan.half + plan.left_pieces)
    missing = pl.ds(plan.cross[0] * PAIR, PAIR)

    @pl.when(outer)
    def _():
        rows[0, missing, :] = jnp.zeros((PAIR, plan.width), rows.dtype)
        tag[0, missing, :] = jnp.zeros((PAIR, LANES), tag.dtype)

    if plan.last_piece is not None:

        @pl.when(inner)
        def _():
            left[0, pl.ds(plan.last_piece * PAIR, PAIR), :] = jnp.zeros(
                (PAIR, plan.width), left.dtype
            )

    steps = []
    for k in range(n_steps + 1):
        copies = Copies(outer, sems.at[pl.ds(k * each, each)])
        columns = pl.ds(k * block, block) if k < n_steps else pl.ds(plan.width, LANES)
        target = rows.at[0, :, columns] if k < n_steps else tag.at[0]
        copy_rows(copies, plan, 1, target, columns, near, wide, narrow)
        for e in range(1, plan.groups):
            for i, d in enumerate(plan.across):
                target = rows.at[e, :, columns] if k < n_steps else tag.at[e]
                copies.one(
                    inner,
                    target.at[pl.ds(d * PAIR, PAIR)],
                    across[e - 1][i].at[:, columns],
                )
        if k < n_steps:
            for piece, count in plan.left_spans():
                span = pl.ds(0, count), columns
                place = left.at[0, pl.ds(piece * PAIR, count), columns]
                if piece == plan.last_piece:
                    copies.one(outer, place, of_wide(wide, piece).at[span])
                else:
                    copies.both(
                        place,
                        of_wide(wide, piece).at[span],
                        late_adapters(narrow, piece, plan).at[span],
                    )
                for e in range(1, plan.groups):
                    copies.one(
                        outer,
                        left.at[e, pl.ds(piece * PAIR, count), columns],
                        across[e - 1][piece].at[span],
                    )
        steps.append(copies)
    for k in range(n_steps):
        steps[k].wait()
        columns = pl.ds(k * block, block)
        for e in range(plan.groups):
            rows_at = jnp.where(inner, e, 0)
            left_at = jnp.where(outer, e, 0)
            product = product_of(rows[rows_at, :, columns], left[left_at, :, columns])
            acc[e] = acc[e] + product if k else product
    steps[n_steps].wait()
    tag_ref[...] = tag[0].astype(jnp.float32)
    for e in range(plan.groups):
        tags = tag[jnp.where(inner, e, 0)].astype(jnp.float32)
        low = fold(acc.at[e], tags, plan.left_rows, plan.slots, plan.share)
        lows[e][...] = pack(low, plan.share)


def reduce_last_kernel(plan, *refs):
    groups, width = plan.groups, plan.width
    before, tag_ref, refs = refs[:groups], refs[groups], refs[groups + 1 :]
    near, wide, last, across = refs[:4]
    lows, tag_out = refs[4 : 4 + groups], refs[4 + groups]
    outer = am_outer(plan)
    inner = jnp.logical_not(outer)
    first_row = plan.cross[0] * PAIR

    def padded(parts, height):
        rows = sum(part.shape[0] for part in parts)
        if rows < height:
            parts = parts + [jnp.zeros((height - rows, width), last.dtype)]
        return jnp.concatenate(parts, axis=0)

    @pl.when(outer)
    def _():
        tags = last[:, width:].astype(jnp.float32)
        tag_out[...] = tag_ref[...]
        tag_out[first_row : first_row + PAIR, :] = tags
        rows = last[:, :width]
        for e in range(groups):
            total = jnp.zeros((PAIR, LANES), jnp.float32)
            for first in range(0, plan.padded, LANES):
                parts = []
                for piece, count in plan.left_spans():
                    if first <= piece * PAIR < first + LANES:
                        source = of_wide(wide, piece) if e == 0 else across[e - 1][piece]
                        parts.append(source[:count, :width])
                product = product_of(rows, padded(parts, LANES))
                mask = slot_mask(tags, first, plan.left_rows, plan.slots, plan.share)
                total += jnp.where(mask, product, 0.0)
            whole = [jnp.zeros((PAIR, LANES), jnp.float32)] * plan.half
            whole[plan.cross[0]] = total
            lows[e][...] = before[e][...] + pack(jnp.concatenate(whole, axis=0), plan.share)

    @pl.when(inner)
    def _():
        tag_out[...] = tag_ref[...]
        if plan.last_piece is None:
            for e in range(groups):
                lows[e][...] = before[e][...]
            return
        at = plan.last_piece * PAIR
        first = at // LANES * LANES
        count = min(PAIR, plan.left_rows - at)
        parts = [jnp.zeros((at - first, width), last.dtype)] if at > first else []
        left = padded(parts + [last[:count, :width]], LANES)
        for e in range(groups):
            if e == 0:
                blocks = {d: near[i][PAIR:] for i, d in enumerate(plan.near)}
                blocks.update({d: wide[i][PAIR:] for i, d in enumerate(plan.cross)})
            else:
                blocks = {d: across[e - 1][i][...] for i, d in enumerate(plan.across)}
            whole = jnp.concatenate([blocks[d] for d in range(plan.half)], axis=0)
            product = product_of(whole[:, :width], left)
            tags = whole[:, width:].astype(jnp.float32)
            mask = slot_mask(tags, first, plan.left_rows, plan.slots, plan.share)
            low = pack(jnp.where(mask, product, 0.0), plan.share)
            lows[e][...] = before[e][...] + low


def reduce_last(plan, lows, tag, near, wide, last, across):
    flat, tree = jax.tree.flatten([near, wide, last, across])
    n_head = plan.groups + 1

    def body(*refs):
        nested = jax.tree.unflatten(tree, refs[n_head : n_head + len(flat)])
        reduce_last_kernel(plan, *refs[:n_head], *nested, *refs[n_head + len(flat) :])

    shapes = [jax.ShapeDtypeStruct(a.shape, a.dtype) for a in (*lows, tag)]
    *lows, tag = pl.pallas_call(
        body,
        out_shape=shapes,
        in_specs=[VMEM] * (n_head + len(flat)),
        out_specs=[VMEM] * n_head,
        compiler_params=params(),
        cost_estimate=pl.CostEstimate(flops=1, bytes_accessed=1, transcendentals=0),
        name="reduce_last",
    )(*lows, tag, *flat)
    return lows, tag


def blocks_call(kernel, blocks, out_shape, out_specs, scratch, flops, moved, name, extra=()):
    flat, tree = jax.tree.flatten(blocks)
    n_extra = len(extra)

    def body(*refs):
        head, rest = refs[:n_extra], refs[n_extra:]
        nested = jax.tree.unflatten(tree, rest[: len(flat)])
        kernel(*head, *nested, *rest[len(flat) :])

    return pl.pallas_call(
        body,
        out_shape=out_shape,
        in_specs=[VMEM] * n_extra + [HBM] * len(flat),
        out_specs=out_specs,
        scratch_shapes=scratch,
        compiler_params=params(),
        cost_estimate=pl.CostEstimate(flops=1, bytes_accessed=1, transcendentals=0),
        name=name,
    )(*extra, *flat)


def reduce_own(plan, near, wide, narrow, own):
    height = plan.half * PAIR
    columns = own.shape[0]
    n_steps = 2
    dtype = own.dtype
    return blocks_call(
        functools.partial(reduce_own_kernel, plan, n_steps),
        [near, wide, narrow, own],
        [
            jax.ShapeDtypeStruct((height * plan.rank // LANES, LANES), jnp.float32),
            jax.ShapeDtypeStruct((height, LANES), jnp.float32),
        ],
        [VMEM] * 2,
        [
            pltpu.VMEM((height, plan.width), dtype),
            pltpu.VMEM((columns, plan.width), dtype),
            pltpu.VMEM((height, columns), jnp.float32),
            pltpu.VMEM((height, LANES), dtype),
            pltpu.SemaphoreType.DMA(((n_steps + 1) * (plan.half + 1),)),
        ],
        2 * height * plan.width * columns,
        2 * plan.width * (height + columns),
        "reduce_own",
    )


def reduce_taken(plan, near, wide, narrow, across):
    height = plan.half * PAIR
    n_steps = 2
    dtype = near[0].dtype
    groups, padded = plan.groups, plan.padded
    *lows, tag = blocks_call(
        functools.partial(reduce_taken_kernel, plan, n_steps),
        [near, wide, narrow, across],
        [jax.ShapeDtypeStruct((height * plan.share // LANES, LANES), jnp.float32)] * groups
        + [jax.ShapeDtypeStruct((height, LANES), jnp.float32)],
        [VMEM] * (groups + 1),
        [
            pltpu.VMEM((groups, height, plan.width), dtype),
            pltpu.VMEM((groups, padded, plan.width), dtype),
            pltpu.VMEM((groups, height, padded), jnp.float32),
            pltpu.VMEM((groups, height, LANES), dtype),
            pltpu.SemaphoreType.DMA(((n_steps + 1) * groups * (plan.half + plan.left_pieces),)),
        ],
        2 * height * plan.width * groups * padded,
        2 * plan.width * (height + padded) * groups,
        "reduce_taken",
    )
    return lows, tag


def add_low(mine_ref, other_ref, share):
    low = (mine_ref[...] + other_ref[...]).astype(jnp.bfloat16).astype(jnp.float32)
    return unpack(low, share)


def spread(low, tags, columns, slots, share):
    blocks = [
        jnp.where(slot_mask(tags, first, columns, slots, share), low, 0.0).astype(jnp.bfloat16)
        for first in range(0, columns, LANES)
    ]
    return jnp.concatenate(blocks, axis=1)


def write_deltas(delta, outs):
    delta = delta.astype(jnp.bfloat16)
    for i, out in enumerate(outs):
        out[...] = delta[i * PAIR : (i + 1) * PAIR]


def expand_own_kernel(plan, mine_ref, other_ref, tag_ref, own, *rest):
    outs, (up, sem) = rest[:-2], rest[-2:]
    copy = pltpu.make_async_copy(own, up, sem)
    copy.start()
    low = add_low(mine_ref, other_ref, plan.rank)
    wide_low = spread(low, tag_ref[...], up.shape[0], plan.slots, plan.rank)
    copy.wait()
    write_deltas(jnp.dot(wide_low, up[...], preferred_element_type=jnp.float32), outs)


def expand_own(plan, mine, other, tag, own):
    columns, features = own.shape
    return blocks_call(
        functools.partial(expand_own_kernel, plan),
        [own],
        [jax.ShapeDtypeStruct((PAIR, features), jnp.bfloat16)] * plan.half,
        [VMEM] * plan.half,
        [pltpu.VMEM(own.shape, own.dtype), pltpu.SemaphoreType.DMA(())],
        2 * tag.shape[0] * columns * features,
        2 * features * (columns + tag.shape[0]),
        "expand_own",
        extra=(mine, other, tag),
    )


def expand_taken_kernel(plan, *refs):
    lows, tag_ref, refs = refs[: 2 * plan.groups], refs[2 * plan.groups], refs[2 * plan.groups + 1 :]
    wide, narrow, across_wide, across_narrow = refs[:4]
    outs, (up, sems) = refs[4:-2], refs[-2:]
    copies = Copies(am_outer(plan), sems)
    for row, rows, column in plan.up_columns():
        part = pl.ds(0, rows), pl.ds(column, plan.features)
        for e in range(plan.groups):
            copies.both(
                up.at[e, pl.ds(row, rows)],
                (of_wide(wide, plan.left_pieces) if e == 0 else across_wide[e - 1]).at[part],
                (narrow if e == 0 else across_narrow[e - 1]).at[part],
            )
    if plan.padded > plan.left_rows:
        up[:, plan.left_rows :, :] = jnp.zeros(
            (plan.groups, plan.padded - plan.left_rows, plan.features), up.dtype
        )
    tags = tag_ref[...]
    wides = [
        spread(
            add_low(lows[2 * e], lows[2 * e + 1], plan.share),
            tags,
            plan.left_rows,
            plan.slots,
            plan.share,
        )
        for e in range(plan.groups)
    ]
    copies.wait()
    delta = None
    for e in range(plan.groups):
        product = jnp.dot(wides[e], up[e], preferred_element_type=jnp.float32)
        delta = product if delta is None else delta + product
    write_deltas(delta, outs)


def expand_taken(plan, lows, tag, wide, narrow, across_wide, across_narrow):
    height, features = tag.shape[0], plan.features
    return blocks_call(
        functools.partial(expand_taken_kernel, plan),
        [wide, narrow, across_wide, across_narrow],
        [jax.ShapeDtypeStruct((PAIR, features), jnp.bfloat16)] * plan.half,
        [VMEM] * plan.half,
        [
            pltpu.VMEM((plan.groups, plan.padded, features), jnp.bfloat16),
            pltpu.SemaphoreType.DMA((plan.groups * len(list(plan.up_columns())),)),
        ],
        2 * height * plan.groups * plan.padded * features,
        2 * features * (plan.groups * plan.padded + height),
        "expand_taken",
        extra=(*lows, tag),
    )


def join_kernel(seg_ref, base_ref, *refs):
    deltas, out_ref = refs[:-1], refs[-1]
    for k in range(len(deltas) * CAP):
        part = k % CAP

        @pl.when(seg_ref[k] >= 0)
        def _():
            span = pl.ds(pl.multiple_of(seg_ref[k] * SEG, SEG), SEG)
            delta = deltas[k // CAP][part * SEG : (part + 1) * SEG, :]
            out_ref[span, :] = (base_ref[span, :] + delta.astype(jnp.float32)).astype(
                out_ref.dtype
            )


def join(seg_of, base, deltas):
    height, features = base.shape
    return pl.pallas_call(
        join_kernel,
        out_shape=jax.ShapeDtypeStruct((height, features), jnp.bfloat16),
        in_specs=[SMEM, VMEM] + [VMEM] * len(deltas),
        out_specs=VMEM,
        compiler_params=params(),
        cost_estimate=pl.CostEstimate(
            flops=height * features, bytes_accessed=8 * height * features, transcendentals=0
        ),
        name="join",
    )(seg_of, base, *deltas)


def swap(value, axis, distance):
    count = lax.axis_size(axis)
    return lax.ppermute(value, axis, [(i, i ^ distance) for i in range(count)])


def send(plan, value, moves):
    shape = (plan.groups, plan.replicas, lax.axis_size("tensor"))

    def place(g, r, c):
        return (g * shape[1] + r) * shape[2] + c

    pairs = [
        (place(g, r, c), place(g ^ flips[0], r ^ flips[1], c ^ flips[2]))
        for senders, *flips in moves
        for g in range(shape[0])
        for r in senders
        for c in range(shape[2])
    ]
    return lax.ppermute(value, ("groups", "replica", "tensor"), pairs)


def return_terms(terms):
    back = {d: swap(terms[d], "replica", d) for d in reversed(range(1, len(terms)))}
    return [back[d] for d in range(1, len(terms))]


def on_device(x, weight, lefts, ups, ids, residency):
    slots, width, rank = lefts.shape
    features = ups.shape[2]
    plan = Plan(
        lax.axis_size("replica"), lax.axis_size("groups"), slots, rank, width, features
    )
    half, n_cross = plan.half, len(plan.cross)
    core = lax.axis_index("tensor")
    outer = am_outer(plan)
    left_rows = jnp.swapaxes(lefts, 1, 2)
    near, wide, seg_of = lay_out(plan, True, ids, residency, x, left_rows, ups)

    near = [swap(block, "replica", d) for block, d in zip(near, plan.near[1:])]
    wide_in = []
    for i in range(plan.wide):
        moves = []
        if i < n_cross:
            moves.append((plan.outer, 0, plan.cross[i], 0))
        if i < plan.adapter_wide:
            moves.append((plan.inner, 0, half, 0))
        wide_in.append(send(plan, wide[i], moves))

    late_ids, _ = lax.optimization_barrier((ids, seg_of))
    near, late_x = lax.optimization_barrier((near, x))
    own_rows, late, _ = lay_out(plan, False, late_ids, residency, x, left_rows, ups)
    near = own_rows + near
    def part(which, rows):
        columns = lax.dynamic_slice(weight, (0, which * features), (weight.shape[0], features))
        return jnp.dot(rows, columns, preferred_element_type=jnp.float32)

    base_other, base_mine = part(1 - core, late_x), part(core, late_x)

    def across_send(i):
        d = plan.across[i]
        block = near[plan.near.index(d)] if d in plan.near else wide_in[plan.cross.index(d)]
        value = block[PAIR:]
        if i < plan.pieces:
            piece = wide_in[i // 2][(i % 2) * PAIR : (i % 2 + 1) * PAIR]
            value = jnp.where(outer, piece, value)
        return [
            send(plan, value, [(plan.outer, e, 0, 0), (plan.inner, e, 0, 0)])
            for e in range(1, plan.groups)
        ]

    across = [across_send(0)]

    wide_in, near, across, late, base_other, base_mine = lax.optimization_barrier(
        (wide_in, near, across, late, base_other, base_mine)
    )
    across += [across_send(i) for i in range(1, half)]
    late_in = []
    for block, (d, _, unit) in zip(late, plan.late_blocks()):
        moves = [(plan.inner, 0, d, 0)]
        if unit < plan.pieces:
            moves.append((plan.outer, 0, half, 0))
        if unit == plan.units - 1:
            late_in[0], block = lax.optimization_barrier((late_in[0], block))
        late_in.append(send(plan, block, moves))
    across_up = [
        send(plan, late_in[0], [(plan.inner, e, 0, 0)]) for e in range(1, plan.groups)
    ]
    base = base_mine + swap(base_other, "tensor", 1)
    late_in[:-1], across[:-1] = lax.optimization_barrier((late_in[:-1], across[:-1]))
    across = [[blocks[e] for blocks in across] for e in range(plan.groups - 1)]

    own_left = left_rows.reshape(slots * rank, width)
    low, tag = reduce_own(plan, near, wide_in, late_in[:-1], own_left)
    other = swap(low, "tensor", 1)
    terms = expand_own(plan, low, other, tag, ups.reshape(slots * rank, features))
    deltas = [terms[0]] + return_terms(terms)

    lows, tag = reduce_taken(plan, near, wide_in, late_in[:-1], across)
    late_in[-1], deltas[:2], across_up, base, lows = lax.optimization_barrier(
        (late_in[-1], deltas[:2], across_up, base, lows)
    )
    lows, tag = reduce_last(plan, lows, tag, near, wide_in, late_in[-1], across)
    pairs = [lows[0], swap(lows[0], "tensor", 1)]
    for e in range(1, plan.groups):
        pairs.append(send(plan, lows[e], [(plan.outer, 0, 0, 0), (plan.inner, e, 0, 0)]))
        pairs.append(send(plan, lows[e], [(plan.outer, 0, 0, 1), (plan.inner, e, 0, 1)]))
    pairs, deltas = lax.optimization_barrier((pairs, deltas))
    across_wide = [blocks[plan.left_pieces] for blocks in across]
    terms = expand_taken(plan, pairs, tag, wide_in, late_in[0], across_wide, across_up)
    deltas += [terms[0]] + return_terms(terms)
    return join(seg_of, base, deltas)


def solution(mesh):
    placed = (
        P(("groups", "replica"), "tensor"),
        P("tensor", None),
        P("replica", "tensor", None),
        P("replica", None, "tensor"),
        P(("groups", "replica")),
        P(),
    )
    return jax.shard_map(
        on_device,
        mesh=mesh,
        in_specs=placed,
        out_specs=P(("groups", "replica"), "tensor"),
        check_vma=False,
    )
```

```python
import functools

import jax
import jax.numpy as jnp
from jax import lax
from jax.experimental import pallas as pl
from jax.experimental.pallas import tpu as pltpu
from jax.sharding import PartitionSpec as P

CAP = 2
SEG = 32
LANES = 128
PAIR = CAP * SEG
VMEM_LIMIT = 24 * 1024 * 1024
HBM = pl.BlockSpec(memory_space=pltpu.HBM)
SMEM = pl.BlockSpec(memory_space=pltpu.SMEM)
VMEM = pl.BlockSpec(memory_space=pltpu.VMEM)


class Plan:
    def __init__(self, replicas, groups, slots, rank, width, features):
        self.replicas, self.groups, self.slots, self.rank = replicas, groups, slots, rank
        self.width, self.features = width, features
        self.half = replicas // 2
        self.turn = self.half // 2
        self.near = [d for d in range(self.half) if not d & self.turn]
        self.cross = [d for d in range(self.half) if d & self.turn]
        self.across = self.near[1:] + self.near[:1] + self.cross
        self.share = rank // groups
        self.left_rows = slots * self.share
        self.padded = -(-self.left_rows // LANES) * LANES
        beside = width // features
        self.up_rows = -(-self.left_rows // (beside * 16)) * 16
        self.left_pieces = -(-self.left_rows // PAIR)
        self.pieces = self.left_pieces + 1
        assert self.up_rows <= PAIR
        self.adapter_wide = -(-self.pieces // 2)
        self.units = 2 * len(self.cross)
        self.last_piece = self.units - 2 if self.units - 2 < self.left_pieces else None
        assert self.pieces <= self.units and self.adapter_wide <= len(self.cross)
        self.wide = len(self.cross)
        self.outer = [r for r in range(replicas) if self.is_outer(r)]
        self.inner = [r for r in range(replicas) if not self.is_outer(r)]

    def is_outer(self, r):
        return (r < self.turn) or (r >= self.replicas - self.turn)

    def up_columns(self):
        for j, row in enumerate(range(0, self.left_rows, self.up_rows)):
            yield row, min(self.up_rows, self.left_rows - row), j * self.features

    def left_spans(self):
        for piece in range(self.left_pieces):
            yield piece, min(PAIR, self.left_rows - piece * PAIR)

    def late_blocks(self):
        blocks = [(self.cross[0], 1, 0)]
        blocks += [(d, 2, 2 * i - 1) for i, d in enumerate(self.cross) if i]
        return blocks + [(self.cross[0], 1, self.units - 1)]

    def late_unit(self, refs, unit):
        if unit in (0, self.units - 1):
            return refs[0 if unit == 0 else -1]
        return refs[(unit + 1) // 2].at[pl.ds((unit - 1) % 2 * PAIR, PAIR)]

    def late_rows(self, refs, i, kind):
        if i == 0:
            return self.late_unit(refs, 0 if kind == 0 else self.units - 1)
        return self.late_unit(refs, 2 * i - 1 + kind)


def params(limit=VMEM_LIMIT):
    return pltpu.CompilerParams(vmem_limit_bytes=limit)


def am_outer(plan):
    me = lax.axis_index("replica")
    return (me < plan.turn) | (me >= plan.replicas - plan.turn)


def of_wide(refs, piece):
    return refs[piece // 2].at[pl.ds((piece % 2) * PAIR, PAIR)]


def late_adapters(late, piece, plan):
    return plan.late_unit(late, 0 if piece == plan.left_pieces else 1 + piece)


def lay_kernel(plan, first_call, ids_ref, residency_ref, x_ref, left_ref, up_ref, *rest):
    n_near = len(plan.near) - 1 if first_call else 1
    n_blocks = plan.wide if first_call else len(plan.late_blocks())
    near, rest = rest[:n_near], rest[n_near:]
    blocks, rest = rest[:n_blocks], rest[n_blocks:]
    seg_out, seg_ref, slot_ref, count_ref, staged, tags, left, up, in_sems, sems = rest
    half, slots, width, share = plan.half, plan.slots, plan.width, plan.share
    me = lax.axis_index("replica")
    first = pl.multiple_of(lax.axis_index("groups") * share, share)
    outer = am_outer(plan)
    rows_outer = outer if first_call else jnp.logical_not(outer)

    for h in range(plan.replicas):
        count_ref[h] = 0
        for p in range(CAP):
            seg_ref[h * CAP + p] = -1
            slot_ref[h * CAP + p] = 0
    for s in range(ids_ref.shape[0]):
        adapter = ids_ref[s]
        holder = adapter // slots
        place = holder * CAP + count_ref[holder]
        count_ref[holder] = count_ref[holder] + 1
        seg_ref[place] = s
        slot_ref[place] = residency_ref[adapter] - holder * slots
    for d in range(half):
        for kind in range(2):
            for p in range(CAP):
                seg_out[(kind * half + d) * CAP + p] = seg_ref[
                    (me ^ (d + kind * half)) * CAP + p
                ]

    def move(moves, tagged):
        arrivals = []
        for source, stage, _ in moves:
            arrivals.append(pltpu.make_async_copy(source, stage, in_sems.at[len(arrivals)]))
            arrivals[-1].start()
        departures = []

        def depart(source, target):
            departures.append(pltpu.make_async_copy(source, target, sems.at[len(departures)]))
            departures[-1].start()

        for d, kind, target in tagged:
            for p in range(CAP):
                slot = slot_ref[(me ^ (d + kind * half)) * CAP + p].astype(jnp.float32)
                tags[d, pl.ds((kind * CAP + p) * SEG, SEG), :] = jnp.full(
                    (SEG, LANES), slot, jnp.float32
                ).astype(tags.dtype)
        for d, kind, target in tagged:
            depart(tags.at[d, pl.ds(kind * PAIR, PAIR)], target.at[:, pl.ds(width, LANES)])
        for arrival, (_, stage, target) in zip(arrivals, moves):
            arrival.wait()
            if target is not None:
                for part, place in target:
                    depart(part, place)
        for departure in departures:
            departure.wait()

    def row_moves(targets):
        moves = []
        for d, kind, target in targets:
            for p in range(CAP):
                seg = jnp.maximum(seg_out[(kind * half + d) * CAP + p], 0)
                stage = staged.at[pl.ds(((kind * half + d) * CAP + p) * SEG, SEG)]
                moves.append(
                    (
                        x_ref.at[pl.ds(pl.multiple_of(seg * SEG, SEG), SEG)],
                        stage,
                        [(stage, target.at[pl.ds(p * SEG, SEG), pl.ds(0, width)])],
                    )
                )
        return moves

    def adapter_moves(target_of):
        moves = []
        for slot in range(slots):
            span = pl.ds(slot * share, share)
            source = pl.ds(first, share)
            moves.append((up_ref.at[slot, source], up.at[span], None))
            moves.append((left_ref.at[slot, source], left.at[span], None))
        outs = [
            (
                up.at[pl.ds(row, rows)],
                target_of(plan.left_pieces).at[pl.ds(0, rows), pl.ds(column, plan.features)],
            )
            for row, rows, column in plan.up_columns()
        ]
        outs += [
            (
                left.at[pl.ds(piece * PAIR, rows)],
                target_of(piece).at[pl.ds(0, rows), pl.ds(0, width)],
            )
            for piece, rows in plan.left_spans()
        ]
        source, stage, _ = moves[-1]
        moves[-1] = (source, stage, outs)
        return moves

    near_d = plan.near[1:] if first_call else plan.near[:1]
    near_targets = [
        (d, kind, near[i].at[pl.ds(kind * PAIR, PAIR)])
        for i, d in enumerate(near_d)
        for kind in range(2)
    ]
    if first_call:
        cross_targets = [
            (d, kind, of_wide(blocks, 2 * i + kind))
            for i, d in enumerate(plan.cross)
            for kind in range(2)
        ]
    else:
        cross_targets = [
            (d, kind, plan.late_rows(blocks, i, kind))
            for i, d in enumerate(plan.cross)
            for kind in range(2)
        ]

    @pl.when(rows_outer)
    def _():
        targets = cross_targets + near_targets
        move(row_moves(targets), targets)

    @pl.when(jnp.logical_not(rows_outer))
    def _():
        if first_call:
            adapters = adapter_moves(lambda piece: of_wide(blocks, piece))
        else:
            adapters = adapter_moves(lambda piece: late_adapters(blocks, piece, plan))
        move(adapters + row_moves(near_targets), near_targets)


def lay_out(plan, first_call, ids, residency, x, left_rows, ups):
    count = 2 * plan.half * CAP
    wide = jax.ShapeDtypeStruct((2 * PAIR, plan.width + LANES), x.dtype)
    late = [
        jax.ShapeDtypeStruct((n * PAIR, plan.width + LANES), x.dtype)
        for _, n, _ in plan.late_blocks()
    ]
    near = [wide] * (len(plan.near) - 1 if first_call else 1)
    blocks = [wide] * plan.wide if first_call else late
    out = pl.pallas_call(
        functools.partial(lay_kernel, plan, first_call),
        out_shape=near + blocks + [jax.ShapeDtypeStruct((count,), jnp.int32)],
        in_specs=[SMEM, SMEM, HBM, HBM, HBM],
        out_specs=[HBM] * (len(near) + len(blocks)) + [SMEM],
        scratch_shapes=[
            pltpu.SMEM((plan.replicas * CAP,), jnp.int32),
            pltpu.SMEM((plan.replicas * CAP,), jnp.int32),
            pltpu.SMEM((plan.replicas,), jnp.int32),
            pltpu.VMEM((count * SEG, plan.width), x.dtype),
            pltpu.VMEM((plan.half, 2 * PAIR, LANES), x.dtype),
            pltpu.VMEM((plan.left_rows, plan.width), x.dtype),
            pltpu.VMEM((plan.left_rows, plan.features), x.dtype),
            pltpu.SemaphoreType.DMA((count + 2 * plan.slots,)),
            pltpu.SemaphoreType.DMA((2 * count + 2 * plan.pieces,)),
        ],
        compiler_params=params(60 * 1024 * 1024),
        cost_estimate=pl.CostEstimate(flops=0, bytes_accessed=x.size, transcendentals=0),
        name="lay_out_first" if first_call else "lay_out_second",
    )(ids, residency, x, left_rows, ups)
    return list(out[: len(near)]), list(out[len(near) : -1]), out[-1]


def slot_mask(tags, first, columns, slots, share):
    lane = lax.broadcasted_iota(jnp.int32, (1, LANES), 1)
    column_slot = jnp.zeros((1, LANES), jnp.float32)
    for j in range(0, LANES, share):
        slot = (first + j) // share if first + j < columns else -1
        column_slot = jnp.where(lane >= j, float(slot), column_slot)
    return tags == column_slot


class Copies:
    def __init__(self, outer, sems):
        self.outer, self.sems, self.waits = outer, sems, []

    def both(self, target, outer_source, inner_source=None):
        sem = self.sems.at[len(self.waits)]
        copy = pltpu.make_async_copy(outer_source, target, sem)
        if inner_source is None:
            copy.start()
        else:
            pl.when(self.outer)(copy.start)
            pl.when(jnp.logical_not(self.outer))(
                pltpu.make_async_copy(inner_source, target, sem).start
            )
        self.waits.append((None, copy))

    def one(self, wanted, target, source):
        copy = pltpu.make_async_copy(source, target, self.sems.at[len(self.waits)])
        pl.when(wanted)(copy.start)
        self.waits.append((wanted, copy))

    def wait(self):
        for wanted, copy in self.waits:
            if wanted is None:
                copy.wait()
            else:
                pl.when(wanted)(copy.wait)


def lane_group(share):
    return lax.broadcasted_iota(jnp.int32, (1, LANES), 1) // share


def spread_lanes(value, share):
    total = value
    for shift in range(share, LANES, share):
        total += pltpu.roll(value, shift, 1)
    return total


def pack(low, share):
    count = LANES // share
    height = low.shape[0] // count
    everywhere = spread_lanes(low, share)
    packed = jnp.zeros((height, LANES), jnp.float32)
    for i in range(count):
        rows = everywhere[i * height : (i + 1) * height]
        packed = jnp.where(lane_group(share) == i, rows, packed)
    return packed


def unpack(packed, share):
    rows = [
        spread_lanes(jnp.where(lane_group(share) == i, packed, 0.0), share)
        for i in range(LANES // share)
    ]
    return jnp.concatenate(rows, axis=0)


def fold(product, tags, columns, slots, share):
    total = jnp.zeros(tags.shape, jnp.float32)
    for first in range(0, product.shape[1], LANES):
        mask = slot_mask(tags, first, columns, slots, share)
        total += jnp.where(mask, product[:, first : first + LANES], 0.0)
    return total


def copy_rows(copies, plan, kind, target, columns, near, wide, narrow):
    span = pl.ds(kind * PAIR, PAIR)
    for i, d in enumerate(plan.near):
        copies.both(target.at[pl.ds(d * PAIR, PAIR)], near[i].at[span, columns])
    for i, d in enumerate(plan.cross):
        place = target.at[pl.ds(d * PAIR, PAIR)]
        if i == 0 and kind == 1:
            copies.one(jnp.logical_not(copies.outer), place, wide[i].at[span, columns])
        else:
            copies.both(
                place, plan.late_rows(narrow, i, kind).at[:, columns], wide[i].at[span, columns]
            )


def product_of(rows, left):
    return lax.dot_general(
        rows, left, (((1,), (1,)), ((), ())), preferred_element_type=jnp.float32
    )


def reduce_own_kernel(plan, n_steps, near, wide, narrow, own, low_ref, tag_ref, *scratch):
    rows, left, acc, tag, sems = scratch
    block = plan.width // n_steps
    outer = am_outer(plan)
    each = plan.half + 1
    steps = []
    for k in range(n_steps + 1):
        copies = Copies(outer, sems.at[pl.ds(k * each, each)])
        columns = pl.ds(k * block, block) if k < n_steps else pl.ds(plan.width, LANES)
        target = rows.at[:, columns] if k < n_steps else tag
        copy_rows(copies, plan, 0, target, columns, near, wide, narrow)
        if k < n_steps:
            copies.both(left.at[:, columns], own.at[:, columns])
        steps.append(copies)
    for k in range(n_steps):
        steps[k].wait()
        columns = pl.ds(k * block, block)
        product = product_of(rows[:, columns], left[:, columns])
        acc[...] = acc[...] + product if k else product
    steps[n_steps].wait()
    tags = tag[...].astype(jnp.float32)
    tag_ref[...] = tags
    low_ref[...] = pack(fold(acc, tags, acc.shape[1], plan.slots, plan.rank), plan.rank)


def reduce_taken_kernel(plan, n_steps, near, wide, narrow, across, *rest):
    lows, tag_ref = rest[: plan.groups], rest[plan.groups]
    rows, left, acc, tag, sems = rest[plan.groups + 1 :]
    block = plan.width // n_steps
    outer = am_outer(plan)
    inner = jnp.logical_not(outer)
    more = plan.groups - 1
    each = plan.half + plan.left_pieces + more * (plan.half + plan.left_pieces)
    missing = pl.ds(plan.cross[0] * PAIR, PAIR)

    @pl.when(outer)
    def _():
        rows[0, missing, :] = jnp.zeros((PAIR, plan.width), rows.dtype)
        tag[0, missing, :] = jnp.zeros((PAIR, LANES), tag.dtype)

    if plan.last_piece is not None:

        @pl.when(inner)
        def _():
            left[0, pl.ds(plan.last_piece * PAIR, PAIR), :] = jnp.zeros(
                (PAIR, plan.width), left.dtype
            )

    steps = []
    for k in range(n_steps + 1):
        copies = Copies(outer, sems.at[pl.ds(k * each, each)])
        columns = pl.ds(k * block, block) if k < n_steps else pl.ds(plan.width, LANES)
        target = rows.at[0, :, columns] if k < n_steps else tag.at[0]
        copy_rows(copies, plan, 1, target, columns, near, wide, narrow)
        for e in range(1, plan.groups):
            for i, d in enumerate(plan.across):
                target = rows.at[e, :, columns] if k < n_steps else tag.at[e]
                copies.one(
                    inner,
                    target.at[pl.ds(d * PAIR, PAIR)],
                    across[e - 1][i].at[:, columns],
                )
        if k < n_steps:
            for piece, count in plan.left_spans():
                span = pl.ds(0, count), columns
                place = left.at[0, pl.ds(piece * PAIR, count), columns]
                if piece == plan.last_piece:
                    copies.one(outer, place, of_wide(wide, piece).at[span])
                else:
                    copies.both(
                        place,
                        of_wide(wide, piece).at[span],
                        late_adapters(narrow, piece, plan).at[span],
                    )
                for e in range(1, plan.groups):
                    copies.one(
                        outer,
                        left.at[e, pl.ds(piece * PAIR, count), columns],
                        across[e - 1][piece].at[span],
                    )
        steps.append(copies)
    for k in range(n_steps):
        steps[k].wait()
        columns = pl.ds(k * block, block)
        for e in range(plan.groups):
            rows_at = jnp.where(inner, e, 0)
            left_at = jnp.where(outer, e, 0)
            product = product_of(rows[rows_at, :, columns], left[left_at, :, columns])
            acc[e] = acc[e] + product if k else product
    steps[n_steps].wait()
    tag_ref[...] = tag[0].astype(jnp.float32)
    for e in range(plan.groups):
        tags = tag[jnp.where(inner, e, 0)].astype(jnp.float32)
        low = fold(acc.at[e], tags, plan.left_rows, plan.slots, plan.share)
        lows[e][...] = pack(low, plan.share)


def reduce_last_kernel(plan, *refs):
    groups, width = plan.groups, plan.width
    before, tag_ref, refs = refs[:groups], refs[groups], refs[groups + 1 :]
    near, wide, last, across = refs[:4]
    lows, tag_out = refs[4 : 4 + groups], refs[4 + groups]
    outer = am_outer(plan)
    inner = jnp.logical_not(outer)
    first_row = plan.cross[0] * PAIR

    def padded(parts, height):
        rows = sum(part.shape[0] for part in parts)
        if rows < height:
            parts = parts + [jnp.zeros((height - rows, width), last.dtype)]
        return jnp.concatenate(parts, axis=0)

    @pl.when(outer)
    def _():
        tags = last[:, width:].astype(jnp.float32)
        tag_out[...] = tag_ref[...]
        tag_out[first_row : first_row + PAIR, :] = tags
        rows = last[:, :width]
        for e in range(groups):
            total = jnp.zeros((PAIR, LANES), jnp.float32)
            for first in range(0, plan.padded, LANES):
                parts = []
                for piece, count in plan.left_spans():
                    if first <= piece * PAIR < first + LANES:
                        source = of_wide(wide, piece) if e == 0 else across[e - 1][piece]
                        parts.append(source[:count, :width])
                product = product_of(rows, padded(parts, LANES))
                mask = slot_mask(tags, first, plan.left_rows, plan.slots, plan.share)
                total += jnp.where(mask, product, 0.0)
            whole = [jnp.zeros((PAIR, LANES), jnp.float32)] * plan.half
            whole[plan.cross[0]] = total
            lows[e][...] = before[e][...] + pack(jnp.concatenate(whole, axis=0), plan.share)

    @pl.when(inner)
    def _():
        tag_out[...] = tag_ref[...]
        if plan.last_piece is None:
            for e in range(groups):
                lows[e][...] = before[e][...]
            return
        at = plan.last_piece * PAIR
        first = at // LANES * LANES
        count = min(PAIR, plan.left_rows - at)
        parts = [jnp.zeros((at - first, width), last.dtype)] if at > first else []
        left = padded(parts + [last[:count, :width]], LANES)
        for e in range(groups):
            if e == 0:
                blocks = {d: near[i][PAIR:] for i, d in enumerate(plan.near)}
                blocks.update({d: wide[i][PAIR:] for i, d in enumerate(plan.cross)})
            else:
                blocks = {d: across[e - 1][i][...] for i, d in enumerate(plan.across)}
            whole = jnp.concatenate([blocks[d] for d in range(plan.half)], axis=0)
            product = product_of(whole[:, :width], left)
            tags = whole[:, width:].astype(jnp.float32)
            mask = slot_mask(tags, first, plan.left_rows, plan.slots, plan.share)
            low = pack(jnp.where(mask, product, 0.0), plan.share)
            lows[e][...] = before[e][...] + low


def reduce_last(plan, lows, tag, near, wide, last, across):
    flat, tree = jax.tree.flatten([near, wide, last, across])
    n_head = plan.groups + 1

    def body(*refs):
        nested = jax.tree.unflatten(tree, refs[n_head : n_head + len(flat)])
        reduce_last_kernel(plan, *refs[:n_head], *nested, *refs[n_head + len(flat) :])

    shapes = [jax.ShapeDtypeStruct(a.shape, a.dtype) for a in (*lows, tag)]
    *lows, tag = pl.pallas_call(
        body,
        out_shape=shapes,
        in_specs=[VMEM] * (n_head + len(flat)),
        out_specs=[VMEM] * n_head,
        compiler_params=params(),
        cost_estimate=pl.CostEstimate(flops=1, bytes_accessed=1, transcendentals=0),
        name="reduce_last",
    )(*lows, tag, *flat)
    return lows, tag


def blocks_call(kernel, blocks, out_shape, out_specs, scratch, flops, moved, name, extra=()):
    flat, tree = jax.tree.flatten(blocks)
    n_extra = len(extra)

    def body(*refs):
        head, rest = refs[:n_extra], refs[n_extra:]
        nested = jax.tree.unflatten(tree, rest[: len(flat)])
        kernel(*head, *nested, *rest[len(flat) :])

    return pl.pallas_call(
        body,
        out_shape=out_shape,
        in_specs=[VMEM] * n_extra + [HBM] * len(flat),
        out_specs=out_specs,
        scratch_shapes=scratch,
        compiler_params=params(),
        cost_estimate=pl.CostEstimate(flops=1, bytes_accessed=1, transcendentals=0),
        name=name,
    )(*extra, *flat)


def reduce_own(plan, near, wide, narrow, own):
    height = plan.half * PAIR
    columns = own.shape[0]
    n_steps = 2
    dtype = own.dtype
    return blocks_call(
        functools.partial(reduce_own_kernel, plan, n_steps),
        [near, wide, narrow, own],
        [
            jax.ShapeDtypeStruct((height * plan.rank // LANES, LANES), jnp.float32),
            jax.ShapeDtypeStruct((height, LANES), jnp.float32),
        ],
        [VMEM] * 2,
        [
            pltpu.VMEM((height, plan.width), dtype),
            pltpu.VMEM((columns, plan.width), dtype),
            pltpu.VMEM((height, columns), jnp.float32),
            pltpu.VMEM((height, LANES), dtype),
            pltpu.SemaphoreType.DMA(((n_steps + 1) * (plan.half + 1),)),
        ],
        2 * height * plan.width * columns,
        2 * plan.width * (height + columns),
        "reduce_own",
    )


def reduce_taken(plan, near, wide, narrow, across):
    height = plan.half * PAIR
    n_steps = 2
    dtype = near[0].dtype
    groups, padded = plan.groups, plan.padded
    *lows, tag = blocks_call(
        functools.partial(reduce_taken_kernel, plan, n_steps),
        [near, wide, narrow, across],
        [jax.ShapeDtypeStruct((height * plan.share // LANES, LANES), jnp.float32)] * groups
        + [jax.ShapeDtypeStruct((height, LANES), jnp.float32)],
        [VMEM] * (groups + 1),
        [
            pltpu.VMEM((groups, height, plan.width), dtype),
            pltpu.VMEM((groups, padded, plan.width), dtype),
            pltpu.VMEM((groups, height, padded), jnp.float32),
            pltpu.VMEM((groups, height, LANES), dtype),
            pltpu.SemaphoreType.DMA(((n_steps + 1) * groups * (plan.half + plan.left_pieces),)),
        ],
        2 * height * plan.width * groups * padded,
        2 * plan.width * (height + padded) * groups,
        "reduce_taken",
    )
    return lows, tag


def add_low(mine_ref, other_ref, share):
    low = (mine_ref[...] + other_ref[...]).astype(jnp.bfloat16).astype(jnp.float32)
    return unpack(low, share)


def spread(low, tags, columns, slots, share):
    blocks = [
        jnp.where(slot_mask(tags, first, columns, slots, share), low, 0.0).astype(jnp.bfloat16)
        for first in range(0, columns, LANES)
    ]
    return jnp.concatenate(blocks, axis=1)


def write_deltas(delta, outs):
    delta = delta.astype(jnp.bfloat16)
    for i, out in enumerate(outs):
        out[...] = delta[i * PAIR : (i + 1) * PAIR]


def expand_own_kernel(plan, mine_ref, other_ref, tag_ref, own, *rest):
    outs, (up, sem) = rest[:-2], rest[-2:]
    copy = pltpu.make_async_copy(own, up, sem)
    copy.start()
    low = add_low(mine_ref, other_ref, plan.rank)
    wide_low = spread(low, tag_ref[...], up.shape[0], plan.slots, plan.rank)
    copy.wait()
    write_deltas(jnp.dot(wide_low, up[...], preferred_element_type=jnp.float32), outs)


def expand_own(plan, mine, other, tag, own):
    columns, features = own.shape
    return blocks_call(
        functools.partial(expand_own_kernel, plan),
        [own],
        [jax.ShapeDtypeStruct((PAIR, features), jnp.bfloat16)] * plan.half,
        [VMEM] * plan.half,
        [pltpu.VMEM(own.shape, own.dtype), pltpu.SemaphoreType.DMA(())],
        2 * tag.shape[0] * columns * features,
        2 * features * (columns + tag.shape[0]),
        "expand_own",
        extra=(mine, other, tag),
    )


def expand_taken_kernel(plan, *refs):
    lows, tag_ref, refs = refs[: 2 * plan.groups], refs[2 * plan.groups], refs[2 * plan.groups + 1 :]
    wide, narrow, across_wide, across_narrow = refs[:4]
    outs, (up, sems) = refs[4:-2], refs[-2:]
    copies = Copies(am_outer(plan), sems)
    for row, rows, column in plan.up_columns():
        part = pl.ds(0, rows), pl.ds(column, plan.features)
        for e in range(plan.groups):
            copies.both(
                up.at[e, pl.ds(row, rows)],
                (of_wide(wide, plan.left_pieces) if e == 0 else across_wide[e - 1]).at[part],
                (narrow if e == 0 else across_narrow[e - 1]).at[part],
            )
    if plan.padded > plan.left_rows:
        up[:, plan.left_rows :, :] = jnp.zeros(
            (plan.groups, plan.padded - plan.left_rows, plan.features), up.dtype
        )
    tags = tag_ref[...]
    wides = [
        spread(
            add_low(lows[2 * e], lows[2 * e + 1], plan.share),
            tags,
            plan.left_rows,
            plan.slots,
            plan.share,
        )
        for e in range(plan.groups)
    ]
    copies.wait()
    delta = None
    for e in range(plan.groups):
        product = jnp.dot(wides[e], up[e], preferred_element_type=jnp.float32)
        delta = product if delta is None else delta + product
    write_deltas(delta, outs)


def expand_taken(plan, lows, tag, wide, narrow, across_wide, across_narrow):
    height, features = tag.shape[0], plan.features
    return blocks_call(
        functools.partial(expand_taken_kernel, plan),
        [wide, narrow, across_wide, across_narrow],
        [jax.ShapeDtypeStruct((PAIR, features), jnp.bfloat16)] * plan.half,
        [VMEM] * plan.half,
        [
            pltpu.VMEM((plan.groups, plan.padded, features), jnp.bfloat16),
            pltpu.SemaphoreType.DMA((plan.groups * len(list(plan.up_columns())),)),
        ],
        2 * height * plan.groups * plan.padded * features,
        2 * features * (plan.groups * plan.padded + height),
        "expand_taken",
        extra=(*lows, tag),
    )


def join_kernel(seg_ref, base_ref, *refs):
    deltas, out_ref = refs[:-1], refs[-1]
    for k in range(len(deltas) * CAP):
        part = k % CAP

        @pl.when(seg_ref[k] >= 0)
        def _():
            span = pl.ds(pl.multiple_of(seg_ref[k] * SEG, SEG), SEG)
            delta = deltas[k // CAP][part * SEG : (part + 1) * SEG, :]
            out_ref[span, :] = (base_ref[span, :] + delta.astype(jnp.float32)).astype(
                out_ref.dtype
            )


def join(seg_of, base, deltas):
    height, features = base.shape
    return pl.pallas_call(
        join_kernel,
        out_shape=jax.ShapeDtypeStruct((height, features), jnp.bfloat16),
        in_specs=[SMEM, VMEM] + [VMEM] * len(deltas),
        out_specs=VMEM,
        compiler_params=params(),
        cost_estimate=pl.CostEstimate(
            flops=height * features, bytes_accessed=8 * height * features, transcendentals=0
        ),
        name="join",
    )(seg_of, base, *deltas)


def swap(value, axis, distance):
    count = lax.axis_size(axis)
    return lax.ppermute(value, axis, [(i, i ^ distance) for i in range(count)])


def send(plan, value, moves):
    shape = (plan.groups, plan.replicas, lax.axis_size("tensor"))

    def place(g, r, c):
        return (g * shape[1] + r) * shape[2] + c

    pairs = [
        (place(g, r, c), place(g ^ flips[0], r ^ flips[1], c ^ flips[2]))
        for senders, *flips in moves
        for g in range(shape[0])
        for r in senders
        for c in range(shape[2])
    ]
    return lax.ppermute(value, ("groups", "replica", "tensor"), pairs)


def return_terms(terms):
    back = {d: swap(terms[d], "replica", d) for d in reversed(range(1, len(terms)))}
    return [back[d] for d in range(1, len(terms))]


def on_device(x, weight, lefts, ups, ids, residency):
    slots, width, rank = lefts.shape
    features = ups.shape[2]
    plan = Plan(
        lax.axis_size("replica"), lax.axis_size("groups"), slots, rank, width, features
    )
    half, n_cross = plan.half, len(plan.cross)
    core = lax.axis_index("tensor")
    outer = am_outer(plan)
    left_rows = jnp.swapaxes(lefts, 1, 2)
    near, wide, seg_of = lay_out(plan, True, ids, residency, x, left_rows, ups)

    near = [swap(block, "replica", d) for block, d in zip(near, plan.near[1:])]
    wide_in = []
    for i in range(plan.wide):
        moves = []
        if i < n_cross:
            moves.append((plan.outer, 0, plan.cross[i], 0))
        if i < plan.adapter_wide:
            moves.append((plan.inner, 0, half, 0))
        wide_in.append(send(plan, wide[i], moves))

    late_ids, _ = lax.optimization_barrier((ids, seg_of))
    near, late_x = lax.optimization_barrier((near, x))
    own_rows, late, _ = lay_out(plan, False, late_ids, residency, x, left_rows, ups)
    near = own_rows + near
    def part(which, rows):
        columns = lax.dynamic_slice(weight, (0, which * features), (weight.shape[0], features))
        return jnp.dot(rows, columns, preferred_element_type=jnp.float32)

    base_other, base_mine = part(1 - core, late_x), part(core, late_x)

    def across_send(i):
        d = plan.across[i]
        block = near[plan.near.index(d)] if d in plan.near else wide_in[plan.cross.index(d)]
        value = block[PAIR:]
        if i < plan.pieces:
            piece = wide_in[i // 2][(i % 2) * PAIR : (i % 2 + 1) * PAIR]
            value = jnp.where(outer, piece, value)
        return [
            send(plan, value, [(plan.outer, e, 0, 0), (plan.inner, e, 0, 0)])
            for e in range(1, plan.groups)
        ]

    across = [across_send(0)]

    wide_in, near, across, late, base_other, base_mine = lax.optimization_barrier(
        (wide_in, near, across, late, base_other, base_mine)
    )
    across += [across_send(i) for i in range(1, half)]
    late_in = []
    for block, (d, _, unit) in zip(late, plan.late_blocks()):
        moves = [(plan.inner, 0, d, 0)]
        if unit < plan.pieces:
            moves.append((plan.outer, 0, half, 0))
        if unit == plan.units - 1:
            late_in[0], block = lax.optimization_barrier((late_in[0], block))
        late_in.append(send(plan, block, moves))
    late_up = late_in[0][: plan.up_rows, :width]
    across_up = [send(plan, late_up, [(plan.inner, e, 0, 0)]) for e in range(1, plan.groups)]
    base = base_mine + swap(base_other, "tensor", 1)
    late_in[:-1], across[:-1] = lax.optimization_barrier((late_in[:-1], across[:-1]))
    across = [[blocks[e] for blocks in across] for e in range(plan.groups - 1)]

    own_left = left_rows.reshape(slots * rank, width)
    low, tag = reduce_own(plan, near, wide_in, late_in[:-1], own_left)
    other = swap(low, "tensor", 1)
    terms = expand_own(plan, low, other, tag, ups.reshape(slots * rank, features))
    deltas = [terms[0]] + return_terms(terms)

    lows, tag = reduce_taken(plan, near, wide_in, late_in[:-1], across)
    late_in[-1], deltas[:2], across_up, base, lows = lax.optimization_barrier(
        (late_in[-1], deltas[:2], across_up, base, lows)
    )
    lows, tag = reduce_last(plan, lows, tag, near, wide_in, late_in[-1], across)
    pairs = [lows[0], swap(lows[0], "tensor", 1)]
    for e in range(1, plan.groups):
        pairs.append(send(plan, lows[e], [(plan.outer, 0, 0, 0), (plan.inner, e, 0, 0)]))
        pairs.append(send(plan, lows[e], [(plan.outer, 0, 0, 1), (plan.inner, e, 0, 1)]))
    pairs, deltas = lax.optimization_barrier((pairs, deltas))
    across_wide = [blocks[plan.left_pieces] for blocks in across]
    terms = expand_taken(plan, pairs, tag, wide_in, late_in[0], across_wide, across_up)
    deltas += [terms[0]] + return_terms(terms)
    return join(seg_of, base, deltas)


def solution(mesh):
    placed = (
        P(("groups", "replica"), "tensor"),
        P("tensor", None),
        P("replica", "tensor", None),
        P("replica", None, "tensor"),
        P(("groups", "replica")),
        P(),
    )
    return jax.shard_map(
        on_device,
        mesh=mesh,
        in_specs=placed,
        out_specs=P(("groups", "replica"), "tensor"),
        check_vma=False,
    )
```

```python
import functools

import jax
import jax.numpy as jnp
from jax import lax
from jax.experimental import pallas as pl
from jax.experimental.pallas import tpu as pltpu
from jax.sharding import PartitionSpec as P

CAP = 2
SEG = 32
LANES = 128
PAIR = CAP * SEG
VMEM_LIMIT = 24 * 1024 * 1024
HBM = pl.BlockSpec(memory_space=pltpu.HBM)
SMEM = pl.BlockSpec(memory_space=pltpu.SMEM)
VMEM = pl.BlockSpec(memory_space=pltpu.VMEM)


class Plan:
    def __init__(self, replicas, groups, slots, rank, width, features):
        self.replicas, self.groups, self.slots, self.rank = replicas, groups, slots, rank
        self.width, self.features = width, features
        self.half = replicas // 2
        self.turn = self.half // 2
        self.near = [d for d in range(self.half) if not d & self.turn]
        self.cross = [d for d in range(self.half) if d & self.turn]
        self.across = self.near[1:] + self.near[:1] + self.cross
        self.share = rank // groups
        self.left_rows = slots * self.share
        self.padded = -(-self.left_rows // LANES) * LANES
        beside = width // features
        self.up_rows = -(-self.left_rows // (beside * 16)) * 16
        self.left_pieces = -(-self.left_rows // PAIR)
        self.pieces = self.left_pieces + 1
        assert self.up_rows <= PAIR
        self.adapter_wide = -(-self.pieces // 2)
        self.units = 2 * len(self.cross)
        self.last_piece = self.units - 2 if self.units - 2 < self.left_pieces else None
        assert self.pieces <= self.units and self.adapter_wide <= len(self.cross)
        self.wide = len(self.cross)
        self.outer = [r for r in range(replicas) if self.is_outer(r)]
        self.inner = [r for r in range(replicas) if not self.is_outer(r)]

    def is_outer(self, r):
        return (r < self.turn) or (r >= self.replicas - self.turn)

    def up_columns(self):
        for j, row in enumerate(range(0, self.left_rows, self.up_rows)):
            yield row, min(self.up_rows, self.left_rows - row), j * self.features

    def left_spans(self):
        for piece in range(self.left_pieces):
            yield piece, min(PAIR, self.left_rows - piece * PAIR)

    def late_blocks(self):
        blocks = [(self.cross[0], 1, 0)]
        blocks += [(d, 2, 2 * i - 1) for i, d in enumerate(self.cross) if i]
        return blocks + [(self.cross[0], 1, self.units - 1)]

    def late_unit(self, refs, unit):
        if unit in (0, self.units - 1):
            return refs[0 if unit == 0 else -1]
        return refs[(unit + 1) // 2].at[pl.ds((unit - 1) % 2 * PAIR, PAIR)]

    def late_rows(self, refs, i, kind):
        if i == 0:
            return self.late_unit(refs, 0 if kind == 0 else self.units - 1)
        return self.late_unit(refs, 2 * i - 1 + kind)


def params(limit=VMEM_LIMIT):
    return pltpu.CompilerParams(vmem_limit_bytes=limit)


def am_outer(plan):
    me = lax.axis_index("replica")
    return (me < plan.turn) | (me >= plan.replicas - plan.turn)


def of_wide(refs, piece):
    return refs[piece // 2].at[pl.ds((piece % 2) * PAIR, PAIR)]


def late_adapters(late, piece, plan):
    return plan.late_unit(late, 0 if piece == plan.left_pieces else 1 + piece)


def lay_kernel(plan, first_call, ids_ref, residency_ref, x_ref, left_ref, up_ref, *rest):
    n_near = len(plan.near) - 1 if first_call else 1
    n_blocks = plan.wide if first_call else len(plan.late_blocks())
    n_tags = len(plan.cross) if first_call else 0
    near, rest = rest[:n_near], rest[n_near:]
    blocks, rest = rest[:n_blocks], rest[n_blocks:]
    tag_outs, rest = rest[:n_tags], rest[n_tags:]
    seg_out, seg_ref, slot_ref, count_ref, staged, tags, left, up, in_sems, sems = rest
    half, slots, width, share = plan.half, plan.slots, plan.width, plan.share
    me = lax.axis_index("replica")
    first = pl.multiple_of(lax.axis_index("groups") * share, share)
    outer = am_outer(plan)
    rows_outer = outer if first_call else jnp.logical_not(outer)

    for h in range(plan.replicas):
        count_ref[h] = 0
        for p in range(CAP):
            seg_ref[h * CAP + p] = -1
            slot_ref[h * CAP + p] = 0
    for s in range(ids_ref.shape[0]):
        adapter = ids_ref[s]
        holder = adapter // slots
        place = holder * CAP + count_ref[holder]
        count_ref[holder] = count_ref[holder] + 1
        seg_ref[place] = s
        slot_ref[place] = residency_ref[adapter] - holder * slots
    for d in range(half):
        for kind in range(2):
            for p in range(CAP):
                seg_out[(kind * half + d) * CAP + p] = seg_ref[
                    (me ^ (d + kind * half)) * CAP + p
                ]

    def move(moves, tagged):
        arrivals = []
        for source, stage, _ in moves:
            arrivals.append(pltpu.make_async_copy(source, stage, in_sems.at[len(arrivals)]))
            arrivals[-1].start()
        departures = []

        def depart(source, target):
            departures.append(pltpu.make_async_copy(source, target, sems.at[len(departures)]))
            departures[-1].start()

        written = [(d, kind) for d, kind, _ in tagged]
        if first_call:
            written += [(d, kind) for d in plan.cross for kind in range(2)]
        for d, kind in written:
            for p in range(CAP):
                slot = slot_ref[(me ^ (d + kind * half)) * CAP + p].astype(jnp.float32)
                tags[d, pl.ds((kind * CAP + p) * SEG, SEG), :] = jnp.full(
                    (SEG, LANES), slot, jnp.float32
                ).astype(tags.dtype)
        for d, kind, target in tagged:
            depart(tags.at[d, pl.ds(kind * PAIR, PAIR)], target.at[:, pl.ds(width, LANES)])
        for d, tag_out in zip(plan.cross, tag_outs):
            depart(tags.at[d], tag_out)
        for arrival, (_, stage, target) in zip(arrivals, moves):
            arrival.wait()
            if target is not None:
                for part, place in target:
                    depart(part, place)
        for departure in departures:
            departure.wait()

    def row_moves(targets):
        moves = []
        for d, kind, target in targets:
            for p in range(CAP):
                seg = jnp.maximum(seg_out[(kind * half + d) * CAP + p], 0)
                stage = staged.at[pl.ds(((kind * half + d) * CAP + p) * SEG, SEG)]
                moves.append(
                    (
                        x_ref.at[pl.ds(pl.multiple_of(seg * SEG, SEG), SEG)],
                        stage,
                        [(stage, target.at[pl.ds(p * SEG, SEG), pl.ds(0, width)])],
                    )
                )
        return moves

    def adapter_moves(target_of):
        moves = []
        for slot in range(slots):
            span = pl.ds(slot * share, share)
            source = pl.ds(first, share)
            moves.append((up_ref.at[slot, source], up.at[span], None))
            moves.append((left_ref.at[slot, source], left.at[span], None))
        outs = [
            (
                up.at[pl.ds(row, rows)],
                target_of(plan.left_pieces).at[pl.ds(0, rows), pl.ds(column, plan.features)],
            )
            for row, rows, column in plan.up_columns()
        ]
        outs += [
            (
                left.at[pl.ds(piece * PAIR, rows)],
                target_of(piece).at[pl.ds(0, rows), pl.ds(0, width)],
            )
            for piece, rows in plan.left_spans()
        ]
        source, stage, _ = moves[-1]
        moves[-1] = (source, stage, outs)
        return moves

    near_d = plan.near[1:] if first_call else plan.near[:1]
    near_targets = [
        (d, kind, near[i].at[pl.ds(kind * PAIR, PAIR)])
        for i, d in enumerate(near_d)
        for kind in range(2)
    ]
    if first_call:
        cross_targets = [
            (d, kind, of_wide(blocks, 2 * i + kind))
            for i, d in enumerate(plan.cross)
            for kind in range(2)
        ]
    else:
        cross_targets = [
            (d, kind, plan.late_rows(blocks, i, kind))
            for i, d in enumerate(plan.cross)
            for kind in range(2)
        ]

    @pl.when(rows_outer)
    def _():
        move(row_moves(cross_targets + near_targets), near_targets)

    @pl.when(jnp.logical_not(rows_outer))
    def _():
        if first_call:
            adapters = adapter_moves(lambda piece: of_wide(blocks, piece))
        else:
            adapters = adapter_moves(lambda piece: late_adapters(blocks, piece, plan))
        move(adapters + row_moves(near_targets), near_targets)


def lay_out(plan, first_call, ids, residency, x, left_rows, ups):
    count = 2 * plan.half * CAP
    tagged = jax.ShapeDtypeStruct((2 * PAIR, plan.width + LANES), x.dtype)
    near = [tagged] * (len(plan.near) - 1 if first_call else 1)
    heights = [2] * plan.wide if first_call else [n for _, n, _ in plan.late_blocks()]
    blocks = [jax.ShapeDtypeStruct((n * PAIR, plan.width), x.dtype) for n in heights]
    if first_call:
        blocks += [jax.ShapeDtypeStruct((2 * PAIR, LANES), x.dtype)] * len(plan.cross)
    out = pl.pallas_call(
        functools.partial(lay_kernel, plan, first_call),
        out_shape=near + blocks + [jax.ShapeDtypeStruct((count,), jnp.int32)],
        in_specs=[SMEM, SMEM, HBM, HBM, HBM],
        out_specs=[HBM] * (len(near) + len(blocks)) + [SMEM],
        scratch_shapes=[
            pltpu.SMEM((plan.replicas * CAP,), jnp.int32),
            pltpu.SMEM((plan.replicas * CAP,), jnp.int32),
            pltpu.SMEM((plan.replicas,), jnp.int32),
            pltpu.VMEM((count * SEG, plan.width), x.dtype),
            pltpu.VMEM((plan.half, 2 * PAIR, LANES), x.dtype),
            pltpu.VMEM((plan.left_rows, plan.width), x.dtype),
            pltpu.VMEM((plan.left_rows, plan.features), x.dtype),
            pltpu.SemaphoreType.DMA((count + 2 * plan.slots,)),
            pltpu.SemaphoreType.DMA((2 * count + 2 * plan.pieces,)),
        ],
        compiler_params=params(60 * 1024 * 1024),
        cost_estimate=pl.CostEstimate(flops=0, bytes_accessed=x.size, transcendentals=0),
        name="lay_out_first" if first_call else "lay_out_second",
    )(ids, residency, x, left_rows, ups)
    return list(out[: len(near)]), list(out[len(near) : -1]), out[-1]


def slot_mask(tags, first, columns, slots, share):
    lane = lax.broadcasted_iota(jnp.int32, (1, LANES), 1)
    column_slot = jnp.zeros((1, LANES), jnp.float32)
    for j in range(0, LANES, share):
        slot = (first + j) // share if first + j < columns else -1
        column_slot = jnp.where(lane >= j, float(slot), column_slot)
    return tags == column_slot


class Copies:
    def __init__(self, outer, sems):
        self.outer, self.sems, self.waits = outer, sems, []

    def both(self, target, outer_source, inner_source=None):
        sem = self.sems.at[len(self.waits)]
        copy = pltpu.make_async_copy(outer_source, target, sem)
        if inner_source is None:
            copy.start()
        else:
            pl.when(self.outer)(copy.start)
            pl.when(jnp.logical_not(self.outer))(
                pltpu.make_async_copy(inner_source, target, sem).start
            )
        self.waits.append((None, copy))

    def one(self, wanted, target, source):
        copy = pltpu.make_async_copy(source, target, self.sems.at[len(self.waits)])
        pl.when(wanted)(copy.start)
        self.waits.append((wanted, copy))

    def wait(self):
        for wanted, copy in self.waits:
            if wanted is None:
                copy.wait()
            else:
                pl.when(wanted)(copy.wait)


def lane_group(share):
    return lax.broadcasted_iota(jnp.int32, (1, LANES), 1) // share


def spread_lanes(value, share):
    total = value
    for shift in range(share, LANES, share):
        total += pltpu.roll(value, shift, 1)
    return total


def pack(low, share):
    count = LANES // share
    height = low.shape[0] // count
    everywhere = spread_lanes(low, share)
    packed = jnp.zeros((height, LANES), jnp.float32)
    for i in range(count):
        rows = everywhere[i * height : (i + 1) * height]
        packed = jnp.where(lane_group(share) == i, rows, packed)
    return packed


def unpack(packed, share):
    rows = [
        spread_lanes(jnp.where(lane_group(share) == i, packed, 0.0), share)
        for i in range(LANES // share)
    ]
    return jnp.concatenate(rows, axis=0)


def fold(product, tags, columns, slots, share):
    total = jnp.zeros(tags.shape, jnp.float32)
    for first in range(0, product.shape[1], LANES):
        mask = slot_mask(tags, first, columns, slots, share)
        total += jnp.where(mask, product[:, first : first + LANES], 0.0)
    return total


def copy_rows(copies, plan, kind, target, columns, near, wide, late):
    span = pl.ds(kind * PAIR, PAIR)
    for i, d in enumerate(plan.near):
        copies.both(target.at[pl.ds(d * PAIR, PAIR)], near[i].at[span, columns])
    for i, d in enumerate(plan.cross):
        place = target.at[pl.ds(d * PAIR, PAIR)]
        if i == 0 and kind == 1:
            copies.one(jnp.logical_not(copies.outer), place, wide[i].at[span, columns])
        else:
            copies.both(
                place, plan.late_rows(late, i, kind).at[:, columns], wide[i].at[span, columns]
            )


def copy_tags(copies, plan, kind, target, near, tags):
    span = pl.ds(kind * PAIR, PAIR)
    for i, d in enumerate(plan.near):
        copies.both(target.at[pl.ds(d * PAIR, PAIR)], near[i].at[span, pl.ds(plan.width, LANES)])
    for i, d in enumerate(plan.cross):
        copies.both(target.at[pl.ds(d * PAIR, PAIR)], tags[i].at[span])


def product_of(rows, left):
    return lax.dot_general(
        rows, left, (((1,), (1,)), ((), ())), preferred_element_type=jnp.float32
    )


def reduce_own_kernel(plan, n_steps, near, wide, late, tags, own, low_ref, tag_ref, *scratch):
    rows, left, acc, tag, sems = scratch
    block = plan.width // n_steps
    outer = am_outer(plan)
    each = plan.half + 1
    steps = []
    for k in range(n_steps + 1):
        copies = Copies(outer, sems.at[pl.ds(k * each, each)])
        if k < n_steps:
            columns = pl.ds(k * block, block)
            copy_rows(copies, plan, 0, rows.at[:, columns], columns, near, wide, late)
            copies.both(left.at[:, columns], own.at[:, columns])
        else:
            copy_tags(copies, plan, 0, tag, near, tags)
        steps.append(copies)
    for k in range(n_steps):
        steps[k].wait()
        columns = pl.ds(k * block, block)
        product = product_of(rows[:, columns], left[:, columns])
        acc[...] = acc[...] + product if k else product
    steps[n_steps].wait()
    tags = tag[...].astype(jnp.float32)
    tag_ref[...] = tags
    low_ref[...] = pack(fold(acc, tags, acc.shape[1], plan.slots, plan.rank), plan.rank)


def reduce_taken_kernel(plan, n_steps, near, wide, late, tags, across, *rest):
    lows, tag_ref = rest[: plan.groups], rest[plan.groups]
    rows, left, acc, tag, sems = rest[plan.groups + 1 :]
    block = plan.width // n_steps
    outer = am_outer(plan)
    inner = jnp.logical_not(outer)
    more = plan.groups - 1
    each = plan.half + plan.left_pieces + more * (plan.half + plan.left_pieces)
    missing = pl.ds(plan.cross[0] * PAIR, PAIR)

    @pl.when(outer)
    def _():
        rows[0, missing, :] = jnp.zeros((PAIR, plan.width), rows.dtype)

    if plan.last_piece is not None:

        @pl.when(inner)
        def _():
            left[0, pl.ds(plan.last_piece * PAIR, PAIR), :] = jnp.zeros(
                (PAIR, plan.width), left.dtype
            )

    steps = []
    for k in range(n_steps + 1):
        copies = Copies(outer, sems.at[pl.ds(k * each, each)])
        columns = pl.ds(k * block, block) if k < n_steps else pl.ds(plan.width, LANES)
        if k < n_steps:
            copy_rows(copies, plan, 1, rows.at[0, :, columns], columns, near, wide, late)
        else:
            copy_tags(copies, plan, 1, tag.at[0], near, tags)
        for e in range(1, plan.groups):
            for i, d in enumerate(plan.across):
                target = rows.at[e, :, columns] if k < n_steps else tag.at[e]
                copies.one(
                    inner,
                    target.at[pl.ds(d * PAIR, PAIR)],
                    across[e - 1][i].at[:, columns],
                )
        if k < n_steps:
            for piece, count in plan.left_spans():
                span = pl.ds(0, count), columns
                place = left.at[0, pl.ds(piece * PAIR, count), columns]
                if piece == plan.last_piece:
                    copies.one(outer, place, of_wide(wide, piece).at[span])
                else:
                    copies.both(
                        place,
                        of_wide(wide, piece).at[span],
                        late_adapters(late, piece, plan).at[span],
                    )
                for e in range(1, plan.groups):
                    copies.one(
                        outer,
                        left.at[e, pl.ds(piece * PAIR, count), columns],
                        across[e - 1][piece].at[span],
                    )
        steps.append(copies)
    for k in range(n_steps):
        steps[k].wait()
        columns = pl.ds(k * block, block)
        for e in range(plan.groups):
            rows_at = jnp.where(inner, e, 0)
            left_at = jnp.where(outer, e, 0)
            product = product_of(rows[rows_at, :, columns], left[left_at, :, columns])
            acc[e] = acc[e] + product if k else product
    steps[n_steps].wait()
    tag_ref[...] = tag[0].astype(jnp.float32)
    for e in range(plan.groups):
        tags = tag[jnp.where(inner, e, 0)].astype(jnp.float32)
        low = fold(acc.at[e], tags, plan.left_rows, plan.slots, plan.share)
        lows[e][...] = pack(low, plan.share)


def reduce_last_kernel(plan, *refs):
    groups, width = plan.groups, plan.width
    before, tag_ref, refs = refs[:groups], refs[groups], refs[groups + 1 :]
    near, wide, last, across = refs[:4]
    lows = refs[4:]
    outer = am_outer(plan)
    inner = jnp.logical_not(outer)
    first_row = plan.cross[0] * PAIR

    def padded(parts, height):
        rows = sum(part.shape[0] for part in parts)
        if rows < height:
            parts = parts + [jnp.zeros((height - rows, width), last.dtype)]
        return jnp.concatenate(parts, axis=0)

    @pl.when(outer)
    def _():
        tags = tag_ref[first_row : first_row + PAIR, :]
        rows = last[...]
        for e in range(groups):
            total = jnp.zeros((PAIR, LANES), jnp.float32)
            for first in range(0, plan.padded, LANES):
                parts = []
                for piece, count in plan.left_spans():
                    if first <= piece * PAIR < first + LANES:
                        source = of_wide(wide, piece) if e == 0 else across[e - 1][piece]
                        parts.append(source[:count, :width])
                product = product_of(rows, padded(parts, LANES))
                mask = slot_mask(tags, first, plan.left_rows, plan.slots, plan.share)
                total += jnp.where(mask, product, 0.0)
            whole = [jnp.zeros((PAIR, LANES), jnp.float32)] * plan.half
            whole[plan.cross[0]] = total
            lows[e][...] = before[e][...] + pack(jnp.concatenate(whole, axis=0), plan.share)

    @pl.when(inner)
    def _():
        if plan.last_piece is None:
            for e in range(groups):
                lows[e][...] = before[e][...]
            return
        at = plan.last_piece * PAIR
        first = at // LANES * LANES
        count = min(PAIR, plan.left_rows - at)
        parts = [jnp.zeros((at - first, width), last.dtype)] if at > first else []
        left = padded(parts + [last[:count, :]], LANES)
        for e in range(groups):
            if e == 0:
                blocks = {d: near[i].at[PAIR:] for i, d in enumerate(plan.near)}
                blocks.update({d: wide[i].at[PAIR:] for i, d in enumerate(plan.cross)})
                tags = tag_ref[...]
            else:
                blocks = {d: across[e - 1][i] for i, d in enumerate(plan.across)}
                tags = [blocks[d][:, width:] for d in range(plan.half)]
                tags = jnp.concatenate(tags, axis=0).astype(jnp.float32)
            whole = jnp.concatenate([blocks[d][:, :width] for d in range(plan.half)], axis=0)
            product = product_of(whole, left)
            mask = slot_mask(tags, first, plan.left_rows, plan.slots, plan.share)
            low = pack(jnp.where(mask, product, 0.0), plan.share)
            lows[e][...] = before[e][...] + low


def reduce_last(plan, lows, tag, near, wide, last, across):
    flat, tree = jax.tree.flatten([near, wide, last, across])
    n_head = plan.groups + 1

    def body(*refs):
        nested = jax.tree.unflatten(tree, refs[n_head : n_head + len(flat)])
        reduce_last_kernel(plan, *refs[:n_head], *nested, *refs[n_head + len(flat) :])

    shapes = [jax.ShapeDtypeStruct(a.shape, a.dtype) for a in lows]
    return pl.pallas_call(
        body,
        out_shape=shapes,
        in_specs=[VMEM] * (n_head + len(flat)),
        out_specs=[VMEM] * len(lows),
        compiler_params=params(),
        cost_estimate=pl.CostEstimate(flops=1, bytes_accessed=1, transcendentals=0),
        name="reduce_last",
    )(*lows, tag, *flat)


def blocks_call(kernel, blocks, out_shape, out_specs, scratch, flops, moved, name, extra=()):
    flat, tree = jax.tree.flatten(blocks)
    n_extra = len(extra)

    def body(*refs):
        head, rest = refs[:n_extra], refs[n_extra:]
        nested = jax.tree.unflatten(tree, rest[: len(flat)])
        kernel(*head, *nested, *rest[len(flat) :])

    return pl.pallas_call(
        body,
        out_shape=out_shape,
        in_specs=[VMEM] * n_extra + [HBM] * len(flat),
        out_specs=out_specs,
        scratch_shapes=scratch,
        compiler_params=params(),
        cost_estimate=pl.CostEstimate(flops=1, bytes_accessed=1, transcendentals=0),
        name=name,
    )(*extra, *flat)


def reduce_own(plan, near, wide, late, tags, own):
    height = plan.half * PAIR
    columns = own.shape[0]
    n_steps = 2
    dtype = own.dtype
    return blocks_call(
        functools.partial(reduce_own_kernel, plan, n_steps),
        [near, wide, late, tags, own],
        [
            jax.ShapeDtypeStruct((height * plan.rank // LANES, LANES), jnp.float32),
            jax.ShapeDtypeStruct((height, LANES), jnp.float32),
        ],
        [VMEM] * 2,
        [
            pltpu.VMEM((height, plan.width), dtype),
            pltpu.VMEM((columns, plan.width), dtype),
            pltpu.VMEM((height, columns), jnp.float32),
            pltpu.VMEM((height, LANES), dtype),
            pltpu.SemaphoreType.DMA(((n_steps + 1) * (plan.half + 1),)),
        ],
        2 * height * plan.width * columns,
        2 * plan.width * (height + columns),
        "reduce_own",
    )


def reduce_taken(plan, near, wide, late, tags, across):
    height = plan.half * PAIR
    n_steps = 2
    dtype = near[0].dtype
    groups, padded = plan.groups, plan.padded
    *lows, tag = blocks_call(
        functools.partial(reduce_taken_kernel, plan, n_steps),
        [near, wide, late, tags, across],
        [jax.ShapeDtypeStruct((height * plan.share // LANES, LANES), jnp.float32)] * groups
        + [jax.ShapeDtypeStruct((height, LANES), jnp.float32)],
        [VMEM] * (groups + 1),
        [
            pltpu.VMEM((groups, height, plan.width), dtype),
            pltpu.VMEM((groups, padded, plan.width), dtype),
            pltpu.VMEM((groups, height, padded), jnp.float32),
            pltpu.VMEM((groups, height, LANES), dtype),
            pltpu.SemaphoreType.DMA(((n_steps + 1) * groups * (plan.half + plan.left_pieces),)),
        ],
        2 * height * plan.width * groups * padded,
        2 * plan.width * (height + padded) * groups,
        "reduce_taken",
    )
    return lows, tag


def add_low(mine_ref, other_ref, share):
    low = (mine_ref[...] + other_ref[...]).astype(jnp.bfloat16).astype(jnp.float32)
    return unpack(low, share)


def spread(low, tags, columns, slots, share):
    blocks = [
        jnp.where(slot_mask(tags, first, columns, slots, share), low, 0.0).astype(jnp.bfloat16)
        for first in range(0, columns, LANES)
    ]
    return jnp.concatenate(blocks, axis=1)


def write_deltas(delta, outs):
    delta = delta.astype(jnp.bfloat16)
    for i, out in enumerate(outs):
        out[...] = delta[i * PAIR : (i + 1) * PAIR]


def expand_own_kernel(plan, mine_ref, other_ref, tag_ref, own, *rest):
    outs, (up, sem) = rest[:-2], rest[-2:]
    copy = pltpu.make_async_copy(own, up, sem)
    copy.start()
    low = add_low(mine_ref, other_ref, plan.rank)
    wide_low = spread(low, tag_ref[...], up.shape[0], plan.slots, plan.rank)
    copy.wait()
    write_deltas(jnp.dot(wide_low, up[...], preferred_element_type=jnp.float32), outs)


def expand_own(plan, mine, other, tag, own):
    columns, features = own.shape
    return blocks_call(
        functools.partial(expand_own_kernel, plan),
        [own],
        [jax.ShapeDtypeStruct((PAIR, features), jnp.bfloat16)] * plan.half,
        [VMEM] * plan.half,
        [pltpu.VMEM(own.shape, own.dtype), pltpu.SemaphoreType.DMA(())],
        2 * tag.shape[0] * columns * features,
        2 * features * (columns + tag.shape[0]),
        "expand_own",
        extra=(mine, other, tag),
    )


def expand_taken_kernel(plan, *refs):
    lows, tag_ref, refs = refs[: 2 * plan.groups], refs[2 * plan.groups], refs[2 * plan.groups + 1 :]
    wide, narrow, across_wide, across_narrow = refs[:4]
    outs, (up, sems) = refs[4:-2], refs[-2:]
    copies = Copies(am_outer(plan), sems)
    for row, rows, column in plan.up_columns():
        part = pl.ds(0, rows), pl.ds(column, plan.features)
        for e in range(plan.groups):
            copies.both(
                up.at[e, pl.ds(row, rows)],
                (of_wide(wide, plan.left_pieces) if e == 0 else across_wide[e - 1]).at[part],
                (narrow if e == 0 else across_narrow[e - 1]).at[part],
            )
    if plan.padded > plan.left_rows:
        up[:, plan.left_rows :, :] = jnp.zeros(
            (plan.groups, plan.padded - plan.left_rows, plan.features), up.dtype
        )
    tags = tag_ref[...]
    wides = [
        spread(
            add_low(lows[2 * e], lows[2 * e + 1], plan.share),
            tags,
            plan.left_rows,
            plan.slots,
            plan.share,
        )
        for e in range(plan.groups)
    ]
    copies.wait()
    delta = None
    for e in range(plan.groups):
        product = jnp.dot(wides[e], up[e], preferred_element_type=jnp.float32)
        delta = product if delta is None else delta + product
    write_deltas(delta, outs)


def expand_taken(plan, lows, tag, wide, narrow, across_wide, across_narrow):
    height, features = tag.shape[0], plan.features
    return blocks_call(
        functools.partial(expand_taken_kernel, plan),
        [wide, narrow, across_wide, across_narrow],
        [jax.ShapeDtypeStruct((PAIR, features), jnp.bfloat16)] * plan.half,
        [VMEM] * plan.half,
        [
            pltpu.VMEM((plan.groups, plan.padded, features), jnp.bfloat16),
            pltpu.SemaphoreType.DMA((plan.groups * len(list(plan.up_columns())),)),
        ],
        2 * height * plan.groups * plan.padded * features,
        2 * features * (plan.groups * plan.padded + height),
        "expand_taken",
        extra=(*lows, tag),
    )


def join_kernel(seg_ref, base_ref, *refs):
    deltas, out_ref = refs[:-1], refs[-1]
    for k in range(len(deltas) * CAP):
        part = k % CAP

        @pl.when(seg_ref[k] >= 0)
        def _():
            span = pl.ds(pl.multiple_of(seg_ref[k] * SEG, SEG), SEG)
            delta = deltas[k // CAP][part * SEG : (part + 1) * SEG, :]
            out_ref[span, :] = (base_ref[span, :] + delta.astype(jnp.float32)).astype(
                out_ref.dtype
            )


def join(seg_of, base, deltas):
    height, features = base.shape
    return pl.pallas_call(
        join_kernel,
        out_shape=jax.ShapeDtypeStruct((height, features), jnp.bfloat16),
        in_specs=[SMEM, VMEM] + [VMEM] * len(deltas),
        out_specs=VMEM,
        compiler_params=params(),
        cost_estimate=pl.CostEstimate(
            flops=height * features, bytes_accessed=8 * height * features, transcendentals=0
        ),
        name="join",
    )(seg_of, base, *deltas)


def swap(value, axis, distance):
    count = lax.axis_size(axis)
    return lax.ppermute(value, axis, [(i, i ^ distance) for i in range(count)])


def send(plan, value, moves):
    shape = (plan.groups, plan.replicas, lax.axis_size("tensor"))

    def place(g, r, c):
        return (g * shape[1] + r) * shape[2] + c

    pairs = [
        (place(g, r, c), place(g ^ flips[0], r ^ flips[1], c ^ flips[2]))
        for senders, *flips in moves
        for g in range(shape[0])
        for r in senders
        for c in range(shape[2])
    ]
    return lax.ppermute(value, ("groups", "replica", "tensor"), pairs)


def return_terms(terms):
    back = {d: swap(terms[d], "replica", d) for d in reversed(range(1, len(terms)))}
    return [back[d] for d in range(1, len(terms))]


def on_device(x, weight, lefts, ups, ids, residency):
    slots, width, rank = lefts.shape
    features = ups.shape[2]
    plan = Plan(
        lax.axis_size("replica"), lax.axis_size("groups"), slots, rank, width, features
    )
    half, n_cross = plan.half, len(plan.cross)
    core = lax.axis_index("tensor")
    outer = am_outer(plan)
    left_rows = jnp.swapaxes(lefts, 1, 2)
    near, wide, seg_of = lay_out(plan, True, ids, residency, x, left_rows, ups)
    wide, tags = wide[: plan.wide], wide[plan.wide :]

    near = [swap(block, "replica", d) for block, d in zip(near, plan.near[1:])]
    wide_in = []
    for i in range(plan.wide):
        moves = []
        if i < n_cross:
            moves.append((plan.outer, 0, plan.cross[i], 0))
        if i < plan.adapter_wide:
            moves.append((plan.inner, 0, half, 0))
        wide_in.append(send(plan, wide[i], moves))

    late_ids, _ = lax.optimization_barrier((ids, seg_of))
    near, late_x = lax.optimization_barrier((near, x))
    own_rows, late, _ = lay_out(plan, False, late_ids, residency, x, left_rows, ups)
    near = own_rows + near
    def part(which, rows):
        columns = lax.dynamic_slice(weight, (0, which * features), (weight.shape[0], features))
        return jnp.dot(rows, columns, preferred_element_type=jnp.float32)

    base_other, base_mine = part(1 - core, late_x), part(core, late_x)

    def across_send(i):
        d = plan.across[i]
        if d in plan.near:
            block = near[plan.near.index(d)][PAIR:]
            value, tag = block[:, :width], block[:, width:]
        else:
            j = plan.cross.index(d)
            value, tag = wide_in[j][PAIR:], tags_in[j][PAIR:]
        if i < plan.pieces:
            piece = wide_in[i // 2][(i % 2) * PAIR : (i % 2 + 1) * PAIR]
            value = jnp.where(outer, piece, value)
        value = jnp.concatenate([value, tag], axis=1)
        return [
            send(plan, value, [(plan.outer, e, 0, 0), (plan.inner, e, 0, 0)])
            for e in range(1, plan.groups)
        ]

    across = [across_send(0)]
    tags_in = [swap(tag, "replica", d) for tag, d in zip(tags, plan.cross)]

    wide_in, near, across, late, tags_in, base_other, base_mine = lax.optimization_barrier(
        (wide_in, near, across, late, tags_in, base_other, base_mine)
    )
    across += [across_send(i) for i in range(1, half)]
    late_in = []
    for block, (d, _, unit) in zip(late, plan.late_blocks()):
        moves = [(plan.inner, 0, d, 0)]
        if unit < plan.pieces:
            moves.append((plan.outer, 0, half, 0))
        if unit == plan.units - 1:
            late_in[0], block = lax.optimization_barrier((late_in[0], block))
        late_in.append(send(plan, block, moves))
    late_up = late_in[0][: plan.up_rows]
    across_up = [send(plan, late_up, [(plan.inner, e, 0, 0)]) for e in range(1, plan.groups)]
    base = base_mine + swap(base_other, "tensor", 1)
    late_in[:-1], across[:-1] = lax.optimization_barrier((late_in[:-1], across[:-1]))
    across = [[blocks[e] for blocks in across] for e in range(plan.groups - 1)]

    own_left = left_rows.reshape(slots * rank, width)
    low, tag = reduce_own(plan, near, wide_in, late_in[:-1], tags_in, own_left)
    other = swap(low, "tensor", 1)
    terms = expand_own(plan, low, other, tag, ups.reshape(slots * rank, features))
    deltas = [terms[0]] + return_terms(terms)

    lows, tag = reduce_taken(plan, near, wide_in, late_in[:-1], tags_in, across)
    late_in[-1], deltas[:2], across_up, base, lows = lax.optimization_barrier(
        (late_in[-1], deltas[:2], across_up, base, lows)
    )
    lows = reduce_last(plan, lows, tag, near, wide_in, late_in[-1], across)
    pairs = [lows[0], swap(lows[0], "tensor", 1)]
    for e in range(1, plan.groups):
        pairs.append(send(plan, lows[e], [(plan.outer, 0, 0, 0), (plan.inner, e, 0, 0)]))
        pairs.append(send(plan, lows[e], [(plan.outer, 0, 0, 1), (plan.inner, e, 0, 1)]))
    pairs, deltas = lax.optimization_barrier((pairs, deltas))
    across_wide = [blocks[plan.left_pieces] for blocks in across]
    terms = expand_taken(plan, pairs, tag, wide_in, late_in[0], across_wide, across_up)
    deltas += [terms[0]] + return_terms(terms)
    return join(seg_of, base, deltas)


def solution(mesh):
    placed = (
        P(("groups", "replica"), "tensor"),
        P("tensor", None),
        P("replica", "tensor", None),
        P("replica", None, "tensor"),
        P(("groups", "replica")),
        P(),
    )
    return jax.shard_map(
        on_device,
        mesh=mesh,
        in_specs=placed,
        out_specs=P(("groups", "replica"), "tensor"),
        check_vma=False,
    )
```

```python
import functools

import jax
import jax.numpy as jnp
from jax import lax
from jax.experimental import pallas as pl
from jax.experimental.pallas import tpu as pltpu
from jax.sharding import PartitionSpec as P

CAP = 2
SEG = 32
LANES = 128
PAIR = CAP * SEG
VMEM_LIMIT = 24 * 1024 * 1024
HBM = pl.BlockSpec(memory_space=pltpu.HBM)
SMEM = pl.BlockSpec(memory_space=pltpu.SMEM)
VMEM = pl.BlockSpec(memory_space=pltpu.VMEM)


class Plan:
    def __init__(self, replicas, groups, slots, rank, width, features):
        self.replicas, self.groups, self.slots, self.rank = replicas, groups, slots, rank
        self.width, self.features = width, features
        self.half = replicas // 2
        self.turn = self.half // 2
        self.near = [d for d in range(self.half) if not d & self.turn]
        self.cross = [d for d in range(self.half) if d & self.turn]
        self.across = self.near[1:] + self.near[:1] + self.cross
        self.share = rank // groups
        self.left_rows = slots * self.share
        self.padded = -(-self.left_rows // LANES) * LANES
        beside = width // features
        self.up_rows = -(-self.left_rows // (beside * 16)) * 16
        self.left_pieces = -(-self.left_rows // PAIR)
        self.pieces = self.left_pieces + 1
        assert self.up_rows <= PAIR
        self.adapter_wide = -(-self.pieces // 2)
        self.units = 2 * len(self.cross)
        self.last_piece = self.units - 2 if self.units - 2 < self.left_pieces else None
        assert self.pieces <= self.units and self.adapter_wide <= len(self.cross)
        self.wide = len(self.cross)
        self.outer = [r for r in range(replicas) if self.is_outer(r)]
        self.inner = [r for r in range(replicas) if not self.is_outer(r)]

    def is_outer(self, r):
        return (r < self.turn) or (r >= self.replicas - self.turn)

    def up_columns(self):
        for j, row in enumerate(range(0, self.left_rows, self.up_rows)):
            yield row, min(self.up_rows, self.left_rows - row), j * self.features

    def left_spans(self):
        for piece in range(self.left_pieces):
            yield piece, min(PAIR, self.left_rows - piece * PAIR)

    def late_blocks(self):
        blocks = [(self.cross[0], 1, 0)]
        blocks += [(d, 2, 2 * i - 1) for i, d in enumerate(self.cross) if i]
        return blocks + [(self.cross[0], 1, self.units - 1)]

    def late_unit(self, refs, unit):
        if unit in (0, self.units - 1):
            return refs[0 if unit == 0 else -1]
        return refs[(unit + 1) // 2].at[pl.ds((unit - 1) % 2 * PAIR, PAIR)]

    def late_rows(self, refs, i, kind):
        if i == 0:
            return self.late_unit(refs, 0 if kind == 0 else self.units - 1)
        return self.late_unit(refs, 2 * i - 1 + kind)


def params(limit=VMEM_LIMIT):
    return pltpu.CompilerParams(vmem_limit_bytes=limit)


def am_outer(plan):
    me = lax.axis_index("replica")
    return (me < plan.turn) | (me >= plan.replicas - plan.turn)


def of_wide(refs, piece):
    return refs[piece // 2].at[pl.ds((piece % 2) * PAIR, PAIR)]


def late_adapters(late, piece, plan):
    return plan.late_unit(late, 0 if piece == plan.left_pieces else 1 + piece)


def lay_kernel(plan, first_call, ids_ref, residency_ref, x_ref, left_ref, up_ref, *rest):
    n_near = len(plan.near) - 1 if first_call else 1
    n_blocks = plan.wide if first_call else len(plan.late_blocks())
    n_tags = len(plan.cross) if first_call else 0
    near, rest = rest[:n_near], rest[n_near:]
    blocks, rest = rest[:n_blocks], rest[n_blocks:]
    tag_outs, rest = rest[:n_tags], rest[n_tags:]
    seg_out, seg_ref, slot_ref, count_ref, staged, tags, left, up, in_sems, sems = rest
    half, slots, width, share = plan.half, plan.slots, plan.width, plan.share
    me = lax.axis_index("replica")
    first = pl.multiple_of(lax.axis_index("groups") * share, share)
    outer = am_outer(plan)
    rows_outer = outer if first_call else jnp.logical_not(outer)

    for h in range(plan.replicas):
        count_ref[h] = 0
        for p in range(CAP):
            seg_ref[h * CAP + p] = -1
            slot_ref[h * CAP + p] = 0
    for s in range(ids_ref.shape[0]):
        adapter = ids_ref[s]
        holder = adapter // slots
        place = holder * CAP + count_ref[holder]
        count_ref[holder] = count_ref[holder] + 1
        seg_ref[place] = s
        slot_ref[place] = residency_ref[adapter] - holder * slots
    for d in range(half):
        for kind in range(2):
            for p in range(CAP):
                seg_out[(kind * half + d) * CAP + p] = seg_ref[
                    (me ^ (d + kind * half)) * CAP + p
                ]

    def move(moves, tagged):
        arrivals = []
        for source, stage, _ in moves:
            arrivals.append(pltpu.make_async_copy(source, stage, in_sems.at[len(arrivals)]))
            arrivals[-1].start()
        departures = []

        def depart(source, target):
            departures.append(pltpu.make_async_copy(source, target, sems.at[len(departures)]))
            departures[-1].start()

        written = [(d, kind) for d, kind, _ in tagged]
        if first_call:
            written += [(d, kind) for d in plan.cross for kind in range(2)]
        for d, kind in written:
            for p in range(CAP):
                slot = slot_ref[(me ^ (d + kind * half)) * CAP + p].astype(jnp.float32)
                tags[d, pl.ds((kind * CAP + p) * SEG, SEG), :] = jnp.full(
                    (SEG, LANES), slot, jnp.float32
                ).astype(tags.dtype)
        for d, kind, target in tagged:
            depart(tags.at[d, pl.ds(kind * PAIR, PAIR)], target.at[:, pl.ds(width, LANES)])
        for d, tag_out in zip(plan.cross, tag_outs):
            depart(tags.at[d], tag_out)
        for arrival, (_, stage, target) in zip(arrivals, moves):
            arrival.wait()
            if target is not None:
                for part, place in target:
                    depart(part, place)
        for departure in departures:
            departure.wait()

    def row_moves(targets):
        moves = []
        for d, kind, target in targets:
            for p in range(CAP):
                seg = jnp.maximum(seg_out[(kind * half + d) * CAP + p], 0)
                stage = staged.at[pl.ds(((kind * half + d) * CAP + p) * SEG, SEG)]
                moves.append(
                    (
                        x_ref.at[pl.ds(pl.multiple_of(seg * SEG, SEG), SEG)],
                        stage,
                        [(stage, target.at[pl.ds(p * SEG, SEG), pl.ds(0, width)])],
                    )
                )
        return moves

    def adapter_moves(target_of):
        moves = []
        for slot in range(slots):
            span = pl.ds(slot * share, share)
            source = pl.ds(first, share)
            moves.append((up_ref.at[slot, source], up.at[span], None))
            moves.append((left_ref.at[slot, source], left.at[span], None))
        outs = [
            (
                up.at[pl.ds(row, rows)],
                target_of(plan.left_pieces).at[pl.ds(0, rows), pl.ds(column, plan.features)],
            )
            for row, rows, column in plan.up_columns()
        ]
        outs += [
            (
                left.at[pl.ds(piece * PAIR, rows)],
                target_of(piece).at[pl.ds(0, rows), pl.ds(0, width)],
            )
            for piece, rows in plan.left_spans()
        ]
        source, stage, _ = moves[-1]
        moves[-1] = (source, stage, outs)
        return moves

    near_d = plan.near[1:] if first_call else plan.near[:1]
    near_targets = [
        (d, kind, near[i].at[pl.ds(kind * PAIR, PAIR)])
        for i, d in enumerate(near_d)
        for kind in range(2)
    ]
    if first_call:
        cross_targets = [
            (d, kind, of_wide(blocks, 2 * i + kind))
            for i, d in enumerate(plan.cross)
            for kind in range(2)
        ]
    else:
        cross_targets = [
            (d, kind, plan.late_rows(blocks, i, kind))
            for i, d in enumerate(plan.cross)
            for kind in range(2)
        ]

    @pl.when(rows_outer)
    def _():
        move(row_moves(cross_targets + near_targets), near_targets)

    @pl.when(jnp.logical_not(rows_outer))
    def _():
        if first_call:
            adapters = adapter_moves(lambda piece: of_wide(blocks, piece))
        else:
            adapters = adapter_moves(lambda piece: late_adapters(blocks, piece, plan))
        move(adapters + row_moves(near_targets), near_targets)


def lay_out(plan, first_call, ids, residency, x, left_rows, ups):
    count = 2 * plan.half * CAP
    tagged = jax.ShapeDtypeStruct((2 * PAIR, plan.width + LANES), x.dtype)
    near = [tagged] * (len(plan.near) - 1 if first_call else 1)
    heights = [2] * plan.wide if first_call else [n for _, n, _ in plan.late_blocks()]
    blocks = [jax.ShapeDtypeStruct((n * PAIR, plan.width), x.dtype) for n in heights]
    if first_call:
        blocks += [jax.ShapeDtypeStruct((2 * PAIR, LANES), x.dtype)] * len(plan.cross)
    out = pl.pallas_call(
        functools.partial(lay_kernel, plan, first_call),
        out_shape=near + blocks + [jax.ShapeDtypeStruct((count,), jnp.int32)],
        in_specs=[SMEM, SMEM, HBM, HBM, HBM],
        out_specs=[HBM] * (len(near) + len(blocks)) + [SMEM],
        scratch_shapes=[
            pltpu.SMEM((plan.replicas * CAP,), jnp.int32),
            pltpu.SMEM((plan.replicas * CAP,), jnp.int32),
            pltpu.SMEM((plan.replicas,), jnp.int32),
            pltpu.VMEM((count * SEG, plan.width), x.dtype),
            pltpu.VMEM((plan.half, 2 * PAIR, LANES), x.dtype),
            pltpu.VMEM((plan.left_rows, plan.width), x.dtype),
            pltpu.VMEM((plan.left_rows, plan.features), x.dtype),
            pltpu.SemaphoreType.DMA((count + 2 * plan.slots,)),
            pltpu.SemaphoreType.DMA((2 * count + 2 * plan.pieces,)),
        ],
        compiler_params=params(60 * 1024 * 1024),
        cost_estimate=pl.CostEstimate(flops=0, bytes_accessed=x.size, transcendentals=0),
        name="lay_out_first" if first_call else "lay_out_second",
    )(ids, residency, x, left_rows, ups)
    return list(out[: len(near)]), list(out[len(near) : -1]), out[-1]


def slot_mask(tags, first, columns, slots, share):
    lane = lax.broadcasted_iota(jnp.int32, (1, LANES), 1)
    column_slot = jnp.zeros((1, LANES), jnp.float32)
    for j in range(0, LANES, share):
        slot = (first + j) // share if first + j < columns else -1
        column_slot = jnp.where(lane >= j, float(slot), column_slot)
    return tags == column_slot


class Copies:
    def __init__(self, outer, sems):
        self.outer, self.sems, self.waits = outer, sems, []

    def both(self, target, outer_source, inner_source=None):
        sem = self.sems.at[len(self.waits)]
        copy = pltpu.make_async_copy(outer_source, target, sem)
        if inner_source is None:
            copy.start()
        else:
            pl.when(self.outer)(copy.start)
            pl.when(jnp.logical_not(self.outer))(
                pltpu.make_async_copy(inner_source, target, sem).start
            )
        self.waits.append((None, copy))

    def one(self, wanted, target, source):
        copy = pltpu.make_async_copy(source, target, self.sems.at[len(self.waits)])
        pl.when(wanted)(copy.start)
        self.waits.append((wanted, copy))

    def wait(self):
        for wanted, copy in self.waits:
            if wanted is None:
                copy.wait()
            else:
                pl.when(wanted)(copy.wait)


def lane_group(share):
    return lax.broadcasted_iota(jnp.int32, (1, LANES), 1) // share


def spread_lanes(value, share):
    total = value
    for shift in range(share, LANES, share):
        total += pltpu.roll(value, shift, 1)
    return total


def pack(low, share):
    count = LANES // share
    height = low.shape[0] // count
    everywhere = spread_lanes(low, share)
    packed = jnp.zeros((height, LANES), jnp.float32)
    for i in range(count):
        rows = everywhere[i * height : (i + 1) * height]
        packed = jnp.where(lane_group(share) == i, rows, packed)
    return packed


def unpack(packed, share):
    rows = [
        spread_lanes(jnp.where(lane_group(share) == i, packed, 0.0), share)
        for i in range(LANES // share)
    ]
    return jnp.concatenate(rows, axis=0)


def fold(product, tags, columns, slots, share):
    total = jnp.zeros(tags.shape, jnp.float32)
    for first in range(0, product.shape[1], LANES):
        mask = slot_mask(tags, first, columns, slots, share)
        total += jnp.where(mask, product[:, first : first + LANES], 0.0)
    return total


def copy_rows(copies, plan, kind, target, columns, near, wide, late):
    span = pl.ds(kind * PAIR, PAIR)
    for i, d in enumerate(plan.near):
        copies.both(target.at[pl.ds(d * PAIR, PAIR)], near[i].at[span, columns])
    for i, d in enumerate(plan.cross):
        place = target.at[pl.ds(d * PAIR, PAIR)]
        if i == 0 and kind == 1:
            copies.one(jnp.logical_not(copies.outer), place, wide[i].at[span, columns])
        else:
            copies.both(
                place, plan.late_rows(late, i, kind).at[:, columns], wide[i].at[span, columns]
            )


def copy_tags(copies, plan, kind, target, near, tags):
    span = pl.ds(kind * PAIR, PAIR)
    for i, d in enumerate(plan.near):
        copies.both(target.at[pl.ds(d * PAIR, PAIR)], near[i].at[span, pl.ds(plan.width, LANES)])
    for i, d in enumerate(plan.cross):
        copies.both(target.at[pl.ds(d * PAIR, PAIR)], tags[i].at[span])


def product_of(rows, left):
    return lax.dot_general(
        rows, left, (((1,), (1,)), ((), ())), preferred_element_type=jnp.float32
    )


def reduce_own_kernel(plan, n_steps, near, wide, late, tags, own, low_ref, tag_ref, *scratch):
    rows, left, acc, tag, sems = scratch
    block = plan.width // n_steps
    outer = am_outer(plan)
    each = plan.half + 1
    steps = []
    for k in range(n_steps + 1):
        copies = Copies(outer, sems.at[pl.ds(k * each, each)])
        if k < n_steps:
            columns = pl.ds(k * block, block)
            copy_rows(copies, plan, 0, rows.at[:, columns], columns, near, wide, late)
            copies.both(left.at[:, columns], own.at[:, columns])
        else:
            copy_tags(copies, plan, 0, tag, near, tags)
        steps.append(copies)
    for k in range(n_steps):
        steps[k].wait()
        columns = pl.ds(k * block, block)
        product = product_of(rows[:, columns], left[:, columns])
        acc[...] = acc[...] + product if k else product
    steps[n_steps].wait()
    tags = tag[...].astype(jnp.float32)
    tag_ref[...] = tags
    low_ref[...] = pack(fold(acc, tags, acc.shape[1], plan.slots, plan.rank), plan.rank)


def reduce_taken_kernel(plan, n_steps, near, wide, late, tags, across, *rest):
    lows, tag_ref = rest[: plan.groups], rest[plan.groups]
    rows, left, acc, tag, sems = rest[plan.groups + 1 :]
    block = plan.width // n_steps
    outer = am_outer(plan)
    inner = jnp.logical_not(outer)
    more = plan.groups - 1
    each = plan.half + plan.left_pieces + more * (plan.half + plan.left_pieces)
    missing = pl.ds(plan.cross[0] * PAIR, PAIR)

    @pl.when(outer)
    def _():
        rows[0, missing, :] = jnp.zeros((PAIR, plan.width), rows.dtype)

    if plan.last_piece is not None:

        @pl.when(inner)
        def _():
            left[0, pl.ds(plan.last_piece * PAIR, PAIR), :] = jnp.zeros(
                (PAIR, plan.width), left.dtype
            )

    steps = []
    for k in range(n_steps + 1):
        copies = Copies(outer, sems.at[pl.ds(k * each, each)])
        columns = pl.ds(k * block, block) if k < n_steps else pl.ds(plan.width, LANES)
        if k < n_steps:
            copy_rows(copies, plan, 1, rows.at[0, :, columns], columns, near, wide, late)
        else:
            copy_tags(copies, plan, 1, tag.at[0], near, tags)
        for e in range(1, plan.groups):
            for i, d in enumerate(plan.across):
                target = rows.at[e, :, columns] if k < n_steps else tag.at[e]
                copies.one(
                    inner,
                    target.at[pl.ds(d * PAIR, PAIR)],
                    across[e - 1][i].at[:, columns],
                )
        if k < n_steps:
            for piece, count in plan.left_spans():
                span = pl.ds(0, count), columns
                place = left.at[0, pl.ds(piece * PAIR, count), columns]
                if piece == plan.last_piece:
                    copies.one(outer, place, of_wide(wide, piece).at[span])
                else:
                    copies.both(
                        place,
                        of_wide(wide, piece).at[span],
                        late_adapters(late, piece, plan).at[span],
                    )
                for e in range(1, plan.groups):
                    copies.one(
                        outer,
                        left.at[e, pl.ds(piece * PAIR, count), columns],
                        across[e - 1][piece].at[span],
                    )
        steps.append(copies)
    for k in range(n_steps):
        steps[k].wait()
        columns = pl.ds(k * block, block)
        for e in range(plan.groups):
            rows_at = jnp.where(inner, e, 0)
            left_at = jnp.where(outer, e, 0)
            product = product_of(rows[rows_at, :, columns], left[left_at, :, columns])
            acc[e] = acc[e] + product if k else product
    steps[n_steps].wait()
    tag_ref[...] = tag[0].astype(jnp.float32)
    for e in range(plan.groups):
        tags = tag[jnp.where(inner, e, 0)].astype(jnp.float32)
        low = fold(acc.at[e], tags, plan.left_rows, plan.slots, plan.share)
        lows[e][...] = pack(low, plan.share)


def reduce_last_kernel(plan, *refs):
    groups, width = plan.groups, plan.width
    before, tag_ref, refs = refs[:groups], refs[groups], refs[groups + 1 :]
    near, wide, last, across = refs[:4]
    lows = refs[4:]
    outer = am_outer(plan)
    inner = jnp.logical_not(outer)
    first_row = plan.cross[0] * PAIR

    def padded(parts, height):
        rows = sum(part.shape[0] for part in parts)
        if rows < height:
            parts = parts + [jnp.zeros((height - rows, width), last.dtype)]
        return jnp.concatenate(parts, axis=0)

    @pl.when(outer)
    def _():
        tags = tag_ref[first_row : first_row + PAIR, :]
        rows = last[...]
        for e in range(groups):
            total = jnp.zeros((PAIR, LANES), jnp.float32)
            for first in range(0, plan.padded, LANES):
                parts = []
                for piece, count in plan.left_spans():
                    if first <= piece * PAIR < first + LANES:
                        source = of_wide(wide, piece) if e == 0 else across[e - 1][piece]
                        parts.append(source[:count, :width])
                product = product_of(rows, padded(parts, LANES))
                mask = slot_mask(tags, first, plan.left_rows, plan.slots, plan.share)
                total += jnp.where(mask, product, 0.0)
            whole = [jnp.zeros((PAIR, LANES), jnp.float32)] * plan.half
            whole[plan.cross[0]] = total
            lows[e][...] = before[e][...] + pack(jnp.concatenate(whole, axis=0), plan.share)

    @pl.when(inner)
    def _():
        if plan.last_piece is None:
            for e in range(groups):
                lows[e][...] = before[e][...]
            return
        at = plan.last_piece * PAIR
        first = at // LANES * LANES
        count = min(PAIR, plan.left_rows - at)
        parts = [jnp.zeros((at - first, width), last.dtype)] if at > first else []
        left = padded(parts + [last[:count, :]], LANES)
        for e in range(groups):
            if e == 0:
                blocks = {d: near[i].at[PAIR:] for i, d in enumerate(plan.near)}
                blocks.update({d: wide[i].at[PAIR:] for i, d in enumerate(plan.cross)})
                tags = tag_ref[...]
            else:
                blocks = {d: across[e - 1][i] for i, d in enumerate(plan.across)}
                tags = [blocks[d][:, width:] for d in range(plan.half)]
                tags = jnp.concatenate(tags, axis=0).astype(jnp.float32)
            whole = jnp.concatenate([blocks[d][:, :width] for d in range(plan.half)], axis=0)
            product = product_of(whole, left)
            mask = slot_mask(tags, first, plan.left_rows, plan.slots, plan.share)
            low = pack(jnp.where(mask, product, 0.0), plan.share)
            lows[e][...] = before[e][...] + low


def reduce_last(plan, lows, tag, near, wide, last, across):
    flat, tree = jax.tree.flatten([near, wide, last, across])
    n_head = plan.groups + 1

    def body(*refs):
        nested = jax.tree.unflatten(tree, refs[n_head : n_head + len(flat)])
        reduce_last_kernel(plan, *refs[:n_head], *nested, *refs[n_head + len(flat) :])

    shapes = [jax.ShapeDtypeStruct(a.shape, a.dtype) for a in lows]
    return pl.pallas_call(
        body,
        out_shape=shapes,
        in_specs=[VMEM] * (n_head + len(flat)),
        out_specs=[VMEM] * len(lows),
        compiler_params=params(),
        cost_estimate=pl.CostEstimate(flops=1, bytes_accessed=1, transcendentals=0),
        name="reduce_last",
    )(*lows, tag, *flat)


def blocks_call(kernel, blocks, out_shape, out_specs, scratch, flops, moved, name, extra=()):
    flat, tree = jax.tree.flatten(blocks)
    n_extra = len(extra)

    def body(*refs):
        head, rest = refs[:n_extra], refs[n_extra:]
        nested = jax.tree.unflatten(tree, rest[: len(flat)])
        kernel(*head, *nested, *rest[len(flat) :])

    return pl.pallas_call(
        body,
        out_shape=out_shape,
        in_specs=[VMEM] * n_extra + [HBM] * len(flat),
        out_specs=out_specs,
        scratch_shapes=scratch,
        compiler_params=params(),
        cost_estimate=pl.CostEstimate(flops=1, bytes_accessed=1, transcendentals=0),
        name=name,
    )(*extra, *flat)


def reduce_own(plan, near, wide, late, tags, own):
    height = plan.half * PAIR
    columns = own.shape[0]
    n_steps = 2
    dtype = own.dtype
    return blocks_call(
        functools.partial(reduce_own_kernel, plan, n_steps),
        [near, wide, late, tags, own],
        [
            jax.ShapeDtypeStruct((height * plan.rank // LANES, LANES), jnp.float32),
            jax.ShapeDtypeStruct((height, LANES), jnp.float32),
        ],
        [VMEM] * 2,
        [
            pltpu.VMEM((height, plan.width), dtype),
            pltpu.VMEM((columns, plan.width), dtype),
            pltpu.VMEM((height, columns), jnp.float32),
            pltpu.VMEM((height, LANES), dtype),
            pltpu.SemaphoreType.DMA(((n_steps + 1) * (plan.half + 1),)),
        ],
        2 * height * plan.width * columns,
        2 * plan.width * (height + columns),
        "reduce_own",
    )


def reduce_taken(plan, near, wide, late, tags, across):
    height = plan.half * PAIR
    n_steps = 2
    dtype = near[0].dtype
    groups, padded = plan.groups, plan.padded
    *lows, tag = blocks_call(
        functools.partial(reduce_taken_kernel, plan, n_steps),
        [near, wide, late, tags, across],
        [jax.ShapeDtypeStruct((height * plan.share // LANES, LANES), jnp.float32)] * groups
        + [jax.ShapeDtypeStruct((height, LANES), jnp.float32)],
        [VMEM] * (groups + 1),
        [
            pltpu.VMEM((groups, height, plan.width), dtype),
            pltpu.VMEM((groups, padded, plan.width), dtype),
            pltpu.VMEM((groups, height, padded), jnp.float32),
            pltpu.VMEM((groups, height, LANES), dtype),
            pltpu.SemaphoreType.DMA(((n_steps + 1) * groups * (plan.half + plan.left_pieces),)),
        ],
        2 * height * plan.width * groups * padded,
        2 * plan.width * (height + padded) * groups,
        "reduce_taken",
    )
    return lows, tag


def add_low(mine_ref, other_ref, share):
    low = (mine_ref[...] + other_ref[...]).astype(jnp.bfloat16).astype(jnp.float32)
    return unpack(low, share)


def spread(low, tags, columns, slots, share):
    blocks = [
        jnp.where(slot_mask(tags, first, columns, slots, share), low, 0.0).astype(jnp.bfloat16)
        for first in range(0, columns, LANES)
    ]
    return jnp.concatenate(blocks, axis=1)


def write_deltas(delta, outs):
    delta = delta.astype(jnp.bfloat16)
    for i, out in enumerate(outs):
        out[...] = delta[i * PAIR : (i + 1) * PAIR]


def expand_own_kernel(plan, mine_ref, other_ref, tag_ref, own, *rest):
    outs, (up, sem) = rest[:-2], rest[-2:]
    copy = pltpu.make_async_copy(own, up, sem)
    copy.start()
    low = add_low(mine_ref, other_ref, plan.rank)
    wide_low = spread(low, tag_ref[...], up.shape[0], plan.slots, plan.rank)
    copy.wait()
    write_deltas(jnp.dot(wide_low, up[...], preferred_element_type=jnp.float32), outs)


def expand_own(plan, mine, other, tag, own):
    columns, features = own.shape
    return blocks_call(
        functools.partial(expand_own_kernel, plan),
        [own],
        [jax.ShapeDtypeStruct((PAIR, features), jnp.bfloat16)] * plan.half,
        [VMEM] * plan.half,
        [pltpu.VMEM(own.shape, own.dtype), pltpu.SemaphoreType.DMA(())],
        2 * tag.shape[0] * columns * features,
        2 * features * (columns + tag.shape[0]),
        "expand_own",
        extra=(mine, other, tag),
    )


def expand_taken_kernel(plan, *refs):
    lows, tag_ref, refs = refs[: 2 * plan.groups], refs[2 * plan.groups], refs[2 * plan.groups + 1 :]
    wide, narrow, across_wide, across_narrow = refs[:4]
    outs, (up, sems) = refs[4:-2], refs[-2:]
    copies = Copies(am_outer(plan), sems)
    for row, rows, column in plan.up_columns():
        part = pl.ds(0, rows), pl.ds(column, plan.features)
        for e in range(plan.groups):
            copies.both(
                up.at[e, pl.ds(row, rows)],
                (of_wide(wide, plan.left_pieces) if e == 0 else across_wide[e - 1]).at[part],
                (narrow if e == 0 else across_narrow[e - 1]).at[part],
            )
    if plan.padded > plan.left_rows:
        up[:, plan.left_rows :, :] = jnp.zeros(
            (plan.groups, plan.padded - plan.left_rows, plan.features), up.dtype
        )
    tags = tag_ref[...]
    wides = [
        spread(
            add_low(lows[2 * e], lows[2 * e + 1], plan.share),
            tags,
            plan.left_rows,
            plan.slots,
            plan.share,
        )
        for e in range(plan.groups)
    ]
    copies.wait()
    delta = None
    for e in range(plan.groups):
        product = jnp.dot(wides[e], up[e], preferred_element_type=jnp.float32)
        delta = product if delta is None else delta + product
    write_deltas(delta, outs)


def expand_taken(plan, lows, tag, wide, narrow, across_wide, across_narrow):
    height, features = tag.shape[0], plan.features
    return blocks_call(
        functools.partial(expand_taken_kernel, plan),
        [wide, narrow, across_wide, across_narrow],
        [jax.ShapeDtypeStruct((PAIR, features), jnp.bfloat16)] * plan.half,
        [VMEM] * plan.half,
        [
            pltpu.VMEM((plan.groups, plan.padded, features), jnp.bfloat16),
            pltpu.SemaphoreType.DMA((plan.groups * len(list(plan.up_columns())),)),
        ],
        2 * height * plan.groups * plan.padded * features,
        2 * features * (plan.groups * plan.padded + height),
        "expand_taken",
        extra=(*lows, tag),
    )


def join_kernel(seg_ref, base_ref, *refs):
    deltas, out_ref = refs[:-1], refs[-1]
    for k in range(len(deltas) * CAP):
        part = k % CAP

        @pl.when(seg_ref[k] >= 0)
        def _():
            span = pl.ds(pl.multiple_of(seg_ref[k] * SEG, SEG), SEG)
            delta = deltas[k // CAP][part * SEG : (part + 1) * SEG, :]
            out_ref[span, :] = (base_ref[span, :] + delta.astype(jnp.float32)).astype(
                out_ref.dtype
            )


def join(seg_of, base, deltas):
    height, features = base.shape
    return pl.pallas_call(
        join_kernel,
        out_shape=jax.ShapeDtypeStruct((height, features), jnp.bfloat16),
        in_specs=[SMEM, VMEM] + [VMEM] * len(deltas),
        out_specs=VMEM,
        compiler_params=params(),
        cost_estimate=pl.CostEstimate(
            flops=height * features, bytes_accessed=8 * height * features, transcendentals=0
        ),
        name="join",
    )(seg_of, base, *deltas)


def swap(value, axis, distance):
    count = lax.axis_size(axis)
    return lax.ppermute(value, axis, [(i, i ^ distance) for i in range(count)])


def send(plan, value, moves):
    shape = (plan.groups, plan.replicas, lax.axis_size("tensor"))

    def place(g, r, c):
        return (g * shape[1] + r) * shape[2] + c

    pairs = [
        (place(g, r, c), place(g ^ flips[0], r ^ flips[1], c ^ flips[2]))
        for senders, *flips in moves
        for g in range(shape[0])
        for r in senders
        for c in range(shape[2])
    ]
    return lax.ppermute(value, ("groups", "replica", "tensor"), pairs)


def return_terms(terms):
    back = {d: swap(terms[d], "replica", d) for d in reversed(range(1, len(terms)))}
    return [back[d] for d in range(1, len(terms))]


def on_device(x, weight, lefts, ups, ids, residency):
    slots, width, rank = lefts.shape
    features = ups.shape[2]
    plan = Plan(
        lax.axis_size("replica"), lax.axis_size("groups"), slots, rank, width, features
    )
    half, n_cross = plan.half, len(plan.cross)
    core = lax.axis_index("tensor")
    outer = am_outer(plan)
    left_rows = jnp.swapaxes(lefts, 1, 2)
    near, wide, seg_of = lay_out(plan, True, ids, residency, x, left_rows, ups)
    wide, tags = wide[: plan.wide], wide[plan.wide :]

    near = [swap(block, "replica", d) for block, d in zip(near, plan.near[1:])]
    wide_in = []
    for i in range(plan.wide):
        moves = []
        if i < n_cross:
            moves.append((plan.outer, 0, plan.cross[i], 0))
        if i < plan.adapter_wide:
            moves.append((plan.inner, 0, half, 0))
        wide_in.append(send(plan, wide[i], moves))

    late_ids, _ = lax.optimization_barrier((ids, seg_of))
    near, late_x = lax.optimization_barrier((near, x))
    own_rows, late, _ = lay_out(plan, False, late_ids, residency, x, left_rows, ups)
    near = own_rows + near
    def part(which, rows):
        columns = lax.dynamic_slice(weight, (0, which * features), (weight.shape[0], features))
        return jnp.dot(rows, columns, preferred_element_type=jnp.float32)

    base_other, base_mine = part(1 - core, late_x), part(core, late_x)

    def across_send(i):
        d = plan.across[i]
        if d in plan.near:
            block = near[plan.near.index(d)][PAIR:]
            value, tag = block[:, :width], block[:, width:]
        else:
            j = plan.cross.index(d)
            value, tag = wide_in[j][PAIR:], tags_in[j][PAIR:]
        if i < plan.pieces:
            piece = wide_in[i // 2][(i % 2) * PAIR : (i % 2 + 1) * PAIR]
            value = jnp.where(outer, piece, value)
        value = jnp.concatenate([value, tag], axis=1)
        return [
            send(plan, value, [(plan.outer, e, 0, 0), (plan.inner, e, 0, 0)])
            for e in range(1, plan.groups)
        ]

    across = [across_send(0)]
    tags_in = [swap(tag, "replica", d) for tag, d in zip(tags, plan.cross)]

    wide_in, near, across, late, tags_in, base_other, base_mine = lax.optimization_barrier(
        (wide_in, near, across, late, tags_in, base_other, base_mine)
    )
    across += [across_send(i) for i in range(1, half)]
    late_in = []
    for block, (d, _, unit) in zip(late, plan.late_blocks()):
        moves = [(plan.inner, 0, d, 0)]
        if unit < plan.pieces:
            moves.append((plan.outer, 0, half, 0))
        if unit == plan.units - 1:
            late_in[0], block = lax.optimization_barrier((late_in[0], block))
        late_in.append(send(plan, block, moves))
    late_up = late_in[0][: plan.up_rows]
    across_up = [send(plan, late_up, [(plan.inner, e, 0, 0)]) for e in range(1, plan.groups)]
    base = base_mine + swap(base_other, "tensor", 1)
    late_in[:-1], across[:-1] = lax.optimization_barrier((late_in[:-1], across[:-1]))
    across = [[blocks[e] for blocks in across] for e in range(plan.groups - 1)]

    own_left = left_rows.reshape(slots * rank, width)
    low, tag = reduce_own(plan, near, wide_in, late_in[:-1], tags_in, own_left)
    other = swap(low, "tensor", 1)
    terms = expand_own(plan, low, other, tag, ups.reshape(slots * rank, features))
    deltas = [terms[0]] + return_terms(terms)

    lows, tag = reduce_taken(plan, near, wide_in, late_in[:-1], tags_in, across)
    late_in[-1], deltas[:2], base, lows = lax.optimization_barrier(
        (late_in[-1], deltas[:2], base, lows)
    )
    lows = reduce_last(plan, lows, tag, near, wide_in, late_in[-1], across)
    pairs = []
    for e in range(plan.groups):
        low = lows[e]
        if e:
            low = send(plan, low, [(plan.outer, 0, 0, 0), (plan.inner, e, 0, 0)])
        pairs += [low, swap(low, "tensor", 1)]
    pairs, deltas = lax.optimization_barrier((pairs, deltas))
    across_wide = [blocks[plan.left_pieces] for blocks in across]
    terms = expand_taken(plan, pairs, tag, wide_in, late_in[0], across_wide, across_up)
    deltas += [terms[0]] + return_terms(terms)
    return join(seg_of, base, deltas)


def solution(mesh):
    placed = (
        P(("groups", "replica"), "tensor"),
        P("tensor", None),
        P("replica", "tensor", None),
        P("replica", None, "tensor"),
        P(("groups", "replica")),
        P(),
    )
    return jax.shard_map(
        on_device,
        mesh=mesh,
        in_specs=placed,
        out_specs=P(("groups", "replica"), "tensor"),
        check_vma=False,
    )
```

```python
import functools

import jax
import jax.numpy as jnp
from jax import lax
from jax.experimental import pallas as pl
from jax.experimental.pallas import tpu as pltpu
from jax.sharding import PartitionSpec as P

CAP = 2
SEG = 32
LANES = 128
PAIR = CAP * SEG
VMEM_LIMIT = 24 * 1024 * 1024
HBM = pl.BlockSpec(memory_space=pltpu.HBM)
SMEM = pl.BlockSpec(memory_space=pltpu.SMEM)
VMEM = pl.BlockSpec(memory_space=pltpu.VMEM)


class Plan:
    def __init__(self, replicas, groups, slots, rank, width, features):
        self.replicas, self.groups, self.slots, self.rank = replicas, groups, slots, rank
        self.width, self.features = width, features
        self.half = replicas // 2
        self.turn = self.half // 2
        self.near = [d for d in range(self.half) if not d & self.turn]
        self.cross = [d for d in range(self.half) if d & self.turn]
        self.across = self.near[1:] + self.near[:1] + self.cross
        self.share = rank // groups
        self.left_rows = slots * self.share
        self.padded = -(-self.left_rows // LANES) * LANES
        beside = width // features
        self.up_rows = -(-self.left_rows // (beside * 16)) * 16
        self.left_pieces = -(-self.left_rows // PAIR)
        self.pieces = self.left_pieces + 1
        assert self.up_rows <= PAIR
        self.adapter_wide = -(-self.pieces // 2)
        self.units = 2 * len(self.cross)
        self.last_piece = self.units - 2 if self.units - 2 < self.left_pieces else None
        assert self.pieces <= self.units and self.adapter_wide <= len(self.cross)
        self.wide = len(self.cross)
        self.outer = [r for r in range(replicas) if self.is_outer(r)]
        self.inner = [r for r in range(replicas) if not self.is_outer(r)]

    def is_outer(self, r):
        return (r < self.turn) or (r >= self.replicas - self.turn)

    def up_columns(self):
        for j, row in enumerate(range(0, self.left_rows, self.up_rows)):
            yield row, min(self.up_rows, self.left_rows - row), j * self.features

    def left_spans(self):
        for piece in range(self.left_pieces):
            yield piece, min(PAIR, self.left_rows - piece * PAIR)

    def late_blocks(self):
        blocks = [(self.cross[0], 1, 0)]
        blocks += [(d, 2, 2 * i - 1) for i, d in enumerate(self.cross) if i]
        return blocks + [(self.cross[0], 1, self.units - 1)]

    def late_unit(self, refs, unit):
        if unit in (0, self.units - 1):
            return refs[0 if unit == 0 else -1]
        return refs[(unit + 1) // 2].at[pl.ds((unit - 1) % 2 * PAIR, PAIR)]

    def late_rows(self, refs, i, kind):
        if i == 0:
            return self.late_unit(refs, 0 if kind == 0 else self.units - 1)
        return self.late_unit(refs, 2 * i - 1 + kind)


def params(limit=VMEM_LIMIT):
    return pltpu.CompilerParams(vmem_limit_bytes=limit)


def am_outer(plan):
    me = lax.axis_index("replica")
    return (me < plan.turn) | (me >= plan.replicas - plan.turn)


def of_wide(refs, piece):
    return refs[piece // 2].at[pl.ds((piece % 2) * PAIR, PAIR)]


def late_adapters(late, piece, plan):
    return plan.late_unit(late, 0 if piece == plan.left_pieces else 1 + piece)


def lay_kernel(plan, first_call, ids_ref, residency_ref, x_ref, left_ref, up_ref, *rest):
    n_near = len(plan.near) - 1 if first_call else 1
    n_blocks = plan.wide if first_call else len(plan.late_blocks())
    n_tags = len(plan.cross) if first_call else 0
    near, rest = rest[:n_near], rest[n_near:]
    blocks, rest = rest[:n_blocks], rest[n_blocks:]
    tag_outs, rest = rest[:n_tags], rest[n_tags:]
    seg_out, seg_ref, slot_ref, count_ref, staged, tags, left, up, in_sems, sems = rest
    half, slots, width, share = plan.half, plan.slots, plan.width, plan.share
    me = lax.axis_index("replica")
    first = pl.multiple_of(lax.axis_index("groups") * share, share)
    outer = am_outer(plan)
    rows_outer = outer if first_call else jnp.logical_not(outer)

    for h in range(plan.replicas):
        count_ref[h] = 0
        for p in range(CAP):
            seg_ref[h * CAP + p] = -1
            slot_ref[h * CAP + p] = 0
    for s in range(ids_ref.shape[0]):
        adapter = ids_ref[s]
        holder = adapter // slots
        place = holder * CAP + count_ref[holder]
        count_ref[holder] = count_ref[holder] + 1
        seg_ref[place] = s
        slot_ref[place] = residency_ref[adapter] - holder * slots
    for d in range(half):
        for kind in range(2):
            for p in range(CAP):
                seg_out[(kind * half + d) * CAP + p] = seg_ref[
                    (me ^ (d + kind * half)) * CAP + p
                ]

    def move(moves, tagged):
        arrivals = []
        for source, stage, _ in moves:
            arrivals.append(pltpu.make_async_copy(source, stage, in_sems.at[len(arrivals)]))
            arrivals[-1].start()
        departures = []

        def depart(source, target):
            departures.append(pltpu.make_async_copy(source, target, sems.at[len(departures)]))
            departures[-1].start()

        written = [(d, kind) for d, kind, _ in tagged]
        if first_call:
            written += [(d, kind) for d in plan.cross for kind in range(2)]
        for d, kind in written:
            for p in range(CAP):
                slot = slot_ref[(me ^ (d + kind * half)) * CAP + p].astype(jnp.float32)
                tags[d, pl.ds((kind * CAP + p) * SEG, SEG), :] = jnp.full(
                    (SEG, LANES), slot, jnp.float32
                ).astype(tags.dtype)
        for d, kind, target in tagged:
            depart(tags.at[d, pl.ds(kind * PAIR, PAIR)], target.at[:, pl.ds(width, LANES)])
        for d, tag_out in zip(plan.cross, tag_outs):
            depart(tags.at[d], tag_out)
        for arrival, (_, stage, target) in zip(arrivals, moves):
            arrival.wait()
            if target is not None:
                for part, place in target:
                    depart(part, place)
        for departure in departures:
            departure.wait()

    def row_moves(targets):
        moves = []
        for d, kind, target in targets:
            for p in range(CAP):
                seg = jnp.maximum(seg_out[(kind * half + d) * CAP + p], 0)
                stage = staged.at[pl.ds(((kind * half + d) * CAP + p) * SEG, SEG)]
                moves.append(
                    (
                        x_ref.at[pl.ds(pl.multiple_of(seg * SEG, SEG), SEG)],
                        stage,
                        [(stage, target.at[pl.ds(p * SEG, SEG), pl.ds(0, width)])],
                    )
                )
        return moves

    def adapter_moves(target_of):
        moves = []
        for slot in range(slots):
            span = pl.ds(slot * share, share)
            source = pl.ds(first, share)
            moves.append((up_ref.at[slot, source], up.at[span], None))
            moves.append((left_ref.at[slot, source], left.at[span], None))
        outs = [
            (
                up.at[pl.ds(row, rows)],
                target_of(plan.left_pieces).at[pl.ds(0, rows), pl.ds(column, plan.features)],
            )
            for row, rows, column in plan.up_columns()
        ]
        outs += [
            (
                left.at[pl.ds(piece * PAIR, rows)],
                target_of(piece).at[pl.ds(0, rows), pl.ds(0, width)],
            )
            for piece, rows in plan.left_spans()
        ]
        source, stage, _ = moves[-1]
        moves[-1] = (source, stage, outs)
        return moves

    near_d = plan.near[1:] if first_call else plan.near[:1]
    near_targets = [
        (d, kind, near[i].at[pl.ds(kind * PAIR, PAIR)])
        for i, d in enumerate(near_d)
        for kind in range(2)
    ]
    if first_call:
        cross_targets = [
            (d, kind, of_wide(blocks, 2 * i + kind))
            for i, d in enumerate(plan.cross)
            for kind in range(2)
        ]
    else:
        cross_targets = [
            (d, kind, plan.late_rows(blocks, i, kind))
            for i, d in enumerate(plan.cross)
            for kind in range(2)
        ]

    @pl.when(rows_outer)
    def _():
        move(row_moves(cross_targets + near_targets), near_targets)

    @pl.when(jnp.logical_not(rows_outer))
    def _():
        if first_call:
            adapters = adapter_moves(lambda piece: of_wide(blocks, piece))
        else:
            adapters = adapter_moves(lambda piece: late_adapters(blocks, piece, plan))
        move(adapters + row_moves(near_targets), near_targets)


def lay_out(plan, first_call, ids, residency, x, left_rows, ups):
    count = 2 * plan.half * CAP
    tagged = jax.ShapeDtypeStruct((2 * PAIR, plan.width + LANES), x.dtype)
    near = [tagged] * (len(plan.near) - 1 if first_call else 1)
    heights = [2] * plan.wide if first_call else [n for _, n, _ in plan.late_blocks()]
    blocks = [jax.ShapeDtypeStruct((n * PAIR, plan.width), x.dtype) for n in heights]
    if first_call:
        blocks += [jax.ShapeDtypeStruct((2 * PAIR, LANES), x.dtype)] * len(plan.cross)
    out = pl.pallas_call(
        functools.partial(lay_kernel, plan, first_call),
        out_shape=near + blocks + [jax.ShapeDtypeStruct((count,), jnp.int32)],
        in_specs=[SMEM, SMEM, HBM, HBM, HBM],
        out_specs=[HBM] * (len(near) + len(blocks)) + [SMEM],
        scratch_shapes=[
            pltpu.SMEM((plan.replicas * CAP,), jnp.int32),
            pltpu.SMEM((plan.replicas * CAP,), jnp.int32),
            pltpu.SMEM((plan.replicas,), jnp.int32),
            pltpu.VMEM((count * SEG, plan.width), x.dtype),
            pltpu.VMEM((plan.half, 2 * PAIR, LANES), x.dtype),
            pltpu.VMEM((plan.left_rows, plan.width), x.dtype),
            pltpu.VMEM((plan.left_rows, plan.features), x.dtype),
            pltpu.SemaphoreType.DMA((count + 2 * plan.slots,)),
            pltpu.SemaphoreType.DMA((2 * count + 2 * plan.pieces,)),
        ],
        compiler_params=params(60 * 1024 * 1024),
        cost_estimate=pl.CostEstimate(flops=0, bytes_accessed=x.size, transcendentals=0),
        name="lay_out_first" if first_call else "lay_out_second",
    )(ids, residency, x, left_rows, ups)
    return list(out[: len(near)]), list(out[len(near) : -1]), out[-1]


def slot_mask(tags, first, columns, slots, share):
    lane = lax.broadcasted_iota(jnp.int32, (1, LANES), 1)
    column_slot = jnp.zeros((1, LANES), jnp.float32)
    for j in range(0, LANES, share):
        slot = (first + j) // share if first + j < columns else -1
        column_slot = jnp.where(lane >= j, float(slot), column_slot)
    return tags == column_slot


class Copies:
    def __init__(self, outer, sems):
        self.outer, self.sems, self.waits = outer, sems, []

    def both(self, target, outer_source, inner_source=None):
        sem = self.sems.at[len(self.waits)]
        copy = pltpu.make_async_copy(outer_source, target, sem)
        if inner_source is None:
            copy.start()
        else:
            pl.when(self.outer)(copy.start)
            pl.when(jnp.logical_not(self.outer))(
                pltpu.make_async_copy(inner_source, target, sem).start
            )
        self.waits.append((None, copy))

    def one(self, wanted, target, source):
        copy = pltpu.make_async_copy(source, target, self.sems.at[len(self.waits)])
        pl.when(wanted)(copy.start)
        self.waits.append((wanted, copy))

    def wait(self):
        for wanted, copy in self.waits:
            if wanted is None:
                copy.wait()
            else:
                pl.when(wanted)(copy.wait)


def lane_group(share):
    return lax.broadcasted_iota(jnp.int32, (1, LANES), 1) // share


def spread_lanes(value, share):
    total = value
    for shift in range(share, LANES, share):
        total += pltpu.roll(value, shift, 1)
    return total


def pack(low, share):
    count = LANES // share
    height = low.shape[0] // count
    everywhere = spread_lanes(low, share)
    packed = jnp.zeros((height, LANES), jnp.float32)
    for i in range(count):
        rows = everywhere[i * height : (i + 1) * height]
        packed = jnp.where(lane_group(share) == i, rows, packed)
    return packed


def unpack(packed, share):
    rows = [
        spread_lanes(jnp.where(lane_group(share) == i, packed, 0.0), share)
        for i in range(LANES // share)
    ]
    return jnp.concatenate(rows, axis=0)


def fold(product, tags, columns, slots, share):
    total = jnp.zeros(tags.shape, jnp.float32)
    for first in range(0, product.shape[1], LANES):
        mask = slot_mask(tags, first, columns, slots, share)
        total += jnp.where(mask, product[:, first : first + LANES], 0.0)
    return total


def copy_rows(copies, plan, kind, target, columns, near, wide, late):
    span = pl.ds(kind * PAIR, PAIR)
    for i, d in enumerate(plan.near):
        copies.both(target.at[pl.ds(d * PAIR, PAIR)], near[i].at[span, columns])
    for i, d in enumerate(plan.cross):
        place = target.at[pl.ds(d * PAIR, PAIR)]
        if i == 0 and kind == 1:
            copies.one(jnp.logical_not(copies.outer), place, wide[i].at[span, columns])
        else:
            copies.both(
                place, plan.late_rows(late, i, kind).at[:, columns], wide[i].at[span, columns]
            )


def copy_tags(copies, plan, kind, target, near, tags):
    span = pl.ds(kind * PAIR, PAIR)
    for i, d in enumerate(plan.near):
        copies.both(target.at[pl.ds(d * PAIR, PAIR)], near[i].at[span, pl.ds(plan.width, LANES)])
    for i, d in enumerate(plan.cross):
        copies.both(target.at[pl.ds(d * PAIR, PAIR)], tags[i].at[span])


def product_of(rows, left):
    return lax.dot_general(
        rows, left, (((1,), (1,)), ((), ())), preferred_element_type=jnp.float32
    )


def reduce_own_kernel(plan, n_steps, near, wide, late, tags, own, low_ref, tag_ref, *scratch):
    rows, left, acc, tag, sems = scratch
    block = plan.width // n_steps
    outer = am_outer(plan)
    each = plan.half + 1
    steps = []
    for k in range(n_steps + 1):
        copies = Copies(outer, sems.at[pl.ds(k * each, each)])
        if k < n_steps:
            columns = pl.ds(k * block, block)
            copy_rows(copies, plan, 0, rows.at[:, columns], columns, near, wide, late)
            copies.both(left.at[:, columns], own.at[:, columns])
        else:
            copy_tags(copies, plan, 0, tag, near, tags)
        steps.append(copies)
    for k in range(n_steps):
        steps[k].wait()
        columns = pl.ds(k * block, block)
        product = product_of(rows[:, columns], left[:, columns])
        acc[...] = acc[...] + product if k else product
    steps[n_steps].wait()
    tags = tag[...].astype(jnp.float32)
    tag_ref[...] = tags
    low_ref[...] = pack(fold(acc, tags, acc.shape[1], plan.slots, plan.rank), plan.rank)


def reduce_taken_kernel(plan, n_steps, near, wide, late, tags, across, *rest):
    lows, tag_ref = rest[: plan.groups], rest[plan.groups]
    rows, left, acc, tag, sems = rest[plan.groups + 1 :]
    block = plan.width // n_steps
    outer = am_outer(plan)
    inner = jnp.logical_not(outer)
    more = plan.groups - 1
    each = plan.half + plan.left_pieces + more * (plan.half + plan.left_pieces)
    missing = pl.ds(plan.cross[0] * PAIR, PAIR)

    @pl.when(outer)
    def _():
        rows[0, missing, :] = jnp.zeros((PAIR, plan.width), rows.dtype)

    if plan.last_piece is not None:

        @pl.when(inner)
        def _():
            left[0, pl.ds(plan.last_piece * PAIR, PAIR), :] = jnp.zeros(
                (PAIR, plan.width), left.dtype
            )

    steps = []
    for k in range(n_steps + 1):
        copies = Copies(outer, sems.at[pl.ds(k * each, each)])
        columns = pl.ds(k * block, block) if k < n_steps else pl.ds(plan.width, LANES)
        if k < n_steps:
            copy_rows(copies, plan, 1, rows.at[0, :, columns], columns, near, wide, late)
        else:
            copy_tags(copies, plan, 1, tag.at[0], near, tags)
        for e in range(1, plan.groups):
            for i, d in enumerate(plan.across):
                target = rows.at[e, :, columns] if k < n_steps else tag.at[e]
                copies.one(
                    inner,
                    target.at[pl.ds(d * PAIR, PAIR)],
                    across[e - 1][i].at[:, columns],
                )
        if k < n_steps:
            for piece, count in plan.left_spans():
                span = pl.ds(0, count), columns
                place = left.at[0, pl.ds(piece * PAIR, count), columns]
                if piece == plan.last_piece:
                    copies.one(outer, place, of_wide(wide, piece).at[span])
                else:
                    copies.both(
                        place,
                        of_wide(wide, piece).at[span],
                        late_adapters(late, piece, plan).at[span],
                    )
                for e in range(1, plan.groups):
                    copies.one(
                        outer,
                        left.at[e, pl.ds(piece * PAIR, count), columns],
                        across[e - 1][piece].at[span],
                    )
        steps.append(copies)
    for k in range(n_steps):
        steps[k].wait()
        columns = pl.ds(k * block, block)
        for e in range(plan.groups):
            rows_at = jnp.where(inner, e, 0)
            left_at = jnp.where(outer, e, 0)
            product = product_of(rows[rows_at, :, columns], left[left_at, :, columns])
            acc[e] = acc[e] + product if k else product
    steps[n_steps].wait()
    tag_ref[...] = tag[0].astype(jnp.float32)
    for e in range(plan.groups):
        tags = tag[jnp.where(inner, e, 0)].astype(jnp.float32)
        low = fold(acc.at[e], tags, plan.left_rows, plan.slots, plan.share)
        lows[e][...] = pack(low, plan.share)


def reduce_last_kernel(plan, *refs):
    groups, width = plan.groups, plan.width
    before, tag_ref, refs = refs[:groups], refs[groups], refs[groups + 1 :]
    near, wide, last, across = refs[:4]
    lows = refs[4:]
    outer = am_outer(plan)
    inner = jnp.logical_not(outer)
    first_row = plan.cross[0] * PAIR

    def padded(parts, height):
        rows = sum(part.shape[0] for part in parts)
        if rows < height:
            parts = parts + [jnp.zeros((height - rows, width), last.dtype)]
        return jnp.concatenate(parts, axis=0)

    @pl.when(outer)
    def _():
        tags = tag_ref[first_row : first_row + PAIR, :]
        rows = last[...]
        for e in range(groups):
            total = jnp.zeros((PAIR, LANES), jnp.float32)
            for first in range(0, plan.padded, LANES):
                parts = []
                for piece, count in plan.left_spans():
                    if first <= piece * PAIR < first + LANES:
                        source = of_wide(wide, piece) if e == 0 else across[e - 1][piece]
                        parts.append(source[:count, :width])
                product = product_of(rows, padded(parts, LANES))
                mask = slot_mask(tags, first, plan.left_rows, plan.slots, plan.share)
                total += jnp.where(mask, product, 0.0)
            whole = [jnp.zeros((PAIR, LANES), jnp.float32)] * plan.half
            whole[plan.cross[0]] = total
            lows[e][...] = before[e][...] + pack(jnp.concatenate(whole, axis=0), plan.share)

    @pl.when(inner)
    def _():
        if plan.last_piece is None:
            for e in range(groups):
                lows[e][...] = before[e][...]
            return
        at = plan.last_piece * PAIR
        first = at // LANES * LANES
        count = min(PAIR, plan.left_rows - at)
        parts = [jnp.zeros((at - first, width), last.dtype)] if at > first else []
        left = padded(parts + [last[:count, :]], LANES)
        for e in range(groups):
            if e == 0:
                blocks = {d: near[i].at[PAIR:] for i, d in enumerate(plan.near)}
                blocks.update({d: wide[i].at[PAIR:] for i, d in enumerate(plan.cross)})
                tags = tag_ref[...]
            else:
                blocks = {d: across[e - 1][i] for i, d in enumerate(plan.across)}
                tags = [blocks[d][:, width:] for d in range(plan.half)]
                tags = jnp.concatenate(tags, axis=0).astype(jnp.float32)
            whole = jnp.concatenate([blocks[d][:, :width] for d in range(plan.half)], axis=0)
            product = product_of(whole, left)
            mask = slot_mask(tags, first, plan.left_rows, plan.slots, plan.share)
            low = pack(jnp.where(mask, product, 0.0), plan.share)
            lows[e][...] = before[e][...] + low


def reduce_last(plan, lows, tag, near, wide, last, across):
    flat, tree = jax.tree.flatten([near, wide, last, across])
    n_head = plan.groups + 1

    def body(*refs):
        nested = jax.tree.unflatten(tree, refs[n_head : n_head + len(flat)])
        reduce_last_kernel(plan, *refs[:n_head], *nested, *refs[n_head + len(flat) :])

    shapes = [jax.ShapeDtypeStruct(a.shape, a.dtype) for a in lows]
    return pl.pallas_call(
        body,
        out_shape=shapes,
        in_specs=[VMEM] * (n_head + len(flat)),
        out_specs=[VMEM] * len(lows),
        compiler_params=params(),
        cost_estimate=pl.CostEstimate(flops=1, bytes_accessed=1, transcendentals=0),
        name="reduce_last",
    )(*lows, tag, *flat)


def blocks_call(kernel, blocks, out_shape, out_specs, scratch, flops, moved, name, extra=()):
    flat, tree = jax.tree.flatten(blocks)
    n_extra = len(extra)

    def body(*refs):
        head, rest = refs[:n_extra], refs[n_extra:]
        nested = jax.tree.unflatten(tree, rest[: len(flat)])
        kernel(*head, *nested, *rest[len(flat) :])

    return pl.pallas_call(
        body,
        out_shape=out_shape,
        in_specs=[VMEM] * n_extra + [HBM] * len(flat),
        out_specs=out_specs,
        scratch_shapes=scratch,
        compiler_params=params(),
        cost_estimate=pl.CostEstimate(flops=1, bytes_accessed=1, transcendentals=0),
        name=name,
    )(*extra, *flat)


def reduce_own(plan, near, wide, late, tags, own):
    height = plan.half * PAIR
    columns = own.shape[0]
    n_steps = 2
    dtype = own.dtype
    return blocks_call(
        functools.partial(reduce_own_kernel, plan, n_steps),
        [near, wide, late, tags, own],
        [
            jax.ShapeDtypeStruct((height * plan.rank // LANES, LANES), jnp.float32),
            jax.ShapeDtypeStruct((height, LANES), jnp.float32),
        ],
        [VMEM] * 2,
        [
            pltpu.VMEM((height, plan.width), dtype),
            pltpu.VMEM((columns, plan.width), dtype),
            pltpu.VMEM((height, columns), jnp.float32),
            pltpu.VMEM((height, LANES), dtype),
            pltpu.SemaphoreType.DMA(((n_steps + 1) * (plan.half + 1),)),
        ],
        2 * height * plan.width * columns,
        2 * plan.width * (height + columns),
        "reduce_own",
    )


def reduce_taken(plan, near, wide, late, tags, across):
    height = plan.half * PAIR
    n_steps = 2
    dtype = near[0].dtype
    groups, padded = plan.groups, plan.padded
    *lows, tag = blocks_call(
        functools.partial(reduce_taken_kernel, plan, n_steps),
        [near, wide, late, tags, across],
        [jax.ShapeDtypeStruct((height * plan.share // LANES, LANES), jnp.float32)] * groups
        + [jax.ShapeDtypeStruct((height, LANES), jnp.float32)],
        [VMEM] * (groups + 1),
        [
            pltpu.VMEM((groups, height, plan.width), dtype),
            pltpu.VMEM((groups, padded, plan.width), dtype),
            pltpu.VMEM((groups, height, padded), jnp.float32),
            pltpu.VMEM((groups, height, LANES), dtype),
            pltpu.SemaphoreType.DMA(((n_steps + 1) * groups * (plan.half + plan.left_pieces),)),
        ],
        2 * height * plan.width * groups * padded,
        2 * plan.width * (height + padded) * groups,
        "reduce_taken",
    )
    return lows, tag


def rounded(low, share):
    return unpack(low.astype(jnp.bfloat16).astype(jnp.float32), share)


def spread(low, tags, columns, slots, share):
    blocks = [
        jnp.where(slot_mask(tags, first, columns, slots, share), low, 0.0).astype(jnp.bfloat16)
        for first in range(0, columns, LANES)
    ]
    return jnp.concatenate(blocks, axis=1)


def write_deltas(delta, outs):
    delta = delta.astype(jnp.bfloat16)
    for i, out in enumerate(outs):
        out[...] = delta[i * PAIR : (i + 1) * PAIR]


def expand_own_kernel(plan, mine_ref, other_ref, tag_ref, own, *rest):
    outs, (up, sem) = rest[:-2], rest[-2:]
    copy = pltpu.make_async_copy(own, up, sem)
    copy.start()
    low = rounded(mine_ref[...] + other_ref[...], plan.rank)
    wide_low = spread(low, tag_ref[...], up.shape[0], plan.slots, plan.rank)
    copy.wait()
    write_deltas(jnp.dot(wide_low, up[...], preferred_element_type=jnp.float32), outs)


def expand_own(plan, mine, other, tag, own):
    columns, features = own.shape
    return blocks_call(
        functools.partial(expand_own_kernel, plan),
        [own],
        [jax.ShapeDtypeStruct((PAIR, features), jnp.bfloat16)] * plan.half,
        [VMEM] * plan.half,
        [pltpu.VMEM(own.shape, own.dtype), pltpu.SemaphoreType.DMA(())],
        2 * tag.shape[0] * columns * features,
        2 * features * (columns + tag.shape[0]),
        "expand_own",
        extra=(mine, other, tag),
    )


def expand_taken_kernel(plan, *refs):
    lows, tag_ref, refs = refs[: 2 * plan.groups], refs[2 * plan.groups], refs[2 * plan.groups + 1 :]
    wide, narrow, across_wide, across_narrow = refs[:4]
    outs, (up, sems) = refs[4:-2], refs[-2:]
    copies = Copies(am_outer(plan), sems)
    for row, rows, column in plan.up_columns():
        part = pl.ds(0, rows), pl.ds(column, plan.features)
        for e in range(plan.groups):
            copies.both(
                up.at[e, pl.ds(row, rows)],
                (of_wide(wide, plan.left_pieces) if e == 0 else across_wide[e - 1]).at[part],
                (narrow if e == 0 else across_narrow[e - 1]).at[part],
            )
    if plan.padded > plan.left_rows:
        up[:, plan.left_rows :, :] = jnp.zeros(
            (plan.groups, plan.padded - plan.left_rows, plan.features), up.dtype
        )
    tags = tag_ref[...]
    wides = []
    for e in range(plan.groups):
        mine, other = lows[2 * e][...], lows[2 * e + 1][...]
        low = jnp.where(am_outer(plan), mine, other) if e else mine + other
        low = rounded(low, plan.share)
        wides.append(spread(low, tags, plan.left_rows, plan.slots, plan.share))
    copies.wait()
    delta = None
    for e in range(plan.groups):
        product = jnp.dot(wides[e], up[e], preferred_element_type=jnp.float32)
        delta = product if delta is None else delta + product
    write_deltas(delta, outs)


def expand_taken(plan, lows, tag, wide, narrow, across_wide, across_narrow):
    height, features = tag.shape[0], plan.features
    return blocks_call(
        functools.partial(expand_taken_kernel, plan),
        [wide, narrow, across_wide, across_narrow],
        [jax.ShapeDtypeStruct((PAIR, features), jnp.bfloat16)] * plan.half,
        [VMEM] * plan.half,
        [
            pltpu.VMEM((plan.groups, plan.padded, features), jnp.bfloat16),
            pltpu.SemaphoreType.DMA((plan.groups * len(list(plan.up_columns())),)),
        ],
        2 * height * plan.groups * plan.padded * features,
        2 * features * (plan.groups * plan.padded + height),
        "expand_taken",
        extra=(*lows, tag),
    )


def join_kernel(order, seg_ref, base_ref, *refs):
    deltas, out_ref = refs[:-1], refs[-1]
    for i in range(len(deltas) * CAP):
        part = i % CAP
        k = order[i // CAP] * CAP + part

        @pl.when(seg_ref[k] >= 0)
        def _():
            span = pl.ds(pl.multiple_of(seg_ref[k] * SEG, SEG), SEG)
            delta = deltas[i // CAP][part * SEG : (part + 1) * SEG, :]
            out_ref[span, :] = (base_ref[span, :] + delta.astype(jnp.float32)).astype(
                out_ref.dtype
            )


def join(plan, seg_of, base, deltas):
    height, features = base.shape
    order = [kind * plan.half + d for kind in range(2) for d in plan.cross + plan.near]
    deltas = [deltas[i] for i in order]
    return pl.pallas_call(
        functools.partial(join_kernel, order),
        out_shape=jax.ShapeDtypeStruct((height, features), jnp.bfloat16),
        in_specs=[SMEM, VMEM] + [VMEM] * len(deltas),
        out_specs=VMEM,
        compiler_params=params(),
        cost_estimate=pl.CostEstimate(
            flops=height * features, bytes_accessed=8 * height * features, transcendentals=0
        ),
        name="join",
    )(seg_of, base, *deltas)


def swap(value, axis, distance):
    count = lax.axis_size(axis)
    return lax.ppermute(value, axis, [(i, i ^ distance) for i in range(count)])


def send(plan, value, moves):
    shape = (plan.groups, plan.replicas, lax.axis_size("tensor"))

    def place(g, r, c):
        return (g * shape[1] + r) * shape[2] + c

    pairs = [
        (place(g, r, c), place(g ^ flips[0], r ^ flips[1], c ^ flips[2]))
        for senders, *flips in moves
        for g in range(shape[0])
        for r in senders
        for c in range(shape[2])
    ]
    return lax.ppermute(value, ("groups", "replica", "tensor"), pairs)


def return_terms(terms):
    back = {d: swap(terms[d], "replica", d) for d in reversed(range(1, len(terms)))}
    return [back[d] for d in range(1, len(terms))]


def on_device(x, weight, lefts, ups, ids, residency):
    slots, width, rank = lefts.shape
    features = ups.shape[2]
    plan = Plan(
        lax.axis_size("replica"), lax.axis_size("groups"), slots, rank, width, features
    )
    half, n_cross = plan.half, len(plan.cross)
    core = lax.axis_index("tensor")
    outer = am_outer(plan)
    left_rows = jnp.swapaxes(lefts, 1, 2)
    near, wide, seg_of = lay_out(plan, True, ids, residency, x, left_rows, ups)
    wide, tags = wide[: plan.wide], wide[plan.wide :]

    near = [swap(block, "replica", d) for block, d in zip(near, plan.near[1:])]
    wide_in = []
    for i in range(plan.wide):
        moves = []
        if i < n_cross:
            moves.append((plan.outer, 0, plan.cross[i], 0))
        if i < plan.adapter_wide:
            moves.append((plan.inner, 0, half, 0))
        wide_in.append(send(plan, wide[i], moves))

    late_ids, _ = lax.optimization_barrier((ids, seg_of))
    near, late_x = lax.optimization_barrier((near, x))
    own_rows, late, _ = lay_out(plan, False, late_ids, residency, x, left_rows, ups)
    near = own_rows + near
    def part(which, rows):
        columns = lax.dynamic_slice(weight, (0, which * features), (weight.shape[0], features))
        return jnp.dot(rows, columns, preferred_element_type=jnp.float32)

    base_other, base_mine = part(1 - core, late_x), part(core, late_x)

    def across_send(i):
        d = plan.across[i]
        if d in plan.near:
            block = near[plan.near.index(d)][PAIR:]
            value, tag = block[:, :width], block[:, width:]
        else:
            j = plan.cross.index(d)
            value, tag = wide_in[j][PAIR:], tags_in[j][PAIR:]
        if i < plan.pieces:
            piece = wide_in[i // 2][(i % 2) * PAIR : (i % 2 + 1) * PAIR]
            value = jnp.where(outer, piece, value)
        value = jnp.concatenate([value, tag], axis=1)
        return [
            send(plan, value, [(plan.outer, e, 0, 0), (plan.inner, e, 0, 0)])
            for e in range(1, plan.groups)
        ]

    across = [across_send(0)]
    tags_in = [swap(tag, "replica", d) for tag, d in zip(tags, plan.cross)]

    wide_in, near, across, late, tags_in, base_other, base_mine = lax.optimization_barrier(
        (wide_in, near, across, late, tags_in, base_other, base_mine)
    )
    across += [across_send(i) for i in range(1, half)]
    late_in = []
    for block, (d, _, unit) in zip(late, plan.late_blocks()):
        moves = [(plan.inner, 0, d, 0)]
        if unit < plan.pieces:
            moves.append((plan.outer, 0, half, 0))
        if unit == plan.units - 1:
            late_in[0], block = lax.optimization_barrier((late_in[0], block))
        late_in.append(send(plan, block, moves))
    late_up = late_in[0][: plan.up_rows]
    across_up = [send(plan, late_up, [(plan.inner, e, 0, 0)]) for e in range(1, plan.groups)]
    base = base_mine + swap(base_other, "tensor", 1)
    late_in[:-1], across[:-1] = lax.optimization_barrier((late_in[:-1], across[:-1]))
    across = [[blocks[e] for blocks in across] for e in range(plan.groups - 1)]

    own_left = left_rows.reshape(slots * rank, width)
    low, tag = reduce_own(plan, near, wide_in, late_in[:-1], tags_in, own_left)
    other = swap(low, "tensor", 1)
    terms = expand_own(plan, low, other, tag, ups.reshape(slots * rank, features))
    deltas = [terms[0]] + return_terms(terms)

    lows, tag = reduce_taken(plan, near, wide_in, late_in[:-1], tags_in, across)
    late_in[-1], deltas[:2], base, lows = lax.optimization_barrier(
        (late_in[-1], deltas[:2], base, lows)
    )
    lows = reduce_last(plan, lows, tag, near, wide_in, late_in[-1], across)
    pairs = []
    for e in range(plan.groups):
        other = swap(lows[e], "tensor", 1)
        if e:
            total = lows[e] + other
            pairs += [total, swap(total, "groups", e)]
        else:
            pairs += [lows[e], other]
    pairs, deltas = lax.optimization_barrier((pairs, deltas))
    across_wide = [blocks[plan.left_pieces] for blocks in across]
    terms = expand_taken(plan, pairs, tag, wide_in, late_in[0], across_wide, across_up)
    deltas += [terms[0]] + return_terms(terms)
    return join(plan, seg_of, base, deltas)


def solution(mesh):
    placed = (
        P(("groups", "replica"), "tensor"),
        P("tensor", None),
        P("replica", "tensor", None),
        P("replica", None, "tensor"),
        P(("groups", "replica")),
        P(),
    )
    return jax.shard_map(
        on_device,
        mesh=mesh,
        in_specs=placed,
        out_specs=P(("groups", "replica"), "tensor"),
        check_vma=False,
    )
```

```python
import functools

import jax
import jax.numpy as jnp
from jax import lax
from jax.experimental import pallas as pl
from jax.experimental.pallas import tpu as pltpu
from jax.sharding import PartitionSpec as P

CAP = 2
SEG = 32
LANES = 128
PAIR = CAP * SEG
VMEM_LIMIT = 24 * 1024 * 1024
HBM = pl.BlockSpec(memory_space=pltpu.HBM)
SMEM = pl.BlockSpec(memory_space=pltpu.SMEM)
VMEM = pl.BlockSpec(memory_space=pltpu.VMEM)


class Plan:
    def __init__(self, replicas, groups, slots, rank, width, features):
        self.replicas, self.groups, self.slots, self.rank = replicas, groups, slots, rank
        self.width, self.features = width, features
        self.half = replicas // 2
        self.turn = self.half // 2
        self.near = [d for d in range(self.half) if not d & self.turn]
        self.cross = [d for d in range(self.half) if d & self.turn]
        self.across = self.near[1:] + self.near[:1] + self.cross
        self.share = rank // groups
        self.left_rows = slots * self.share
        self.padded = -(-self.left_rows // LANES) * LANES
        beside = width // features
        self.up_rows = -(-self.left_rows // (beside * 16)) * 16
        self.left_pieces = -(-self.left_rows // PAIR)
        self.pieces = self.left_pieces + 1
        assert self.up_rows <= PAIR
        self.adapter_wide = -(-self.pieces // 2)
        self.units = 2 * len(self.cross)
        self.last_piece = self.units - 2 if self.units - 2 < self.left_pieces else None
        assert self.pieces <= self.units and self.adapter_wide <= len(self.cross)
        self.wide = len(self.cross)
        self.outer = [r for r in range(replicas) if self.is_outer(r)]
        self.inner = [r for r in range(replicas) if not self.is_outer(r)]

    def is_outer(self, r):
        return (r < self.turn) or (r >= self.replicas - self.turn)

    def up_columns(self):
        for j, row in enumerate(range(0, self.left_rows, self.up_rows)):
            yield row, min(self.up_rows, self.left_rows - row), j * self.features

    def left_spans(self):
        for piece in range(self.left_pieces):
            yield piece, min(PAIR, self.left_rows - piece * PAIR)

    def late_blocks(self):
        return self.cross + self.cross[::-1]

    def late_rows(self, refs, i, kind):
        return refs[i if kind == 0 else self.units - 1 - i]


def params(limit=VMEM_LIMIT):
    return pltpu.CompilerParams(vmem_limit_bytes=limit)


def am_outer(plan):
    me = lax.axis_index("replica")
    return (me < plan.turn) | (me >= plan.replicas - plan.turn)


def of_wide(refs, piece):
    return refs[piece // 2].at[pl.ds((piece % 2) * PAIR, PAIR)]


def late_adapters(late, piece, plan):
    return late[0 if piece == plan.left_pieces else 1 + piece]


def lay_kernel(plan, first_call, ids_ref, residency_ref, x_ref, left_ref, up_ref, *rest):
    n_near = len(plan.near) - 1 if first_call else 1
    n_blocks = plan.wide if first_call else len(plan.late_blocks())
    n_tags = len(plan.cross) if first_call else 0
    near, rest = rest[:n_near], rest[n_near:]
    blocks, rest = rest[:n_blocks], rest[n_blocks:]
    tag_outs, rest = rest[:n_tags], rest[n_tags:]
    seg_out, seg_ref, slot_ref, count_ref, staged, tags, left, up, in_sems, sems = rest
    half, slots, width, share = plan.half, plan.slots, plan.width, plan.share
    me = lax.axis_index("replica")
    first = pl.multiple_of(lax.axis_index("groups") * share, share)
    outer = am_outer(plan)
    rows_outer = outer if first_call else jnp.logical_not(outer)

    for h in range(plan.replicas):
        count_ref[h] = 0
        for p in range(CAP):
            seg_ref[h * CAP + p] = -1
            slot_ref[h * CAP + p] = 0
    for s in range(ids_ref.shape[0]):
        adapter = ids_ref[s]
        holder = adapter // slots
        place = holder * CAP + count_ref[holder]
        count_ref[holder] = count_ref[holder] + 1
        seg_ref[place] = s
        slot_ref[place] = residency_ref[adapter] - holder * slots
    for d in range(half):
        for kind in range(2):
            for p in range(CAP):
                seg_out[(kind * half + d) * CAP + p] = seg_ref[
                    (me ^ (d + kind * half)) * CAP + p
                ]

    def move(moves, tagged):
        arrivals = []
        for source, stage, _ in moves:
            arrivals.append(pltpu.make_async_copy(source, stage, in_sems.at[len(arrivals)]))
            arrivals[-1].start()
        departures = []

        def depart(source, target):
            departures.append(pltpu.make_async_copy(source, target, sems.at[len(departures)]))
            departures[-1].start()

        written = [(d, kind) for d, kind, _ in tagged]
        if first_call:
            written += [(d, kind) for d in plan.cross for kind in range(2)]
        for d, kind in written:
            for p in range(CAP):
                slot = slot_ref[(me ^ (d + kind * half)) * CAP + p].astype(jnp.float32)
                tags[d, pl.ds((kind * CAP + p) * SEG, SEG), :] = jnp.full(
                    (SEG, LANES), slot, jnp.float32
                ).astype(tags.dtype)
        for d, kind, target in tagged:
            depart(tags.at[d, pl.ds(kind * PAIR, PAIR)], target.at[:, pl.ds(width, LANES)])
        for d, tag_out in zip(plan.cross, tag_outs):
            depart(tags.at[d], tag_out)
        for arrival, (_, stage, target) in zip(arrivals, moves):
            arrival.wait()
            if target is not None:
                for part, place in target:
                    depart(part, place)
        for departure in departures:
            departure.wait()

    def row_moves(targets):
        moves = []
        for d, kind, target in targets:
            for p in range(CAP):
                seg = jnp.maximum(seg_out[(kind * half + d) * CAP + p], 0)
                stage = staged.at[pl.ds(((kind * half + d) * CAP + p) * SEG, SEG)]
                moves.append(
                    (
                        x_ref.at[pl.ds(pl.multiple_of(seg * SEG, SEG), SEG)],
                        stage,
                        [(stage, target.at[pl.ds(p * SEG, SEG), pl.ds(0, width)])],
                    )
                )
        return moves

    def adapter_moves(target_of):
        moves = []
        for slot in range(slots):
            span = pl.ds(slot * share, share)
            source = pl.ds(first, share)
            moves.append((up_ref.at[slot, source], up.at[span], None))
            moves.append((left_ref.at[slot, source], left.at[span], None))
        outs = [
            (
                up.at[pl.ds(row, rows)],
                target_of(plan.left_pieces).at[pl.ds(0, rows), pl.ds(column, plan.features)],
            )
            for row, rows, column in plan.up_columns()
        ]
        outs += [
            (
                left.at[pl.ds(piece * PAIR, rows)],
                target_of(piece).at[pl.ds(0, rows), pl.ds(0, width)],
            )
            for piece, rows in plan.left_spans()
        ]
        source, stage, _ = moves[-1]
        moves[-1] = (source, stage, outs)
        return moves

    near_d = plan.near[1:] if first_call else plan.near[:1]
    near_targets = [
        (d, kind, near[i].at[pl.ds(kind * PAIR, PAIR)])
        for i, d in enumerate(near_d)
        for kind in range(2)
    ]
    if first_call:
        cross_targets = [
            (d, kind, of_wide(blocks, 2 * i + kind))
            for i, d in enumerate(plan.cross)
            for kind in range(2)
        ]
    else:
        cross_targets = [
            (d, kind, plan.late_rows(blocks, i, kind))
            for i, d in enumerate(plan.cross)
            for kind in range(2)
        ]

    @pl.when(rows_outer)
    def _():
        move(row_moves(cross_targets + near_targets), near_targets)

    @pl.when(jnp.logical_not(rows_outer))
    def _():
        if first_call:
            adapters = adapter_moves(lambda piece: of_wide(blocks, piece))
        else:
            adapters = adapter_moves(lambda piece: late_adapters(blocks, piece, plan))
        move(adapters + row_moves(near_targets), near_targets)


def lay_out(plan, first_call, ids, residency, x, left_rows, ups):
    count = 2 * plan.half * CAP
    tagged = jax.ShapeDtypeStruct((2 * PAIR, plan.width + LANES), x.dtype)
    near = [tagged] * (len(plan.near) - 1 if first_call else 1)
    heights = [2] * plan.wide if first_call else [1] * plan.units
    blocks = [jax.ShapeDtypeStruct((n * PAIR, plan.width), x.dtype) for n in heights]
    if first_call:
        blocks += [jax.ShapeDtypeStruct((2 * PAIR, LANES), x.dtype)] * len(plan.cross)
    out = pl.pallas_call(
        functools.partial(lay_kernel, plan, first_call),
        out_shape=near + blocks + [jax.ShapeDtypeStruct((count,), jnp.int32)],
        in_specs=[SMEM, SMEM, HBM, HBM, HBM],
        out_specs=[HBM] * (len(near) + len(blocks)) + [SMEM],
        scratch_shapes=[
            pltpu.SMEM((plan.replicas * CAP,), jnp.int32),
            pltpu.SMEM((plan.replicas * CAP,), jnp.int32),
            pltpu.SMEM((plan.replicas,), jnp.int32),
            pltpu.VMEM((count * SEG, plan.width), x.dtype),
            pltpu.VMEM((plan.half, 2 * PAIR, LANES), x.dtype),
            pltpu.VMEM((plan.left_rows, plan.width), x.dtype),
            pltpu.VMEM((plan.left_rows, plan.features), x.dtype),
            pltpu.SemaphoreType.DMA((count + 2 * plan.slots,)),
            pltpu.SemaphoreType.DMA((2 * count + 2 * plan.pieces,)),
        ],
        compiler_params=params(60 * 1024 * 1024),
        cost_estimate=pl.CostEstimate(flops=0, bytes_accessed=x.size, transcendentals=0),
        name="lay_out_first" if first_call else "lay_out_second",
    )(ids, residency, x, left_rows, ups)
    return list(out[: len(near)]), list(out[len(near) : -1]), out[-1]


def slot_mask(tags, first, columns, slots, share):
    lane = lax.broadcasted_iota(jnp.int32, (1, LANES), 1)
    column_slot = jnp.zeros((1, LANES), jnp.float32)
    for j in range(0, LANES, share):
        slot = (first + j) // share if first + j < columns else -1
        column_slot = jnp.where(lane >= j, float(slot), column_slot)
    return tags == column_slot


class Copies:
    def __init__(self, outer, sems):
        self.outer, self.sems, self.waits = outer, sems, []

    def both(self, target, outer_source, inner_source=None):
        sem = self.sems.at[len(self.waits)]
        copy = pltpu.make_async_copy(outer_source, target, sem)
        if inner_source is None:
            copy.start()
        else:
            pl.when(self.outer)(copy.start)
            pl.when(jnp.logical_not(self.outer))(
                pltpu.make_async_copy(inner_source, target, sem).start
            )
        self.waits.append((None, copy))

    def one(self, wanted, target, source):
        copy = pltpu.make_async_copy(source, target, self.sems.at[len(self.waits)])
        pl.when(wanted)(copy.start)
        self.waits.append((wanted, copy))

    def wait(self):
        for wanted, copy in self.waits:
            if wanted is None:
                copy.wait()
            else:
                pl.when(wanted)(copy.wait)


def lane_group(share):
    return lax.broadcasted_iota(jnp.int32, (1, LANES), 1) // share


def spread_lanes(value, share):
    total = value
    for shift in range(share, LANES, share):
        total += pltpu.roll(value, shift, 1)
    return total


def pack(low, share):
    count = LANES // share
    height = low.shape[0] // count
    everywhere = spread_lanes(low, share)
    packed = jnp.zeros((height, LANES), jnp.float32)
    for i in range(count):
        rows = everywhere[i * height : (i + 1) * height]
        packed = jnp.where(lane_group(share) == i, rows, packed)
    return packed


def unpack(packed, share):
    rows = [
        spread_lanes(jnp.where(lane_group(share) == i, packed, 0.0), share)
        for i in range(LANES // share)
    ]
    return jnp.concatenate(rows, axis=0)


def fold(product, tags, columns, slots, share):
    total = jnp.zeros(tags.shape, jnp.float32)
    for first in range(0, product.shape[1], LANES):
        mask = slot_mask(tags, first, columns, slots, share)
        total += jnp.where(mask, product[:, first : first + LANES], 0.0)
    return total


def copy_rows(copies, plan, kind, target, columns, near, wide, late):
    span = pl.ds(kind * PAIR, PAIR)
    for i, d in enumerate(plan.near):
        copies.both(target.at[pl.ds(d * PAIR, PAIR)], near[i].at[span, columns])
    for i, d in enumerate(plan.cross):
        place = target.at[pl.ds(d * PAIR, PAIR)]
        if i == 0 and kind == 1:
            copies.one(jnp.logical_not(copies.outer), place, wide[i].at[span, columns])
        else:
            copies.both(
                place, plan.late_rows(late, i, kind).at[:, columns], wide[i].at[span, columns]
            )


def copy_tags(copies, plan, kind, target, near, tags):
    span = pl.ds(kind * PAIR, PAIR)
    for i, d in enumerate(plan.near):
        copies.both(target.at[pl.ds(d * PAIR, PAIR)], near[i].at[span, pl.ds(plan.width, LANES)])
    for i, d in enumerate(plan.cross):
        copies.both(target.at[pl.ds(d * PAIR, PAIR)], tags[i].at[span])


def product_of(rows, left):
    return lax.dot_general(
        rows, left, (((1,), (1,)), ((), ())), preferred_element_type=jnp.float32
    )


def reduce_own_kernel(plan, n_steps, near, wide, late, tags, own, low_ref, tag_ref, *scratch):
    rows, left, acc, tag, sems = scratch
    block = plan.width // n_steps
    outer = am_outer(plan)
    each = plan.half + 1
    steps = []
    for k in range(n_steps + 1):
        copies = Copies(outer, sems.at[pl.ds(k * each, each)])
        if k < n_steps:
            columns = pl.ds(k * block, block)
            copy_rows(copies, plan, 0, rows.at[:, columns], columns, near, wide, late)
            copies.both(left.at[:, columns], own.at[:, columns])
        else:
            copy_tags(copies, plan, 0, tag, near, tags)
        steps.append(copies)
    for k in range(n_steps):
        steps[k].wait()
        columns = pl.ds(k * block, block)
        product = product_of(rows[:, columns], left[:, columns])
        acc[...] = acc[...] + product if k else product
    steps[n_steps].wait()
    tags = tag[...].astype(jnp.float32)
    tag_ref[...] = tags
    low_ref[...] = pack(fold(acc, tags, acc.shape[1], plan.slots, plan.rank), plan.rank)


def reduce_taken_kernel(plan, n_steps, near, wide, late, tags, across, *rest):
    lows, tag_ref = rest[: plan.groups], rest[plan.groups]
    rows, left, acc, tag, sems = rest[plan.groups + 1 :]
    block = plan.width // n_steps
    outer = am_outer(plan)
    inner = jnp.logical_not(outer)
    more = plan.groups - 1
    each = plan.half + plan.left_pieces + more * (plan.half + plan.left_pieces)
    missing = pl.ds(plan.cross[0] * PAIR, PAIR)

    @pl.when(outer)
    def _():
        rows[0, missing, :] = jnp.zeros((PAIR, plan.width), rows.dtype)

    if plan.last_piece is not None:

        @pl.when(inner)
        def _():
            left[0, pl.ds(plan.last_piece * PAIR, PAIR), :] = jnp.zeros(
                (PAIR, plan.width), left.dtype
            )

    steps = []
    for k in range(n_steps + 1):
        copies = Copies(outer, sems.at[pl.ds(k * each, each)])
        columns = pl.ds(k * block, block) if k < n_steps else pl.ds(plan.width, LANES)
        if k < n_steps:
            copy_rows(copies, plan, 1, rows.at[0, :, columns], columns, near, wide, late)
        else:
            copy_tags(copies, plan, 1, tag.at[0], near, tags)
        for e in range(1, plan.groups):
            for i, d in enumerate(plan.across):
                target = rows.at[e, :, columns] if k < n_steps else tag.at[e]
                copies.one(
                    inner,
                    target.at[pl.ds(d * PAIR, PAIR)],
                    across[e - 1][i].at[:, columns],
                )
        if k < n_steps:
            for piece, count in plan.left_spans():
                span = pl.ds(0, count), columns
                place = left.at[0, pl.ds(piece * PAIR, count), columns]
                if piece == plan.last_piece:
                    copies.one(outer, place, of_wide(wide, piece).at[span])
                else:
                    copies.both(
                        place,
                        of_wide(wide, piece).at[span],
                        late_adapters(late, piece, plan).at[span],
                    )
                for e in range(1, plan.groups):
                    copies.one(
                        outer,
                        left.at[e, pl.ds(piece * PAIR, count), columns],
                        across[e - 1][piece].at[span],
                    )
        steps.append(copies)
    for k in range(n_steps):
        steps[k].wait()
        columns = pl.ds(k * block, block)
        for e in range(plan.groups):
            rows_at = jnp.where(inner, e, 0)
            left_at = jnp.where(outer, e, 0)
            product = product_of(rows[rows_at, :, columns], left[left_at, :, columns])
            acc[e] = acc[e] + product if k else product
    steps[n_steps].wait()
    tag_ref[...] = tag[0].astype(jnp.float32)
    for e in range(plan.groups):
        tags = tag[jnp.where(inner, e, 0)].astype(jnp.float32)
        low = fold(acc.at[e], tags, plan.left_rows, plan.slots, plan.share)
        lows[e][...] = pack(low, plan.share)


def reduce_last_kernel(plan, *refs):
    groups, width = plan.groups, plan.width
    before, tag_ref, refs = refs[:groups], refs[groups], refs[groups + 1 :]
    near, wide, last, across = refs[:4]
    lows = refs[4:]
    outer = am_outer(plan)
    inner = jnp.logical_not(outer)
    first_row = plan.cross[0] * PAIR

    def padded(parts, height):
        rows = sum(part.shape[0] for part in parts)
        if rows < height:
            parts = parts + [jnp.zeros((height - rows, width), last.dtype)]
        return jnp.concatenate(parts, axis=0)

    @pl.when(outer)
    def _():
        tags = tag_ref[first_row : first_row + PAIR, :]
        rows = last[...]
        for e in range(groups):
            total = jnp.zeros((PAIR, LANES), jnp.float32)
            for first in range(0, plan.padded, LANES):
                parts = []
                for piece, count in plan.left_spans():
                    if first <= piece * PAIR < first + LANES:
                        source = of_wide(wide, piece) if e == 0 else across[e - 1][piece]
                        parts.append(source[:count, :width])
                product = product_of(rows, padded(parts, LANES))
                mask = slot_mask(tags, first, plan.left_rows, plan.slots, plan.share)
                total += jnp.where(mask, product, 0.0)
            whole = [jnp.zeros((PAIR, LANES), jnp.float32)] * plan.half
            whole[plan.cross[0]] = total
            lows[e][...] = before[e][...] + pack(jnp.concatenate(whole, axis=0), plan.share)

    @pl.when(inner)
    def _():
        if plan.last_piece is None:
            for e in range(groups):
                lows[e][...] = before[e][...]
            return
        at = plan.last_piece * PAIR
        first = at // LANES * LANES
        count = min(PAIR, plan.left_rows - at)
        parts = [jnp.zeros((at - first, width), last.dtype)] if at > first else []
        left = padded(parts + [last[:count, :]], LANES)
        for e in range(groups):
            if e == 0:
                blocks = {d: near[i].at[PAIR:] for i, d in enumerate(plan.near)}
                blocks.update({d: wide[i].at[PAIR:] for i, d in enumerate(plan.cross)})
                tags = tag_ref[...]
            else:
                blocks = {d: across[e - 1][i] for i, d in enumerate(plan.across)}
                tags = [blocks[d][:, width:] for d in range(plan.half)]
                tags = jnp.concatenate(tags, axis=0).astype(jnp.float32)
            whole = jnp.concatenate([blocks[d][:, :width] for d in range(plan.half)], axis=0)
            product = product_of(whole, left)
            mask = slot_mask(tags, first, plan.left_rows, plan.slots, plan.share)
            low = pack(jnp.where(mask, product, 0.0), plan.share)
            lows[e][...] = before[e][...] + low


def reduce_last(plan, lows, tag, near, wide, last, across):
    flat, tree = jax.tree.flatten([near, wide, last, across])
    n_head = plan.groups + 1

    def body(*refs):
        nested = jax.tree.unflatten(tree, refs[n_head : n_head + len(flat)])
        reduce_last_kernel(plan, *refs[:n_head], *nested, *refs[n_head + len(flat) :])

    shapes = [jax.ShapeDtypeStruct(a.shape, a.dtype) for a in lows]
    return pl.pallas_call(
        body,
        out_shape=shapes,
        in_specs=[VMEM] * (n_head + len(flat)),
        out_specs=[VMEM] * len(lows),
        compiler_params=params(),
        cost_estimate=pl.CostEstimate(flops=1, bytes_accessed=1, transcendentals=0),
        name="reduce_last",
    )(*lows, tag, *flat)


def blocks_call(kernel, blocks, out_shape, out_specs, scratch, flops, moved, name, extra=()):
    flat, tree = jax.tree.flatten(blocks)
    n_extra = len(extra)

    def body(*refs):
        head, rest = refs[:n_extra], refs[n_extra:]
        nested = jax.tree.unflatten(tree, rest[: len(flat)])
        kernel(*head, *nested, *rest[len(flat) :])

    return pl.pallas_call(
        body,
        out_shape=out_shape,
        in_specs=[VMEM] * n_extra + [HBM] * len(flat),
        out_specs=out_specs,
        scratch_shapes=scratch,
        compiler_params=params(),
        cost_estimate=pl.CostEstimate(flops=1, bytes_accessed=1, transcendentals=0),
        name=name,
    )(*extra, *flat)


def reduce_own(plan, near, wide, late, tags, own):
    height = plan.half * PAIR
    columns = own.shape[0]
    n_steps = 2
    dtype = own.dtype
    return blocks_call(
        functools.partial(reduce_own_kernel, plan, n_steps),
        [near, wide, late, tags, own],
        [
            jax.ShapeDtypeStruct((height * plan.rank // LANES, LANES), jnp.float32),
            jax.ShapeDtypeStruct((height, LANES), jnp.float32),
        ],
        [VMEM] * 2,
        [
            pltpu.VMEM((height, plan.width), dtype),
            pltpu.VMEM((columns, plan.width), dtype),
            pltpu.VMEM((height, columns), jnp.float32),
            pltpu.VMEM((height, LANES), dtype),
            pltpu.SemaphoreType.DMA(((n_steps + 1) * (plan.half + 1),)),
        ],
        2 * height * plan.width * columns,
        2 * plan.width * (height + columns),
        "reduce_own",
    )


def reduce_taken(plan, near, wide, late, tags, across):
    height = plan.half * PAIR
    n_steps = 2
    dtype = near[0].dtype
    groups, padded = plan.groups, plan.padded
    *lows, tag = blocks_call(
        functools.partial(reduce_taken_kernel, plan, n_steps),
        [near, wide, late, tags, across],
        [jax.ShapeDtypeStruct((height * plan.share // LANES, LANES), jnp.float32)] * groups
        + [jax.ShapeDtypeStruct((height, LANES), jnp.float32)],
        [VMEM] * (groups + 1),
        [
            pltpu.VMEM((groups, height, plan.width), dtype),
            pltpu.VMEM((groups, padded, plan.width), dtype),
            pltpu.VMEM((groups, height, padded), jnp.float32),
            pltpu.VMEM((groups, height, LANES), dtype),
            pltpu.SemaphoreType.DMA(((n_steps + 1) * groups * (plan.half + plan.left_pieces),)),
        ],
        2 * height * plan.width * groups * padded,
        2 * plan.width * (height + padded) * groups,
        "reduce_taken",
    )
    return lows, tag


def rounded(low, share):
    return unpack(low.astype(jnp.bfloat16).astype(jnp.float32), share)


def spread(low, tags, columns, slots, share):
    blocks = [
        jnp.where(slot_mask(tags, first, columns, slots, share), low, 0.0).astype(jnp.bfloat16)
        for first in range(0, columns, LANES)
    ]
    return jnp.concatenate(blocks, axis=1)


def write_deltas(delta, outs):
    delta = delta.astype(jnp.bfloat16)
    for i, out in enumerate(outs):
        out[...] = delta[i * PAIR : (i + 1) * PAIR]


def expand_own_kernel(plan, mine_ref, other_ref, tag_ref, own, *rest):
    outs, (up, sem) = rest[:-2], rest[-2:]
    copy = pltpu.make_async_copy(own, up, sem)
    copy.start()
    low = rounded(mine_ref[...] + other_ref[...], plan.rank)
    wide_low = spread(low, tag_ref[...], up.shape[0], plan.slots, plan.rank)
    copy.wait()
    write_deltas(jnp.dot(wide_low, up[...], preferred_element_type=jnp.float32), outs)


def expand_own(plan, mine, other, tag, own):
    columns, features = own.shape
    return blocks_call(
        functools.partial(expand_own_kernel, plan),
        [own],
        [jax.ShapeDtypeStruct((PAIR, features), jnp.bfloat16)] * plan.half,
        [VMEM] * plan.half,
        [pltpu.VMEM(own.shape, own.dtype), pltpu.SemaphoreType.DMA(())],
        2 * tag.shape[0] * columns * features,
        2 * features * (columns + tag.shape[0]),
        "expand_own",
        extra=(mine, other, tag),
    )


def expand_taken_kernel(plan, *refs):
    lows, tag_ref, refs = refs[: 2 * plan.groups], refs[2 * plan.groups], refs[2 * plan.groups + 1 :]
    wide, narrow, across_wide, across_narrow = refs[:4]
    outs, (up, sems) = refs[4:-2], refs[-2:]
    copies = Copies(am_outer(plan), sems)
    for row, rows, column in plan.up_columns():
        part = pl.ds(0, rows), pl.ds(column, plan.features)
        for e in range(plan.groups):
            copies.both(
                up.at[e, pl.ds(row, rows)],
                (of_wide(wide, plan.left_pieces) if e == 0 else across_wide[e - 1]).at[part],
                (narrow if e == 0 else across_narrow[e - 1]).at[part],
            )
    if plan.padded > plan.left_rows:
        up[:, plan.left_rows :, :] = jnp.zeros(
            (plan.groups, plan.padded - plan.left_rows, plan.features), up.dtype
        )
    tags = tag_ref[...]
    wides = []
    for e in range(plan.groups):
        mine, other = lows[2 * e][...], lows[2 * e + 1][...]
        low = jnp.where(am_outer(plan), mine, other) if e else mine + other
        low = rounded(low, plan.share)
        wides.append(spread(low, tags, plan.left_rows, plan.slots, plan.share))
    copies.wait()
    delta = None
    for e in range(plan.groups):
        product = jnp.dot(wides[e], up[e], preferred_element_type=jnp.float32)
        delta = product if delta is None else delta + product
    write_deltas(delta, outs)


def expand_taken(plan, lows, tag, wide, narrow, across_wide, across_narrow):
    height, features = tag.shape[0], plan.features
    return blocks_call(
        functools.partial(expand_taken_kernel, plan),
        [wide, narrow, across_wide, across_narrow],
        [jax.ShapeDtypeStruct((PAIR, features), jnp.bfloat16)] * plan.half,
        [VMEM] * plan.half,
        [
            pltpu.VMEM((plan.groups, plan.padded, features), jnp.bfloat16),
            pltpu.SemaphoreType.DMA((plan.groups * len(list(plan.up_columns())),)),
        ],
        2 * height * plan.groups * plan.padded * features,
        2 * features * (plan.groups * plan.padded + height),
        "expand_taken",
        extra=(*lows, tag),
    )


def join_kernel(order, seg_ref, base_ref, *refs):
    deltas, out_ref = refs[:-1], refs[-1]
    for i in range(len(deltas) * CAP):
        part = i % CAP
        k = order[i // CAP] * CAP + part

        @pl.when(seg_ref[k] >= 0)
        def _():
            span = pl.ds(pl.multiple_of(seg_ref[k] * SEG, SEG), SEG)
            delta = deltas[i // CAP][part * SEG : (part + 1) * SEG, :]
            out_ref[span, :] = (base_ref[span, :] + delta.astype(jnp.float32)).astype(
                out_ref.dtype
            )


def join(plan, seg_of, base, deltas):
    height, features = base.shape
    order = [kind * plan.half + d for kind in range(2) for d in plan.cross + plan.near]
    deltas = [deltas[i] for i in order]
    return pl.pallas_call(
        functools.partial(join_kernel, order),
        out_shape=jax.ShapeDtypeStruct((height, features), jnp.bfloat16),
        in_specs=[SMEM, VMEM] + [VMEM] * len(deltas),
        out_specs=VMEM,
        compiler_params=params(),
        cost_estimate=pl.CostEstimate(
            flops=height * features, bytes_accessed=8 * height * features, transcendentals=0
        ),
        name="join",
    )(seg_of, base, *deltas)


def swap(value, axis, distance):
    count = lax.axis_size(axis)
    return lax.ppermute(value, axis, [(i, i ^ distance) for i in range(count)])


def send(plan, value, moves):
    shape = (plan.groups, plan.replicas, lax.axis_size("tensor"))

    def place(g, r, c):
        return (g * shape[1] + r) * shape[2] + c

    pairs = [
        (place(g, r, c), place(g ^ flips[0], r ^ flips[1], c ^ flips[2]))
        for senders, *flips in moves
        for g in range(shape[0])
        for r in senders
        for c in range(shape[2])
    ]
    return lax.ppermute(value, ("groups", "replica", "tensor"), pairs)


def return_terms(terms):
    back = {d: swap(terms[d], "replica", d) for d in reversed(range(1, len(terms)))}
    return [back[d] for d in range(1, len(terms))]


def on_device(x, weight, lefts, ups, ids, residency):
    slots, width, rank = lefts.shape
    features = ups.shape[2]
    plan = Plan(
        lax.axis_size("replica"), lax.axis_size("groups"), slots, rank, width, features
    )
    half, n_cross = plan.half, len(plan.cross)
    core = lax.axis_index("tensor")
    outer = am_outer(plan)
    left_rows = jnp.swapaxes(lefts, 1, 2)
    near, wide, seg_of = lay_out(plan, True, ids, residency, x, left_rows, ups)
    wide, tags = wide[: plan.wide], wide[plan.wide :]

    near = [swap(block, "replica", d) for block, d in zip(near, plan.near[1:])]
    wide_in = []
    for i in range(plan.wide):
        moves = []
        if i < n_cross:
            moves.append((plan.outer, 0, plan.cross[i], 0))
        if i < plan.adapter_wide:
            moves.append((plan.inner, 0, half, 0))
        wide_in.append(send(plan, wide[i], moves))

    late_ids, _ = lax.optimization_barrier((ids, seg_of))
    near, late_x = lax.optimization_barrier((near, x))
    own_rows, late, _ = lay_out(plan, False, late_ids, residency, x, left_rows, ups)
    near = own_rows + near
    def part(which, rows):
        columns = lax.dynamic_slice(weight, (0, which * features), (weight.shape[0], features))
        return jnp.dot(rows, columns, preferred_element_type=jnp.float32)

    base_other, base_mine = part(1 - core, late_x), part(core, late_x)

    def across_send(i):
        d = plan.across[i]
        if d in plan.near:
            block = near[plan.near.index(d)][PAIR:]
            value, tag = block[:, :width], block[:, width:]
        else:
            j = plan.cross.index(d)
            value, tag = wide_in[j][PAIR:], tags_in[j][PAIR:]
        if i < plan.pieces:
            piece = wide_in[i // 2][(i % 2) * PAIR : (i % 2 + 1) * PAIR]
            value = jnp.where(outer, piece, value)
        value = jnp.concatenate([value, tag], axis=1)
        return [
            send(plan, value, [(plan.outer, e, 0, 0), (plan.inner, e, 0, 0)])
            for e in range(1, plan.groups)
        ]

    across = [across_send(0), across_send(1)]
    tags_in = [swap(tag, "replica", d) for tag, d in zip(tags, plan.cross)]

    wide_in, near, across[0], late, tags_in, base_other, base_mine = lax.optimization_barrier(
        (wide_in, near, across[0], late, tags_in, base_other, base_mine)
    )
    across += [across_send(i) for i in range(2, half)]
    late_in = []
    for unit, d in enumerate(plan.late_blocks()):
        moves = [(plan.inner, 0, d, 0)]
        if unit < plan.pieces:
            moves.append((plan.outer, 0, half, 0))
        block = late[unit]
        if unit >= 2:
            late_in[unit - 2], across[1], block = lax.optimization_barrier(
                (late_in[unit - 2], across[1], block)
            )
        late_in.append(send(plan, block, moves))
    late_up = late_in[0][: plan.up_rows]
    across_up = [send(plan, late_up, [(plan.inner, e, 0, 0)]) for e in range(1, plan.groups)]
    base = base_mine + swap(base_other, "tensor", 1)
    late_in[:n_cross], across[:-1] = lax.optimization_barrier((late_in[:n_cross], across[:-1]))
    across = [[blocks[e] for blocks in across] for e in range(plan.groups - 1)]

    own_left = left_rows.reshape(slots * rank, width)
    low, tag = reduce_own(plan, near, wide_in, late_in[:n_cross], tags_in, own_left)
    other = swap(low, "tensor", 1)
    terms = expand_own(plan, low, other, tag, ups.reshape(slots * rank, features))
    deltas = [terms[0]] + return_terms(terms)

    lows, tag = reduce_taken(plan, near, wide_in, late_in[:-1], tags_in, across)
    late_in[-1], deltas[:2], lows, base = lax.optimization_barrier(
        (late_in[-1], deltas[:2], lows, base)
    )
    lows = reduce_last(plan, lows, tag, near, wide_in, late_in[-1], across)
    pairs = []
    for e in range(plan.groups):
        other = swap(lows[e], "tensor", 1)
        if e:
            total = lows[e] + other
            pairs += [total, swap(total, "groups", e)]
        else:
            pairs += [lows[e], other]
    pairs, deltas = lax.optimization_barrier((pairs, deltas))
    across_wide = [blocks[plan.left_pieces] for blocks in across]
    terms = expand_taken(plan, pairs, tag, wide_in, late_in[0], across_wide, across_up)
    deltas += [terms[0]] + return_terms(terms)
    return join(plan, seg_of, base, deltas)


def solution(mesh):
    placed = (
        P(("groups", "replica"), "tensor"),
        P("tensor", None),
        P("replica", "tensor", None),
        P("replica", None, "tensor"),
        P(("groups", "replica")),
        P(),
    )
    return jax.shard_map(
        on_device,
        mesh=mesh,
        in_specs=placed,
        out_specs=P(("groups", "replica"), "tensor"),
        check_vma=False,
    )
```

```python
import functools

import jax
import jax.numpy as jnp
from jax import lax
from jax.experimental import pallas as pl
from jax.experimental.pallas import tpu as pltpu
from jax.sharding import PartitionSpec as P

CAP = 2
SEG = 32
LANES = 128
PAIR = CAP * SEG
VMEM_LIMIT = 24 * 1024 * 1024
HBM = pl.BlockSpec(memory_space=pltpu.HBM)
SMEM = pl.BlockSpec(memory_space=pltpu.SMEM)
VMEM = pl.BlockSpec(memory_space=pltpu.VMEM)


class Plan:
    def __init__(self, replicas, groups, slots, rank, width, features):
        self.replicas, self.groups, self.slots, self.rank = replicas, groups, slots, rank
        self.width, self.features = width, features
        self.half = replicas // 2
        self.turn = self.half // 2
        self.near = [d for d in range(self.half) if not d & self.turn]
        self.cross = [d for d in range(self.half) if d & self.turn]
        self.across = self.near[1:] + self.near[:1] + self.cross
        self.share = rank // groups
        self.left_rows = slots * self.share
        self.padded = -(-self.left_rows // LANES) * LANES
        beside = width // features
        self.up_rows = -(-self.left_rows // (beside * 16)) * 16
        self.left_pieces = -(-self.left_rows // PAIR)
        self.pieces = self.left_pieces + 1
        assert self.up_rows <= PAIR
        self.adapter_wide = -(-self.pieces // 2)
        self.units = 2 * len(self.cross)
        self.last_piece = self.units - 2 if self.units - 2 < self.left_pieces else None
        assert self.pieces <= self.units and self.adapter_wide <= len(self.cross)
        self.wide = len(self.cross)
        self.outer = [r for r in range(replicas) if self.is_outer(r)]
        self.inner = [r for r in range(replicas) if not self.is_outer(r)]

    def is_outer(self, r):
        return (r < self.turn) or (r >= self.replicas - self.turn)

    def up_columns(self):
        for j, row in enumerate(range(0, self.left_rows, self.up_rows)):
            yield row, min(self.up_rows, self.left_rows - row), j * self.features

    def left_spans(self):
        for piece in range(self.left_pieces):
            yield piece, min(PAIR, self.left_rows - piece * PAIR)

    def late_blocks(self):
        return self.cross + self.cross[::-1]

    def late_rows(self, refs, i, kind):
        return refs[i if kind == 0 else self.units - 1 - i]


def params(limit=VMEM_LIMIT):
    return pltpu.CompilerParams(vmem_limit_bytes=limit)


def am_outer(plan):
    me = lax.axis_index("replica")
    return (me < plan.turn) | (me >= plan.replicas - plan.turn)


def of_wide(refs, piece):
    return refs[piece // 2].at[pl.ds((piece % 2) * PAIR, PAIR)]


def late_adapters(late, piece, plan):
    return late[0 if piece == plan.left_pieces else 1 + piece]


def lay_kernel(plan, first_call, ids_ref, residency_ref, x_ref, left_ref, up_ref, *rest):
    n_near = len(plan.near) - 1 if first_call else 1
    n_blocks = plan.wide if first_call else len(plan.late_blocks())
    n_tags = len(plan.cross) if first_call else 0
    near, rest = rest[:n_near], rest[n_near:]
    blocks, rest = rest[:n_blocks], rest[n_blocks:]
    tag_outs, rest = rest[:n_tags], rest[n_tags:]
    seg_out, seg_ref, slot_ref, count_ref, staged, tags, left, up, in_sems, sems = rest
    half, slots, width, share = plan.half, plan.slots, plan.width, plan.share
    me = lax.axis_index("replica")
    first = pl.multiple_of(lax.axis_index("groups") * share, share)
    outer = am_outer(plan)
    rows_outer = outer if first_call else jnp.logical_not(outer)

    for h in range(plan.replicas):
        count_ref[h] = 0
        for p in range(CAP):
            seg_ref[h * CAP + p] = -1
            slot_ref[h * CAP + p] = 0
    for s in range(ids_ref.shape[0]):
        adapter = ids_ref[s]
        holder = adapter // slots
        place = holder * CAP + count_ref[holder]
        count_ref[holder] = count_ref[holder] + 1
        seg_ref[place] = s
        slot_ref[place] = residency_ref[adapter] - holder * slots
    for d in range(half):
        for kind in range(2):
            for p in range(CAP):
                seg_out[(kind * half + d) * CAP + p] = seg_ref[
                    (me ^ (d + kind * half)) * CAP + p
                ]

    def move(moves, tagged):
        arrivals = []
        for source, stage, _ in moves:
            arrivals.append(pltpu.make_async_copy(source, stage, in_sems.at[len(arrivals)]))
            arrivals[-1].start()
        departures = []

        def depart(source, target):
            departures.append(pltpu.make_async_copy(source, target, sems.at[len(departures)]))
            departures[-1].start()

        written = [(d, kind) for d, kind, _ in tagged]
        if first_call:
            written += [(d, kind) for d in plan.cross for kind in range(2)]
        for d, kind in written:
            for p in range(CAP):
                slot = slot_ref[(me ^ (d + kind * half)) * CAP + p].astype(jnp.float32)
                tags[d, pl.ds((kind * CAP + p) * SEG, SEG), :] = jnp.full(
                    (SEG, LANES), slot, jnp.float32
                ).astype(tags.dtype)
        for d, kind, target in tagged:
            depart(tags.at[d, pl.ds(kind * PAIR, PAIR)], target.at[:, pl.ds(width, LANES)])
        for d, tag_out in zip(plan.cross, tag_outs):
            depart(tags.at[d], tag_out)
        for arrival, (_, stage, target) in zip(arrivals, moves):
            arrival.wait()
            if target is not None:
                for part, place in target:
                    depart(part, place)
        for departure in departures:
            departure.wait()

    def row_moves(targets):
        moves = []
        for d, kind, target in targets:
            for p in range(CAP):
                seg = jnp.maximum(seg_out[(kind * half + d) * CAP + p], 0)
                stage = staged.at[pl.ds(((kind * half + d) * CAP + p) * SEG, SEG)]
                moves.append(
                    (
                        x_ref.at[pl.ds(pl.multiple_of(seg * SEG, SEG), SEG)],
                        stage,
                        [(stage, target.at[pl.ds(p * SEG, SEG), pl.ds(0, width)])],
                    )
                )
        return moves

    def adapter_moves(target_of):
        moves = []
        for slot in range(slots):
            span = pl.ds(slot * share, share)
            source = pl.ds(first, share)
            moves.append((up_ref.at[slot, source], up.at[span], None))
            moves.append((left_ref.at[slot, source], left.at[span], None))
        outs = [
            (
                up.at[pl.ds(row, rows)],
                target_of(plan.left_pieces).at[pl.ds(0, rows), pl.ds(column, plan.features)],
            )
            for row, rows, column in plan.up_columns()
        ]
        outs += [
            (
                left.at[pl.ds(piece * PAIR, rows)],
                target_of(piece).at[pl.ds(0, rows), pl.ds(0, width)],
            )
            for piece, rows in plan.left_spans()
        ]
        source, stage, _ = moves[-1]
        moves[-1] = (source, stage, outs)
        return moves

    near_d = plan.near[1:] if first_call else plan.near[:1]
    near_targets = [
        (d, kind, near[i].at[pl.ds(kind * PAIR, PAIR)])
        for i, d in enumerate(near_d)
        for kind in range(2)
    ]
    if first_call:
        cross_targets = [
            (d, kind, of_wide(blocks, 2 * i + kind))
            for i, d in enumerate(plan.cross)
            for kind in range(2)
        ]
    else:
        cross_targets = [
            (d, kind, plan.late_rows(blocks, i, kind))
            for i, d in enumerate(plan.cross)
            for kind in range(2)
        ]

    @pl.when(rows_outer)
    def _():
        move(row_moves(cross_targets + near_targets), near_targets)

    @pl.when(jnp.logical_not(rows_outer))
    def _():
        if first_call:
            adapters = adapter_moves(lambda piece: of_wide(blocks, piece))
        else:
            adapters = adapter_moves(lambda piece: late_adapters(blocks, piece, plan))
        move(adapters + row_moves(near_targets), near_targets)


def lay_out(plan, first_call, ids, residency, x, left_rows, ups):
    count = 2 * plan.half * CAP
    tagged = jax.ShapeDtypeStruct((2 * PAIR, plan.width + LANES), x.dtype)
    near = [tagged] * (len(plan.near) - 1 if first_call else 1)
    heights = [2] * plan.wide if first_call else [1] * plan.units
    blocks = [jax.ShapeDtypeStruct((n * PAIR, plan.width), x.dtype) for n in heights]
    if first_call:
        blocks += [jax.ShapeDtypeStruct((2 * PAIR, LANES), x.dtype)] * len(plan.cross)
    out = pl.pallas_call(
        functools.partial(lay_kernel, plan, first_call),
        out_shape=near + blocks + [jax.ShapeDtypeStruct((count,), jnp.int32)],
        in_specs=[SMEM, SMEM, HBM, HBM, HBM],
        out_specs=[HBM] * (len(near) + len(blocks)) + [SMEM],
        scratch_shapes=[
            pltpu.SMEM((plan.replicas * CAP,), jnp.int32),
            pltpu.SMEM((plan.replicas * CAP,), jnp.int32),
            pltpu.SMEM((plan.replicas,), jnp.int32),
            pltpu.VMEM((count * SEG, plan.width), x.dtype),
            pltpu.VMEM((plan.half, 2 * PAIR, LANES), x.dtype),
            pltpu.VMEM((plan.left_rows, plan.width), x.dtype),
            pltpu.VMEM((plan.left_rows, plan.features), x.dtype),
            pltpu.SemaphoreType.DMA((count + 2 * plan.slots,)),
            pltpu.SemaphoreType.DMA((2 * count + 2 * plan.pieces,)),
        ],
        compiler_params=params(60 * 1024 * 1024),
        cost_estimate=pl.CostEstimate(flops=0, bytes_accessed=x.size, transcendentals=0),
        name="lay_out_first" if first_call else "lay_out_second",
    )(ids, residency, x, left_rows, ups)
    return list(out[: len(near)]), list(out[len(near) : -1]), out[-1]


def slot_mask(tags, first, columns, slots, share):
    lane = lax.broadcasted_iota(jnp.int32, (1, LANES), 1)
    column_slot = jnp.zeros((1, LANES), jnp.float32)
    for j in range(0, LANES, share):
        slot = (first + j) // share if first + j < columns else -1
        column_slot = jnp.where(lane >= j, float(slot), column_slot)
    return tags == column_slot


class Copies:
    def __init__(self, outer, sems):
        self.outer, self.sems, self.waits = outer, sems, []

    def both(self, target, outer_source, inner_source=None):
        sem = self.sems.at[len(self.waits)]
        copy = pltpu.make_async_copy(outer_source, target, sem)
        if inner_source is None:
            copy.start()
        else:
            pl.when(self.outer)(copy.start)
            pl.when(jnp.logical_not(self.outer))(
                pltpu.make_async_copy(inner_source, target, sem).start
            )
        self.waits.append((None, copy))

    def one(self, wanted, target, source):
        copy = pltpu.make_async_copy(source, target, self.sems.at[len(self.waits)])
        pl.when(wanted)(copy.start)
        self.waits.append((wanted, copy))

    def wait(self):
        for wanted, copy in self.waits:
            if wanted is None:
                copy.wait()
            else:
                pl.when(wanted)(copy.wait)


def lane_group(share):
    return lax.broadcasted_iota(jnp.int32, (1, LANES), 1) // share


def spread_lanes(value, share):
    total = value
    for shift in range(share, LANES, share):
        total += pltpu.roll(value, shift, 1)
    return total


def pack(low, share):
    count = LANES // share
    height = low.shape[0] // count
    everywhere = spread_lanes(low, share)
    packed = jnp.zeros((height, LANES), jnp.float32)
    for i in range(count):
        rows = everywhere[i * height : (i + 1) * height]
        packed = jnp.where(lane_group(share) == i, rows, packed)
    return packed


def unpack(packed, share):
    rows = [
        spread_lanes(jnp.where(lane_group(share) == i, packed, 0.0), share)
        for i in range(LANES // share)
    ]
    return jnp.concatenate(rows, axis=0)


def fold(product, tags, columns, slots, share):
    total = jnp.zeros(tags.shape, jnp.float32)
    for first in range(0, product.shape[1], LANES):
        mask = slot_mask(tags, first, columns, slots, share)
        total += jnp.where(mask, product[:, first : first + LANES], 0.0)
    return total


def copy_rows(copies, plan, kind, target, columns, near, wide, late):
    span = pl.ds(kind * PAIR, PAIR)
    for i, d in enumerate(plan.near):
        copies.both(target.at[pl.ds(d * PAIR, PAIR)], near[i].at[span, columns])
    for i, d in enumerate(plan.cross):
        place = target.at[pl.ds(d * PAIR, PAIR)]
        if i == 0 and kind == 1:
            copies.one(jnp.logical_not(copies.outer), place, wide[i].at[span, columns])
        else:
            copies.both(
                place, plan.late_rows(late, i, kind).at[:, columns], wide[i].at[span, columns]
            )


def copy_tags(copies, plan, kind, target, near, tags):
    span = pl.ds(kind * PAIR, PAIR)
    for i, d in enumerate(plan.near):
        copies.both(target.at[pl.ds(d * PAIR, PAIR)], near[i].at[span, pl.ds(plan.width, LANES)])
    for i, d in enumerate(plan.cross):
        copies.both(target.at[pl.ds(d * PAIR, PAIR)], tags[i].at[span])


def product_of(rows, left):
    return lax.dot_general(
        rows, left, (((1,), (1,)), ((), ())), preferred_element_type=jnp.float32
    )


def reduce_own_kernel(plan, n_steps, near, wide, late, tags, own, low_ref, tag_ref, *scratch):
    rows, left, acc, tag, sems = scratch
    block = plan.width // n_steps
    outer = am_outer(plan)
    each = plan.half + 1
    steps = []
    for k in range(n_steps + 1):
        copies = Copies(outer, sems.at[pl.ds(k * each, each)])
        if k < n_steps:
            columns = pl.ds(k * block, block)
            copy_rows(copies, plan, 0, rows.at[:, columns], columns, near, wide, late)
            copies.both(left.at[:, columns], own.at[:, columns])
        else:
            copy_tags(copies, plan, 0, tag, near, tags)
        steps.append(copies)
    for k in range(n_steps):
        steps[k].wait()
        columns = pl.ds(k * block, block)
        product = product_of(rows[:, columns], left[:, columns])
        acc[...] = acc[...] + product if k else product
    steps[n_steps].wait()
    tags = tag[...].astype(jnp.float32)
    tag_ref[...] = tags
    low_ref[...] = pack(fold(acc, tags, acc.shape[1], plan.slots, plan.rank), plan.rank)


def reduce_taken_kernel(plan, n_steps, near, wide, late, tags, across, *rest):
    lows, tag_ref = rest[: plan.groups], rest[plan.groups]
    rows, left, acc, tag, sems = rest[plan.groups + 1 :]
    block = plan.width // n_steps
    outer = am_outer(plan)
    inner = jnp.logical_not(outer)
    more = plan.groups - 1
    each = plan.half + plan.left_pieces + more * (plan.half + plan.left_pieces)
    missing = pl.ds(plan.cross[0] * PAIR, PAIR)

    @pl.when(outer)
    def _():
        rows[0, missing, :] = jnp.zeros((PAIR, plan.width), rows.dtype)

    if plan.last_piece is not None:

        @pl.when(inner)
        def _():
            left[0, pl.ds(plan.last_piece * PAIR, PAIR), :] = jnp.zeros(
                (PAIR, plan.width), left.dtype
            )

    steps = []
    for k in range(n_steps + 1):
        copies = Copies(outer, sems.at[pl.ds(k * each, each)])
        columns = pl.ds(k * block, block) if k < n_steps else pl.ds(plan.width, LANES)
        if k < n_steps:
            copy_rows(copies, plan, 1, rows.at[0, :, columns], columns, near, wide, late)
        else:
            copy_tags(copies, plan, 1, tag.at[0], near, tags)
        for e in range(1, plan.groups):
            for i, d in enumerate(plan.across):
                target = rows.at[e, :, columns] if k < n_steps else tag.at[e]
                copies.one(
                    inner,
                    target.at[pl.ds(d * PAIR, PAIR)],
                    across[e - 1][i].at[:, columns],
                )
        if k < n_steps:
            for piece, count in plan.left_spans():
                span = pl.ds(0, count), columns
                place = left.at[0, pl.ds(piece * PAIR, count), columns]
                if piece == plan.last_piece:
                    copies.one(outer, place, of_wide(wide, piece).at[span])
                else:
                    copies.both(
                        place,
                        of_wide(wide, piece).at[span],
                        late_adapters(late, piece, plan).at[span],
                    )
                for e in range(1, plan.groups):
                    copies.one(
                        outer,
                        left.at[e, pl.ds(piece * PAIR, count), columns],
                        across[e - 1][piece].at[span],
                    )
        steps.append(copies)
    for k in range(n_steps):
        steps[k].wait()
        columns = pl.ds(k * block, block)
        for e in range(plan.groups):
            rows_at = jnp.where(inner, e, 0)
            left_at = jnp.where(outer, e, 0)
            product = product_of(rows[rows_at, :, columns], left[left_at, :, columns])
            acc[e] = acc[e] + product if k else product
    steps[n_steps].wait()
    tag_ref[...] = tag[0].astype(jnp.float32)
    for e in range(plan.groups):
        tags = tag[jnp.where(inner, e, 0)].astype(jnp.float32)
        low = fold(acc.at[e], tags, plan.left_rows, plan.slots, plan.share)
        lows[e][...] = pack(low, plan.share)


def reduce_last_kernel(plan, *refs):
    groups, width = plan.groups, plan.width
    before, tag_ref, refs = refs[:groups], refs[groups], refs[groups + 1 :]
    near, wide, last, across = refs[:4]
    lows = refs[4:]
    outer = am_outer(plan)
    inner = jnp.logical_not(outer)
    first_row = plan.cross[0] * PAIR

    def padded(parts, height):
        rows = sum(part.shape[0] for part in parts)
        if rows < height:
            parts = parts + [jnp.zeros((height - rows, width), last.dtype)]
        return jnp.concatenate(parts, axis=0)

    @pl.when(outer)
    def _():
        tags = tag_ref[first_row : first_row + PAIR, :]
        rows = last[...]
        for e in range(groups):
            total = jnp.zeros((PAIR, LANES), jnp.float32)
            for first in range(0, plan.padded, LANES):
                parts = []
                for piece, count in plan.left_spans():
                    if first <= piece * PAIR < first + LANES:
                        source = of_wide(wide, piece) if e == 0 else across[e - 1][piece]
                        parts.append(source[:count, :width])
                product = product_of(rows, padded(parts, LANES))
                mask = slot_mask(tags, first, plan.left_rows, plan.slots, plan.share)
                total += jnp.where(mask, product, 0.0)
            whole = [jnp.zeros((PAIR, LANES), jnp.float32)] * plan.half
            whole[plan.cross[0]] = total
            lows[e][...] = before[e][...] + pack(jnp.concatenate(whole, axis=0), plan.share)

    @pl.when(inner)
    def _():
        if plan.last_piece is None:
            for e in range(groups):
                lows[e][...] = before[e][...]
            return
        at = plan.last_piece * PAIR
        first = at // LANES * LANES
        count = min(PAIR, plan.left_rows - at)
        parts = [jnp.zeros((at - first, width), last.dtype)] if at > first else []
        left = padded(parts + [last[:count, :]], LANES)
        for e in range(groups):
            if e == 0:
                blocks = {d: near[i].at[PAIR:] for i, d in enumerate(plan.near)}
                blocks.update({d: wide[i].at[PAIR:] for i, d in enumerate(plan.cross)})
                tags = tag_ref[...]
            else:
                blocks = {d: across[e - 1][i] for i, d in enumerate(plan.across)}
                tags = [blocks[d][:, width:] for d in range(plan.half)]
                tags = jnp.concatenate(tags, axis=0).astype(jnp.float32)
            whole = jnp.concatenate([blocks[d][:, :width] for d in range(plan.half)], axis=0)
            product = product_of(whole, left)
            mask = slot_mask(tags, first, plan.left_rows, plan.slots, plan.share)
            low = pack(jnp.where(mask, product, 0.0), plan.share)
            lows[e][...] = before[e][...] + low


def reduce_last(plan, lows, tag, near, wide, last, across):
    flat, tree = jax.tree.flatten([near, wide, last, across])
    n_head = plan.groups + 1

    def body(*refs):
        nested = jax.tree.unflatten(tree, refs[n_head : n_head + len(flat)])
        reduce_last_kernel(plan, *refs[:n_head], *nested, *refs[n_head + len(flat) :])

    shapes = [jax.ShapeDtypeStruct(a.shape, a.dtype) for a in lows]
    return pl.pallas_call(
        body,
        out_shape=shapes,
        in_specs=[VMEM] * (n_head + len(flat)),
        out_specs=[VMEM] * len(lows),
        compiler_params=params(),
        cost_estimate=pl.CostEstimate(flops=1, bytes_accessed=1, transcendentals=0),
        name="reduce_last",
    )(*lows, tag, *flat)


def blocks_call(kernel, blocks, out_shape, out_specs, scratch, flops, moved, name, extra=()):
    flat, tree = jax.tree.flatten(blocks)
    n_extra = len(extra)

    def body(*refs):
        head, rest = refs[:n_extra], refs[n_extra:]
        nested = jax.tree.unflatten(tree, rest[: len(flat)])
        kernel(*head, *nested, *rest[len(flat) :])

    return pl.pallas_call(
        body,
        out_shape=out_shape,
        in_specs=[VMEM] * n_extra + [HBM] * len(flat),
        out_specs=out_specs,
        scratch_shapes=scratch,
        compiler_params=params(),
        cost_estimate=pl.CostEstimate(flops=1, bytes_accessed=1, transcendentals=0),
        name=name,
    )(*extra, *flat)


def reduce_own(plan, near, wide, late, tags, own):
    height = plan.half * PAIR
    columns = own.shape[0]
    n_steps = 2
    dtype = own.dtype
    return blocks_call(
        functools.partial(reduce_own_kernel, plan, n_steps),
        [near, wide, late, tags, own],
        [
            jax.ShapeDtypeStruct((height * plan.rank // LANES, LANES), jnp.float32),
            jax.ShapeDtypeStruct((height, LANES), jnp.float32),
        ],
        [VMEM] * 2,
        [
            pltpu.VMEM((height, plan.width), dtype),
            pltpu.VMEM((columns, plan.width), dtype),
            pltpu.VMEM((height, columns), jnp.float32),
            pltpu.VMEM((height, LANES), dtype),
            pltpu.SemaphoreType.DMA(((n_steps + 1) * (plan.half + 1),)),
        ],
        2 * height * plan.width * columns,
        2 * plan.width * (height + columns),
        "reduce_own",
    )


def reduce_taken(plan, near, wide, late, tags, across):
    height = plan.half * PAIR
    n_steps = 2
    dtype = near[0].dtype
    groups, padded = plan.groups, plan.padded
    *lows, tag = blocks_call(
        functools.partial(reduce_taken_kernel, plan, n_steps),
        [near, wide, late, tags, across],
        [jax.ShapeDtypeStruct((height * plan.share // LANES, LANES), jnp.float32)] * groups
        + [jax.ShapeDtypeStruct((height, LANES), jnp.float32)],
        [VMEM] * (groups + 1),
        [
            pltpu.VMEM((groups, height, plan.width), dtype),
            pltpu.VMEM((groups, padded, plan.width), dtype),
            pltpu.VMEM((groups, height, padded), jnp.float32),
            pltpu.VMEM((groups, height, LANES), dtype),
            pltpu.SemaphoreType.DMA(((n_steps + 1) * groups * (plan.half + plan.left_pieces),)),
        ],
        2 * height * plan.width * groups * padded,
        2 * plan.width * (height + padded) * groups,
        "reduce_taken",
    )
    return lows, tag


def rounded(low, share):
    return unpack(low.astype(jnp.bfloat16).astype(jnp.float32), share)


def spread(low, tags, columns, slots, share):
    blocks = [
        jnp.where(slot_mask(tags, first, columns, slots, share), low, 0.0).astype(jnp.bfloat16)
        for first in range(0, columns, LANES)
    ]
    return jnp.concatenate(blocks, axis=1)


def write_deltas(delta, outs):
    delta = delta.astype(jnp.bfloat16)
    for i, out in enumerate(outs):
        out[...] = delta[i * PAIR : (i + 1) * PAIR]


def expand_own_kernel(plan, mine_ref, other_ref, tag_ref, own, *rest):
    outs, (up, sem) = rest[:-2], rest[-2:]
    copy = pltpu.make_async_copy(own, up, sem)
    copy.start()
    low = rounded(mine_ref[...] + other_ref[...], plan.rank)
    wide_low = spread(low, tag_ref[...], up.shape[0], plan.slots, plan.rank)
    copy.wait()
    write_deltas(jnp.dot(wide_low, up[...], preferred_element_type=jnp.float32), outs)


def expand_own(plan, mine, other, tag, own):
    columns, features = own.shape
    return blocks_call(
        functools.partial(expand_own_kernel, plan),
        [own],
        [jax.ShapeDtypeStruct((PAIR, features), jnp.bfloat16)] * plan.half,
        [VMEM] * plan.half,
        [pltpu.VMEM(own.shape, own.dtype), pltpu.SemaphoreType.DMA(())],
        2 * tag.shape[0] * columns * features,
        2 * features * (columns + tag.shape[0]),
        "expand_own",
        extra=(mine, other, tag),
    )


def expand_taken_kernel(plan, *refs):
    lows, tag_ref, refs = refs[: 2 * plan.groups], refs[2 * plan.groups], refs[2 * plan.groups + 1 :]
    wide, narrow, across_wide, across_narrow = refs[:4]
    outs, (up, sems) = refs[4:-2], refs[-2:]
    copies = Copies(am_outer(plan), sems)
    for row, rows, column in plan.up_columns():
        part = pl.ds(0, rows), pl.ds(column, plan.features)
        for e in range(plan.groups):
            copies.both(
                up.at[e, pl.ds(row, rows)],
                (of_wide(wide, plan.left_pieces) if e == 0 else across_wide[e - 1]).at[part],
                (narrow if e == 0 else across_narrow[e - 1]).at[part],
            )
    if plan.padded > plan.left_rows:
        up[:, plan.left_rows :, :] = jnp.zeros(
            (plan.groups, plan.padded - plan.left_rows, plan.features), up.dtype
        )
    tags = tag_ref[...]
    wides = []
    for e in range(plan.groups):
        mine, other = lows[2 * e][...], lows[2 * e + 1][...]
        low = jnp.where(am_outer(plan), mine, other) if e else mine + other
        low = rounded(low, plan.share)
        wides.append(spread(low, tags, plan.left_rows, plan.slots, plan.share))
    copies.wait()
    delta = None
    for e in range(plan.groups):
        product = jnp.dot(wides[e], up[e], preferred_element_type=jnp.float32)
        delta = product if delta is None else delta + product
    write_deltas(delta, outs)


def expand_taken(plan, lows, tag, wide, narrow, across_wide, across_narrow):
    height, features = tag.shape[0], plan.features
    return blocks_call(
        functools.partial(expand_taken_kernel, plan),
        [wide, narrow, across_wide, across_narrow],
        [jax.ShapeDtypeStruct((PAIR, features), jnp.bfloat16)] * plan.half,
        [VMEM] * plan.half,
        [
            pltpu.VMEM((plan.groups, plan.padded, features), jnp.bfloat16),
            pltpu.SemaphoreType.DMA((plan.groups * len(list(plan.up_columns())),)),
        ],
        2 * height * plan.groups * plan.padded * features,
        2 * features * (plan.groups * plan.padded + height),
        "expand_taken",
        extra=(*lows, tag),
    )


def join_kernel(order, seg_ref, base_ref, *refs):
    deltas, out_ref = refs[:-1], refs[-1]
    for i in range(len(deltas) * CAP):
        part = i % CAP
        k = order[i // CAP] * CAP + part

        @pl.when(seg_ref[k] >= 0)
        def _():
            span = pl.ds(pl.multiple_of(seg_ref[k] * SEG, SEG), SEG)
            delta = deltas[i // CAP][part * SEG : (part + 1) * SEG, :]
            out_ref[span, :] = (base_ref[span, :] + delta.astype(jnp.float32)).astype(
                out_ref.dtype
            )


def join(plan, seg_of, base, deltas):
    height, features = base.shape
    order = [kind * plan.half + d for kind in range(2) for d in plan.cross + plan.near]
    deltas = [deltas[i] for i in order]
    return pl.pallas_call(
        functools.partial(join_kernel, order),
        out_shape=jax.ShapeDtypeStruct((height, features), jnp.bfloat16),
        in_specs=[SMEM, VMEM] + [VMEM] * len(deltas),
        out_specs=VMEM,
        compiler_params=params(),
        cost_estimate=pl.CostEstimate(
            flops=height * features, bytes_accessed=8 * height * features, transcendentals=0
        ),
        name="join",
    )(seg_of, base, *deltas)


def swap(value, axis, distance):
    count = lax.axis_size(axis)
    return lax.ppermute(value, axis, [(i, i ^ distance) for i in range(count)])


def send(plan, value, moves):
    shape = (plan.groups, plan.replicas, lax.axis_size("tensor"))

    def place(g, r, c):
        return (g * shape[1] + r) * shape[2] + c

    pairs = [
        (place(g, r, c), place(g ^ flips[0], r ^ flips[1], c ^ flips[2]))
        for senders, *flips in moves
        for g in range(shape[0])
        for r in senders
        for c in range(shape[2])
    ]
    return lax.ppermute(value, ("groups", "replica", "tensor"), pairs)


def return_terms(terms):
    back = {d: swap(terms[d], "replica", d) for d in reversed(range(1, len(terms)))}
    return [back[d] for d in range(1, len(terms))]


def on_device(x, weight, lefts, ups, ids, residency):
    slots, width, rank = lefts.shape
    features = ups.shape[2]
    plan = Plan(
        lax.axis_size("replica"), lax.axis_size("groups"), slots, rank, width, features
    )
    half, n_cross = plan.half, len(plan.cross)
    core = lax.axis_index("tensor")
    outer = am_outer(plan)
    left_rows = jnp.swapaxes(lefts, 1, 2)
    near, wide, seg_of = lay_out(plan, True, ids, residency, x, left_rows, ups)
    wide, tags = wide[: plan.wide], wide[plan.wide :]

    near = [swap(block, "replica", d) for block, d in zip(near, plan.near[1:])]
    wide_in = []
    for i in range(plan.wide):
        moves = []
        if i < n_cross:
            moves.append((plan.outer, 0, plan.cross[i], 0))
        if i < plan.adapter_wide:
            moves.append((plan.inner, 0, half, 0))
        wide_in.append(send(plan, wide[i], moves))

    late_ids, _ = lax.optimization_barrier((ids, seg_of))
    near, late_x = lax.optimization_barrier((near, x))
    own_rows, late, _ = lay_out(plan, False, late_ids, residency, x, left_rows, ups)
    near = own_rows + near
    def part(which, rows):
        columns = lax.dynamic_slice(weight, (0, which * features), (weight.shape[0], features))
        return jnp.dot(rows, columns, preferred_element_type=jnp.float32)

    base_other, base_mine = part(1 - core, late_x), part(core, late_x)

    def across_send(i):
        d = plan.across[i]
        if d in plan.near:
            block = near[plan.near.index(d)][PAIR:]
            value, tag = block[:, :width], block[:, width:]
        else:
            j = plan.cross.index(d)
            value, tag = wide_in[j][PAIR:], tags_in[j][PAIR:]
        if i < plan.pieces:
            piece = wide_in[i // 2][(i % 2) * PAIR : (i % 2 + 1) * PAIR]
            value = jnp.where(outer, piece, value)
        value = jnp.concatenate([value, tag], axis=1)
        return [
            send(plan, value, [(plan.outer, e, 0, 0), (plan.inner, e, 0, 0)])
            for e in range(1, plan.groups)
        ]

    across = [across_send(0), across_send(1)]
    tags_in = [swap(tag, "replica", d) for tag, d in zip(tags, plan.cross)]

    wide_in, near, across[0], late, tags_in, base_other, base_mine = lax.optimization_barrier(
        (wide_in, near, across[0], late, tags_in, base_other, base_mine)
    )
    late_in = []
    for unit, d in enumerate(plan.late_blocks()):
        moves = [(plan.inner, 0, d, 0)]
        if unit < plan.pieces:
            moves.append((plan.outer, 0, half, 0))
        block = late[unit]
        if unit == 2:
            late_in[0], across[1], tags_in, block = lax.optimization_barrier(
                (late_in[0], across[1], tags_in, block)
            )
        elif unit > 2:
            late_in[unit - 2], block = lax.optimization_barrier((late_in[unit - 2], block))
        late_in.append(send(plan, block, moves))
    across += [across_send(i) for i in range(2, half)]
    late_up = late_in[0][: plan.up_rows]
    across_up = [send(plan, late_up, [(plan.inner, e, 0, 0)]) for e in range(1, plan.groups)]
    base = base_mine + swap(base_other, "tensor", 1)
    late_in[:n_cross], across[:-1] = lax.optimization_barrier((late_in[:n_cross], across[:-1]))
    across = [[blocks[e] for blocks in across] for e in range(plan.groups - 1)]

    own_left = left_rows.reshape(slots * rank, width)
    low, tag = reduce_own(plan, near, wide_in, late_in[:n_cross], tags_in, own_left)
    other = swap(low, "tensor", 1)
    terms = expand_own(plan, low, other, tag, ups.reshape(slots * rank, features))
    deltas = [terms[0]] + return_terms(terms)

    lows, tag = reduce_taken(plan, near, wide_in, late_in[:-1], tags_in, across)
    late_in[-1], deltas[:2], lows, base = lax.optimization_barrier(
        (late_in[-1], deltas[:2], lows, base)
    )
    lows = reduce_last(plan, lows, tag, near, wide_in, late_in[-1], across)
    pairs = []
    for e in range(plan.groups):
        other = swap(lows[e], "tensor", 1)
        if e:
            total = lows[e] + other
            pairs += [total, swap(total, "groups", e)]
        else:
            pairs += [lows[e], other]
    pairs, deltas = lax.optimization_barrier((pairs, deltas))
    across_wide = [blocks[plan.left_pieces] for blocks in across]
    terms = expand_taken(plan, pairs, tag, wide_in, late_in[0], across_wide, across_up)
    deltas += [terms[0]] + return_terms(terms)
    return join(plan, seg_of, base, deltas)


def solution(mesh):
    placed = (
        P(("groups", "replica"), "tensor"),
        P("tensor", None),
        P("replica", "tensor", None),
        P("replica", None, "tensor"),
        P(("groups", "replica")),
        P(),
    )
    return jax.shard_map(
        on_device,
        mesh=mesh,
        in_specs=placed,
        out_specs=P(("groups", "replica"), "tensor"),
        check_vma=False,
    )
```

```python
import functools

import jax
import jax.numpy as jnp
from jax import lax
from jax.experimental import pallas as pl
from jax.experimental.pallas import tpu as pltpu
from jax.sharding import PartitionSpec as P

CAP = 2
SEG = 32
LANES = 128
PAIR = CAP * SEG
VMEM_LIMIT = 24 * 1024 * 1024
HBM = pl.BlockSpec(memory_space=pltpu.HBM)
SMEM = pl.BlockSpec(memory_space=pltpu.SMEM)
VMEM = pl.BlockSpec(memory_space=pltpu.VMEM)


class Plan:
    def __init__(self, replicas, groups, slots, rank, width, features):
        self.replicas, self.groups, self.slots, self.rank = replicas, groups, slots, rank
        self.width, self.features = width, features
        self.half = replicas // 2
        self.turn = self.half // 2
        self.near = [d for d in range(self.half) if not d & self.turn]
        self.cross = [d for d in range(self.half) if d & self.turn]
        self.across = self.near[1:] + self.near[:1] + self.cross
        self.share = rank // groups
        self.left_rows = slots * self.share
        self.padded = -(-self.left_rows // LANES) * LANES
        beside = width // features
        self.up_rows = -(-self.left_rows // (beside * 16)) * 16
        self.left_pieces = -(-self.left_rows // PAIR)
        self.pieces = self.left_pieces + 1
        assert self.up_rows <= PAIR
        self.adapter_wide = -(-self.pieces // 2)
        self.units = 2 * len(self.cross)
        self.last_piece = self.units - 2 if self.units - 2 < self.left_pieces else None
        assert self.pieces <= self.units and self.adapter_wide <= len(self.cross)
        self.wide = len(self.cross)
        self.outer = [r for r in range(replicas) if self.is_outer(r)]
        self.inner = [r for r in range(replicas) if not self.is_outer(r)]

    def is_outer(self, r):
        return (r < self.turn) or (r >= self.replicas - self.turn)

    def up_columns(self):
        for j, row in enumerate(range(0, self.left_rows, self.up_rows)):
            yield row, min(self.up_rows, self.left_rows - row), j * self.features

    def left_spans(self):
        for piece in range(self.left_pieces):
            yield piece, min(PAIR, self.left_rows - piece * PAIR)

    def late_blocks(self):
        return self.cross + self.cross[::-1]

    def late_rows(self, refs, i, kind):
        return refs[i if kind == 0 else self.units - 1 - i]


def params(limit=VMEM_LIMIT):
    return pltpu.CompilerParams(vmem_limit_bytes=limit)


def am_outer(plan):
    me = lax.axis_index("replica")
    return (me < plan.turn) | (me >= plan.replicas - plan.turn)


def of_wide(refs, piece):
    return refs[piece // 2].at[pl.ds((piece % 2) * PAIR, PAIR)]


def late_adapters(late, piece, plan):
    return late[0 if piece == plan.left_pieces else 1 + piece]


def lay_kernel(plan, first_call, ids_ref, residency_ref, x_ref, left_ref, up_ref, *rest):
    n_near = len(plan.near) - 1 if first_call else 1
    n_blocks = plan.wide if first_call else len(plan.late_blocks())
    n_tags = len(plan.cross) if first_call else 0
    near, rest = rest[:n_near], rest[n_near:]
    blocks, rest = rest[:n_blocks], rest[n_blocks:]
    tag_outs, rest = rest[:n_tags], rest[n_tags:]
    seg_out, seg_ref, slot_ref, count_ref, staged, tags, left, up, in_sems, sems = rest
    half, slots, width, share = plan.half, plan.slots, plan.width, plan.share
    me = lax.axis_index("replica")
    first = pl.multiple_of(lax.axis_index("groups") * share, share)
    outer = am_outer(plan)
    rows_outer = outer if first_call else jnp.logical_not(outer)

    def copy_in(i, source, stage):
        return pltpu.make_async_copy(source, stage, in_sems.at[i])

    quarter = x_ref.shape[0] // 4
    x_in = [
        copy_in(i, x_ref.at[pl.ds(i * quarter, quarter)], staged.at[pl.ds(i * quarter, quarter)])
        for i in range(4)
    ]
    adapters_in = []
    for slot in range(slots):
        source = pl.ds(first, share)
        stage = pl.ds(slot * share, share)
        n = len(adapters_in)
        adapters_in.append(copy_in(n, left_ref.at[slot, source], left.at[stage]))
        adapters_in.append(copy_in(n + 1, up_ref.at[slot, source], up.at[stage]))

    @pl.when(rows_outer)
    def _():
        for copy in x_in:
            copy.start()

    @pl.when(jnp.logical_not(rows_outer))
    def _():
        for copy in adapters_in:
            copy.start()

    scale = 2**16 // slots + 1
    assert all(a * scale >> 16 == a // slots for a in range(residency_ref.shape[0]))
    for h in range(plan.replicas):
        count_ref[h] = 0
        for p in range(CAP):
            seg_ref[h * CAP + p] = -1
            slot_ref[h * CAP + p] = 0
    for s in range(ids_ref.shape[0]):
        adapter = ids_ref[s]
        holder = (adapter * scale) >> 16
        count = count_ref[holder]
        place = holder * CAP + count
        count_ref[holder] = count + 1
        seg_ref[place] = s
        slot_ref[place] = residency_ref[adapter] - holder * slots
    for d in range(half):
        for kind in range(2):
            for p in range(CAP):
                seg_out[(kind * half + d) * CAP + p] = seg_ref[
                    (me ^ (d + kind * half)) * CAP + p
                ]

    def segment(d, kind, p):
        seg = jnp.maximum(seg_out[(kind * half + d) * CAP + p], 0)
        return pl.ds(pl.multiple_of(seg * SEG, SEG), SEG)

    def write_tags(targets):
        written = [(d, kind) for d, kind, _ in targets]
        if first_call:
            written += [(d, kind) for d in plan.cross for kind in range(2)]
        for d, kind in written:
            for p in range(CAP):
                slot = slot_ref[(me ^ (d + kind * half)) * CAP + p].astype(jnp.float32)
                tags[d, pl.ds((kind * CAP + p) * SEG, SEG), :] = jnp.full(
                    (SEG, LANES), slot, jnp.float32
                ).astype(tags.dtype)

    near_d = plan.near[1:] if first_call else plan.near[:1]
    near_targets = [
        (d, kind, near[i].at[pl.ds(kind * PAIR, PAIR)])
        for i, d in enumerate(near_d)
        for kind in range(2)
    ]
    cross_targets = [
        (
            d,
            kind,
            of_wide(blocks, 2 * i + kind) if first_call else plan.late_rows(blocks, i, kind),
        )
        for i, d in enumerate(plan.cross)
        for kind in range(2)
    ]
    departures = []

    def depart(source, target):
        copy = pltpu.make_async_copy(source, target, sems.at[len(departures)])
        copy.start()
        departures.append(copy)

    def depart_tags():
        for d, kind, target in near_targets:
            depart(tags.at[d, pl.ds(kind * PAIR, PAIR)], target.at[:, pl.ds(width, LANES)])
        for d, tag_out in zip(plan.cross, tag_outs):
            depart(tags.at[d], tag_out)

    def finish():
        for copy in departures:
            copy.wait()
        departures.clear()

    @pl.when(rows_outer)
    def _():
        write_tags(near_targets)
        for copy in x_in:
            copy.wait()
        for d, kind, target in cross_targets + near_targets:
            for p in range(CAP):
                place = target.at[pl.ds(p * SEG, SEG), pl.ds(0, width)]
                depart(staged.at[segment(d, kind, p)], place)
        depart_tags()
        finish()

    @pl.when(jnp.logical_not(rows_outer))
    def _():
        rows_in = []
        for d, kind, target in near_targets:
            for p in range(CAP):
                stage = staged.at[pl.ds(len(rows_in) * SEG, SEG)]
                copy = copy_in(
                    len(adapters_in) + len(rows_in), x_ref.at[segment(d, kind, p)], stage
                )
                copy.start()
                place = target.at[pl.ds(p * SEG, SEG), pl.ds(0, width)]
                rows_in.append((copy, stage, place))
        write_tags(near_targets)
        depart_tags()
        for slot in range(slots):
            adapters_in[2 * slot].wait()
            piece, at = divmod(slot * share, PAIR)
            unit = (
                of_wide(blocks, piece) if first_call else late_adapters(blocks, piece, plan)
            )
            depart(
                left.at[pl.ds(slot * share, share)],
                unit.at[pl.ds(at, share), pl.ds(0, width)],
            )
        for slot in range(slots):
            adapters_in[2 * slot + 1].wait()
        piece = plan.left_pieces
        unit = of_wide(blocks, piece) if first_call else late_adapters(blocks, piece, plan)
        for row, rows, column in plan.up_columns():
            depart(up.at[pl.ds(row, rows)], unit.at[pl.ds(0, rows), pl.ds(column, plan.features)])
        for copy, stage, place in rows_in:
            copy.wait()
            depart(stage, place)
        finish()


def lay_out(plan, first_call, ids, residency, x, left_rows, ups):
    count = 2 * plan.half * CAP
    tagged = jax.ShapeDtypeStruct((2 * PAIR, plan.width + LANES), x.dtype)
    near = [tagged] * (len(plan.near) - 1 if first_call else 1)
    heights = [2] * plan.wide if first_call else [1] * plan.units
    blocks = [jax.ShapeDtypeStruct((n * PAIR, plan.width), x.dtype) for n in heights]
    if first_call:
        blocks += [jax.ShapeDtypeStruct((2 * PAIR, LANES), x.dtype)] * len(plan.cross)
    out = pl.pallas_call(
        functools.partial(lay_kernel, plan, first_call),
        out_shape=near + blocks + [jax.ShapeDtypeStruct((count,), jnp.int32)],
        in_specs=[SMEM, SMEM, HBM, HBM, HBM],
        out_specs=[HBM] * (len(near) + len(blocks)) + [SMEM],
        scratch_shapes=[
            pltpu.SMEM((plan.replicas * CAP,), jnp.int32),
            pltpu.SMEM((plan.replicas * CAP,), jnp.int32),
            pltpu.SMEM((plan.replicas,), jnp.int32),
            pltpu.VMEM((count * SEG, plan.width), x.dtype),
            pltpu.VMEM((plan.half, 2 * PAIR, LANES), x.dtype),
            pltpu.VMEM((plan.left_rows, plan.width), x.dtype),
            pltpu.VMEM((plan.left_rows, plan.features), x.dtype),
            pltpu.SemaphoreType.DMA((count + 2 * plan.slots,)),
            pltpu.SemaphoreType.DMA((2 * count + 2 * plan.pieces,)),
        ],
        compiler_params=params(60 * 1024 * 1024),
        cost_estimate=pl.CostEstimate(flops=0, bytes_accessed=x.size, transcendentals=0),
        name="lay_out_first" if first_call else "lay_out_second",
    )(ids, residency, x, left_rows, ups)
    return list(out[: len(near)]), list(out[len(near) : -1]), out[-1]


def slot_mask(tags, first, columns, slots, share):
    lane = lax.broadcasted_iota(jnp.int32, (1, LANES), 1)
    column_slot = jnp.zeros((1, LANES), jnp.float32)
    for j in range(0, LANES, share):
        slot = (first + j) // share if first + j < columns else -1
        column_slot = jnp.where(lane >= j, float(slot), column_slot)
    return tags == column_slot


class Copies:
    def __init__(self, outer, sems):
        self.outer, self.sems, self.waits = outer, sems, []

    def both(self, target, outer_source, inner_source=None):
        sem = self.sems.at[len(self.waits)]
        copy = pltpu.make_async_copy(outer_source, target, sem)
        if inner_source is None:
            copy.start()
        else:
            pl.when(self.outer)(copy.start)
            pl.when(jnp.logical_not(self.outer))(
                pltpu.make_async_copy(inner_source, target, sem).start
            )
        self.waits.append((None, copy))

    def one(self, wanted, target, source):
        copy = pltpu.make_async_copy(source, target, self.sems.at[len(self.waits)])
        pl.when(wanted)(copy.start)
        self.waits.append((wanted, copy))

    def wait(self):
        for wanted, copy in self.waits:
            if wanted is None:
                copy.wait()
            else:
                pl.when(wanted)(copy.wait)


def lane_group(share):
    return lax.broadcasted_iota(jnp.int32, (1, LANES), 1) // share


def spread_lanes(value, share):
    total = value
    for shift in range(share, LANES, share):
        total += pltpu.roll(value, shift, 1)
    return total


def pack(low, share):
    count = LANES // share
    height = low.shape[0] // count
    everywhere = spread_lanes(low, share)
    packed = jnp.zeros((height, LANES), jnp.float32)
    for i in range(count):
        rows = everywhere[i * height : (i + 1) * height]
        packed = jnp.where(lane_group(share) == i, rows, packed)
    return packed


def unpack(packed, share):
    rows = [
        spread_lanes(jnp.where(lane_group(share) == i, packed, 0.0), share)
        for i in range(LANES // share)
    ]
    return jnp.concatenate(rows, axis=0)


def fold(product, tags, columns, slots, share):
    total = jnp.zeros(tags.shape, jnp.float32)
    for first in range(0, product.shape[1], LANES):
        mask = slot_mask(tags, first, columns, slots, share)
        total += jnp.where(mask, product[:, first : first + LANES], 0.0)
    return total


def copy_rows(copies, plan, kind, target, columns, near, wide, late):
    span = pl.ds(kind * PAIR, PAIR)
    for i, d in enumerate(plan.near):
        copies.both(target.at[pl.ds(d * PAIR, PAIR)], near[i].at[span, columns])
    for i, d in enumerate(plan.cross):
        place = target.at[pl.ds(d * PAIR, PAIR)]
        if i == 0 and kind == 1:
            copies.one(jnp.logical_not(copies.outer), place, wide[i].at[span, columns])
        else:
            copies.both(
                place, plan.late_rows(late, i, kind).at[:, columns], wide[i].at[span, columns]
            )


def copy_tags(copies, plan, kind, target, near, tags):
    span = pl.ds(kind * PAIR, PAIR)
    for i, d in enumerate(plan.near):
        copies.both(target.at[pl.ds(d * PAIR, PAIR)], near[i].at[span, pl.ds(plan.width, LANES)])
    for i, d in enumerate(plan.cross):
        copies.both(target.at[pl.ds(d * PAIR, PAIR)], tags[i].at[span])


def product_of(rows, left):
    return lax.dot_general(
        rows, left, (((1,), (1,)), ((), ())), preferred_element_type=jnp.float32
    )


def reduce_own_kernel(plan, n_steps, near, wide, late, tags, own, low_ref, tag_ref, *scratch):
    rows, left, acc, tag, sems = scratch
    block = plan.width // n_steps
    outer = am_outer(plan)
    each = plan.half + 1
    steps = []
    for k in range(n_steps + 1):
        copies = Copies(outer, sems.at[pl.ds(k * each, each)])
        if k < n_steps:
            columns = pl.ds(k * block, block)
            copy_rows(copies, plan, 0, rows.at[:, columns], columns, near, wide, late)
            copies.both(left.at[:, columns], own.at[:, columns])
        else:
            copy_tags(copies, plan, 0, tag, near, tags)
        steps.append(copies)
    for k in range(n_steps):
        steps[k].wait()
        columns = pl.ds(k * block, block)
        product = product_of(rows[:, columns], left[:, columns])
        acc[...] = acc[...] + product if k else product
    steps[n_steps].wait()
    tags = tag[...].astype(jnp.float32)
    tag_ref[...] = tags
    low_ref[...] = pack(fold(acc, tags, acc.shape[1], plan.slots, plan.rank), plan.rank)


def reduce_taken_kernel(plan, n_steps, near, wide, late, tags, across, *rest):
    lows, tag_ref = rest[: plan.groups], rest[plan.groups]
    rows, left, acc, tag, sems = rest[plan.groups + 1 :]
    block = plan.width // n_steps
    outer = am_outer(plan)
    inner = jnp.logical_not(outer)
    more = plan.groups - 1
    each = plan.half + plan.left_pieces + more * (plan.half + plan.left_pieces)
    missing = pl.ds(plan.cross[0] * PAIR, PAIR)

    @pl.when(outer)
    def _():
        rows[0, missing, :] = jnp.zeros((PAIR, plan.width), rows.dtype)

    if plan.last_piece is not None:

        @pl.when(inner)
        def _():
            left[0, pl.ds(plan.last_piece * PAIR, PAIR), :] = jnp.zeros(
                (PAIR, plan.width), left.dtype
            )

    steps = []
    for k in range(n_steps + 1):
        copies = Copies(outer, sems.at[pl.ds(k * each, each)])
        columns = pl.ds(k * block, block) if k < n_steps else pl.ds(plan.width, LANES)
        if k < n_steps:
            copy_rows(copies, plan, 1, rows.at[0, :, columns], columns, near, wide, late)
        else:
            copy_tags(copies, plan, 1, tag.at[0], near, tags)
        for e in range(1, plan.groups):
            for i, d in enumerate(plan.across):
                target = rows.at[e, :, columns] if k < n_steps else tag.at[e]
                copies.one(
                    inner,
                    target.at[pl.ds(d * PAIR, PAIR)],
                    across[e - 1][i].at[:, columns],
                )
        if k < n_steps:
            for piece, count in plan.left_spans():
                span = pl.ds(0, count), columns
                place = left.at[0, pl.ds(piece * PAIR, count), columns]
                if piece == plan.last_piece:
                    copies.one(outer, place, of_wide(wide, piece).at[span])
                else:
                    copies.both(
                        place,
                        of_wide(wide, piece).at[span],
                        late_adapters(late, piece, plan).at[span],
                    )
                for e in range(1, plan.groups):
                    copies.one(
                        outer,
                        left.at[e, pl.ds(piece * PAIR, count), columns],
                        across[e - 1][piece].at[span],
                    )
        steps.append(copies)
    for k in range(n_steps):
        steps[k].wait()
        columns = pl.ds(k * block, block)
        for e in range(plan.groups):
            rows_at = jnp.where(inner, e, 0)
            left_at = jnp.where(outer, e, 0)
            product = product_of(rows[rows_at, :, columns], left[left_at, :, columns])
            acc[e] = acc[e] + product if k else product
    steps[n_steps].wait()
    tag_ref[...] = tag[0].astype(jnp.float32)
    for e in range(plan.groups):
        tags = tag[jnp.where(inner, e, 0)].astype(jnp.float32)
        low = fold(acc.at[e], tags, plan.left_rows, plan.slots, plan.share)
        lows[e][...] = pack(low, plan.share)


def reduce_last_kernel(plan, *refs):
    groups, width = plan.groups, plan.width
    before, tag_ref, refs = refs[:groups], refs[groups], refs[groups + 1 :]
    near, wide, last, across = refs[:4]
    lows = refs[4:]
    outer = am_outer(plan)
    inner = jnp.logical_not(outer)
    first_row = plan.cross[0] * PAIR

    def padded(parts, height):
        rows = sum(part.shape[0] for part in parts)
        if rows < height:
            parts = parts + [jnp.zeros((height - rows, width), last.dtype)]
        return jnp.concatenate(parts, axis=0)

    @pl.when(outer)
    def _():
        tags = tag_ref[first_row : first_row + PAIR, :]
        rows = last[...]
        for e in range(groups):
            total = jnp.zeros((PAIR, LANES), jnp.float32)
            for first in range(0, plan.padded, LANES):
                parts = []
                for piece, count in plan.left_spans():
                    if first <= piece * PAIR < first + LANES:
                        source = of_wide(wide, piece) if e == 0 else across[e - 1][piece]
                        parts.append(source[:count, :width])
                product = product_of(rows, padded(parts, LANES))
                mask = slot_mask(tags, first, plan.left_rows, plan.slots, plan.share)
                total += jnp.where(mask, product, 0.0)
            whole = [jnp.zeros((PAIR, LANES), jnp.float32)] * plan.half
            whole[plan.cross[0]] = total
            lows[e][...] = before[e][...] + pack(jnp.concatenate(whole, axis=0), plan.share)

    @pl.when(inner)
    def _():
        if plan.last_piece is None:
            for e in range(groups):
                lows[e][...] = before[e][...]
            return
        at = plan.last_piece * PAIR
        first = at // LANES * LANES
        count = min(PAIR, plan.left_rows - at)
        parts = [jnp.zeros((at - first, width), last.dtype)] if at > first else []
        left = padded(parts + [last[:count, :]], LANES)
        for e in range(groups):
            if e == 0:
                blocks = {d: near[i].at[PAIR:] for i, d in enumerate(plan.near)}
                blocks.update({d: wide[i].at[PAIR:] for i, d in enumerate(plan.cross)})
                tags = tag_ref[...]
            else:
                blocks = {d: across[e - 1][i] for i, d in enumerate(plan.across)}
                tags = [blocks[d][:, width:] for d in range(plan.half)]
                tags = jnp.concatenate(tags, axis=0).astype(jnp.float32)
            whole = jnp.concatenate([blocks[d][:, :width] for d in range(plan.half)], axis=0)
            product = product_of(whole, left)
            mask = slot_mask(tags, first, plan.left_rows, plan.slots, plan.share)
            low = pack(jnp.where(mask, product, 0.0), plan.share)
            lows[e][...] = before[e][...] + low


def reduce_last(plan, lows, tag, near, wide, last, across):
    flat, tree = jax.tree.flatten([near, wide, last, across])
    n_head = plan.groups + 1

    def body(*refs):
        nested = jax.tree.unflatten(tree, refs[n_head : n_head + len(flat)])
        reduce_last_kernel(plan, *refs[:n_head], *nested, *refs[n_head + len(flat) :])

    shapes = [jax.ShapeDtypeStruct(a.shape, a.dtype) for a in lows]
    return pl.pallas_call(
        body,
        out_shape=shapes,
        in_specs=[VMEM] * (n_head + len(flat)),
        out_specs=[VMEM] * len(lows),
        compiler_params=params(),
        cost_estimate=pl.CostEstimate(flops=1, bytes_accessed=1, transcendentals=0),
        name="reduce_last",
    )(*lows, tag, *flat)


def blocks_call(kernel, blocks, out_shape, out_specs, scratch, flops, moved, name, extra=()):
    flat, tree = jax.tree.flatten(blocks)
    n_extra = len(extra)

    def body(*refs):
        head, rest = refs[:n_extra], refs[n_extra:]
        nested = jax.tree.unflatten(tree, rest[: len(flat)])
        kernel(*head, *nested, *rest[len(flat) :])

    return pl.pallas_call(
        body,
        out_shape=out_shape,
        in_specs=[VMEM] * n_extra + [HBM] * len(flat),
        out_specs=out_specs,
        scratch_shapes=scratch,
        compiler_params=params(),
        cost_estimate=pl.CostEstimate(flops=1, bytes_accessed=1, transcendentals=0),
        name=name,
    )(*extra, *flat)


def reduce_own(plan, near, wide, late, tags, own):
    height = plan.half * PAIR
    columns = own.shape[0]
    n_steps = 2
    dtype = own.dtype
    return blocks_call(
        functools.partial(reduce_own_kernel, plan, n_steps),
        [near, wide, late, tags, own],
        [
            jax.ShapeDtypeStruct((height * plan.rank // LANES, LANES), jnp.float32),
            jax.ShapeDtypeStruct((height, LANES), jnp.float32),
        ],
        [VMEM] * 2,
        [
            pltpu.VMEM((height, plan.width), dtype),
            pltpu.VMEM((columns, plan.width), dtype),
            pltpu.VMEM((height, columns), jnp.float32),
            pltpu.VMEM((height, LANES), dtype),
            pltpu.SemaphoreType.DMA(((n_steps + 1) * (plan.half + 1),)),
        ],
        2 * height * plan.width * columns,
        2 * plan.width * (height + columns),
        "reduce_own",
    )


def reduce_taken(plan, near, wide, late, tags, across):
    height = plan.half * PAIR
    n_steps = 2
    dtype = near[0].dtype
    groups, padded = plan.groups, plan.padded
    *lows, tag = blocks_call(
        functools.partial(reduce_taken_kernel, plan, n_steps),
        [near, wide, late, tags, across],
        [jax.ShapeDtypeStruct((height * plan.share // LANES, LANES), jnp.float32)] * groups
        + [jax.ShapeDtypeStruct((height, LANES), jnp.float32)],
        [VMEM] * (groups + 1),
        [
            pltpu.VMEM((groups, height, plan.width), dtype),
            pltpu.VMEM((groups, padded, plan.width), dtype),
            pltpu.VMEM((groups, height, padded), jnp.float32),
            pltpu.VMEM((groups, height, LANES), dtype),
            pltpu.SemaphoreType.DMA(((n_steps + 1) * groups * (plan.half + plan.left_pieces),)),
        ],
        2 * height * plan.width * groups * padded,
        2 * plan.width * (height + padded) * groups,
        "reduce_taken",
    )
    return lows, tag


def rounded(low, share):
    return unpack(low.astype(jnp.bfloat16).astype(jnp.float32), share)


def spread(low, tags, columns, slots, share):
    blocks = [
        jnp.where(slot_mask(tags, first, columns, slots, share), low, 0.0).astype(jnp.bfloat16)
        for first in range(0, columns, LANES)
    ]
    return jnp.concatenate(blocks, axis=1)


def write_deltas(delta, outs):
    delta = delta.astype(jnp.bfloat16)
    for i, out in enumerate(outs):
        out[...] = delta[i * PAIR : (i + 1) * PAIR]


def expand_own_kernel(plan, mine_ref, other_ref, tag_ref, own, *rest):
    outs, (up, sem) = rest[:-2], rest[-2:]
    copy = pltpu.make_async_copy(own, up, sem)
    copy.start()
    low = rounded(mine_ref[...] + other_ref[...], plan.rank)
    wide_low = spread(low, tag_ref[...], up.shape[0], plan.slots, plan.rank)
    copy.wait()
    write_deltas(jnp.dot(wide_low, up[...], preferred_element_type=jnp.float32), outs)


def expand_own(plan, mine, other, tag, own):
    columns, features = own.shape
    return blocks_call(
        functools.partial(expand_own_kernel, plan),
        [own],
        [jax.ShapeDtypeStruct((PAIR, features), jnp.bfloat16)] * plan.half,
        [VMEM] * plan.half,
        [pltpu.VMEM(own.shape, own.dtype), pltpu.SemaphoreType.DMA(())],
        2 * tag.shape[0] * columns * features,
        2 * features * (columns + tag.shape[0]),
        "expand_own",
        extra=(mine, other, tag),
    )


def expand_taken_kernel(plan, *refs):
    lows, tag_ref, refs = refs[: 2 * plan.groups], refs[2 * plan.groups], refs[2 * plan.groups + 1 :]
    wide, narrow, across_wide, across_narrow = refs[:4]
    outs, (up, sems) = refs[4:-2], refs[-2:]
    copies = Copies(am_outer(plan), sems)
    for row, rows, column in plan.up_columns():
        part = pl.ds(0, rows), pl.ds(column, plan.features)
        for e in range(plan.groups):
            copies.both(
                up.at[e, pl.ds(row, rows)],
                (of_wide(wide, plan.left_pieces) if e == 0 else across_wide[e - 1]).at[part],
                (narrow if e == 0 else across_narrow[e - 1]).at[part],
            )
    if plan.padded > plan.left_rows:
        up[:, plan.left_rows :, :] = jnp.zeros(
            (plan.groups, plan.padded - plan.left_rows, plan.features), up.dtype
        )
    tags = tag_ref[...]
    wides = []
    for e in range(plan.groups):
        mine, other = lows[2 * e][...], lows[2 * e + 1][...]
        low = jnp.where(am_outer(plan), mine, other) if e else mine + other
        low = rounded(low, plan.share)
        wides.append(spread(low, tags, plan.left_rows, plan.slots, plan.share))
    copies.wait()
    delta = None
    for e in range(plan.groups):
        product = jnp.dot(wides[e], up[e], preferred_element_type=jnp.float32)
        delta = product if delta is None else delta + product
    write_deltas(delta, outs)


def expand_taken(plan, lows, tag, wide, narrow, across_wide, across_narrow):
    height, features = tag.shape[0], plan.features
    return blocks_call(
        functools.partial(expand_taken_kernel, plan),
        [wide, narrow, across_wide, across_narrow],
        [jax.ShapeDtypeStruct((PAIR, features), jnp.bfloat16)] * plan.half,
        [VMEM] * plan.half,
        [
            pltpu.VMEM((plan.groups, plan.padded, features), jnp.bfloat16),
            pltpu.SemaphoreType.DMA((plan.groups * len(list(plan.up_columns())),)),
        ],
        2 * height * plan.groups * plan.padded * features,
        2 * features * (plan.groups * plan.padded + height),
        "expand_taken",
        extra=(*lows, tag),
    )


def join_kernel(order, seg_ref, base_ref, *refs):
    deltas, out_ref = refs[:-1], refs[-1]
    for i in range(len(deltas) * CAP):
        part = i % CAP
        k = order[i // CAP] * CAP + part

        @pl.when(seg_ref[k] >= 0)
        def _():
            span = pl.ds(pl.multiple_of(seg_ref[k] * SEG, SEG), SEG)
            delta = deltas[i // CAP][part * SEG : (part + 1) * SEG, :]
            out_ref[span, :] = (base_ref[span, :] + delta.astype(jnp.float32)).astype(
                out_ref.dtype
            )


def join(plan, seg_of, base, deltas):
    height, features = base.shape
    order = [kind * plan.half + d for kind in range(2) for d in plan.cross + plan.near]
    deltas = [deltas[i] for i in order]
    return pl.pallas_call(
        functools.partial(join_kernel, order),
        out_shape=jax.ShapeDtypeStruct((height, features), jnp.bfloat16),
        in_specs=[SMEM, VMEM] + [VMEM] * len(deltas),
        out_specs=VMEM,
        compiler_params=params(),
        cost_estimate=pl.CostEstimate(
            flops=height * features, bytes_accessed=8 * height * features, transcendentals=0
        ),
        name="join",
    )(seg_of, base, *deltas)


def swap(value, axis, distance):
    count = lax.axis_size(axis)
    return lax.ppermute(value, axis, [(i, i ^ distance) for i in range(count)])


def send(plan, value, moves):
    shape = (plan.groups, plan.replicas, lax.axis_size("tensor"))

    def place(g, r, c):
        return (g * shape[1] + r) * shape[2] + c

    pairs = [
        (place(g, r, c), place(g ^ flips[0], r ^ flips[1], c ^ flips[2]))
        for senders, *flips in moves
        for g in range(shape[0])
        for r in senders
        for c in range(shape[2])
    ]
    return lax.ppermute(value, ("groups", "replica", "tensor"), pairs)


def return_terms(terms):
    back = {d: swap(terms[d], "replica", d) for d in reversed(range(1, len(terms)))}
    return [back[d] for d in range(1, len(terms))]


def on_device(x, weight, lefts, ups, ids, residency):
    slots, width, rank = lefts.shape
    features = ups.shape[2]
    plan = Plan(
        lax.axis_size("replica"), lax.axis_size("groups"), slots, rank, width, features
    )
    half, n_cross = plan.half, len(plan.cross)
    core = lax.axis_index("tensor")
    outer = am_outer(plan)
    left_rows = jnp.swapaxes(lefts, 1, 2)
    near, wide, seg_of = lay_out(plan, True, ids, residency, x, left_rows, ups)
    wide, tags = wide[: plan.wide], wide[plan.wide :]

    near = [swap(block, "replica", d) for block, d in zip(near, plan.near[1:])]
    wide_in = []
    for i in range(plan.wide):
        moves = []
        if i < n_cross:
            moves.append((plan.outer, 0, plan.cross[i], 0))
        if i < plan.adapter_wide:
            moves.append((plan.inner, 0, half, 0))
        wide_in.append(send(plan, wide[i], moves))

    late_ids, _ = lax.optimization_barrier((ids, seg_of))
    near, late_x = lax.optimization_barrier((near, x))
    own_rows, late, _ = lay_out(plan, False, late_ids, residency, x, left_rows, ups)
    near = own_rows + near
    def part(which, rows):
        columns = lax.dynamic_slice(weight, (0, which * features), (weight.shape[0], features))
        return jnp.dot(rows, columns, preferred_element_type=jnp.float32)

    base_other, base_mine = part(1 - core, late_x), part(core, late_x)

    def across_send(i):
        d = plan.across[i]
        if d in plan.near:
            block = near[plan.near.index(d)][PAIR:]
            value, tag = block[:, :width], block[:, width:]
        else:
            j = plan.cross.index(d)
            value, tag = wide_in[j][PAIR:], tags_in[j][PAIR:]
        if i < plan.pieces:
            piece = wide_in[i // 2][(i % 2) * PAIR : (i % 2 + 1) * PAIR]
            value = jnp.where(outer, piece, value)
        value = jnp.concatenate([value, tag], axis=1)
        return [
            send(plan, value, [(plan.outer, e, 0, 0), (plan.inner, e, 0, 0)])
            for e in range(1, plan.groups)
        ]

    across = [across_send(0), across_send(1)]
    tags_in = [swap(tag, "replica", d) for tag, d in zip(tags, plan.cross)]

    wide_in, near, across[0], late, tags_in, base_other, base_mine = lax.optimization_barrier(
        (wide_in, near, across[0], late, tags_in, base_other, base_mine)
    )
    late_in = []
    for unit, d in enumerate(plan.late_blocks()):
        moves = [(plan.inner, 0, d, 0)]
        if unit < plan.pieces:
            moves.append((plan.outer, 0, half, 0))
        block = late[unit]
        if unit == 2:
            late_in[0], across[1], tags_in, block = lax.optimization_barrier(
                (late_in[0], across[1], tags_in, block)
            )
        elif unit > 2:
            late_in[unit - 2], block = lax.optimization_barrier((late_in[unit - 2], block))
        late_in.append(send(plan, block, moves))
    across += [across_send(i) for i in range(2, half)]
    late_up = late_in[0][: plan.up_rows]
    across_up = [send(plan, late_up, [(plan.inner, e, 0, 0)]) for e in range(1, plan.groups)]
    base = base_mine + swap(base_other, "tensor", 1)
    late_in[:n_cross], across[:-1] = lax.optimization_barrier((late_in[:n_cross], across[:-1]))
    across = [[blocks[e] for blocks in across] for e in range(plan.groups - 1)]

    own_left = left_rows.reshape(slots * rank, width)
    low, tag = reduce_own(plan, near, wide_in, late_in[:n_cross], tags_in, own_left)
    other = swap(low, "tensor", 1)
    terms = expand_own(plan, low, other, tag, ups.reshape(slots * rank, features))
    deltas = [terms[0]] + return_terms(terms)

    lows, tag = reduce_taken(plan, near, wide_in, late_in[:-1], tags_in, across)
    late_in[-1], deltas[:2], lows, base = lax.optimization_barrier(
        (late_in[-1], deltas[:2], lows, base)
    )
    lows = reduce_last(plan, lows, tag, near, wide_in, late_in[-1], across)
    pairs = []
    for e in range(plan.groups):
        other = swap(lows[e], "tensor", 1)
        if e:
            total = lows[e] + other
            pairs += [total, swap(total, "groups", e)]
        else:
            pairs += [lows[e], other]
    pairs, deltas = lax.optimization_barrier((pairs, deltas))
    across_wide = [blocks[plan.left_pieces] for blocks in across]
    terms = expand_taken(plan, pairs, tag, wide_in, late_in[0], across_wide, across_up)
    deltas += [terms[0]] + return_terms(terms)
    return join(plan, seg_of, base, deltas)


def solution(mesh):
    placed = (
        P(("groups", "replica"), "tensor"),
        P("tensor", None),
        P("replica", "tensor", None),
        P("replica", None, "tensor"),
        P(("groups", "replica")),
        P(),
    )
    return jax.shard_map(
        on_device,
        mesh=mesh,
        in_specs=placed,
        out_specs=P(("groups", "replica"), "tensor"),
        check_vma=False,
    )
```

```python
import functools

import jax
import jax.numpy as jnp
from jax import lax
from jax.experimental import pallas as pl
from jax.experimental.pallas import tpu as pltpu
from jax.sharding import PartitionSpec as P

CAP = 2
SEG = 32
LANES = 128
PAIR = CAP * SEG
VMEM_LIMIT = 24 * 1024 * 1024
HBM = pl.BlockSpec(memory_space=pltpu.HBM)
SMEM = pl.BlockSpec(memory_space=pltpu.SMEM)
VMEM = pl.BlockSpec(memory_space=pltpu.VMEM)


class Plan:
    def __init__(self, replicas, groups, slots, rank, width, features):
        self.replicas, self.groups, self.slots, self.rank = replicas, groups, slots, rank
        self.width, self.features = width, features
        self.half = replicas // 2
        self.turn = self.half // 2
        self.near = [d for d in range(self.half) if not d & self.turn]
        self.cross = [d for d in range(self.half) if d & self.turn]
        self.across = self.near[1:] + self.near[:1] + self.cross
        self.share = rank // groups
        self.left_rows = slots * self.share
        self.padded = -(-self.left_rows // LANES) * LANES
        beside = width // features
        self.up_rows = -(-self.left_rows // (beside * 16)) * 16
        self.left_pieces = -(-self.left_rows // PAIR)
        self.pieces = self.left_pieces + 1
        assert self.up_rows <= PAIR
        self.adapter_wide = -(-self.pieces // 2)
        self.units = 2 * len(self.cross)
        self.last_piece = self.units - 2 if self.units - 2 < self.left_pieces else None
        assert self.pieces <= self.units and self.adapter_wide <= len(self.cross)
        self.wide = len(self.cross)
        self.outer = [r for r in range(replicas) if self.is_outer(r)]
        self.inner = [r for r in range(replicas) if not self.is_outer(r)]

    def is_outer(self, r):
        return (r < self.turn) or (r >= self.replicas - self.turn)

    def up_columns(self):
        for j, row in enumerate(range(0, self.left_rows, self.up_rows)):
            yield row, min(self.up_rows, self.left_rows - row), j * self.features

    def left_spans(self):
        for piece in range(self.left_pieces):
            yield piece, min(PAIR, self.left_rows - piece * PAIR)

    def late_blocks(self):
        return self.cross + self.cross[::-1]

    def late_rows(self, refs, i, kind):
        return refs[i if kind == 0 else self.units - 1 - i]


def params(limit=VMEM_LIMIT):
    return pltpu.CompilerParams(vmem_limit_bytes=limit)


def am_outer(plan):
    me = lax.axis_index("replica")
    return (me < plan.turn) | (me >= plan.replicas - plan.turn)


def of_wide(refs, piece):
    return refs[piece // 2].at[pl.ds((piece % 2) * PAIR, PAIR)]


def late_adapters(late, piece, plan):
    return late[0 if piece == plan.left_pieces else 1 + piece]


def lay_kernel(plan, first_call, ids_ref, residency_ref, x_ref, left_ref, up_ref, *rest):
    n_near = len(plan.near) - 1 if first_call else 1
    n_blocks = plan.wide if first_call else len(plan.late_blocks())
    n_tags = len(plan.cross) if first_call else 0
    near, rest = rest[:n_near], rest[n_near:]
    blocks, rest = rest[:n_blocks], rest[n_blocks:]
    tag_outs, rest = rest[:n_tags], rest[n_tags:]
    seg_out, seg_ref, slot_ref, count_ref, staged, tags, left, up, in_sems, sems = rest
    half, slots, width, share = plan.half, plan.slots, plan.width, plan.share
    me = lax.axis_index("replica")
    first = pl.multiple_of(lax.axis_index("groups") * share, share)
    outer = am_outer(plan)
    rows_outer = outer if first_call else jnp.logical_not(outer)

    def copy_in(i, source, stage):
        return pltpu.make_async_copy(source, stage, in_sems.at[i])

    adapters_in = []
    for slot in range(slots):
        source = pl.ds(first, share)
        stage = pl.ds(slot * share, share)
        n = len(adapters_in)
        adapters_in.append(copy_in(n, left_ref.at[slot, source], left.at[stage]))
        adapters_in.append(copy_in(n + 1, up_ref.at[slot, source], up.at[stage]))

    @pl.when(jnp.logical_not(rows_outer))
    def _():
        for copy in adapters_in:
            copy.start()

    scale = 2**16 // slots + 1
    assert all(a * scale >> 16 == a // slots for a in range(residency_ref.shape[0]))
    for h in range(plan.replicas):
        count_ref[h] = 0
        for p in range(CAP):
            seg_ref[h * CAP + p] = -1
            slot_ref[h * CAP + p] = 0
    for s in range(ids_ref.shape[0]):
        adapter = ids_ref[s]
        holder = (adapter * scale) >> 16
        count = count_ref[holder]
        place = holder * CAP + count
        count_ref[holder] = count + 1
        seg_ref[place] = s
        slot_ref[place] = residency_ref[adapter] - holder * slots
    for d in range(half):
        for kind in range(2):
            for p in range(CAP):
                seg_out[(kind * half + d) * CAP + p] = seg_ref[
                    (me ^ (d + kind * half)) * CAP + p
                ]

    def segment(d, kind, p):
        seg = jnp.maximum(seg_out[(kind * half + d) * CAP + p], 0)
        return pl.ds(pl.multiple_of(seg * SEG, SEG), SEG)

    def write_tags(targets):
        written = [(d, kind) for d, kind, _ in targets]
        if first_call:
            written += [(d, kind) for d in plan.cross for kind in range(2)]
        for d, kind in written:
            for p in range(CAP):
                slot = slot_ref[(me ^ (d + kind * half)) * CAP + p].astype(jnp.float32)
                tags[d, pl.ds((kind * CAP + p) * SEG, SEG), :] = jnp.full(
                    (SEG, LANES), slot, jnp.float32
                ).astype(tags.dtype)

    near_d = plan.near[1:] if first_call else plan.near[:1]
    near_targets = [
        (d, kind, near[i].at[pl.ds(kind * PAIR, PAIR)])
        for i, d in enumerate(near_d)
        for kind in range(2)
    ]
    cross_targets = [
        (
            d,
            kind,
            of_wide(blocks, 2 * i + kind) if first_call else plan.late_rows(blocks, i, kind),
        )
        for i, d in enumerate(plan.cross)
        for kind in range(2)
    ]
    departures = []

    def depart(source, target):
        copy = pltpu.make_async_copy(source, target, sems.at[len(departures)])
        copy.start()
        departures.append(copy)

    def depart_tags():
        for d, kind, target in near_targets:
            depart(tags.at[d, pl.ds(kind * PAIR, PAIR)], target.at[:, pl.ds(width, LANES)])
        for d, tag_out in zip(plan.cross, tag_outs):
            depart(tags.at[d], tag_out)

    def finish():
        for copy in departures:
            copy.wait()
        departures.clear()

    def start_rows(targets):
        rows_in = []
        for d, kind, target in targets:
            for p in range(CAP):
                stage = staged.at[pl.ds(len(rows_in) * SEG, SEG)]
                copy = copy_in(
                    len(adapters_in) + len(rows_in), x_ref.at[segment(d, kind, p)], stage
                )
                copy.start()
                place = target.at[pl.ds(p * SEG, SEG), pl.ds(0, width)]
                rows_in.append((copy, stage, place))
        return rows_in

    def depart_rows(rows_in):
        for copy, stage, place in rows_in:
            copy.wait()
            depart(stage, place)
        finish()

    @pl.when(rows_outer)
    def _():
        rows_in = start_rows(cross_targets + near_targets)
        write_tags(near_targets)
        depart_tags()
        depart_rows(rows_in)

    @pl.when(jnp.logical_not(rows_outer))
    def _():
        rows_in = start_rows(near_targets)
        write_tags(near_targets)
        depart_tags()
        for slot in range(slots):
            adapters_in[2 * slot].wait()
            piece, at = divmod(slot * share, PAIR)
            unit = (
                of_wide(blocks, piece) if first_call else late_adapters(blocks, piece, plan)
            )
            depart(
                left.at[pl.ds(slot * share, share)],
                unit.at[pl.ds(at, share), pl.ds(0, width)],
            )
        for slot in range(slots):
            adapters_in[2 * slot + 1].wait()
        piece = plan.left_pieces
        unit = of_wide(blocks, piece) if first_call else late_adapters(blocks, piece, plan)
        for row, rows, column in plan.up_columns():
            depart(up.at[pl.ds(row, rows)], unit.at[pl.ds(0, rows), pl.ds(column, plan.features)])
        depart_rows(rows_in)


def lay_out(plan, first_call, ids, residency, x, left_rows, ups):
    count = 2 * plan.half * CAP
    tagged = jax.ShapeDtypeStruct((2 * PAIR, plan.width + LANES), x.dtype)
    near = [tagged] * (len(plan.near) - 1 if first_call else 1)
    heights = [2] * plan.wide if first_call else [1] * plan.units
    blocks = [jax.ShapeDtypeStruct((n * PAIR, plan.width), x.dtype) for n in heights]
    if first_call:
        blocks += [jax.ShapeDtypeStruct((2 * PAIR, LANES), x.dtype)] * len(plan.cross)
    out = pl.pallas_call(
        functools.partial(lay_kernel, plan, first_call),
        out_shape=near + blocks + [jax.ShapeDtypeStruct((count,), jnp.int32)],
        in_specs=[SMEM, SMEM, HBM, HBM, HBM],
        out_specs=[HBM] * (len(near) + len(blocks)) + [SMEM],
        scratch_shapes=[
            pltpu.SMEM((plan.replicas * CAP,), jnp.int32),
            pltpu.SMEM((plan.replicas * CAP,), jnp.int32),
            pltpu.SMEM((plan.replicas,), jnp.int32),
            pltpu.VMEM((count * SEG, plan.width), x.dtype),
            pltpu.VMEM((plan.half, 2 * PAIR, LANES), x.dtype),
            pltpu.VMEM((plan.left_rows, plan.width), x.dtype),
            pltpu.VMEM((plan.left_rows, plan.features), x.dtype),
            pltpu.SemaphoreType.DMA((count + 2 * plan.slots,)),
            pltpu.SemaphoreType.DMA((2 * count + 2 * plan.pieces,)),
        ],
        compiler_params=params(60 * 1024 * 1024),
        cost_estimate=pl.CostEstimate(flops=0, bytes_accessed=x.size, transcendentals=0),
        name="lay_out_first" if first_call else "lay_out_second",
    )(ids, residency, x, left_rows, ups)
    return list(out[: len(near)]), list(out[len(near) : -1]), out[-1]


def slot_mask(tags, first, columns, slots, share):
    lane = lax.broadcasted_iota(jnp.int32, (1, LANES), 1)
    column_slot = jnp.zeros((1, LANES), jnp.float32)
    for j in range(0, LANES, share):
        slot = (first + j) // share if first + j < columns else -1
        column_slot = jnp.where(lane >= j, float(slot), column_slot)
    return tags == column_slot


class Copies:
    def __init__(self, outer, sems):
        self.outer, self.sems, self.waits = outer, sems, []

    def both(self, target, outer_source, inner_source=None):
        sem = self.sems.at[len(self.waits)]
        copy = pltpu.make_async_copy(outer_source, target, sem)
        if inner_source is None:
            copy.start()
        else:
            pl.when(self.outer)(copy.start)
            pl.when(jnp.logical_not(self.outer))(
                pltpu.make_async_copy(inner_source, target, sem).start
            )
        self.waits.append((None, copy))

    def one(self, wanted, target, source):
        copy = pltpu.make_async_copy(source, target, self.sems.at[len(self.waits)])
        pl.when(wanted)(copy.start)
        self.waits.append((wanted, copy))

    def wait(self):
        for wanted, copy in self.waits:
            if wanted is None:
                copy.wait()
            else:
                pl.when(wanted)(copy.wait)


def lane_group(share):
    return lax.broadcasted_iota(jnp.int32, (1, LANES), 1) // share


def spread_lanes(value, share):
    total = value
    for shift in range(share, LANES, share):
        total += pltpu.roll(value, shift, 1)
    return total


def pack(low, share):
    count = LANES // share
    height = low.shape[0] // count
    everywhere = spread_lanes(low, share)
    packed = jnp.zeros((height, LANES), jnp.float32)
    for i in range(count):
        rows = everywhere[i * height : (i + 1) * height]
        packed = jnp.where(lane_group(share) == i, rows, packed)
    return packed


def unpack(packed, share):
    rows = [
        spread_lanes(jnp.where(lane_group(share) == i, packed, 0.0), share)
        for i in range(LANES // share)
    ]
    return jnp.concatenate(rows, axis=0)


def fold(product, tags, columns, slots, share):
    total = jnp.zeros(tags.shape, jnp.float32)
    for first in range(0, product.shape[1], LANES):
        mask = slot_mask(tags, first, columns, slots, share)
        total += jnp.where(mask, product[:, first : first + LANES], 0.0)
    return total


def copy_rows(copies, plan, kind, target, columns, near, wide, late):
    span = pl.ds(kind * PAIR, PAIR)
    for i, d in enumerate(plan.near):
        copies.both(target.at[pl.ds(d * PAIR, PAIR)], near[i].at[span, columns])
    for i, d in enumerate(plan.cross):
        place = target.at[pl.ds(d * PAIR, PAIR)]
        if i == 0 and kind == 1:
            copies.one(jnp.logical_not(copies.outer), place, wide[i].at[span, columns])
        else:
            copies.both(
                place, plan.late_rows(late, i, kind).at[:, columns], wide[i].at[span, columns]
            )


def copy_tags(copies, plan, kind, target, near, tags):
    span = pl.ds(kind * PAIR, PAIR)
    for i, d in enumerate(plan.near):
        copies.both(target.at[pl.ds(d * PAIR, PAIR)], near[i].at[span, pl.ds(plan.width, LANES)])
    for i, d in enumerate(plan.cross):
        copies.both(target.at[pl.ds(d * PAIR, PAIR)], tags[i].at[span])


def product_of(rows, left):
    return lax.dot_general(
        rows, left, (((1,), (1,)), ((), ())), preferred_element_type=jnp.float32
    )


def reduce_own_kernel(plan, n_steps, near, wide, late, tags, own, low_ref, tag_ref, *scratch):
    rows, left, acc, tag, sems = scratch
    block = plan.width // n_steps
    outer = am_outer(plan)
    each = plan.half + 1
    steps = []
    for k in range(n_steps + 1):
        copies = Copies(outer, sems.at[pl.ds(k * each, each)])
        if k < n_steps:
            columns = pl.ds(k * block, block)
            copy_rows(copies, plan, 0, rows.at[:, columns], columns, near, wide, late)
            copies.both(left.at[:, columns], own.at[:, columns])
        else:
            copy_tags(copies, plan, 0, tag, near, tags)
        steps.append(copies)
    for k in range(n_steps):
        steps[k].wait()
        columns = pl.ds(k * block, block)
        product = product_of(rows[:, columns], left[:, columns])
        acc[...] = acc[...] + product if k else product
    steps[n_steps].wait()
    tags = tag[...].astype(jnp.float32)
    tag_ref[...] = tags
    low_ref[...] = pack(fold(acc, tags, acc.shape[1], plan.slots, plan.rank), plan.rank)


def reduce_taken_kernel(plan, n_steps, near, wide, late, tags, across, *rest):
    lows, tag_ref = rest[: plan.groups], rest[plan.groups]
    rows, left, acc, tag, sems = rest[plan.groups + 1 :]
    block = plan.width // n_steps
    outer = am_outer(plan)
    inner = jnp.logical_not(outer)
    more = plan.groups - 1
    each = plan.half + plan.left_pieces + more * (plan.half + plan.left_pieces)
    missing = pl.ds(plan.cross[0] * PAIR, PAIR)

    @pl.when(outer)
    def _():
        rows[0, missing, :] = jnp.zeros((PAIR, plan.width), rows.dtype)

    if plan.last_piece is not None:

        @pl.when(inner)
        def _():
            left[0, pl.ds(plan.last_piece * PAIR, PAIR), :] = jnp.zeros(
                (PAIR, plan.width), left.dtype
            )

    steps = []
    for k in range(n_steps + 1):
        copies = Copies(outer, sems.at[pl.ds(k * each, each)])
        columns = pl.ds(k * block, block) if k < n_steps else pl.ds(plan.width, LANES)
        if k < n_steps:
            copy_rows(copies, plan, 1, rows.at[0, :, columns], columns, near, wide, late)
        else:
            copy_tags(copies, plan, 1, tag.at[0], near, tags)
        for e in range(1, plan.groups):
            for i, d in enumerate(plan.across):
                target = rows.at[e, :, columns] if k < n_steps else tag.at[e]
                copies.one(
                    inner,
                    target.at[pl.ds(d * PAIR, PAIR)],
                    across[e - 1][i].at[:, columns],
                )
        if k < n_steps:
            for piece, count in plan.left_spans():
                span = pl.ds(0, count), columns
                place = left.at[0, pl.ds(piece * PAIR, count), columns]
                if piece == plan.last_piece:
                    copies.one(outer, place, of_wide(wide, piece).at[span])
                else:
                    copies.both(
                        place,
                        of_wide(wide, piece).at[span],
                        late_adapters(late, piece, plan).at[span],
                    )
                for e in range(1, plan.groups):
                    copies.one(
                        outer,
                        left.at[e, pl.ds(piece * PAIR, count), columns],
                        across[e - 1][piece].at[span],
                    )
        steps.append(copies)
    for k in range(n_steps):
        steps[k].wait()
        columns = pl.ds(k * block, block)
        for e in range(plan.groups):
            rows_at = jnp.where(inner, e, 0)
            left_at = jnp.where(outer, e, 0)
            product = product_of(rows[rows_at, :, columns], left[left_at, :, columns])
            acc[e] = acc[e] + product if k else product
    steps[n_steps].wait()
    tag_ref[...] = tag[0].astype(jnp.float32)
    for e in range(plan.groups):
        tags = tag[jnp.where(inner, e, 0)].astype(jnp.float32)
        low = fold(acc.at[e], tags, plan.left_rows, plan.slots, plan.share)
        lows[e][...] = pack(low, plan.share)


def reduce_last_kernel(plan, *refs):
    groups, width = plan.groups, plan.width
    before, tag_ref, refs = refs[:groups], refs[groups], refs[groups + 1 :]
    near, wide, last, across = refs[:4]
    lows = refs[4:]
    outer = am_outer(plan)
    inner = jnp.logical_not(outer)
    first_row = plan.cross[0] * PAIR

    def padded(parts, height):
        rows = sum(part.shape[0] for part in parts)
        if rows < height:
            parts = parts + [jnp.zeros((height - rows, width), last.dtype)]
        return jnp.concatenate(parts, axis=0)

    @pl.when(outer)
    def _():
        tags = tag_ref[first_row : first_row + PAIR, :]
        rows = last[...]
        for e in range(groups):
            total = jnp.zeros((PAIR, LANES), jnp.float32)
            for first in range(0, plan.padded, LANES):
                parts = []
                for piece, count in plan.left_spans():
                    if first <= piece * PAIR < first + LANES:
                        source = of_wide(wide, piece) if e == 0 else across[e - 1][piece]
                        parts.append(source[:count, :width])
                product = product_of(rows, padded(parts, LANES))
                mask = slot_mask(tags, first, plan.left_rows, plan.slots, plan.share)
                total += jnp.where(mask, product, 0.0)
            whole = [jnp.zeros((PAIR, LANES), jnp.float32)] * plan.half
            whole[plan.cross[0]] = total
            lows[e][...] = before[e][...] + pack(jnp.concatenate(whole, axis=0), plan.share)

    @pl.when(inner)
    def _():
        if plan.last_piece is None:
            for e in range(groups):
                lows[e][...] = before[e][...]
            return
        at = plan.last_piece * PAIR
        first = at // LANES * LANES
        count = min(PAIR, plan.left_rows - at)
        parts = [jnp.zeros((at - first, width), last.dtype)] if at > first else []
        left = padded(parts + [last[:count, :]], LANES)
        for e in range(groups):
            if e == 0:
                blocks = {d: near[i].at[PAIR:] for i, d in enumerate(plan.near)}
                blocks.update({d: wide[i].at[PAIR:] for i, d in enumerate(plan.cross)})
                tags = tag_ref[...]
            else:
                blocks = {d: across[e - 1][i] for i, d in enumerate(plan.across)}
                tags = [blocks[d][:, width:] for d in range(plan.half)]
                tags = jnp.concatenate(tags, axis=0).astype(jnp.float32)
            whole = jnp.concatenate([blocks[d][:, :width] for d in range(plan.half)], axis=0)
            product = product_of(whole, left)
            mask = slot_mask(tags, first, plan.left_rows, plan.slots, plan.share)
            low = pack(jnp.where(mask, product, 0.0), plan.share)
            lows[e][...] = before[e][...] + low


def reduce_last(plan, lows, tag, near, wide, last, across):
    flat, tree = jax.tree.flatten([near, wide, last, across])
    n_head = plan.groups + 1

    def body(*refs):
        nested = jax.tree.unflatten(tree, refs[n_head : n_head + len(flat)])
        reduce_last_kernel(plan, *refs[:n_head], *nested, *refs[n_head + len(flat) :])

    shapes = [jax.ShapeDtypeStruct(a.shape, a.dtype) for a in lows]
    return pl.pallas_call(
        body,
        out_shape=shapes,
        in_specs=[VMEM] * (n_head + len(flat)),
        out_specs=[VMEM] * len(lows),
        compiler_params=params(),
        cost_estimate=pl.CostEstimate(flops=1, bytes_accessed=1, transcendentals=0),
        name="reduce_last",
    )(*lows, tag, *flat)


def blocks_call(kernel, blocks, out_shape, out_specs, scratch, flops, moved, name, extra=()):
    flat, tree = jax.tree.flatten(blocks)
    n_extra = len(extra)

    def body(*refs):
        head, rest = refs[:n_extra], refs[n_extra:]
        nested = jax.tree.unflatten(tree, rest[: len(flat)])
        kernel(*head, *nested, *rest[len(flat) :])

    return pl.pallas_call(
        body,
        out_shape=out_shape,
        in_specs=[VMEM] * n_extra + [HBM] * len(flat),
        out_specs=out_specs,
        scratch_shapes=scratch,
        compiler_params=params(),
        cost_estimate=pl.CostEstimate(flops=1, bytes_accessed=1, transcendentals=0),
        name=name,
    )(*extra, *flat)


def reduce_own(plan, near, wide, late, tags, own):
    height = plan.half * PAIR
    columns = own.shape[0]
    n_steps = 2
    dtype = own.dtype
    return blocks_call(
        functools.partial(reduce_own_kernel, plan, n_steps),
        [near, wide, late, tags, own],
        [
            jax.ShapeDtypeStruct((height * plan.rank // LANES, LANES), jnp.float32),
            jax.ShapeDtypeStruct((height, LANES), jnp.float32),
        ],
        [VMEM] * 2,
        [
            pltpu.VMEM((height, plan.width), dtype),
            pltpu.VMEM((columns, plan.width), dtype),
            pltpu.VMEM((height, columns), jnp.float32),
            pltpu.VMEM((height, LANES), dtype),
            pltpu.SemaphoreType.DMA(((n_steps + 1) * (plan.half + 1),)),
        ],
        2 * height * plan.width * columns,
        2 * plan.width * (height + columns),
        "reduce_own",
    )


def reduce_taken(plan, near, wide, late, tags, across):
    height = plan.half * PAIR
    n_steps = 2
    dtype = near[0].dtype
    groups, padded = plan.groups, plan.padded
    *lows, tag = blocks_call(
        functools.partial(reduce_taken_kernel, plan, n_steps),
        [near, wide, late, tags, across],
        [jax.ShapeDtypeStruct((height * plan.share // LANES, LANES), jnp.float32)] * groups
        + [jax.ShapeDtypeStruct((height, LANES), jnp.float32)],
        [VMEM] * (groups + 1),
        [
            pltpu.VMEM((groups, height, plan.width), dtype),
            pltpu.VMEM((groups, padded, plan.width), dtype),
            pltpu.VMEM((groups, height, padded), jnp.float32),
            pltpu.VMEM((groups, height, LANES), dtype),
            pltpu.SemaphoreType.DMA(((n_steps + 1) * groups * (plan.half + plan.left_pieces),)),
        ],
        2 * height * plan.width * groups * padded,
        2 * plan.width * (height + padded) * groups,
        "reduce_taken",
    )
    return lows, tag


def rounded(low, share):
    return unpack(low.astype(jnp.bfloat16).astype(jnp.float32), share)


def spread(low, tags, columns, slots, share):
    blocks = [
        jnp.where(slot_mask(tags, first, columns, slots, share), low, 0.0).astype(jnp.bfloat16)
        for first in range(0, columns, LANES)
    ]
    return jnp.concatenate(blocks, axis=1)


def write_deltas(delta, outs):
    delta = delta.astype(jnp.bfloat16)
    for i, out in enumerate(outs):
        out[...] = delta[i * PAIR : (i + 1) * PAIR]


def expand_own_kernel(plan, mine_ref, other_ref, tag_ref, own, *rest):
    outs, (up, sem) = rest[:-2], rest[-2:]
    copy = pltpu.make_async_copy(own, up, sem)
    copy.start()
    low = rounded(mine_ref[...] + other_ref[...], plan.rank)
    wide_low = spread(low, tag_ref[...], up.shape[0], plan.slots, plan.rank)
    copy.wait()
    write_deltas(jnp.dot(wide_low, up[...], preferred_element_type=jnp.float32), outs)


def expand_own(plan, mine, other, tag, own):
    columns, features = own.shape
    return blocks_call(
        functools.partial(expand_own_kernel, plan),
        [own],
        [jax.ShapeDtypeStruct((PAIR, features), jnp.bfloat16)] * plan.half,
        [VMEM] * plan.half,
        [pltpu.VMEM(own.shape, own.dtype), pltpu.SemaphoreType.DMA(())],
        2 * tag.shape[0] * columns * features,
        2 * features * (columns + tag.shape[0]),
        "expand_own",
        extra=(mine, other, tag),
    )


def expand_taken_kernel(plan, *refs):
    lows, tag_ref, refs = refs[: 2 * plan.groups], refs[2 * plan.groups], refs[2 * plan.groups + 1 :]
    wide, narrow, across_wide, across_narrow = refs[:4]
    outs, (up, sems) = refs[4:-2], refs[-2:]
    copies = Copies(am_outer(plan), sems)
    for row, rows, column in plan.up_columns():
        part = pl.ds(0, rows), pl.ds(column, plan.features)
        for e in range(plan.groups):
            copies.both(
                up.at[e, pl.ds(row, rows)],
                (of_wide(wide, plan.left_pieces) if e == 0 else across_wide[e - 1]).at[part],
                (narrow if e == 0 else across_narrow[e - 1]).at[part],
            )
    if plan.padded > plan.left_rows:
        up[:, plan.left_rows :, :] = jnp.zeros(
            (plan.groups, plan.padded - plan.left_rows, plan.features), up.dtype
        )
    tags = tag_ref[...]
    wides = []
    for e in range(plan.groups):
        mine, other = lows[2 * e][...], lows[2 * e + 1][...]
        low = jnp.where(am_outer(plan), mine, other) if e else mine + other
        low = rounded(low, plan.share)
        wides.append(spread(low, tags, plan.left_rows, plan.slots, plan.share))
    copies.wait()
    delta = None
    for e in range(plan.groups):
        product = jnp.dot(wides[e], up[e], preferred_element_type=jnp.float32)
        delta = product if delta is None else delta + product
    write_deltas(delta, outs)


def expand_taken(plan, lows, tag, wide, narrow, across_wide, across_narrow):
    height, features = tag.shape[0], plan.features
    return blocks_call(
        functools.partial(expand_taken_kernel, plan),
        [wide, narrow, across_wide, across_narrow],
        [jax.ShapeDtypeStruct((PAIR, features), jnp.bfloat16)] * plan.half,
        [VMEM] * plan.half,
        [
            pltpu.VMEM((plan.groups, plan.padded, features), jnp.bfloat16),
            pltpu.SemaphoreType.DMA((plan.groups * len(list(plan.up_columns())),)),
        ],
        2 * height * plan.groups * plan.padded * features,
        2 * features * (plan.groups * plan.padded + height),
        "expand_taken",
        extra=(*lows, tag),
    )


def join_kernel(order, seg_ref, base_ref, *refs):
    deltas, out_ref = refs[:-1], refs[-1]
    for i in range(len(deltas) * CAP):
        part = i % CAP
        k = order[i // CAP] * CAP + part

        @pl.when(seg_ref[k] >= 0)
        def _():
            span = pl.ds(pl.multiple_of(seg_ref[k] * SEG, SEG), SEG)
            delta = deltas[i // CAP][part * SEG : (part + 1) * SEG, :]
            out_ref[span, :] = (base_ref[span, :] + delta.astype(jnp.float32)).astype(
                out_ref.dtype
            )


def join(plan, seg_of, base, deltas):
    height, features = base.shape
    order = [kind * plan.half + d for kind in range(2) for d in plan.cross + plan.near]
    deltas = [deltas[i] for i in order]
    return pl.pallas_call(
        functools.partial(join_kernel, order),
        out_shape=jax.ShapeDtypeStruct((height, features), jnp.bfloat16),
        in_specs=[SMEM, VMEM] + [VMEM] * len(deltas),
        out_specs=VMEM,
        compiler_params=params(),
        cost_estimate=pl.CostEstimate(
            flops=height * features, bytes_accessed=8 * height * features, transcendentals=0
        ),
        name="join",
    )(seg_of, base, *deltas)


def swap(value, axis, distance):
    count = lax.axis_size(axis)
    return lax.ppermute(value, axis, [(i, i ^ distance) for i in range(count)])


def send(plan, value, moves):
    shape = (plan.groups, plan.replicas, lax.axis_size("tensor"))

    def place(g, r, c):
        return (g * shape[1] + r) * shape[2] + c

    pairs = [
        (place(g, r, c), place(g ^ flips[0], r ^ flips[1], c ^ flips[2]))
        for senders, *flips in moves
        for g in range(shape[0])
        for r in senders
        for c in range(shape[2])
    ]
    return lax.ppermute(value, ("groups", "replica", "tensor"), pairs)


def return_terms(terms):
    back = {d: swap(terms[d], "replica", d) for d in reversed(range(1, len(terms)))}
    return [back[d] for d in range(1, len(terms))]


def on_device(x, weight, lefts, ups, ids, residency):
    slots, width, rank = lefts.shape
    features = ups.shape[2]
    plan = Plan(
        lax.axis_size("replica"), lax.axis_size("groups"), slots, rank, width, features
    )
    half, n_cross = plan.half, len(plan.cross)
    core = lax.axis_index("tensor")
    outer = am_outer(plan)
    left_rows = jnp.swapaxes(lefts, 1, 2)
    near, wide, seg_of = lay_out(plan, True, ids, residency, x, left_rows, ups)
    wide, tags = wide[: plan.wide], wide[plan.wide :]

    near = [swap(block, "replica", d) for block, d in zip(near, plan.near[1:])]
    wide_in = []
    for i in range(plan.wide):
        moves = []
        if i < n_cross:
            moves.append((plan.outer, 0, plan.cross[i], 0))
        if i < plan.adapter_wide:
            moves.append((plan.inner, 0, half, 0))
        wide_in.append(send(plan, wide[i], moves))

    late_ids, _ = lax.optimization_barrier((ids, seg_of))
    near, late_x = lax.optimization_barrier((near, x))
    own_rows, late, _ = lay_out(plan, False, late_ids, residency, x, left_rows, ups)
    near = own_rows + near
    def part(which, rows):
        columns = lax.dynamic_slice(weight, (0, which * features), (weight.shape[0], features))
        return jnp.dot(rows, columns, preferred_element_type=jnp.float32)

    base_other, base_mine = part(1 - core, late_x), part(core, late_x)

    def across_send(i):
        d = plan.across[i]
        if d in plan.near:
            block = near[plan.near.index(d)][PAIR:]
            value, tag = block[:, :width], block[:, width:]
        else:
            j = plan.cross.index(d)
            value, tag = wide_in[j][PAIR:], tags_in[j][PAIR:]
        if i < plan.pieces:
            piece = wide_in[i // 2][(i % 2) * PAIR : (i % 2 + 1) * PAIR]
            value = jnp.where(outer, piece, value)
        value = jnp.concatenate([value, tag], axis=1)
        return [
            send(plan, value, [(plan.outer, e, 0, 0), (plan.inner, e, 0, 0)])
            for e in range(1, plan.groups)
        ]

    across = [across_send(0), across_send(1)]
    tags_in = [swap(tag, "replica", d) for tag, d in zip(tags, plan.cross)]

    wide_in[0], near, across[0], late, base_other, base_mine = lax.optimization_barrier(
        (wide_in[0], near, across[0], late, base_other, base_mine)
    )
    late_in = []
    for unit, d in enumerate(plan.late_blocks()):
        moves = [(plan.inner, 0, d, 0)]
        if unit < plan.pieces:
            moves.append((plan.outer, 0, half, 0))
        block = late[unit]
        if unit == 1:
            near, wide_in, tags_in, block = lax.optimization_barrier(
                (near, wide_in, tags_in, block)
            )
        elif unit == 2:
            late_in[0], wide_in, tags_in, block, base_other = lax.optimization_barrier(
                (late_in[0], wide_in, tags_in, block, base_other)
            )
        elif unit > 2:
            late_in[unit - 2], block = lax.optimization_barrier((late_in[unit - 2], block))
        late_in.append(send(plan, block, moves))
    across += [across_send(i) for i in range(2, half)]
    late_up = late_in[0][: plan.up_rows]
    across_up = [send(plan, late_up, [(plan.inner, e, 0, 0)]) for e in range(1, plan.groups)]
    base = base_mine + swap(base_other, "tensor", 1)
    late_in[:n_cross], across[:-1] = lax.optimization_barrier((late_in[:n_cross], across[:-1]))
    across = [[blocks[e] for blocks in across] for e in range(plan.groups - 1)]

    own_left = left_rows.reshape(slots * rank, width)
    low, tag = reduce_own(plan, near, wide_in, late_in[:n_cross], tags_in, own_left)
    other = swap(low, "tensor", 1)
    terms = expand_own(plan, low, other, tag, ups.reshape(slots * rank, features))
    deltas = [terms[0]] + return_terms(terms)

    lows, tag = reduce_taken(plan, near, wide_in, late_in[:-1], tags_in, across)
    late_in[-1], deltas[:2], lows, base = lax.optimization_barrier(
        (late_in[-1], deltas[:2], lows, base)
    )
    lows = reduce_last(plan, lows, tag, near, wide_in, late_in[-1], across)
    pairs = []
    for e in range(plan.groups):
        other = swap(lows[e], "tensor", 1)
        if e:
            total = lows[e] + other
            pairs += [total, swap(total, "groups", e)]
        else:
            pairs += [lows[e], other]
    pairs, deltas = lax.optimization_barrier((pairs, deltas))
    across_wide = [blocks[plan.left_pieces] for blocks in across]
    terms = expand_taken(plan, pairs, tag, wide_in, late_in[0], across_wide, across_up)
    deltas += [terms[0]] + return_terms(terms)
    return join(plan, seg_of, base, deltas)


def solution(mesh):
    placed = (
        P(("groups", "replica"), "tensor"),
        P("tensor", None),
        P("replica", "tensor", None),
        P("replica", None, "tensor"),
        P(("groups", "replica")),
        P(),
    )
    return jax.shard_map(
        on_device,
        mesh=mesh,
        in_specs=placed,
        out_specs=P(("groups", "replica"), "tensor"),
        check_vma=False,
    )
```

```python
import functools

import jax
import jax.numpy as jnp
from jax import lax
from jax.experimental import pallas as pl
from jax.experimental.pallas import tpu as pltpu
from jax.sharding import PartitionSpec as P

CAP = 2
SEG = 32
LANES = 128
PAIR = CAP * SEG
VMEM_LIMIT = 24 * 1024 * 1024
HBM = pl.BlockSpec(memory_space=pltpu.HBM)
SMEM = pl.BlockSpec(memory_space=pltpu.SMEM)
VMEM = pl.BlockSpec(memory_space=pltpu.VMEM)


class Plan:
    def __init__(self, replicas, groups, slots, rank, width, features):
        self.replicas, self.groups, self.slots, self.rank = replicas, groups, slots, rank
        self.width, self.features = width, features
        self.half = replicas // 2
        self.turn = self.half // 2
        self.near = [d for d in range(self.half) if not d & self.turn]
        self.cross = [d for d in range(self.half) if d & self.turn]
        self.across = self.near[1:] + self.near[:1] + self.cross
        self.share = rank // groups
        self.left_rows = slots * self.share
        self.padded = -(-self.left_rows // LANES) * LANES
        beside = width // features
        self.up_rows = -(-self.left_rows // (beside * 16)) * 16
        self.left_pieces = -(-self.left_rows // PAIR)
        self.pieces = self.left_pieces + 1
        assert self.up_rows <= PAIR
        self.adapter_wide = -(-self.pieces // 2)
        self.units = 2 * len(self.cross)
        self.last_piece = self.units - 2 if self.units - 2 < self.left_pieces else None
        assert self.pieces <= self.units and self.adapter_wide <= len(self.cross)
        self.wide = len(self.cross)
        self.outer = [r for r in range(replicas) if self.is_outer(r)]
        self.inner = [r for r in range(replicas) if not self.is_outer(r)]

    def is_outer(self, r):
        return (r < self.turn) or (r >= self.replicas - self.turn)

    def up_columns(self):
        for j, row in enumerate(range(0, self.left_rows, self.up_rows)):
            yield row, min(self.up_rows, self.left_rows - row), j * self.features

    def left_spans(self):
        for piece in range(self.left_pieces):
            yield piece, min(PAIR, self.left_rows - piece * PAIR)

    def late_blocks(self):
        return self.cross + self.cross[::-1]

    def late_rows(self, refs, i, kind):
        return refs[i if kind == 0 else self.units - 1 - i]


def params(limit=VMEM_LIMIT):
    return pltpu.CompilerParams(vmem_limit_bytes=limit)


def am_outer(plan):
    me = lax.axis_index("replica")
    return (me < plan.turn) | (me >= plan.replicas - plan.turn)


def of_wide(refs, piece):
    return refs[piece // 2].at[pl.ds((piece % 2) * PAIR, PAIR)]


def late_adapters(late, piece, plan):
    return late[0 if piece == plan.left_pieces else 1 + piece]


def lay_kernel(plan, first_call, ids_ref, residency_ref, x_ref, left_ref, up_ref, *rest):
    n_near = len(plan.near) - 1 if first_call else 1
    n_blocks = plan.wide if first_call else len(plan.late_blocks())
    n_tags = len(plan.cross) if first_call else 0
    near, rest = rest[:n_near], rest[n_near:]
    blocks, rest = rest[:n_blocks], rest[n_blocks:]
    tag_outs, rest = rest[:n_tags], rest[n_tags:]
    seg_out, seg_ref, slot_ref, count_ref, staged, tags, left, up, in_sems, sems = rest
    half, slots, width, share = plan.half, plan.slots, plan.width, plan.share
    me = lax.axis_index("replica")
    first = pl.multiple_of(lax.axis_index("groups") * share, share)
    outer = am_outer(plan)
    rows_outer = outer if first_call else jnp.logical_not(outer)

    def copy_in(i, source, stage):
        return pltpu.make_async_copy(source, stage, in_sems.at[i])

    adapters_in = []
    for slot in range(slots):
        source = pl.ds(first, share)
        stage = pl.ds(slot * share, share)
        n = len(adapters_in)
        adapters_in.append(copy_in(n, left_ref.at[slot, source], left.at[stage]))
        adapters_in.append(copy_in(n + 1, up_ref.at[slot, source], up.at[stage]))

    @pl.when(jnp.logical_not(rows_outer))
    def _():
        for copy in adapters_in:
            copy.start()

    scale = 2**16 // slots + 1
    assert all(a * scale >> 16 == a // slots for a in range(residency_ref.shape[0]))
    for h in range(plan.replicas):
        count_ref[h] = 0
        for p in range(CAP):
            seg_ref[h * CAP + p] = -1
            slot_ref[h * CAP + p] = 0
    for s in range(ids_ref.shape[0]):
        adapter = ids_ref[s]
        holder = (adapter * scale) >> 16
        count = count_ref[holder]
        place = holder * CAP + count
        count_ref[holder] = count + 1
        seg_ref[place] = s
        slot_ref[place] = residency_ref[adapter] - holder * slots
    for d in range(half):
        for kind in range(2):
            for p in range(CAP):
                seg_out[(kind * half + d) * CAP + p] = seg_ref[
                    (me ^ (d + kind * half)) * CAP + p
                ]

    def segment(d, kind, p):
        seg = jnp.maximum(seg_out[(kind * half + d) * CAP + p], 0)
        return pl.ds(pl.multiple_of(seg * SEG, SEG), SEG)

    def write_tags(targets):
        written = [(d, kind) for d, kind, _ in targets]
        if first_call:
            written += [(d, kind) for d in plan.cross for kind in range(2)]
        for d, kind in written:
            for p in range(CAP):
                slot = slot_ref[(me ^ (d + kind * half)) * CAP + p].astype(jnp.float32)
                tags[d, pl.ds((kind * CAP + p) * SEG, SEG), :] = jnp.full(
                    (SEG, LANES), slot, jnp.float32
                ).astype(tags.dtype)

    near_d = plan.near[1:] if first_call else plan.near[:1]
    near_targets = [
        (d, kind, near[i].at[pl.ds(kind * PAIR, PAIR)])
        for i, d in enumerate(near_d)
        for kind in range(2)
    ]
    cross_targets = [
        (
            d,
            kind,
            of_wide(blocks, 2 * i + kind) if first_call else plan.late_rows(blocks, i, kind),
        )
        for i, d in enumerate(plan.cross)
        for kind in range(2)
    ]
    departures = []

    def depart(source, target):
        copy = pltpu.make_async_copy(source, target, sems.at[len(departures)])
        copy.start()
        departures.append(copy)

    def depart_tags():
        for d, kind, target in near_targets:
            depart(tags.at[d, pl.ds(kind * PAIR, PAIR)], target.at[:, pl.ds(width, LANES)])
        for d, tag_out in zip(plan.cross, tag_outs):
            depart(tags.at[d], tag_out)

    def finish():
        for copy in departures:
            copy.wait()
        departures.clear()

    def start_rows(targets):
        rows_in = []
        for d, kind, target in targets:
            for p in range(CAP):
                stage = staged.at[pl.ds(len(rows_in) * SEG, SEG)]
                copy = copy_in(
                    len(adapters_in) + len(rows_in), x_ref.at[segment(d, kind, p)], stage
                )
                copy.start()
                place = target.at[pl.ds(p * SEG, SEG), pl.ds(0, width)]
                rows_in.append((copy, stage, place))
        return rows_in

    def depart_rows(rows_in):
        for copy, stage, place in rows_in:
            copy.wait()
            depart(stage, place)
        finish()

    @pl.when(rows_outer)
    def _():
        rows_in = start_rows(cross_targets + near_targets)
        write_tags(near_targets)
        depart_tags()
        depart_rows(rows_in)

    @pl.when(jnp.logical_not(rows_outer))
    def _():
        rows_in = start_rows(near_targets)
        write_tags(near_targets)
        depart_tags()
        for slot in range(slots):
            adapters_in[2 * slot].wait()
            piece, at = divmod(slot * share, PAIR)
            unit = (
                of_wide(blocks, piece) if first_call else late_adapters(blocks, piece, plan)
            )
            depart(
                left.at[pl.ds(slot * share, share)],
                unit.at[pl.ds(at, share), pl.ds(0, width)],
            )
        for slot in range(slots):
            adapters_in[2 * slot + 1].wait()
        piece = plan.left_pieces
        unit = of_wide(blocks, piece) if first_call else late_adapters(blocks, piece, plan)
        for row, rows, column in plan.up_columns():
            depart(up.at[pl.ds(row, rows)], unit.at[pl.ds(0, rows), pl.ds(column, plan.features)])
        depart_rows(rows_in)


def lay_out(plan, first_call, ids, residency, x, left_rows, ups):
    count = 2 * plan.half * CAP
    tagged = jax.ShapeDtypeStruct((2 * PAIR, plan.width + LANES), x.dtype)
    near = [tagged] * (len(plan.near) - 1 if first_call else 1)
    heights = [2] * plan.wide if first_call else [1] * plan.units
    blocks = [jax.ShapeDtypeStruct((n * PAIR, plan.width), x.dtype) for n in heights]
    if first_call:
        blocks += [jax.ShapeDtypeStruct((2 * PAIR, LANES), x.dtype)] * len(plan.cross)
    out = pl.pallas_call(
        functools.partial(lay_kernel, plan, first_call),
        out_shape=near + blocks + [jax.ShapeDtypeStruct((count,), jnp.int32)],
        in_specs=[SMEM, SMEM, HBM, HBM, HBM],
        out_specs=[HBM] * (len(near) + len(blocks)) + [SMEM],
        scratch_shapes=[
            pltpu.SMEM((plan.replicas * CAP,), jnp.int32),
            pltpu.SMEM((plan.replicas * CAP,), jnp.int32),
            pltpu.SMEM((plan.replicas,), jnp.int32),
            pltpu.VMEM((count * SEG, plan.width), x.dtype),
            pltpu.VMEM((plan.half, 2 * PAIR, LANES), x.dtype),
            pltpu.VMEM((plan.left_rows, plan.width), x.dtype),
            pltpu.VMEM((plan.left_rows, plan.features), x.dtype),
            pltpu.SemaphoreType.DMA((count + 2 * plan.slots,)),
            pltpu.SemaphoreType.DMA((2 * count + 2 * plan.pieces,)),
        ],
        compiler_params=params(60 * 1024 * 1024),
        cost_estimate=pl.CostEstimate(flops=0, bytes_accessed=x.size, transcendentals=0),
        name="lay_out_first" if first_call else "lay_out_second",
    )(ids, residency, x, left_rows, ups)
    return list(out[: len(near)]), list(out[len(near) : -1]), out[-1]


def slot_mask(tags, first, columns, slots, share):
    lane = lax.broadcasted_iota(jnp.int32, (1, LANES), 1)
    column_slot = jnp.zeros((1, LANES), jnp.float32)
    for j in range(0, LANES, share):
        slot = (first + j) // share if first + j < columns else -1
        column_slot = jnp.where(lane >= j, float(slot), column_slot)
    return tags == column_slot


class Copies:
    def __init__(self, outer, sems):
        self.outer, self.sems, self.waits = outer, sems, []

    def both(self, target, outer_source, inner_source=None):
        sem = self.sems.at[len(self.waits)]
        copy = pltpu.make_async_copy(outer_source, target, sem)
        if inner_source is None:
            copy.start()
        else:
            pl.when(self.outer)(copy.start)
            pl.when(jnp.logical_not(self.outer))(
                pltpu.make_async_copy(inner_source, target, sem).start
            )
        self.waits.append((None, copy))

    def one(self, wanted, target, source):
        copy = pltpu.make_async_copy(source, target, self.sems.at[len(self.waits)])
        pl.when(wanted)(copy.start)
        self.waits.append((wanted, copy))

    def wait(self):
        for wanted, copy in self.waits:
            if wanted is None:
                copy.wait()
            else:
                pl.when(wanted)(copy.wait)


def lane_group(share):
    return lax.broadcasted_iota(jnp.int32, (1, LANES), 1) // share


def spread_lanes(value, share):
    total = value
    for shift in range(share, LANES, share):
        total += pltpu.roll(value, shift, 1)
    return total


def pack(low, share):
    count = LANES // share
    height = low.shape[0] // count
    everywhere = spread_lanes(low, share)
    packed = jnp.zeros((height, LANES), jnp.float32)
    for i in range(count):
        rows = everywhere[i * height : (i + 1) * height]
        packed = jnp.where(lane_group(share) == i, rows, packed)
    return packed


def unpack(packed, share):
    rows = [
        spread_lanes(jnp.where(lane_group(share) == i, packed, 0.0), share)
        for i in range(LANES // share)
    ]
    return jnp.concatenate(rows, axis=0)


def fold(product, tags, columns, slots, share):
    total = jnp.zeros(tags.shape, jnp.float32)
    for first in range(0, product.shape[1], LANES):
        mask = slot_mask(tags, first, columns, slots, share)
        total += jnp.where(mask, product[:, first : first + LANES], 0.0)
    return total


def copy_rows(copies, plan, kind, target, columns, near, wide, late):
    span = pl.ds(kind * PAIR, PAIR)
    for i, d in enumerate(plan.near):
        copies.both(target.at[pl.ds(d * PAIR, PAIR)], near[i].at[span, columns])
    for i, d in enumerate(plan.cross):
        place = target.at[pl.ds(d * PAIR, PAIR)]
        if i == 0 and kind == 1:
            copies.one(jnp.logical_not(copies.outer), place, wide[i].at[span, columns])
        else:
            copies.both(
                place, plan.late_rows(late, i, kind).at[:, columns], wide[i].at[span, columns]
            )


def copy_tags(copies, plan, kind, target, near, tags):
    span = pl.ds(kind * PAIR, PAIR)
    for i, d in enumerate(plan.near):
        copies.both(target.at[pl.ds(d * PAIR, PAIR)], near[i].at[span, pl.ds(plan.width, LANES)])
    for i, d in enumerate(plan.cross):
        copies.both(target.at[pl.ds(d * PAIR, PAIR)], tags[i].at[span])


def product_of(rows, left):
    return lax.dot_general(
        rows, left, (((1,), (1,)), ((), ())), preferred_element_type=jnp.float32
    )


def reduce_own_kernel(plan, n_steps, near, wide, late, tags, own, low_ref, tag_ref, *scratch):
    rows, left, acc, tag, sems = scratch
    block = plan.width // n_steps
    outer = am_outer(plan)
    each = plan.half + 1
    steps = []
    for k in range(n_steps + 1):
        copies = Copies(outer, sems.at[pl.ds(k * each, each)])
        if k < n_steps:
            columns = pl.ds(k * block, block)
            copy_rows(copies, plan, 0, rows.at[:, columns], columns, near, wide, late)
            copies.both(left.at[:, columns], own.at[:, columns])
        else:
            copy_tags(copies, plan, 0, tag, near, tags)
        steps.append(copies)
    for k in range(n_steps):
        steps[k].wait()
        columns = pl.ds(k * block, block)
        product = product_of(rows[:, columns], left[:, columns])
        acc[...] = acc[...] + product if k else product
    steps[n_steps].wait()
    tags = tag[...].astype(jnp.float32)
    tag_ref[...] = tags
    low_ref[...] = pack(fold(acc, tags, acc.shape[1], plan.slots, plan.rank), plan.rank)


def reduce_taken_kernel(plan, n_steps, near, wide, late, tags, across, *rest):
    lows, tag_ref = rest[: plan.groups], rest[plan.groups]
    rows, left, acc, tag, sems = rest[plan.groups + 1 :]
    block = plan.width // n_steps
    outer = am_outer(plan)
    inner = jnp.logical_not(outer)
    more = plan.groups - 1
    each = plan.half + plan.left_pieces + more * (plan.half + plan.left_pieces)
    missing = pl.ds(plan.cross[0] * PAIR, PAIR)

    @pl.when(outer)
    def _():
        rows[0, missing, :] = jnp.zeros((PAIR, plan.width), rows.dtype)

    if plan.last_piece is not None:

        @pl.when(inner)
        def _():
            left[0, pl.ds(plan.last_piece * PAIR, PAIR), :] = jnp.zeros(
                (PAIR, plan.width), left.dtype
            )

    steps = []
    for k in range(n_steps + 1):
        copies = Copies(outer, sems.at[pl.ds(k * each, each)])
        columns = pl.ds(k * block, block) if k < n_steps else pl.ds(plan.width, LANES)
        if k < n_steps:
            copy_rows(copies, plan, 1, rows.at[0, :, columns], columns, near, wide, late)
        else:
            copy_tags(copies, plan, 1, tag.at[0], near, tags)
        for e in range(1, plan.groups):
            for i, d in enumerate(plan.across):
                target = rows.at[e, :, columns] if k < n_steps else tag.at[e]
                copies.one(
                    inner,
                    target.at[pl.ds(d * PAIR, PAIR)],
                    across[e - 1][i].at[:, columns],
                )
        if k < n_steps:
            for piece, count in plan.left_spans():
                span = pl.ds(0, count), columns
                place = left.at[0, pl.ds(piece * PAIR, count), columns]
                if piece == plan.last_piece:
                    copies.one(outer, place, of_wide(wide, piece).at[span])
                else:
                    copies.both(
                        place,
                        of_wide(wide, piece).at[span],
                        late_adapters(late, piece, plan).at[span],
                    )
                for e in range(1, plan.groups):
                    copies.one(
                        outer,
                        left.at[e, pl.ds(piece * PAIR, count), columns],
                        across[e - 1][piece].at[span],
                    )
        steps.append(copies)
    for k in range(n_steps):
        steps[k].wait()
        columns = pl.ds(k * block, block)
        for e in range(plan.groups):
            rows_at = jnp.where(inner, e, 0)
            left_at = jnp.where(outer, e, 0)
            product = product_of(rows[rows_at, :, columns], left[left_at, :, columns])
            acc[e] = acc[e] + product if k else product
    steps[n_steps].wait()
    tag_ref[...] = tag[0].astype(jnp.float32)
    for e in range(plan.groups):
        tags = tag[jnp.where(inner, e, 0)].astype(jnp.float32)
        low = fold(acc.at[e], tags, plan.left_rows, plan.slots, plan.share)
        lows[e][...] = pack(low, plan.share)


def reduce_last_kernel(plan, *refs):
    groups, width = plan.groups, plan.width
    before, tag_ref, refs = refs[:groups], refs[groups], refs[groups + 1 :]
    near, wide, last, across = refs[:4]
    lows = refs[4:]
    outer = am_outer(plan)
    inner = jnp.logical_not(outer)
    first_row = plan.cross[0] * PAIR

    def padded(parts, height):
        rows = sum(part.shape[0] for part in parts)
        if rows < height:
            parts = parts + [jnp.zeros((height - rows, width), last.dtype)]
        return jnp.concatenate(parts, axis=0)

    @pl.when(outer)
    def _():
        tags = tag_ref[first_row : first_row + PAIR, :]
        rows = last[...]
        for e in range(groups):
            total = jnp.zeros((PAIR, LANES), jnp.float32)
            for first in range(0, plan.padded, LANES):
                parts = []
                for piece, count in plan.left_spans():
                    if first <= piece * PAIR < first + LANES:
                        source = of_wide(wide, piece) if e == 0 else across[e - 1][piece]
                        parts.append(source[:count, :width])
                product = product_of(rows, padded(parts, LANES))
                mask = slot_mask(tags, first, plan.left_rows, plan.slots, plan.share)
                total += jnp.where(mask, product, 0.0)
            whole = [jnp.zeros((PAIR, LANES), jnp.float32)] * plan.half
            whole[plan.cross[0]] = total
            lows[e][...] = before[e][...] + pack(jnp.concatenate(whole, axis=0), plan.share)

    @pl.when(inner)
    def _():
        if plan.last_piece is None:
            for e in range(groups):
                lows[e][...] = before[e][...]
            return
        at = plan.last_piece * PAIR
        first = at // LANES * LANES
        count = min(PAIR, plan.left_rows - at)
        parts = [jnp.zeros((at - first, width), last.dtype)] if at > first else []
        left = padded(parts + [last[:count, :]], LANES)
        for e in range(groups):
            if e == 0:
                blocks = {d: near[i].at[PAIR:] for i, d in enumerate(plan.near)}
                blocks.update({d: wide[i].at[PAIR:] for i, d in enumerate(plan.cross)})
                tags = tag_ref[...]
            else:
                blocks = {d: across[e - 1][i] for i, d in enumerate(plan.across)}
                tags = [blocks[d][:, width:] for d in range(plan.half)]
                tags = jnp.concatenate(tags, axis=0).astype(jnp.float32)
            whole = jnp.concatenate([blocks[d][:, :width] for d in range(plan.half)], axis=0)
            product = product_of(whole, left)
            mask = slot_mask(tags, first, plan.left_rows, plan.slots, plan.share)
            low = pack(jnp.where(mask, product, 0.0), plan.share)
            lows[e][...] = before[e][...] + low


def reduce_last(plan, lows, tag, near, wide, last, across):
    flat, tree = jax.tree.flatten([near, wide, last, across])
    n_head = plan.groups + 1

    def body(*refs):
        nested = jax.tree.unflatten(tree, refs[n_head : n_head + len(flat)])
        reduce_last_kernel(plan, *refs[:n_head], *nested, *refs[n_head + len(flat) :])

    shapes = [jax.ShapeDtypeStruct(a.shape, a.dtype) for a in lows]
    return pl.pallas_call(
        body,
        out_shape=shapes,
        in_specs=[VMEM] * (n_head + len(flat)),
        out_specs=[VMEM] * len(lows),
        compiler_params=params(),
        cost_estimate=pl.CostEstimate(flops=1, bytes_accessed=1, transcendentals=0),
        name="reduce_last",
    )(*lows, tag, *flat)


def blocks_call(kernel, blocks, out_shape, out_specs, scratch, flops, moved, name, extra=()):
    flat, tree = jax.tree.flatten(blocks)
    n_extra = len(extra)

    def body(*refs):
        head, rest = refs[:n_extra], refs[n_extra:]
        nested = jax.tree.unflatten(tree, rest[: len(flat)])
        kernel(*head, *nested, *rest[len(flat) :])

    return pl.pallas_call(
        body,
        out_shape=out_shape,
        in_specs=[VMEM] * n_extra + [HBM] * len(flat),
        out_specs=out_specs,
        scratch_shapes=scratch,
        compiler_params=params(),
        cost_estimate=pl.CostEstimate(flops=1, bytes_accessed=1, transcendentals=0),
        name=name,
    )(*extra, *flat)


def reduce_own(plan, near, wide, late, tags, own):
    height = plan.half * PAIR
    columns = own.shape[0]
    n_steps = 2
    dtype = own.dtype
    return blocks_call(
        functools.partial(reduce_own_kernel, plan, n_steps),
        [near, wide, late, tags, own],
        [
            jax.ShapeDtypeStruct((height * plan.rank // LANES, LANES), jnp.float32),
            jax.ShapeDtypeStruct((height, LANES), jnp.float32),
        ],
        [VMEM] * 2,
        [
            pltpu.VMEM((height, plan.width), dtype),
            pltpu.VMEM((columns, plan.width), dtype),
            pltpu.VMEM((height, columns), jnp.float32),
            pltpu.VMEM((height, LANES), dtype),
            pltpu.SemaphoreType.DMA(((n_steps + 1) * (plan.half + 1),)),
        ],
        2 * height * plan.width * columns,
        2 * plan.width * (height + columns),
        "reduce_own",
    )


def reduce_taken(plan, near, wide, late, tags, across):
    height = plan.half * PAIR
    n_steps = 2
    dtype = near[0].dtype
    groups, padded = plan.groups, plan.padded
    *lows, tag = blocks_call(
        functools.partial(reduce_taken_kernel, plan, n_steps),
        [near, wide, late, tags, across],
        [jax.ShapeDtypeStruct((height * plan.share // LANES, LANES), jnp.float32)] * groups
        + [jax.ShapeDtypeStruct((height, LANES), jnp.float32)],
        [VMEM] * (groups + 1),
        [
            pltpu.VMEM((groups, height, plan.width), dtype),
            pltpu.VMEM((groups, padded, plan.width), dtype),
            pltpu.VMEM((groups, height, padded), jnp.float32),
            pltpu.VMEM((groups, height, LANES), dtype),
            pltpu.SemaphoreType.DMA(((n_steps + 1) * groups * (plan.half + plan.left_pieces),)),
        ],
        2 * height * plan.width * groups * padded,
        2 * plan.width * (height + padded) * groups,
        "reduce_taken",
    )
    return lows, tag


def rounded(low, share):
    return unpack(low.astype(jnp.bfloat16).astype(jnp.float32), share)


def spread(low, tags, columns, slots, share):
    blocks = [
        jnp.where(slot_mask(tags, first, columns, slots, share), low, 0.0).astype(jnp.bfloat16)
        for first in range(0, columns, LANES)
    ]
    return jnp.concatenate(blocks, axis=1)


def write_deltas(delta, outs):
    delta = delta.astype(jnp.bfloat16)
    for i, out in enumerate(outs):
        out[...] = delta[i * PAIR : (i + 1) * PAIR]


def expand_own_kernel(plan, mine_ref, other_ref, tag_ref, own, *rest):
    outs, (up, sem) = rest[:-2], rest[-2:]
    copy = pltpu.make_async_copy(own, up, sem)
    copy.start()
    low = rounded(mine_ref[...] + other_ref[...], plan.rank)
    wide_low = spread(low, tag_ref[...], up.shape[0], plan.slots, plan.rank)
    copy.wait()
    write_deltas(jnp.dot(wide_low, up[...], preferred_element_type=jnp.float32), outs)


def expand_own(plan, mine, other, tag, own):
    columns, features = own.shape
    return blocks_call(
        functools.partial(expand_own_kernel, plan),
        [own],
        [jax.ShapeDtypeStruct((PAIR, features), jnp.bfloat16)] * plan.half,
        [VMEM] * plan.half,
        [pltpu.VMEM(own.shape, own.dtype), pltpu.SemaphoreType.DMA(())],
        2 * tag.shape[0] * columns * features,
        2 * features * (columns + tag.shape[0]),
        "expand_own",
        extra=(mine, other, tag),
    )


def expand_taken_kernel(plan, *refs):
    lows, tag_ref, refs = refs[: 2 * plan.groups], refs[2 * plan.groups], refs[2 * plan.groups + 1 :]
    wide, narrow, across_wide, across_narrow = refs[:4]
    outs, (up, sems) = refs[4:-2], refs[-2:]
    copies = Copies(am_outer(plan), sems)
    for row, rows, column in plan.up_columns():
        part = pl.ds(0, rows), pl.ds(column, plan.features)
        for e in range(plan.groups):
            copies.both(
                up.at[e, pl.ds(row, rows)],
                (of_wide(wide, plan.left_pieces) if e == 0 else across_wide[e - 1]).at[part],
                (narrow if e == 0 else across_narrow[e - 1]).at[part],
            )
    if plan.padded > plan.left_rows:
        up[:, plan.left_rows :, :] = jnp.zeros(
            (plan.groups, plan.padded - plan.left_rows, plan.features), up.dtype
        )
    tags = tag_ref[...]
    wides = []
    for e in range(plan.groups):
        mine, other = lows[2 * e][...], lows[2 * e + 1][...]
        low = jnp.where(am_outer(plan), mine, other) if e else mine + other
        low = rounded(low, plan.share)
        wides.append(spread(low, tags, plan.left_rows, plan.slots, plan.share))
    copies.wait()
    delta = None
    for e in range(plan.groups):
        product = jnp.dot(wides[e], up[e], preferred_element_type=jnp.float32)
        delta = product if delta is None else delta + product
    write_deltas(delta, outs)


def expand_taken(plan, lows, tag, wide, narrow, across_wide, across_narrow):
    height, features = tag.shape[0], plan.features
    return blocks_call(
        functools.partial(expand_taken_kernel, plan),
        [wide, narrow, across_wide, across_narrow],
        [jax.ShapeDtypeStruct((PAIR, features), jnp.bfloat16)] * plan.half,
        [VMEM] * plan.half,
        [
            pltpu.VMEM((plan.groups, plan.padded, features), jnp.bfloat16),
            pltpu.SemaphoreType.DMA((plan.groups * len(list(plan.up_columns())),)),
        ],
        2 * height * plan.groups * plan.padded * features,
        2 * features * (plan.groups * plan.padded + height),
        "expand_taken",
        extra=(*lows, tag),
    )


def join_kernel(order, seg_ref, base_ref, *refs):
    n = len(order)
    deltas, (out_ref, rows, sems) = refs[:n], refs[-3:]

    def parts():
        for i in range(n * CAP):
            seg = seg_ref[order[i // CAP] * CAP + i % CAP]
            span = pl.ds(pl.multiple_of(jnp.maximum(seg, 0) * SEG, SEG), SEG)
            place = pl.ds(i * SEG, SEG)
            yield i, seg, span, pltpu.make_async_copy(
                rows.at[place], out_ref.at[span], sems.at[i]
            )

    for i, seg, span, copy in parts():

        @pl.when(seg >= 0)
        def _():
            part = i % CAP
            delta = deltas[i // CAP][part * SEG : (part + 1) * SEG, :]
            total = base_ref[span, :] + delta.astype(jnp.float32)
            rows[i * SEG : (i + 1) * SEG, :] = total.astype(rows.dtype)
            copy.start()

    for _, seg, _, copy in parts():
        pl.when(seg >= 0)(copy.wait)


def join(plan, seg_of, base, deltas, kind, before=None):
    height, features = base.shape
    order = [kind * plan.half + d for d in plan.cross + plan.near]
    deltas = [deltas[i] for i in order]
    n = len(deltas)
    more = [] if before is None else [before]
    return pl.pallas_call(
        functools.partial(join_kernel, order),
        out_shape=jax.ShapeDtypeStruct((height, features), jnp.bfloat16),
        in_specs=[SMEM, VMEM] + [VMEM] * n + [HBM] * len(more),
        out_specs=HBM,
        scratch_shapes=[
            pltpu.VMEM((n * PAIR, features), jnp.bfloat16),
            pltpu.SemaphoreType.DMA((n * CAP,)),
        ],
        input_output_aliases={2 + n: 0} if more else {},
        compiler_params=params(),
        cost_estimate=pl.CostEstimate(
            flops=height * features, bytes_accessed=4 * height * features, transcendentals=0
        ),
        name="join_taken" if more else "join_own",
    )(seg_of, base, *deltas, *more)


def swap(value, axis, distance):
    count = lax.axis_size(axis)
    return lax.ppermute(value, axis, [(i, i ^ distance) for i in range(count)])


def send(plan, value, moves):
    shape = (plan.groups, plan.replicas, lax.axis_size("tensor"))

    def place(g, r, c):
        return (g * shape[1] + r) * shape[2] + c

    pairs = [
        (place(g, r, c), place(g ^ flips[0], r ^ flips[1], c ^ flips[2]))
        for senders, *flips in moves
        for g in range(shape[0])
        for r in senders
        for c in range(shape[2])
    ]
    return lax.ppermute(value, ("groups", "replica", "tensor"), pairs)


def return_terms(terms):
    back = {d: swap(terms[d], "replica", d) for d in reversed(range(1, len(terms)))}
    return [back[d] for d in range(1, len(terms))]


def on_device(x, weight, lefts, ups, ids, residency):
    slots, width, rank = lefts.shape
    features = ups.shape[2]
    plan = Plan(
        lax.axis_size("replica"), lax.axis_size("groups"), slots, rank, width, features
    )
    half, n_cross = plan.half, len(plan.cross)
    core = lax.axis_index("tensor")
    outer = am_outer(plan)
    left_rows = jnp.swapaxes(lefts, 1, 2)
    near, wide, seg_of = lay_out(plan, True, ids, residency, x, left_rows, ups)
    wide, tags = wide[: plan.wide], wide[plan.wide :]

    near = [swap(block, "replica", d) for block, d in zip(near, plan.near[1:])]
    wide_in = []
    for i in range(plan.wide):
        moves = []
        if i < n_cross:
            moves.append((plan.outer, 0, plan.cross[i], 0))
        if i < plan.adapter_wide:
            moves.append((plan.inner, 0, half, 0))
        wide_in.append(send(plan, wide[i], moves))

    late_ids, _ = lax.optimization_barrier((ids, seg_of))
    near, late_x = lax.optimization_barrier((near, x))
    own_rows, late, _ = lay_out(plan, False, late_ids, residency, x, left_rows, ups)
    near = own_rows + near
    def part(which, rows):
        columns = lax.dynamic_slice(weight, (0, which * features), (weight.shape[0], features))
        return jnp.dot(rows, columns, preferred_element_type=jnp.float32)

    base_other, base_mine = part(1 - core, late_x), part(core, late_x)

    def across_send(i):
        d = plan.across[i]
        if d in plan.near:
            block = near[plan.near.index(d)][PAIR:]
            value, tag = block[:, :width], block[:, width:]
        else:
            j = plan.cross.index(d)
            value, tag = wide_in[j][PAIR:], tags_in[j][PAIR:]
        if i < plan.pieces:
            piece = wide_in[i // 2][(i % 2) * PAIR : (i % 2 + 1) * PAIR]
            value = jnp.where(outer, piece, value)
        value = jnp.concatenate([value, tag], axis=1)
        return [
            send(plan, value, [(plan.outer, e, 0, 0), (plan.inner, e, 0, 0)])
            for e in range(1, plan.groups)
        ]

    across = [across_send(0), across_send(1)]
    tags_in = [swap(tag, "replica", d) for tag, d in zip(tags, plan.cross)]

    wide_in[0], near, across[0], late, base_other, base_mine = lax.optimization_barrier(
        (wide_in[0], near, across[0], late, base_other, base_mine)
    )
    late_in = []
    for unit, d in enumerate(plan.late_blocks()):
        moves = [(plan.inner, 0, d, 0)]
        if unit < plan.pieces:
            moves.append((plan.outer, 0, half, 0))
        block = late[unit]
        if unit == 1:
            near, wide_in, tags_in, block = lax.optimization_barrier(
                (near, wide_in, tags_in, block)
            )
        elif unit == 2:
            late_in[0], wide_in, tags_in, block, base_other = lax.optimization_barrier(
                (late_in[0], wide_in, tags_in, block, base_other)
            )
        elif unit > 2:
            late_in[unit - 2], block = lax.optimization_barrier((late_in[unit - 2], block))
        late_in.append(send(plan, block, moves))
    across += [across_send(i) for i in range(2, half)]
    late_up = late_in[0][: plan.up_rows]
    across_up = [send(plan, late_up, [(plan.inner, e, 0, 0)]) for e in range(1, plan.groups)]
    base = base_mine + swap(base_other, "tensor", 1)
    late_in[:n_cross], across[:-1] = lax.optimization_barrier((late_in[:n_cross], across[:-1]))
    across = [[blocks[e] for blocks in across] for e in range(plan.groups - 1)]

    own_left = left_rows.reshape(slots * rank, width)
    low, tag = reduce_own(plan, near, wide_in, late_in[:n_cross], tags_in, own_left)
    other = swap(low, "tensor", 1)
    terms = expand_own(plan, low, other, tag, ups.reshape(slots * rank, features))
    deltas = [terms[0]] + return_terms(terms)

    lows, tag = reduce_taken(plan, near, wide_in, late_in[:-1], tags_in, across)
    late_in[-1], deltas[:2], lows, base = lax.optimization_barrier(
        (late_in[-1], deltas[:2], lows, base)
    )
    lows = reduce_last(plan, lows, tag, near, wide_in, late_in[-1], across)
    pairs = []
    for e in range(plan.groups):
        other = swap(lows[e], "tensor", 1)
        if e:
            total = lows[e] + other
            pairs += [total, swap(total, "groups", e)]
        else:
            pairs += [lows[e], other]
    pairs, deltas = lax.optimization_barrier((pairs, deltas))
    across_wide = [blocks[plan.left_pieces] for blocks in across]
    terms = expand_taken(plan, pairs, tag, wide_in, late_in[0], across_wide, across_up)
    deltas += [terms[0]] + return_terms(terms)
    own = join(plan, seg_of, base, deltas, 0)
    return join(plan, seg_of, base, deltas, 1, own)


def solution(mesh):
    placed = (
        P(("groups", "replica"), "tensor"),
        P("tensor", None),
        P("replica", "tensor", None),
        P("replica", None, "tensor"),
        P(("groups", "replica")),
        P(),
    )
    return jax.shard_map(
        on_device,
        mesh=mesh,
        in_specs=placed,
        out_specs=P(("groups", "replica"), "tensor"),
        check_vma=False,
    )
```

```python
import functools

import jax
import jax.numpy as jnp
from jax import lax
from jax.experimental import pallas as pl
from jax.experimental.pallas import tpu as pltpu
from jax.sharding import PartitionSpec as P

CAP = 2
SEG = 32
LANES = 128
PAIR = CAP * SEG
VMEM_LIMIT = 24 * 1024 * 1024
HBM = pl.BlockSpec(memory_space=pltpu.HBM)
SMEM = pl.BlockSpec(memory_space=pltpu.SMEM)
VMEM = pl.BlockSpec(memory_space=pltpu.VMEM)


class Plan:
    def __init__(self, replicas, groups, slots, rank, width, features):
        self.replicas, self.groups, self.slots, self.rank = replicas, groups, slots, rank
        self.width, self.features = width, features
        self.half = replicas // 2
        self.turn = self.half // 2
        self.near = [d for d in range(self.half) if not d & self.turn]
        self.cross = [d for d in range(self.half) if d & self.turn]
        self.across = self.near[1:] + self.near[:1] + self.cross
        self.share = rank // groups
        self.left_rows = slots * self.share
        self.padded = -(-self.left_rows // LANES) * LANES
        beside = width // features
        self.up_rows = -(-self.left_rows // (beside * 16)) * 16
        self.left_pieces = -(-self.left_rows // PAIR)
        self.pieces = self.left_pieces + 1
        assert self.up_rows <= PAIR
        self.adapter_wide = -(-self.pieces // 2)
        self.units = 2 * len(self.cross)
        self.last_piece = self.units - 2 if self.units - 2 < self.left_pieces else None
        assert self.pieces <= self.units and self.adapter_wide <= len(self.cross)
        self.wide = len(self.cross)
        self.outer = [r for r in range(replicas) if self.is_outer(r)]
        self.inner = [r for r in range(replicas) if not self.is_outer(r)]

    def is_outer(self, r):
        return (r < self.turn) or (r >= self.replicas - self.turn)

    def up_columns(self):
        for j, row in enumerate(range(0, self.left_rows, self.up_rows)):
            yield row, min(self.up_rows, self.left_rows - row), j * self.features

    def left_spans(self):
        for piece in range(self.left_pieces):
            yield piece, min(PAIR, self.left_rows - piece * PAIR)

    def late_blocks(self):
        return self.cross + self.cross[::-1]

    def late_rows(self, refs, i, kind):
        return refs[i if kind == 0 else self.units - 1 - i]


def params(limit=VMEM_LIMIT):
    return pltpu.CompilerParams(vmem_limit_bytes=limit)


def am_outer(plan):
    me = lax.axis_index("replica")
    return (me < plan.turn) | (me >= plan.replicas - plan.turn)


def of_wide(refs, piece):
    return refs[piece // 2].at[pl.ds((piece % 2) * PAIR, PAIR)]


def late_adapters(late, piece, plan):
    return late[0 if piece == plan.left_pieces else 1 + piece]


def lay_kernel(plan, first_call, ids_ref, residency_ref, x_ref, left_ref, up_ref, *rest):
    n_near = len(plan.near) - 1 if first_call else 1
    n_blocks = plan.wide if first_call else len(plan.late_blocks())
    n_tags = len(plan.cross) if first_call else 0
    near, rest = rest[:n_near], rest[n_near:]
    blocks, rest = rest[:n_blocks], rest[n_blocks:]
    tag_outs, rest = rest[:n_tags], rest[n_tags:]
    seg_out, seg_ref, slot_ref, count_ref, staged, tags, left, up, in_sems, sems = rest
    half, slots, width, share = plan.half, plan.slots, plan.width, plan.share
    me = lax.axis_index("replica")
    first = pl.multiple_of(lax.axis_index("groups") * share, share)
    outer = am_outer(plan)
    rows_outer = outer if first_call else jnp.logical_not(outer)

    def copy_in(i, source, stage):
        return pltpu.make_async_copy(source, stage, in_sems.at[i])

    adapters_in = []
    for slot in range(slots):
        source = pl.ds(first, share)
        stage = pl.ds(slot * share, share)
        n = len(adapters_in)
        adapters_in.append(copy_in(n, left_ref.at[slot, source], left.at[stage]))
        adapters_in.append(copy_in(n + 1, up_ref.at[slot, source], up.at[stage]))

    @pl.when(jnp.logical_not(rows_outer))
    def _():
        for copy in adapters_in:
            copy.start()

    scale = 2**16 // slots + 1
    assert all(a * scale >> 16 == a // slots for a in range(residency_ref.shape[0]))
    for h in range(plan.replicas):
        count_ref[h] = 0
        for p in range(CAP):
            seg_ref[h * CAP + p] = -1
            slot_ref[h * CAP + p] = 0
    for s in range(ids_ref.shape[0]):
        adapter = ids_ref[s]
        holder = (adapter * scale) >> 16
        count = count_ref[holder]
        place = holder * CAP + count
        count_ref[holder] = count + 1
        seg_ref[place] = s
        slot_ref[place] = residency_ref[adapter] - holder * slots
    for d in range(half):
        for kind in range(2):
            for p in range(CAP):
                seg_out[(kind * half + d) * CAP + p] = seg_ref[
                    (me ^ (d + kind * half)) * CAP + p
                ]

    def segment(d, kind, p):
        seg = jnp.maximum(seg_out[(kind * half + d) * CAP + p], 0)
        return pl.ds(pl.multiple_of(seg * SEG, SEG), SEG)

    def write_tags(targets):
        written = [(d, kind) for d, kind, _ in targets]
        if first_call:
            written += [(d, kind) for d in plan.cross for kind in range(2)]
        for d, kind in written:
            for p in range(CAP):
                slot = slot_ref[(me ^ (d + kind * half)) * CAP + p].astype(jnp.float32)
                tags[d, pl.ds((kind * CAP + p) * SEG, SEG), :] = jnp.full(
                    (SEG, LANES), slot, jnp.float32
                ).astype(tags.dtype)

    near_d = plan.near[1:] if first_call else plan.near[:1]
    near_targets = [
        (d, kind, near[i].at[pl.ds(kind * PAIR, PAIR)])
        for i, d in enumerate(near_d)
        for kind in range(2)
    ]
    cross_targets = [
        (
            d,
            kind,
            of_wide(blocks, 2 * i + kind) if first_call else plan.late_rows(blocks, i, kind),
        )
        for i, d in enumerate(plan.cross)
        for kind in range(2)
    ]
    departures = []

    def depart(source, target):
        copy = pltpu.make_async_copy(source, target, sems.at[len(departures)])
        copy.start()
        departures.append(copy)

    def depart_tags():
        for d, kind, target in near_targets:
            depart(tags.at[d, pl.ds(kind * PAIR, PAIR)], target.at[:, pl.ds(width, LANES)])
        for d, tag_out in zip(plan.cross, tag_outs):
            depart(tags.at[d], tag_out)

    def finish():
        for copy in departures:
            copy.wait()
        departures.clear()

    def start_rows(targets):
        rows_in = []
        for d, kind, target in targets:
            for p in range(CAP):
                stage = staged.at[pl.ds(len(rows_in) * SEG, SEG)]
                copy = copy_in(
                    len(adapters_in) + len(rows_in), x_ref.at[segment(d, kind, p)], stage
                )
                copy.start()
                place = target.at[pl.ds(p * SEG, SEG), pl.ds(0, width)]
                rows_in.append((copy, stage, place))
        return rows_in

    def depart_rows(rows_in):
        for copy, stage, place in rows_in:
            copy.wait()
            depart(stage, place)
        finish()

    @pl.when(rows_outer)
    def _():
        rows_in = start_rows(cross_targets + near_targets)
        write_tags(near_targets)
        depart_tags()
        depart_rows(rows_in)

    @pl.when(jnp.logical_not(rows_outer))
    def _():
        rows_in = start_rows(near_targets)
        write_tags(near_targets)
        depart_tags()
        for slot in range(slots):
            adapters_in[2 * slot].wait()
            piece, at = divmod(slot * share, PAIR)
            unit = (
                of_wide(blocks, piece) if first_call else late_adapters(blocks, piece, plan)
            )
            depart(
                left.at[pl.ds(slot * share, share)],
                unit.at[pl.ds(at, share), pl.ds(0, width)],
            )
        for slot in range(slots):
            adapters_in[2 * slot + 1].wait()
        piece = plan.left_pieces
        unit = of_wide(blocks, piece) if first_call else late_adapters(blocks, piece, plan)
        for row, rows, column in plan.up_columns():
            depart(up.at[pl.ds(row, rows)], unit.at[pl.ds(0, rows), pl.ds(column, plan.features)])
        depart_rows(rows_in)


def lay_out(plan, first_call, ids, residency, x, left_rows, ups):
    count = 2 * plan.half * CAP
    tagged = jax.ShapeDtypeStruct((2 * PAIR, plan.width + LANES), x.dtype)
    near = [tagged] * (len(plan.near) - 1 if first_call else 1)
    heights = [2] * plan.wide if first_call else [1] * plan.units
    blocks = [jax.ShapeDtypeStruct((n * PAIR, plan.width), x.dtype) for n in heights]
    if first_call:
        blocks += [jax.ShapeDtypeStruct((2 * PAIR, LANES), x.dtype)] * len(plan.cross)
    out = pl.pallas_call(
        functools.partial(lay_kernel, plan, first_call),
        out_shape=near + blocks + [jax.ShapeDtypeStruct((count,), jnp.int32)],
        in_specs=[SMEM, SMEM, HBM, HBM, HBM],
        out_specs=[HBM] * (len(near) + len(blocks)) + [SMEM],
        scratch_shapes=[
            pltpu.SMEM((plan.replicas * CAP,), jnp.int32),
            pltpu.SMEM((plan.replicas * CAP,), jnp.int32),
            pltpu.SMEM((plan.replicas,), jnp.int32),
            pltpu.VMEM((count * SEG, plan.width), x.dtype),
            pltpu.VMEM((plan.half, 2 * PAIR, LANES), x.dtype),
            pltpu.VMEM((plan.left_rows, plan.width), x.dtype),
            pltpu.VMEM((plan.left_rows, plan.features), x.dtype),
            pltpu.SemaphoreType.DMA((count + 2 * plan.slots,)),
            pltpu.SemaphoreType.DMA((2 * count + 2 * plan.pieces,)),
        ],
        compiler_params=params(60 * 1024 * 1024),
        cost_estimate=pl.CostEstimate(flops=0, bytes_accessed=x.size, transcendentals=0),
        name="lay_out_first" if first_call else "lay_out_second",
    )(ids, residency, x, left_rows, ups)
    return list(out[: len(near)]), list(out[len(near) : -1]), out[-1]


def slot_mask(tags, first, columns, slots, share):
    lane = lax.broadcasted_iota(jnp.int32, (1, LANES), 1)
    column_slot = jnp.zeros((1, LANES), jnp.float32)
    for j in range(0, LANES, share):
        slot = (first + j) // share if first + j < columns else -1
        column_slot = jnp.where(lane >= j, float(slot), column_slot)
    return tags == column_slot


class Copies:
    def __init__(self, outer, sems):
        self.outer, self.sems, self.waits = outer, sems, []

    def both(self, target, outer_source, inner_source=None):
        sem = self.sems.at[len(self.waits)]
        copy = pltpu.make_async_copy(outer_source, target, sem)
        if inner_source is None:
            copy.start()
        else:
            pl.when(self.outer)(copy.start)
            pl.when(jnp.logical_not(self.outer))(
                pltpu.make_async_copy(inner_source, target, sem).start
            )
        self.waits.append((None, copy))

    def one(self, wanted, target, source):
        copy = pltpu.make_async_copy(source, target, self.sems.at[len(self.waits)])
        pl.when(wanted)(copy.start)
        self.waits.append((wanted, copy))

    def wait(self):
        for wanted, copy in self.waits:
            if wanted is None:
                copy.wait()
            else:
                pl.when(wanted)(copy.wait)


def lane_group(share):
    return lax.broadcasted_iota(jnp.int32, (1, LANES), 1) // share


def spread_lanes(value, share):
    total = value
    for shift in range(share, LANES, share):
        total += pltpu.roll(value, shift, 1)
    return total


def pack(low, share):
    count = LANES // share
    height = low.shape[0] // count
    everywhere = spread_lanes(low, share)
    packed = jnp.zeros((height, LANES), jnp.float32)
    for i in range(count):
        rows = everywhere[i * height : (i + 1) * height]
        packed = jnp.where(lane_group(share) == i, rows, packed)
    return packed


def unpack(packed, share):
    rows = [
        spread_lanes(jnp.where(lane_group(share) == i, packed, 0.0), share)
        for i in range(LANES // share)
    ]
    return jnp.concatenate(rows, axis=0)


def fold(product, tags, columns, slots, share):
    total = jnp.zeros(tags.shape, jnp.float32)
    for first in range(0, product.shape[1], LANES):
        mask = slot_mask(tags, first, columns, slots, share)
        total += jnp.where(mask, product[:, first : first + LANES], 0.0)
    return total


def copy_rows(copies, plan, kind, target, columns, near, wide, late):
    span = pl.ds(kind * PAIR, PAIR)
    for i, d in enumerate(plan.near):
        copies.both(target.at[pl.ds(d * PAIR, PAIR)], near[i].at[span, columns])
    for i, d in enumerate(plan.cross):
        place = target.at[pl.ds(d * PAIR, PAIR)]
        if i == 0 and kind == 1:
            copies.one(jnp.logical_not(copies.outer), place, wide[i].at[span, columns])
        else:
            copies.both(
                place, plan.late_rows(late, i, kind).at[:, columns], wide[i].at[span, columns]
            )


def copy_tags(copies, plan, kind, target, near, tags):
    span = pl.ds(kind * PAIR, PAIR)
    for i, d in enumerate(plan.near):
        copies.both(target.at[pl.ds(d * PAIR, PAIR)], near[i].at[span, pl.ds(plan.width, LANES)])
    for i, d in enumerate(plan.cross):
        copies.both(target.at[pl.ds(d * PAIR, PAIR)], tags[i].at[span])


def product_of(rows, left):
    return lax.dot_general(
        rows, left, (((1,), (1,)), ((), ())), preferred_element_type=jnp.float32
    )


def reduce_own_kernel(plan, n_steps, near, wide, late, tags, own, low_ref, tag_ref, *scratch):
    rows, left, acc, tag, sems = scratch
    block = plan.width // n_steps
    outer = am_outer(plan)
    each = plan.half + 1
    steps = []
    for k in range(n_steps + 1):
        copies = Copies(outer, sems.at[pl.ds(k * each, each)])
        if k < n_steps:
            columns = pl.ds(k * block, block)
            copy_rows(copies, plan, 0, rows.at[:, columns], columns, near, wide, late)
            copies.both(left.at[:, columns], own.at[:, columns])
        else:
            copy_tags(copies, plan, 0, tag, near, tags)
        steps.append(copies)
    for k in range(n_steps):
        steps[k].wait()
        columns = pl.ds(k * block, block)
        product = product_of(rows[:, columns], left[:, columns])
        acc[...] = acc[...] + product if k else product
    steps[n_steps].wait()
    tags = tag[...].astype(jnp.float32)
    tag_ref[...] = tags
    low_ref[...] = pack(fold(acc, tags, acc.shape[1], plan.slots, plan.rank), plan.rank)


def reduce_taken_kernel(plan, n_steps, near, wide, late, tags, across, *rest):
    lows, tag_ref = rest[: plan.groups], rest[plan.groups]
    rows, left, acc, tag, sems = rest[plan.groups + 1 :]
    block = plan.width // n_steps
    outer = am_outer(plan)
    inner = jnp.logical_not(outer)
    more = plan.groups - 1
    each = plan.half + plan.left_pieces + more * (plan.half + plan.left_pieces)
    missing = pl.ds(plan.cross[0] * PAIR, PAIR)

    @pl.when(outer)
    def _():
        rows[0, missing, :] = jnp.zeros((PAIR, plan.width), rows.dtype)

    if plan.last_piece is not None:

        @pl.when(inner)
        def _():
            left[0, pl.ds(plan.last_piece * PAIR, PAIR), :] = jnp.zeros(
                (PAIR, plan.width), left.dtype
            )

    steps = []
    for k in range(n_steps + 1):
        copies = Copies(outer, sems.at[pl.ds(k * each, each)])
        columns = pl.ds(k * block, block) if k < n_steps else pl.ds(plan.width, LANES)
        if k < n_steps:
            copy_rows(copies, plan, 1, rows.at[0, :, columns], columns, near, wide, late)
        else:
            copy_tags(copies, plan, 1, tag.at[0], near, tags)
        for e in range(1, plan.groups):
            for i, d in enumerate(plan.across):
                target = rows.at[e, :, columns] if k < n_steps else tag.at[e]
                copies.one(
                    inner,
                    target.at[pl.ds(d * PAIR, PAIR)],
                    across[e - 1][i].at[:, columns],
                )
        if k < n_steps:
            for piece, count in plan.left_spans():
                span = pl.ds(0, count), columns
                place = left.at[0, pl.ds(piece * PAIR, count), columns]
                if piece == plan.last_piece:
                    copies.one(outer, place, of_wide(wide, piece).at[span])
                else:
                    copies.both(
                        place,
                        of_wide(wide, piece).at[span],
                        late_adapters(late, piece, plan).at[span],
                    )
                for e in range(1, plan.groups):
                    copies.one(
                        outer,
                        left.at[e, pl.ds(piece * PAIR, count), columns],
                        across[e - 1][piece].at[span],
                    )
        steps.append(copies)
    for k in range(n_steps):
        steps[k].wait()
        columns = pl.ds(k * block, block)
        for e in range(plan.groups):
            rows_at = jnp.where(inner, e, 0)
            left_at = jnp.where(outer, e, 0)
            product = product_of(rows[rows_at, :, columns], left[left_at, :, columns])
            acc[e] = acc[e] + product if k else product
    steps[n_steps].wait()
    tag_ref[...] = tag[0].astype(jnp.float32)
    for e in range(plan.groups):
        tags = tag[jnp.where(inner, e, 0)].astype(jnp.float32)
        low = fold(acc.at[e], tags, plan.left_rows, plan.slots, plan.share)
        lows[e][...] = pack(low, plan.share)


def reduce_last_kernel(plan, *refs):
    groups, width = plan.groups, plan.width
    before, tag_ref, refs = refs[:groups], refs[groups], refs[groups + 1 :]
    near, wide, last, across = refs[:4]
    lows = refs[4:]
    outer = am_outer(plan)
    inner = jnp.logical_not(outer)
    first_row = plan.cross[0] * PAIR

    def padded(parts, height):
        rows = sum(part.shape[0] for part in parts)
        if rows < height:
            parts = parts + [jnp.zeros((height - rows, width), last.dtype)]
        return jnp.concatenate(parts, axis=0)

    @pl.when(outer)
    def _():
        tags = tag_ref[first_row : first_row + PAIR, :]
        rows = last[...]
        for e in range(groups):
            total = jnp.zeros((PAIR, LANES), jnp.float32)
            for first in range(0, plan.padded, LANES):
                parts = []
                for piece, count in plan.left_spans():
                    if first <= piece * PAIR < first + LANES:
                        source = of_wide(wide, piece) if e == 0 else across[e - 1][piece]
                        parts.append(source[:count, :width])
                product = product_of(rows, padded(parts, LANES))
                mask = slot_mask(tags, first, plan.left_rows, plan.slots, plan.share)
                total += jnp.where(mask, product, 0.0)
            whole = [jnp.zeros((PAIR, LANES), jnp.float32)] * plan.half
            whole[plan.cross[0]] = total
            lows[e][...] = before[e][...] + pack(jnp.concatenate(whole, axis=0), plan.share)

    @pl.when(inner)
    def _():
        if plan.last_piece is None:
            for e in range(groups):
                lows[e][...] = before[e][...]
            return
        at = plan.last_piece * PAIR
        first = at // LANES * LANES
        count = min(PAIR, plan.left_rows - at)
        parts = [jnp.zeros((at - first, width), last.dtype)] if at > first else []
        left = padded(parts + [last[:count, :]], LANES)
        for e in range(groups):
            if e == 0:
                blocks = {d: near[i].at[PAIR:] for i, d in enumerate(plan.near)}
                blocks.update({d: wide[i].at[PAIR:] for i, d in enumerate(plan.cross)})
                tags = tag_ref[...]
            else:
                blocks = {d: across[e - 1][i] for i, d in enumerate(plan.across)}
                tags = [blocks[d][:, width:] for d in range(plan.half)]
                tags = jnp.concatenate(tags, axis=0).astype(jnp.float32)
            whole = jnp.concatenate([blocks[d][:, :width] for d in range(plan.half)], axis=0)
            product = product_of(whole, left)
            mask = slot_mask(tags, first, plan.left_rows, plan.slots, plan.share)
            low = pack(jnp.where(mask, product, 0.0), plan.share)
            lows[e][...] = before[e][...] + low


def reduce_last(plan, lows, tag, near, wide, last, across):
    flat, tree = jax.tree.flatten([near, wide, last, across])
    n_head = plan.groups + 1

    def body(*refs):
        nested = jax.tree.unflatten(tree, refs[n_head : n_head + len(flat)])
        reduce_last_kernel(plan, *refs[:n_head], *nested, *refs[n_head + len(flat) :])

    shapes = [jax.ShapeDtypeStruct(a.shape, a.dtype) for a in lows]
    return pl.pallas_call(
        body,
        out_shape=shapes,
        in_specs=[VMEM] * (n_head + len(flat)),
        out_specs=[VMEM] * len(lows),
        compiler_params=params(),
        cost_estimate=pl.CostEstimate(flops=1, bytes_accessed=1, transcendentals=0),
        name="reduce_last",
    )(*lows, tag, *flat)


def blocks_call(kernel, blocks, out_shape, out_specs, scratch, flops, moved, name, extra=()):
    flat, tree = jax.tree.flatten(blocks)
    n_extra = len(extra)

    def body(*refs):
        head, rest = refs[:n_extra], refs[n_extra:]
        nested = jax.tree.unflatten(tree, rest[: len(flat)])
        kernel(*head, *nested, *rest[len(flat) :])

    return pl.pallas_call(
        body,
        out_shape=out_shape,
        in_specs=[VMEM] * n_extra + [HBM] * len(flat),
        out_specs=out_specs,
        scratch_shapes=scratch,
        compiler_params=params(),
        cost_estimate=pl.CostEstimate(flops=1, bytes_accessed=1, transcendentals=0),
        name=name,
    )(*extra, *flat)


def reduce_own(plan, near, wide, late, tags, own):
    height = plan.half * PAIR
    columns = own.shape[0]
    n_steps = 2
    dtype = own.dtype
    return blocks_call(
        functools.partial(reduce_own_kernel, plan, n_steps),
        [near, wide, late, tags, own],
        [
            jax.ShapeDtypeStruct((height * plan.rank // LANES, LANES), jnp.float32),
            jax.ShapeDtypeStruct((height, LANES), jnp.float32),
        ],
        [VMEM] * 2,
        [
            pltpu.VMEM((height, plan.width), dtype),
            pltpu.VMEM((columns, plan.width), dtype),
            pltpu.VMEM((height, columns), jnp.float32),
            pltpu.VMEM((height, LANES), dtype),
            pltpu.SemaphoreType.DMA(((n_steps + 1) * (plan.half + 1),)),
        ],
        2 * height * plan.width * columns,
        2 * plan.width * (height + columns),
        "reduce_own",
    )


def reduce_taken(plan, near, wide, late, tags, across):
    height = plan.half * PAIR
    n_steps = 2
    dtype = near[0].dtype
    groups, padded = plan.groups, plan.padded
    *lows, tag = blocks_call(
        functools.partial(reduce_taken_kernel, plan, n_steps),
        [near, wide, late, tags, across],
        [jax.ShapeDtypeStruct((height * plan.share // LANES, LANES), jnp.float32)] * groups
        + [jax.ShapeDtypeStruct((height, LANES), jnp.float32)],
        [VMEM] * (groups + 1),
        [
            pltpu.VMEM((groups, height, plan.width), dtype),
            pltpu.VMEM((groups, padded, plan.width), dtype),
            pltpu.VMEM((groups, height, padded), jnp.float32),
            pltpu.VMEM((groups, height, LANES), dtype),
            pltpu.SemaphoreType.DMA(((n_steps + 1) * groups * (plan.half + plan.left_pieces),)),
        ],
        2 * height * plan.width * groups * padded,
        2 * plan.width * (height + padded) * groups,
        "reduce_taken",
    )
    return lows, tag


def rounded(low, share):
    return unpack(low.astype(jnp.bfloat16).astype(jnp.float32), share)


def spread(low, tags, columns, slots, share):
    blocks = [
        jnp.where(slot_mask(tags, first, columns, slots, share), low, 0.0).astype(jnp.bfloat16)
        for first in range(0, columns, LANES)
    ]
    return jnp.concatenate(blocks, axis=1)


def write_deltas(delta, outs):
    delta = delta.astype(jnp.bfloat16)
    for i, out in enumerate(outs):
        out[...] = delta[i * PAIR : (i + 1) * PAIR]


def expand_own_kernel(plan, mine_ref, other_ref, tag_ref, own, *rest):
    outs, (up, sem) = rest[:-2], rest[-2:]
    copy = pltpu.make_async_copy(own, up, sem)
    copy.start()
    low = rounded(mine_ref[...] + other_ref[...], plan.rank)
    wide_low = spread(low, tag_ref[...], up.shape[0], plan.slots, plan.rank)
    copy.wait()
    write_deltas(jnp.dot(wide_low, up[...], preferred_element_type=jnp.float32), outs)


def expand_own(plan, mine, other, tag, own):
    columns, features = own.shape
    return blocks_call(
        functools.partial(expand_own_kernel, plan),
        [own],
        [jax.ShapeDtypeStruct((PAIR, features), jnp.bfloat16)] * plan.half,
        [VMEM] * plan.half,
        [pltpu.VMEM(own.shape, own.dtype), pltpu.SemaphoreType.DMA(())],
        2 * tag.shape[0] * columns * features,
        2 * features * (columns + tag.shape[0]),
        "expand_own",
        extra=(mine, other, tag),
    )


def expand_taken_kernel(plan, *refs):
    lows, tag_ref, refs = refs[: 2 * plan.groups], refs[2 * plan.groups], refs[2 * plan.groups + 1 :]
    wide, narrow, across_wide, across_narrow = refs[:4]
    outs, (up, sems) = refs[4:-2], refs[-2:]
    copies = Copies(am_outer(plan), sems)
    for row, rows, column in plan.up_columns():
        part = pl.ds(0, rows), pl.ds(column, plan.features)
        for e in range(plan.groups):
            copies.both(
                up.at[e, pl.ds(row, rows)],
                (of_wide(wide, plan.left_pieces) if e == 0 else across_wide[e - 1]).at[part],
                (narrow if e == 0 else across_narrow[e - 1]).at[part],
            )
    if plan.padded > plan.left_rows:
        up[:, plan.left_rows :, :] = jnp.zeros(
            (plan.groups, plan.padded - plan.left_rows, plan.features), up.dtype
        )
    tags = tag_ref[...]
    wides = []
    for e in range(plan.groups):
        mine, other = lows[2 * e][...], lows[2 * e + 1][...]
        low = jnp.where(am_outer(plan), mine, other) if e else mine + other
        low = rounded(low, plan.share)
        wides.append(spread(low, tags, plan.left_rows, plan.slots, plan.share))
    copies.wait()
    delta = None
    for e in range(plan.groups):
        product = jnp.dot(wides[e], up[e], preferred_element_type=jnp.float32)
        delta = product if delta is None else delta + product
    write_deltas(delta, outs)


def expand_taken(plan, lows, tag, wide, narrow, across_wide, across_narrow):
    height, features = tag.shape[0], plan.features
    return blocks_call(
        functools.partial(expand_taken_kernel, plan),
        [wide, narrow, across_wide, across_narrow],
        [jax.ShapeDtypeStruct((PAIR, features), jnp.bfloat16)] * plan.half,
        [VMEM] * plan.half,
        [
            pltpu.VMEM((plan.groups, plan.padded, features), jnp.bfloat16),
            pltpu.SemaphoreType.DMA((plan.groups * len(list(plan.up_columns())),)),
        ],
        2 * height * plan.groups * plan.padded * features,
        2 * features * (plan.groups * plan.padded + height),
        "expand_taken",
        extra=(*lows, tag),
    )


def join_kernel(order, seg_ref, base_ref, *refs):
    n = len(order)
    deltas, (out_ref, rows, sems) = refs[:n], refs[-3:]

    def parts():
        for i in range(n * CAP):
            seg = seg_ref[order[i // CAP] * CAP + i % CAP]
            span = pl.ds(pl.multiple_of(jnp.maximum(seg, 0) * SEG, SEG), SEG)
            place = pl.ds(i * SEG, SEG)
            yield i, seg, span, pltpu.make_async_copy(
                rows.at[place], out_ref.at[span], sems.at[i]
            )

    for i, seg, span, copy in parts():

        @pl.when(seg >= 0)
        def _():
            part = i % CAP
            delta = deltas[i // CAP][part * SEG : (part + 1) * SEG, :]
            total = base_ref[span, :] + delta.astype(jnp.float32)
            rows[i * SEG : (i + 1) * SEG, :] = total.astype(rows.dtype)
            copy.start()

    for _, seg, _, copy in parts():
        pl.when(seg >= 0)(copy.wait)


def join(seg_of, base, deltas, order, name, before=None):
    height, features = base.shape
    deltas = [deltas[i] for i in order]
    n = len(deltas)
    more = [] if before is None else [before]
    return pl.pallas_call(
        functools.partial(join_kernel, order),
        out_shape=jax.ShapeDtypeStruct((height, features), jnp.bfloat16),
        in_specs=[SMEM, VMEM] + [VMEM] * n + [HBM] * len(more),
        out_specs=HBM,
        scratch_shapes=[
            pltpu.VMEM((n * PAIR, features), jnp.bfloat16),
            pltpu.SemaphoreType.DMA((n * CAP,)),
        ],
        input_output_aliases={2 + n: 0} if more else {},
        compiler_params=params(),
        cost_estimate=pl.CostEstimate(
            flops=height * features, bytes_accessed=4 * height * features, transcendentals=0
        ),
        name=name,
    )(seg_of, base, *deltas, *more)


def swap(value, axis, distance):
    count = lax.axis_size(axis)
    return lax.ppermute(value, axis, [(i, i ^ distance) for i in range(count)])


def send(plan, value, moves):
    shape = (plan.groups, plan.replicas, lax.axis_size("tensor"))

    def place(g, r, c):
        return (g * shape[1] + r) * shape[2] + c

    pairs = [
        (place(g, r, c), place(g ^ flips[0], r ^ flips[1], c ^ flips[2]))
        for senders, *flips in moves
        for g in range(shape[0])
        for r in senders
        for c in range(shape[2])
    ]
    return lax.ppermute(value, ("groups", "replica", "tensor"), pairs)


def return_terms(terms):
    back = {d: swap(terms[d], "replica", d) for d in reversed(range(1, len(terms)))}
    return [back[d] for d in range(1, len(terms))]


def on_device(x, weight, lefts, ups, ids, residency):
    slots, width, rank = lefts.shape
    features = ups.shape[2]
    plan = Plan(
        lax.axis_size("replica"), lax.axis_size("groups"), slots, rank, width, features
    )
    half, n_cross = plan.half, len(plan.cross)
    core = lax.axis_index("tensor")
    outer = am_outer(plan)
    left_rows = jnp.swapaxes(lefts, 1, 2)
    near, wide, seg_of = lay_out(plan, True, ids, residency, x, left_rows, ups)
    wide, tags = wide[: plan.wide], wide[plan.wide :]

    near = [swap(block, "replica", d) for block, d in zip(near, plan.near[1:])]
    wide_in = []
    for i in range(plan.wide):
        moves = []
        if i < n_cross:
            moves.append((plan.outer, 0, plan.cross[i], 0))
        if i < plan.adapter_wide:
            moves.append((plan.inner, 0, half, 0))
        wide_in.append(send(plan, wide[i], moves))

    late_ids, _ = lax.optimization_barrier((ids, seg_of))
    near, late_x = lax.optimization_barrier((near, x))
    own_rows, late, _ = lay_out(plan, False, late_ids, residency, x, left_rows, ups)
    near = own_rows + near
    def part(which, rows):
        columns = lax.dynamic_slice(weight, (0, which * features), (weight.shape[0], features))
        return jnp.dot(rows, columns, preferred_element_type=jnp.float32)

    base_other, base_mine = part(1 - core, late_x), part(core, late_x)

    def across_send(i):
        d = plan.across[i]
        if d in plan.near:
            block = near[plan.near.index(d)][PAIR:]
            value, tag = block[:, :width], block[:, width:]
        else:
            j = plan.cross.index(d)
            value, tag = wide_in[j][PAIR:], tags_in[j][PAIR:]
        if i < plan.pieces:
            piece = wide_in[i // 2][(i % 2) * PAIR : (i % 2 + 1) * PAIR]
            value = jnp.where(outer, piece, value)
        value = jnp.concatenate([value, tag], axis=1)
        return [
            send(plan, value, [(plan.outer, e, 0, 0), (plan.inner, e, 0, 0)])
            for e in range(1, plan.groups)
        ]

    across = [across_send(0), across_send(1)]
    tags_in = [swap(tag, "replica", d) for tag, d in zip(tags, plan.cross)]

    wide_in[0], near, across[0], late, base_other, base_mine = lax.optimization_barrier(
        (wide_in[0], near, across[0], late, base_other, base_mine)
    )
    late_in = []
    for unit, d in enumerate(plan.late_blocks()):
        moves = [(plan.inner, 0, d, 0)]
        if unit < plan.pieces:
            moves.append((plan.outer, 0, half, 0))
        block = late[unit]
        if unit == 1:
            near, wide_in, tags_in, block = lax.optimization_barrier(
                (near, wide_in, tags_in, block)
            )
        elif unit == 2:
            late_in[0], wide_in, tags_in, block, base_other = lax.optimization_barrier(
                (late_in[0], wide_in, tags_in, block, base_other)
            )
        elif unit > 2:
            late_in[unit - 2], block = lax.optimization_barrier((late_in[unit - 2], block))
        late_in.append(send(plan, block, moves))
    across += [across_send(i) for i in range(2, half)]
    late_up = late_in[0][: plan.up_rows]
    across_up = [send(plan, late_up, [(plan.inner, e, 0, 0)]) for e in range(1, plan.groups)]
    base = base_mine + swap(base_other, "tensor", 1)
    late_in[:n_cross], across[:-1] = lax.optimization_barrier((late_in[:n_cross], across[:-1]))
    across = [[blocks[e] for blocks in across] for e in range(plan.groups - 1)]

    own_left = left_rows.reshape(slots * rank, width)
    low, tag = reduce_own(plan, near, wide_in, late_in[:n_cross], tags_in, own_left)
    other = swap(low, "tensor", 1)
    terms = expand_own(plan, low, other, tag, ups.reshape(slots * rank, features))
    deltas = [terms[0]] + return_terms(terms)

    lows, tag = reduce_taken(plan, near, wide_in, late_in[:-1], tags_in, across)
    late_in[-1], deltas[:2], lows, base = lax.optimization_barrier(
        (late_in[-1], deltas[:2], lows, base)
    )
    lows = reduce_last(plan, lows, tag, near, wide_in, late_in[-1], across)
    pairs = []
    for e in range(plan.groups):
        other = swap(lows[e], "tensor", 1)
        if e:
            total = lows[e] + other
            pairs += [total, swap(total, "groups", e)]
        else:
            pairs += [lows[e], other]
    pairs, deltas = lax.optimization_barrier((pairs, deltas))
    across_wide = [blocks[plan.left_pieces] for blocks in across]
    terms = expand_taken(plan, pairs, tag, wide_in, late_in[0], across_wide, across_up)
    deltas += [terms[0]] + return_terms(terms)
    own = [d for d in plan.cross + plan.near] + [half]
    rows = join(seg_of, base, deltas, own, "join_own")
    rows = join(seg_of, base, deltas, [half + d for d in plan.cross], "join_cross", rows)
    last = [half + d for d in plan.near if d]
    return join(seg_of, base, deltas, last, "join_near", rows)


def solution(mesh):
    placed = (
        P(("groups", "replica"), "tensor"),
        P("tensor", None),
        P("replica", "tensor", None),
        P("replica", None, "tensor"),
        P(("groups", "replica")),
        P(),
    )
    return jax.shard_map(
        on_device,
        mesh=mesh,
        in_specs=placed,
        out_specs=P(("groups", "replica"), "tensor"),
        check_vma=False,
    )
```

```python
import functools

import jax
import jax.numpy as jnp
from jax import lax
from jax.experimental import pallas as pl
from jax.experimental.pallas import tpu as pltpu
from jax.sharding import PartitionSpec as P

CAP = 2
SEG = 32
LANES = 128
PAIR = CAP * SEG
VMEM_LIMIT = 24 * 1024 * 1024
HBM = pl.BlockSpec(memory_space=pltpu.HBM)
SMEM = pl.BlockSpec(memory_space=pltpu.SMEM)
VMEM = pl.BlockSpec(memory_space=pltpu.VMEM)


class Plan:
    def __init__(self, replicas, groups, slots, rank, width, features):
        self.replicas, self.groups, self.slots, self.rank = replicas, groups, slots, rank
        self.width, self.features = width, features
        self.half = replicas // 2
        self.turn = self.half // 2
        self.near = [d for d in range(self.half) if not d & self.turn]
        self.cross = [d for d in range(self.half) if d & self.turn]
        self.across = self.near[1:] + self.near[:1] + self.cross
        self.share = rank // groups
        self.left_rows = slots * self.share
        self.padded = -(-self.left_rows // LANES) * LANES
        beside = width // features
        self.up_rows = -(-self.left_rows // (beside * 16)) * 16
        self.left_pieces = -(-self.left_rows // PAIR)
        self.pieces = self.left_pieces + 1
        assert self.up_rows <= PAIR
        self.adapter_wide = -(-self.pieces // 2)
        self.units = 2 * len(self.cross)
        self.last_piece = self.units - 2 if self.units - 2 < self.left_pieces else None
        assert self.pieces <= self.units and self.adapter_wide <= len(self.cross)
        self.wide = len(self.cross)
        self.outer = [r for r in range(replicas) if self.is_outer(r)]
        self.inner = [r for r in range(replicas) if not self.is_outer(r)]

    def is_outer(self, r):
        return (r < self.turn) or (r >= self.replicas - self.turn)

    def up_columns(self):
        for j, row in enumerate(range(0, self.left_rows, self.up_rows)):
            yield row, min(self.up_rows, self.left_rows - row), j * self.features

    def left_spans(self):
        for piece in range(self.left_pieces):
            yield piece, min(PAIR, self.left_rows - piece * PAIR)

    def late_blocks(self):
        return self.cross + self.cross[::-1]

    def late_rows(self, refs, i, kind):
        return refs[i if kind == 0 else self.units - 1 - i]


def params(limit=VMEM_LIMIT):
    return pltpu.CompilerParams(vmem_limit_bytes=limit)


def am_outer(plan):
    me = lax.axis_index("replica")
    return (me < plan.turn) | (me >= plan.replicas - plan.turn)


def of_wide(refs, piece):
    return refs[piece // 2].at[pl.ds((piece % 2) * PAIR, PAIR)]


def late_adapters(late, piece, plan):
    return late[0 if piece == plan.left_pieces else 1 + piece]


def lay_kernel(plan, first_call, ids_ref, residency_ref, x_ref, left_ref, up_ref, *rest):
    n_near = len(plan.near) - 1 if first_call else 1
    n_blocks = plan.wide if first_call else len(plan.late_blocks())
    n_tags = len(plan.cross) if first_call else 0
    near, rest = rest[:n_near], rest[n_near:]
    blocks, rest = rest[:n_blocks], rest[n_blocks:]
    tag_outs, rest = rest[:n_tags], rest[n_tags:]
    seg_out, seg_ref, slot_ref, count_ref, staged, tags, left, up, in_sems, sems = rest
    half, slots, width, share = plan.half, plan.slots, plan.width, plan.share
    me = lax.axis_index("replica")
    first = pl.multiple_of(lax.axis_index("groups") * share, share)
    outer = am_outer(plan)
    rows_outer = outer if first_call else jnp.logical_not(outer)

    def copy_in(i, source, stage):
        return pltpu.make_async_copy(source, stage, in_sems.at[i])

    adapters_in = []
    for slot in range(slots):
        source = pl.ds(first, share)
        stage = pl.ds(slot * share, share)
        n = len(adapters_in)
        adapters_in.append(copy_in(n, left_ref.at[slot, source], left.at[stage]))
        adapters_in.append(copy_in(n + 1, up_ref.at[slot, source], up.at[stage]))

    @pl.when(jnp.logical_not(rows_outer))
    def _():
        for copy in adapters_in:
            copy.start()

    scale = 2**16 // slots + 1
    assert all(a * scale >> 16 == a // slots for a in range(residency_ref.shape[0]))
    for h in range(plan.replicas):
        count_ref[h] = 0
        for p in range(CAP):
            seg_ref[h * CAP + p] = -1
            slot_ref[h * CAP + p] = 0
    for s in range(ids_ref.shape[0]):
        adapter = ids_ref[s]
        holder = (adapter * scale) >> 16
        count = count_ref[holder]
        place = holder * CAP + count
        count_ref[holder] = count + 1
        seg_ref[place] = s
        slot_ref[place] = residency_ref[adapter] - holder * slots
    for d in range(half):
        for kind in range(2):
            for p in range(CAP):
                seg_out[(kind * half + d) * CAP + p] = seg_ref[
                    (me ^ (d + kind * half)) * CAP + p
                ]

    def segment(d, kind, p):
        seg = jnp.maximum(seg_out[(kind * half + d) * CAP + p], 0)
        return pl.ds(pl.multiple_of(seg * SEG, SEG), SEG)

    def write_tags(targets):
        written = [(d, kind) for d, kind, _ in targets]
        if first_call:
            written += [(d, kind) for d in plan.cross for kind in range(2)]
        for d, kind in written:
            for p in range(CAP):
                slot = slot_ref[(me ^ (d + kind * half)) * CAP + p].astype(jnp.float32)
                tags[d, pl.ds((kind * CAP + p) * SEG, SEG), :] = jnp.full(
                    (SEG, LANES), slot, jnp.float32
                ).astype(tags.dtype)

    near_d = plan.near[1:] if first_call else plan.near[:1]
    near_targets = [
        (d, kind, near[i].at[pl.ds(kind * PAIR, PAIR)])
        for i, d in enumerate(near_d)
        for kind in range(2)
    ]
    cross_targets = [
        (
            d,
            kind,
            of_wide(blocks, 2 * i + kind) if first_call else plan.late_rows(blocks, i, kind),
        )
        for i, d in enumerate(plan.cross)
        for kind in range(2)
    ]
    departures = []

    def depart(source, target):
        copy = pltpu.make_async_copy(source, target, sems.at[len(departures)])
        copy.start()
        departures.append(copy)

    def depart_tags():
        for d, kind, target in near_targets:
            depart(tags.at[d, pl.ds(kind * PAIR, PAIR)], target.at[:, pl.ds(width, LANES)])
        for d, tag_out in zip(plan.cross, tag_outs):
            depart(tags.at[d], tag_out)

    def finish():
        for copy in departures:
            copy.wait()
        departures.clear()

    def start_rows(targets):
        rows_in = []
        for d, kind, target in targets:
            for p in range(CAP):
                stage = staged.at[pl.ds(len(rows_in) * SEG, SEG)]
                copy = copy_in(
                    len(adapters_in) + len(rows_in), x_ref.at[segment(d, kind, p)], stage
                )
                copy.start()
                place = target.at[pl.ds(p * SEG, SEG), pl.ds(0, width)]
                rows_in.append((copy, stage, place))
        return rows_in

    def depart_rows(rows_in):
        for copy, stage, place in rows_in:
            copy.wait()
            depart(stage, place)
        finish()

    @pl.when(rows_outer)
    def _():
        rows_in = start_rows(cross_targets + near_targets)
        write_tags(near_targets)
        depart_tags()
        depart_rows(rows_in)

    @pl.when(jnp.logical_not(rows_outer))
    def _():
        rows_in = start_rows(near_targets)
        write_tags(near_targets)
        depart_tags()
        for slot in range(slots):
            adapters_in[2 * slot].wait()
            piece, at = divmod(slot * share, PAIR)
            unit = (
                of_wide(blocks, piece) if first_call else late_adapters(blocks, piece, plan)
            )
            depart(
                left.at[pl.ds(slot * share, share)],
                unit.at[pl.ds(at, share), pl.ds(0, width)],
            )
        for slot in range(slots):
            adapters_in[2 * slot + 1].wait()
        piece = plan.left_pieces
        unit = of_wide(blocks, piece) if first_call else late_adapters(blocks, piece, plan)
        for row, rows, column in plan.up_columns():
            depart(up.at[pl.ds(row, rows)], unit.at[pl.ds(0, rows), pl.ds(column, plan.features)])
        depart_rows(rows_in)


def lay_out(plan, first_call, ids, residency, x, left_rows, ups):
    count = 2 * plan.half * CAP
    tagged = jax.ShapeDtypeStruct((2 * PAIR, plan.width + LANES), x.dtype)
    near = [tagged] * (len(plan.near) - 1 if first_call else 1)
    heights = [2] * plan.wide if first_call else [1] * plan.units
    blocks = [jax.ShapeDtypeStruct((n * PAIR, plan.width), x.dtype) for n in heights]
    if first_call:
        blocks += [jax.ShapeDtypeStruct((2 * PAIR, LANES), x.dtype)] * len(plan.cross)
    out = pl.pallas_call(
        functools.partial(lay_kernel, plan, first_call),
        out_shape=near + blocks + [jax.ShapeDtypeStruct((count,), jnp.int32)],
        in_specs=[SMEM, SMEM, HBM, HBM, HBM],
        out_specs=[HBM] * (len(near) + len(blocks)) + [SMEM],
        scratch_shapes=[
            pltpu.SMEM((plan.replicas * CAP,), jnp.int32),
            pltpu.SMEM((plan.replicas * CAP,), jnp.int32),
            pltpu.SMEM((plan.replicas,), jnp.int32),
            pltpu.VMEM((count * SEG, plan.width), x.dtype),
            pltpu.VMEM((plan.half, 2 * PAIR, LANES), x.dtype),
            pltpu.VMEM((plan.left_rows, plan.width), x.dtype),
            pltpu.VMEM((plan.left_rows, plan.features), x.dtype),
            pltpu.SemaphoreType.DMA((count + 2 * plan.slots,)),
            pltpu.SemaphoreType.DMA((2 * count + 2 * plan.pieces,)),
        ],
        compiler_params=params(60 * 1024 * 1024),
        cost_estimate=pl.CostEstimate(flops=0, bytes_accessed=x.size, transcendentals=0),
        name="lay_out_first" if first_call else "lay_out_second",
    )(ids, residency, x, left_rows, ups)
    return list(out[: len(near)]), list(out[len(near) : -1]), out[-1]


def slot_mask(tags, first, columns, slots, share):
    lane = lax.broadcasted_iota(jnp.int32, (1, LANES), 1)
    column_slot = jnp.zeros((1, LANES), jnp.float32)
    for j in range(0, LANES, share):
        slot = (first + j) // share if first + j < columns else -1
        column_slot = jnp.where(lane >= j, float(slot), column_slot)
    return tags == column_slot


class Copies:
    def __init__(self, outer, sems):
        self.outer, self.sems, self.waits = outer, sems, []

    def both(self, target, outer_source, inner_source=None):
        sem = self.sems.at[len(self.waits)]
        copy = pltpu.make_async_copy(outer_source, target, sem)
        if inner_source is None:
            copy.start()
        else:
            pl.when(self.outer)(copy.start)
            pl.when(jnp.logical_not(self.outer))(
                pltpu.make_async_copy(inner_source, target, sem).start
            )
        self.waits.append((None, copy))

    def one(self, wanted, target, source):
        copy = pltpu.make_async_copy(source, target, self.sems.at[len(self.waits)])
        pl.when(wanted)(copy.start)
        self.waits.append((wanted, copy))

    def wait(self):
        for wanted, copy in self.waits:
            if wanted is None:
                copy.wait()
            else:
                pl.when(wanted)(copy.wait)


def lane_group(share):
    return lax.broadcasted_iota(jnp.int32, (1, LANES), 1) // share


def spread_lanes(value, share):
    total = value
    for shift in range(share, LANES, share):
        total += pltpu.roll(value, shift, 1)
    return total


def pack(low, share):
    count = LANES // share
    height = low.shape[0] // count
    everywhere = spread_lanes(low, share)
    packed = jnp.zeros((height, LANES), jnp.float32)
    for i in range(count):
        rows = everywhere[i * height : (i + 1) * height]
        packed = jnp.where(lane_group(share) == i, rows, packed)
    return packed


def unpack(packed, share):
    rows = [
        spread_lanes(jnp.where(lane_group(share) == i, packed, 0.0), share)
        for i in range(LANES // share)
    ]
    return jnp.concatenate(rows, axis=0)


def fold(product, tags, columns, slots, share):
    total = jnp.zeros(tags.shape, jnp.float32)
    for first in range(0, product.shape[1], LANES):
        mask = slot_mask(tags, first, columns, slots, share)
        total += jnp.where(mask, product[:, first : first + LANES], 0.0)
    return total


def copy_rows(copies, plan, kind, target, columns, near, wide, late):
    span = pl.ds(kind * PAIR, PAIR)
    for i, d in enumerate(plan.near):
        copies.both(target.at[pl.ds(d * PAIR, PAIR)], near[i].at[span, columns])
    for i, d in enumerate(plan.cross):
        place = target.at[pl.ds(d * PAIR, PAIR)]
        if i == 0 and kind == 1:
            copies.one(jnp.logical_not(copies.outer), place, wide[i].at[span, columns])
        else:
            copies.both(
                place, plan.late_rows(late, i, kind).at[:, columns], wide[i].at[span, columns]
            )


def copy_tags(copies, plan, kind, target, near, tags):
    span = pl.ds(kind * PAIR, PAIR)
    for i, d in enumerate(plan.near):
        copies.both(target.at[pl.ds(d * PAIR, PAIR)], near[i].at[span, pl.ds(plan.width, LANES)])
    for i, d in enumerate(plan.cross):
        copies.both(target.at[pl.ds(d * PAIR, PAIR)], tags[i].at[span])


def product_of(rows, left):
    return lax.dot_general(
        rows, left, (((1,), (1,)), ((), ())), preferred_element_type=jnp.float32
    )


def reduce_own_kernel(plan, n_steps, near, wide, late, tags, own, low_ref, tag_ref, *scratch):
    rows, left, acc, tag, sems = scratch
    block = plan.width // n_steps
    outer = am_outer(plan)
    each = plan.half + 1
    steps = []
    for k in range(n_steps + 1):
        copies = Copies(outer, sems.at[pl.ds(k * each, each)])
        if k < n_steps:
            columns = pl.ds(k * block, block)
            copy_rows(copies, plan, 0, rows.at[:, columns], columns, near, wide, late)
            copies.both(left.at[:, columns], own.at[:, columns])
        else:
            copy_tags(copies, plan, 0, tag, near, tags)
        steps.append(copies)
    for k in range(n_steps):
        steps[k].wait()
        columns = pl.ds(k * block, block)
        product = product_of(rows[:, columns], left[:, columns])
        acc[...] = acc[...] + product if k else product
    steps[n_steps].wait()
    tags = tag[...].astype(jnp.float32)
    tag_ref[...] = tags
    low_ref[...] = pack(fold(acc, tags, acc.shape[1], plan.slots, plan.rank), plan.rank)


def reduce_taken_kernel(plan, n_steps, near, wide, late, tags, across, *rest):
    lows, tag_ref = rest[: plan.groups], rest[plan.groups]
    rows, left, acc, tag, sems = rest[plan.groups + 1 :]
    block = plan.width // n_steps
    outer = am_outer(plan)
    inner = jnp.logical_not(outer)
    more = plan.groups - 1
    each = plan.half + plan.left_pieces + more * (plan.half + plan.left_pieces)
    missing = pl.ds(plan.cross[0] * PAIR, PAIR)

    @pl.when(outer)
    def _():
        rows[0, missing, :] = jnp.zeros((PAIR, plan.width), rows.dtype)

    if plan.last_piece is not None:

        @pl.when(inner)
        def _():
            left[0, pl.ds(plan.last_piece * PAIR, PAIR), :] = jnp.zeros(
                (PAIR, plan.width), left.dtype
            )

    steps = []
    for k in range(n_steps + 1):
        copies = Copies(outer, sems.at[pl.ds(k * each, each)])
        columns = pl.ds(k * block, block) if k < n_steps else pl.ds(plan.width, LANES)
        if k < n_steps:
            copy_rows(copies, plan, 1, rows.at[0, :, columns], columns, near, wide, late)
        else:
            copy_tags(copies, plan, 1, tag.at[0], near, tags)
        for e in range(1, plan.groups):
            for i, d in enumerate(plan.across):
                target = rows.at[e, :, columns] if k < n_steps else tag.at[e]
                copies.one(
                    inner,
                    target.at[pl.ds(d * PAIR, PAIR)],
                    across[e - 1][i].at[:, columns],
                )
        if k < n_steps:
            for piece, count in plan.left_spans():
                span = pl.ds(0, count), columns
                place = left.at[0, pl.ds(piece * PAIR, count), columns]
                if piece == plan.last_piece:
                    copies.one(outer, place, of_wide(wide, piece).at[span])
                else:
                    copies.both(
                        place,
                        of_wide(wide, piece).at[span],
                        late_adapters(late, piece, plan).at[span],
                    )
                for e in range(1, plan.groups):
                    copies.one(
                        outer,
                        left.at[e, pl.ds(piece * PAIR, count), columns],
                        across[e - 1][piece].at[span],
                    )
        steps.append(copies)
    for k in range(n_steps):
        steps[k].wait()
        columns = pl.ds(k * block, block)
        for e in range(plan.groups):
            rows_at = jnp.where(inner, e, 0)
            left_at = jnp.where(outer, e, 0)
            product = product_of(rows[rows_at, :, columns], left[left_at, :, columns])
            acc[e] = acc[e] + product if k else product
    steps[n_steps].wait()
    tag_ref[...] = tag[0].astype(jnp.float32)
    for e in range(plan.groups):
        tags = tag[jnp.where(inner, e, 0)].astype(jnp.float32)
        low = fold(acc.at[e], tags, plan.left_rows, plan.slots, plan.share)
        lows[e][...] = pack(low, plan.share)


def reduce_last_kernel(plan, *refs):
    groups, width = plan.groups, plan.width
    before, tag_ref, refs = refs[:groups], refs[groups], refs[groups + 1 :]
    near, wide, last, across = refs[:4]
    lows = refs[4:]
    outer = am_outer(plan)
    inner = jnp.logical_not(outer)
    first_row = plan.cross[0] * PAIR

    def padded(parts, height):
        rows = sum(part.shape[0] for part in parts)
        if rows < height:
            parts = parts + [jnp.zeros((height - rows, width), last.dtype)]
        return jnp.concatenate(parts, axis=0)

    @pl.when(outer)
    def _():
        tags = tag_ref[first_row : first_row + PAIR, :]
        rows = last[...]
        for e in range(groups):
            total = jnp.zeros((PAIR, LANES), jnp.float32)
            for first in range(0, plan.padded, LANES):
                parts = []
                for piece, count in plan.left_spans():
                    if first <= piece * PAIR < first + LANES:
                        source = of_wide(wide, piece) if e == 0 else across[e - 1][piece]
                        parts.append(source[:count, :width])
                product = product_of(rows, padded(parts, LANES))
                mask = slot_mask(tags, first, plan.left_rows, plan.slots, plan.share)
                total += jnp.where(mask, product, 0.0)
            whole = [jnp.zeros((PAIR, LANES), jnp.float32)] * plan.half
            whole[plan.cross[0]] = total
            lows[e][...] = before[e][...] + pack(jnp.concatenate(whole, axis=0), plan.share)

    @pl.when(inner)
    def _():
        if plan.last_piece is None:
            for e in range(groups):
                lows[e][...] = before[e][...]
            return
        at = plan.last_piece * PAIR
        first = at // LANES * LANES
        count = min(PAIR, plan.left_rows - at)
        parts = [jnp.zeros((at - first, width), last.dtype)] if at > first else []
        left = padded(parts + [last[:count, :]], LANES)
        for e in range(groups):
            if e == 0:
                blocks = {d: near[i].at[PAIR:] for i, d in enumerate(plan.near)}
                blocks.update({d: wide[i].at[PAIR:] for i, d in enumerate(plan.cross)})
                tags = tag_ref[...]
            else:
                blocks = {d: across[e - 1][i] for i, d in enumerate(plan.across)}
                tags = [blocks[d][:, width:] for d in range(plan.half)]
                tags = jnp.concatenate(tags, axis=0).astype(jnp.float32)
            whole = jnp.concatenate([blocks[d][:, :width] for d in range(plan.half)], axis=0)
            product = product_of(whole, left)
            mask = slot_mask(tags, first, plan.left_rows, plan.slots, plan.share)
            low = pack(jnp.where(mask, product, 0.0), plan.share)
            lows[e][...] = before[e][...] + low


def reduce_last(plan, lows, tag, near, wide, last, across):
    flat, tree = jax.tree.flatten([near, wide, last, across])
    n_head = plan.groups + 1

    def body(*refs):
        nested = jax.tree.unflatten(tree, refs[n_head : n_head + len(flat)])
        reduce_last_kernel(plan, *refs[:n_head], *nested, *refs[n_head + len(flat) :])

    shapes = [jax.ShapeDtypeStruct(a.shape, a.dtype) for a in lows]
    return pl.pallas_call(
        body,
        out_shape=shapes,
        in_specs=[VMEM] * (n_head + len(flat)),
        out_specs=[VMEM] * len(lows),
        compiler_params=params(),
        cost_estimate=pl.CostEstimate(flops=1, bytes_accessed=1, transcendentals=0),
        name="reduce_last",
    )(*lows, tag, *flat)


def blocks_call(kernel, blocks, out_shape, out_specs, scratch, flops, moved, name, extra=()):
    flat, tree = jax.tree.flatten(blocks)
    n_extra = len(extra)

    def body(*refs):
        head, rest = refs[:n_extra], refs[n_extra:]
        nested = jax.tree.unflatten(tree, rest[: len(flat)])
        kernel(*head, *nested, *rest[len(flat) :])

    return pl.pallas_call(
        body,
        out_shape=out_shape,
        in_specs=[VMEM] * n_extra + [HBM] * len(flat),
        out_specs=out_specs,
        scratch_shapes=scratch,
        compiler_params=params(),
        cost_estimate=pl.CostEstimate(flops=1, bytes_accessed=1, transcendentals=0),
        name=name,
    )(*extra, *flat)


def reduce_own(plan, near, wide, late, tags, own):
    height = plan.half * PAIR
    columns = own.shape[0]
    n_steps = 2
    dtype = own.dtype
    return blocks_call(
        functools.partial(reduce_own_kernel, plan, n_steps),
        [near, wide, late, tags, own],
        [
            jax.ShapeDtypeStruct((height * plan.rank // LANES, LANES), jnp.float32),
            jax.ShapeDtypeStruct((height, LANES), jnp.float32),
        ],
        [VMEM] * 2,
        [
            pltpu.VMEM((height, plan.width), dtype),
            pltpu.VMEM((columns, plan.width), dtype),
            pltpu.VMEM((height, columns), jnp.float32),
            pltpu.VMEM((height, LANES), dtype),
            pltpu.SemaphoreType.DMA(((n_steps + 1) * (plan.half + 1),)),
        ],
        2 * height * plan.width * columns,
        2 * plan.width * (height + columns),
        "reduce_own",
    )


def reduce_taken(plan, near, wide, late, tags, across):
    height = plan.half * PAIR
    n_steps = 2
    dtype = near[0].dtype
    groups, padded = plan.groups, plan.padded
    *lows, tag = blocks_call(
        functools.partial(reduce_taken_kernel, plan, n_steps),
        [near, wide, late, tags, across],
        [jax.ShapeDtypeStruct((height * plan.share // LANES, LANES), jnp.float32)] * groups
        + [jax.ShapeDtypeStruct((height, LANES), jnp.float32)],
        [VMEM] * (groups + 1),
        [
            pltpu.VMEM((groups, height, plan.width), dtype),
            pltpu.VMEM((groups, padded, plan.width), dtype),
            pltpu.VMEM((groups, height, padded), jnp.float32),
            pltpu.VMEM((groups, height, LANES), dtype),
            pltpu.SemaphoreType.DMA(((n_steps + 1) * groups * (plan.half + plan.left_pieces),)),
        ],
        2 * height * plan.width * groups * padded,
        2 * plan.width * (height + padded) * groups,
        "reduce_taken",
    )
    return lows, tag


def rounded(low, share):
    return unpack(low.astype(jnp.bfloat16).astype(jnp.float32), share)


def spread(low, tags, columns, slots, share):
    blocks = [
        jnp.where(slot_mask(tags, first, columns, slots, share), low, 0.0).astype(jnp.bfloat16)
        for first in range(0, columns, LANES)
    ]
    return jnp.concatenate(blocks, axis=1)


def write_deltas(delta, outs):
    delta = delta.astype(jnp.bfloat16)
    for i, out in enumerate(outs):
        out[...] = delta[i * PAIR : (i + 1) * PAIR]


def expand_own_kernel(plan, mine_ref, other_ref, tag_ref, own, *rest):
    outs, (up, sem) = rest[:-2], rest[-2:]
    copy = pltpu.make_async_copy(own, up, sem)
    copy.start()
    low = rounded(mine_ref[...] + other_ref[...], plan.rank)
    wide_low = spread(low, tag_ref[...], up.shape[0], plan.slots, plan.rank)
    copy.wait()
    write_deltas(jnp.dot(wide_low, up[...], preferred_element_type=jnp.float32), outs)


def expand_own(plan, mine, other, tag, own):
    columns, features = own.shape
    return blocks_call(
        functools.partial(expand_own_kernel, plan),
        [own],
        [jax.ShapeDtypeStruct((PAIR, features), jnp.bfloat16)] * plan.half,
        [VMEM] * plan.half,
        [pltpu.VMEM(own.shape, own.dtype), pltpu.SemaphoreType.DMA(())],
        2 * tag.shape[0] * columns * features,
        2 * features * (columns + tag.shape[0]),
        "expand_own",
        extra=(mine, other, tag),
    )


def expand_taken_kernel(plan, *refs):
    lows, tag_ref, refs = refs[: 2 * plan.groups], refs[2 * plan.groups], refs[2 * plan.groups + 1 :]
    wide, narrow, across_wide, across_narrow = refs[:4]
    outs, (up, sems) = refs[4:-2], refs[-2:]
    copies = Copies(am_outer(plan), sems)
    for row, rows, column in plan.up_columns():
        part = pl.ds(0, rows), pl.ds(column, plan.features)
        for e in range(plan.groups):
            copies.both(
                up.at[e, pl.ds(row, rows)],
                (of_wide(wide, plan.left_pieces) if e == 0 else across_wide[e - 1]).at[part],
                (narrow if e == 0 else across_narrow[e - 1]).at[part],
            )
    if plan.padded > plan.left_rows:
        up[:, plan.left_rows :, :] = jnp.zeros(
            (plan.groups, plan.padded - plan.left_rows, plan.features), up.dtype
        )
    tags = tag_ref[...]
    wides = []
    for e in range(plan.groups):
        mine, other = lows[2 * e][...], lows[2 * e + 1][...]
        low = jnp.where(am_outer(plan), mine, other) if e else mine + other
        low = rounded(low, plan.share)
        wides.append(spread(low, tags, plan.left_rows, plan.slots, plan.share))
    copies.wait()
    delta = None
    for e in range(plan.groups):
        product = jnp.dot(wides[e], up[e], preferred_element_type=jnp.float32)
        delta = product if delta is None else delta + product
    write_deltas(delta, outs)


def expand_taken(plan, lows, tag, wide, narrow, across_wide, across_narrow):
    height, features = tag.shape[0], plan.features
    return blocks_call(
        functools.partial(expand_taken_kernel, plan),
        [wide, narrow, across_wide, across_narrow],
        [jax.ShapeDtypeStruct((PAIR, features), jnp.bfloat16)] * plan.half,
        [VMEM] * plan.half,
        [
            pltpu.VMEM((plan.groups, plan.padded, features), jnp.bfloat16),
            pltpu.SemaphoreType.DMA((plan.groups * len(list(plan.up_columns())),)),
        ],
        2 * height * plan.groups * plan.padded * features,
        2 * features * (plan.groups * plan.padded + height),
        "expand_taken",
        extra=(*lows, tag),
    )


def join_kernel(order, seg_ref, base_ref, *refs):
    n = len(order)
    deltas, (out_ref, rows, sems) = refs[:n], refs[-3:]

    def parts():
        for i in range(n * CAP):
            seg = seg_ref[order[i // CAP] * CAP + i % CAP]
            span = pl.ds(pl.multiple_of(jnp.maximum(seg, 0) * SEG, SEG), SEG)
            place = pl.ds(i * SEG, SEG)
            yield i, seg, span, pltpu.make_async_copy(
                rows.at[place], out_ref.at[span], sems.at[i]
            )

    for i, seg, span, copy in parts():

        @pl.when(seg >= 0)
        def _():
            part = i % CAP
            delta = deltas[i // CAP][part * SEG : (part + 1) * SEG, :]
            total = base_ref[span, :] + delta.astype(jnp.float32)
            rows[i * SEG : (i + 1) * SEG, :] = total.astype(rows.dtype)
            copy.start()

    for _, seg, _, copy in parts():
        pl.when(seg >= 0)(copy.wait)


def join(seg_of, base, deltas, order, name, before=None):
    height, features = base.shape
    deltas = [deltas[i] for i in order]
    n = len(deltas)
    more = [] if before is None else [before]
    return pl.pallas_call(
        functools.partial(join_kernel, order),
        out_shape=jax.ShapeDtypeStruct((height, features), jnp.bfloat16),
        in_specs=[SMEM, VMEM] + [VMEM] * n + [HBM] * len(more),
        out_specs=HBM,
        scratch_shapes=[
            pltpu.VMEM((n * PAIR, features), jnp.bfloat16),
            pltpu.SemaphoreType.DMA((n * CAP,)),
        ],
        input_output_aliases={2 + n: 0} if more else {},
        compiler_params=params(),
        cost_estimate=pl.CostEstimate(
            flops=height * features, bytes_accessed=4 * height * features, transcendentals=0
        ),
        name=name,
    )(seg_of, base, *deltas, *more)


def swap(value, axis, distance):
    count = lax.axis_size(axis)
    return lax.ppermute(value, axis, [(i, i ^ distance) for i in range(count)])


def send(plan, value, moves):
    shape = (plan.groups, plan.replicas, lax.axis_size("tensor"))

    def place(g, r, c):
        return (g * shape[1] + r) * shape[2] + c

    pairs = [
        (place(g, r, c), place(g ^ flips[0], r ^ flips[1], c ^ flips[2]))
        for senders, *flips in moves
        for g in range(shape[0])
        for r in senders
        for c in range(shape[2])
    ]
    return lax.ppermute(value, ("groups", "replica", "tensor"), pairs)


def return_terms(terms):
    back = {d: swap(terms[d], "replica", d) for d in reversed(range(1, len(terms)))}
    return [back[d] for d in range(1, len(terms))]


def on_device(x, weight, lefts, ups, ids, residency):
    slots, width, rank = lefts.shape
    features = ups.shape[2]
    plan = Plan(
        lax.axis_size("replica"), lax.axis_size("groups"), slots, rank, width, features
    )
    half, n_cross = plan.half, len(plan.cross)
    core = lax.axis_index("tensor")
    outer = am_outer(plan)
    left_rows = jnp.swapaxes(lefts, 1, 2)
    near, wide, seg_of = lay_out(plan, True, ids, residency, x, left_rows, ups)
    wide, tags = wide[: plan.wide], wide[plan.wide :]

    near = [swap(block, "replica", d) for block, d in zip(near, plan.near[1:])]
    wide_in = []
    for i in range(plan.wide):
        moves = []
        if i < n_cross:
            moves.append((plan.outer, 0, plan.cross[i], 0))
        if i < plan.adapter_wide:
            moves.append((plan.inner, 0, half, 0))
        wide_in.append(send(plan, wide[i], moves))

    late_ids, _ = lax.optimization_barrier((ids, seg_of))
    near, late_x = lax.optimization_barrier((near, x))
    own_rows, late, _ = lay_out(plan, False, late_ids, residency, x, left_rows, ups)
    near = own_rows + near
    def part(which, rows):
        columns = lax.dynamic_slice(weight, (0, which * features), (weight.shape[0], features))
        return jnp.dot(rows, columns, preferred_element_type=jnp.float32)

    base_other, base_mine = part(1 - core, late_x), part(core, late_x)

    def across_send(i):
        d = plan.across[i]
        if d in plan.near:
            block = near[plan.near.index(d)][PAIR:]
            value, tag = block[:, :width], block[:, width:]
        else:
            j = plan.cross.index(d)
            value, tag = wide_in[j][PAIR:], tags_in[j][PAIR:]
        if i < plan.pieces:
            piece = wide_in[i // 2][(i % 2) * PAIR : (i % 2 + 1) * PAIR]
            value = jnp.where(outer, piece, value)
        value = jnp.concatenate([value, tag], axis=1)
        return [
            send(plan, value, [(plan.outer, e, 0, 0), (plan.inner, e, 0, 0)])
            for e in range(1, plan.groups)
        ]

    across = [across_send(0), across_send(1)]
    tags_in = [swap(tag, "replica", d) for tag, d in zip(tags, plan.cross)]

    wide_in[0], near, across[0], late, base_other, base_mine = lax.optimization_barrier(
        (wide_in[0], near, across[0], late, base_other, base_mine)
    )
    late_in = []
    for unit, d in enumerate(plan.late_blocks()):
        moves = [(plan.inner, 0, d, 0)]
        if unit < plan.pieces:
            moves.append((plan.outer, 0, half, 0))
        block = late[unit]
        if unit == 1:
            near, wide_in, tags_in, block = lax.optimization_barrier(
                (near, wide_in, tags_in, block)
            )
        elif unit == 2:
            late_in[0], wide_in, tags_in, block, base_other = lax.optimization_barrier(
                (late_in[0], wide_in, tags_in, block, base_other)
            )
        elif unit > 2:
            late_in[unit - 2], block = lax.optimization_barrier((late_in[unit - 2], block))
        late_in.append(send(plan, block, moves))
    across += [across_send(i) for i in range(2, half)]
    late_up = late_in[0][: plan.up_rows]
    across_up = [send(plan, late_up, [(plan.inner, e, 0, 0)]) for e in range(1, plan.groups)]
    base = base_mine + swap(base_other, "tensor", 1)
    late_in[:n_cross], across[:-1] = lax.optimization_barrier((late_in[:n_cross], across[:-1]))
    across = [[blocks[e] for blocks in across] for e in range(plan.groups - 1)]

    own_left = left_rows.reshape(slots * rank, width)
    low, tag = reduce_own(plan, near, wide_in, late_in[:n_cross], tags_in, own_left)
    other = swap(low, "tensor", 1)
    terms = expand_own(plan, low, other, tag, ups.reshape(slots * rank, features))
    deltas = [terms[0]] + return_terms(terms)

    lows, tag = reduce_taken(plan, near, wide_in, late_in[:-1], tags_in, across)
    late_in[-1], deltas[:2], lows, base = lax.optimization_barrier(
        (late_in[-1], deltas[:2], lows, base)
    )
    lows = reduce_last(plan, lows, tag, near, wide_in, late_in[-1], across)
    pairs = []
    for e in range(plan.groups):
        other = swap(lows[e], "tensor", 1)
        if e:
            total = lows[e] + other
            pairs += [total, swap(total, "groups", e)]
        else:
            pairs += [lows[e], other]
    pairs, deltas = lax.optimization_barrier((pairs, deltas))
    across_wide = [blocks[plan.left_pieces] for blocks in across]
    terms = expand_taken(plan, pairs, tag, wide_in, late_in[0], across_wide, across_up)
    deltas += [terms[0]] + return_terms(terms)
    own = [d for d in plan.cross + plan.near] + [half]
    rows = join(seg_of, base, deltas, own, "join_own")
    rows = join(seg_of, base, deltas, [half + d for d in plan.cross[::-1]], "join_cross", rows)
    last = [half + d for d in plan.near if d]
    return join(seg_of, base, deltas, last, "join_near", rows)


def solution(mesh):
    placed = (
        P(("groups", "replica"), "tensor"),
        P("tensor", None),
        P("replica", "tensor", None),
        P("replica", None, "tensor"),
        P(("groups", "replica")),
        P(),
    )
    return jax.shard_map(
        on_device,
        mesh=mesh,
        in_specs=placed,
        out_specs=P(("groups", "replica"), "tensor"),
        check_vma=False,
    )
```
